32 devices in a mesh: index: 16 (over z, y, x), query: 2 (over core).
Axes of the slice: x: 2, y: 2, z: 4, core: 2. Of those that a mesh axis runs over, the one named last changes fastest.
Arguments:
- table: bfloat16 [8192, 768], P('index'), may hold values from -150 to 150, as said below
- ages: int32 [8192], P('index'), may hold values from 0 to 63
- refresh_ids: int32 [4096], P('index'), may hold values from 0 to 8191, as said below
- fresh_rows: bfloat16 [4096, 768], P('index'), may hold values from -150 to 150, as said below
- neg_ids: int32 [16, 2048], P('index'), may hold values from 0 to 8191, as said below
- queries: bfloat16 [8192, 768], P(('index', 'query')), may hold values from -150 to 150, as said below
- pos_ids: int32 [8192], P(('index', 'query')), may hold values from 0 to 8191, as said below
Outputs:
- new_table: bfloat16 [8192, 768], P('index')
- new_ages: int32 [8192], P('index')
- loss: float32 [8192], P(('index', 'query'))
The draws below stay inside these ranges and needn't reach their ends.
Inputs may be any that keep to these rules, and one draw needn't show every extreme that they name: `refresh_ids`: all ids are distinct. Owner o holds rows o * 512 to (o + 1) * 512 - 1; at most 32 of the 256 ids of one refresher fall in one owner's rows, and in every draw some owner receives exactly 32 from every refresher. `neg_ids`: the 2048 ids of one list are distinct; at most 256 of them fall in one owner's block of 512 rows, and in every draw some owner receives exactly 256 from every list. `pos_ids`: the positive of query i is one of the ids of list i // 512. `table`: Real-valued embeddings. `fresh_rows`: Real-valued embeddings. `queries`: Real-valued embeddings.
All inputs are finite; a program needn't handle non-finite values.
Results may differ from the reference program's by a relative error of at most 0.001.
Values may be sent and summed in bfloat16 or wider, within the bound.
No kernel may reach another device: no remote copies, remote signals or barrier semaphores. Data moves between devices by JAX's collectives and lax.ppermute only.
A program may use at most 64 MiB of HBM per device.

```python
import math
import jax
import jax.numpy as jnp
from jax import lax

D = 768
ROWS_DEV = 512
REF_DEV = 256
NEG = 2048
GROUPS = 16
CAP = 32
GQ = 512
CAPN = 256
ROWS = 8192
REFRESH = 4096
QUERIES = 8192


def column_scale(key):
    col_key = jax.random.fold_in(key, 30)
    return jnp.exp(jax.random.uniform(col_key, (1, D), jnp.float32, 0.0, math.log(10.0)))


def embedding_base(key, row_count):
    key_base, key_rows = jax.random.split(key, 2)
    base = jnp.clip(jax.random.normal(key_base, (row_count, D), jnp.float32), -5.0, 5.0)
    row_scale = jnp.exp(jax.random.uniform(key_rows, (row_count, 1), jnp.float32, 0.0, math.log(10.0)))
    return (base, row_scale)


def embedding_draw(key, salt, row_count):
    base, row_scale = embedding_base(jax.random.fold_in(key, salt), row_count)
    return (0.3 * base * row_scale * column_scale(key)).astype(jnp.bfloat16)


def slot_draw(key, list_count, owner_count, capacity, pick_count):
    key_hot, key_one, key_level, key_noise = jax.random.split(key, 4)
    slot_count = owner_count * capacity
    owner_of = jnp.arange(slot_count, dtype=jnp.int32) // capacity
    hot_all = jax.random.randint(key_hot, (), 0, owner_count)
    hot_one = jax.random.randint(key_one, (list_count, 1), 0, owner_count)
    levels = jax.random.randint(key_level, (list_count, owner_count), 0, 4)
    level_slot = jnp.take(levels, owner_of, axis=1)
    forced = (owner_of[None, :] == hot_all) | (owner_of[None, :] == hot_one)
    level_slot = jnp.where(forced, 8, level_slot)
    noise = jax.random.randint(key_noise, (list_count, slot_count), 0, 4096)
    priority = (level_slot * 4096 + noise) * slot_count + jnp.arange(slot_count, dtype=jnp.int32)[None, :]
    unused, chosen = lax.top_k(priority, pick_count)
    return chosen.astype(jnp.int32)


def shuffle_rows(key, values, length):
    orders = jax.vmap(lambda one_key: jax.random.permutation(one_key, length))(jax.random.split(key, values.shape[0]))
    return jnp.take_along_axis(values, orders, axis=1)


def negative_lists(key):
    chosen = slot_draw(jax.random.fold_in(key, 1), GROUPS, GROUPS, CAPN, NEG)
    perm_keys = jax.random.split(jax.random.fold_in(key, 2), GROUPS * GROUPS)
    perms = jax.vmap(lambda one_key: jax.random.permutation(one_key, ROWS_DEV)[:CAPN])(perm_keys)
    perms = perms.reshape(GROUPS, GROUPS * CAPN).astype(jnp.int32)
    local_row = jnp.take_along_axis(perms, chosen, axis=1)
    list_ids = chosen // CAPN * ROWS_DEV + local_row
    return shuffle_rows(jax.random.fold_in(key, 3), list_ids, NEG).astype(jnp.int32)


def positive_lists(key):
    lists = negative_lists(jax.random.fold_in(key, 11))
    choose = jax.random.randint(jax.random.fold_in(key, 12), (GROUPS, GQ), 0, NEG)
    return (lists, jnp.take_along_axis(lists, choose, axis=1).astype(jnp.int32))


def draw_table(key, part):
    return embedding_draw(key, 31, ROWS)


def draw_fresh_rows(key, part):
    return embedding_draw(key, 32, REFRESH)


def draw_refresh_ids(key, part):
    chosen = slot_draw(jax.random.fold_in(key, 21), GROUPS, GROUPS, CAP, REF_DEV)
    owner_of = chosen // CAP
    slot_rank = chosen - owner_of * CAP
    perms = jax.vmap(lambda one_key: jax.random.permutation(one_key, ROWS_DEV))(jax.random.split(jax.random.fold_in(key, 22), GROUPS)).astype(jnp.int32)
    position = jnp.arange(GROUPS, dtype=jnp.int32)[:, None] * CAP + slot_rank
    local_row = perms[owner_of, position]
    refresh_list = owner_of * ROWS_DEV + local_row
    refresh_list = shuffle_rows(jax.random.fold_in(key, 23), refresh_list, REF_DEV)
    return refresh_list.reshape(REFRESH).astype(jnp.int32)


def draw_neg_ids(key, part):
    return negative_lists(jax.random.fold_in(key, 11))


def draw_pos_ids(key, part):
    lists, positive = positive_lists(key)
    return positive.reshape(QUERIES).astype(jnp.int32)


def draw_queries(key, part):
    base_table, unused_rows = embedding_base(jax.random.fold_in(key, 31), ROWS)
    base_fresh, unused_fresh = embedding_base(jax.random.fold_in(key, 32), REFRESH)
    refresh_list = draw_refresh_ids(key, part)
    base_new = base_table.at[refresh_list].set(base_fresh)
    lists, positive = positive_lists(key)
    others = jax.random.randint(jax.random.fold_in(key, 34), (GROUPS, GQ * 2), 0, NEG)
    other_ids = jnp.take_along_axis(lists, others, axis=1).reshape(QUERIES, 2)
    first_ids = positive.reshape(QUERIES)
    coeff = jax.random.uniform(jax.random.fold_in(key, 35), (QUERIES, 3), jnp.float32, 0.4, 1.0)
    mixed = coeff[:, 0:1] * base_new[first_ids]
    mixed = mixed + coeff[:, 1:2] * base_new[other_ids[:, 0]]
    mixed = mixed + coeff[:, 2:3] * base_new[other_ids[:, 1]]
    noise = jnp.clip(jax.random.normal(jax.random.fold_in(key, 36), (QUERIES, D), jnp.float32), -5.0, 5.0)
    query_row = jnp.exp(jax.random.uniform(jax.random.fold_in(key, 37), (QUERIES, 1), jnp.float32, 0.0, math.log(10.0)))
    return (0.08 * query_row * (mixed + 0.4 * noise) * column_scale(key)).astype(jnp.bfloat16)


def place_ends(entries, stream_key, least, high):
    longest = entries.shape.index(max(entries.shape))
    spots = []
    for shift in (0, 1):
        where = [jax.random.randint(jax.random.fold_in(stream_key, axis), (), 0, length) for axis, length in enumerate(entries.shape)]
        where[longest] = (where[longest] + shift) % entries.shape[longest]
        spots.append(tuple(where))
    return entries.at[spots[0]].set(least).at[spots[1]].set(high)


def setup_inputs(seed: int = 0) -> dict:
    arg_keys = jax.random.split(jax.random.key(seed), 8)
    return {
        "table": draw_table(jax.random.fold_in(arg_keys[7], 71), 0),
        "ages": place_ends(jax.random.randint(arg_keys[1], (ROWS,), 0, 64), jax.random.fold_in(arg_keys[1], 1), 0, 63).astype(jnp.int32),
        "refresh_ids": draw_refresh_ids(jax.random.fold_in(arg_keys[7], 71), 0),
        "fresh_rows": draw_fresh_rows(jax.random.fold_in(arg_keys[7], 71), 0),
        "neg_ids": draw_neg_ids(jax.random.fold_in(arg_keys[7], 71), 0),
        "queries": draw_queries(jax.random.fold_in(arg_keys[7], 71), 0),
        "pos_ids": draw_pos_ids(jax.random.fold_in(arg_keys[7], 71), 0),
    }


score_scale = 20.0
age_scale = 16.0
epsilon = 1e-06

def inverse_norm(matrix):
    values = matrix.astype(jnp.float32)
    squares = lax.optimization_barrier(jnp.sum(values * values, axis=-1))
    return lax.rsqrt(squares / matrix.shape[-1] + epsilon)

def reference(table, ages, refresh_ids, fresh_rows, neg_ids, queries, pos_ids):
    new_table = table.at[refresh_ids].set(fresh_rows)
    new_ages = ages.at[refresh_ids].set(0)
    group_count = neg_ids.shape[0]
    grouped_queries = queries.reshape(group_count, -1, D)
    grouped_positive = pos_ids.reshape(group_count, -1)

    def one_group(inputs):
        list_ids, query_group, positive_group = inputs
        picked_rows = new_table[list_ids]
        rounded = jnp.exp(-new_ages[list_ids].astype(jnp.float32) / age_scale).astype(jnp.bfloat16)
        rounded = lax.optimization_barrier(rounded)
        weights = rounded.astype(jnp.float32)
        raw_product = jnp.dot(query_group, picked_rows.T, preferred_element_type=jnp.float32)
        scores = raw_product * (score_scale / D) * inverse_norm(query_group)[:, None] * inverse_norm(picked_rows)[None, :]
        weighted = lax.optimization_barrier(jnp.sum(weights[None, :] * jnp.exp(scores), axis=1))
        is_positive = list_ids[None, :] == positive_group[:, None]
        positive_score = lax.optimization_barrier(jnp.sum(jnp.where(is_positive, scores, 0.0), axis=1))
        positive_weight = lax.optimization_barrier(jnp.sum(jnp.where(is_positive, weights[None, :], 0.0), axis=1))
        return jnp.log(weighted) - positive_score - jnp.log(positive_weight)
    losses = lax.map(one_group, (neg_ids, grouped_queries, grouped_positive))
    return (new_table, new_ages, losses.reshape(-1))
```

```python
import functools
import math

import jax
import jax.numpy as jnp
from jax import lax
from jax.experimental import pallas as pl
from jax.experimental.pallas import tpu as pltpu
from jax.sharding import Mesh, PartitionSpec as P

score_scale = 20.0
age_scale = 16.0
epsilon = 1e-06
LOG2E = math.log2(math.e)
MASKED = -1e30
LANES = 128
VMEM_LIMIT = 48 * 1024 * 1024

NT = (((1,), (1,)), ((), ()))
NN = (((1,), (0,)), ((), ()))


def one_hot(ids, count):
    rows = lax.broadcasted_iota(jnp.int32, (count, ids.shape[1]), 0)
    return jnp.where(rows == ids, 1.0, 0.0).astype(jnp.bfloat16)


def split_one_hot(ids, high_count):
    return one_hot(ids >> 7, high_count), one_hot(ids & 127, LANES)


def bitmap(ids, high_count):
    high, low = split_one_hot(ids, high_count)
    return lax.dot_general(low, high, NT, preferred_element_type=jnp.float32)


def meta_kernel(
    place, ref_ids, neg, log_weight, lw_out, row_out, pack_out, apply_out, own_out, *, rows_dev, cap, replicas
):
    outer, inner, core = place[0], place[1], place[2]
    planes, plane_refresh = ref_ids.shape
    plane_rows = log_weight.shape[1]
    owners_plane = plane_rows // rows_dev
    high_count = planes * plane_rows // LANES
    plane_ids = ref_ids[pl.ds(outer, 1), :]
    table_ids = outer * plane_rows + lax.broadcasted_iota(jnp.int32, (1, plane_rows), 1)

    refreshed_map = jnp.zeros((LANES, high_count), jnp.float32)
    for plane in range(planes):
        refreshed_map += bitmap(ref_ids[plane : plane + 1, :], high_count)
    refreshed_map = refreshed_map.astype(jnp.bfloat16)

    table_high, table_low = split_one_hot(table_ids, high_count)
    fresh_high, fresh_low = split_one_hot(plane_ids, high_count)

    def lookup(one_map, high, low):
        hit = lax.dot_general(one_map, high, NN, preferred_element_type=jnp.float32)
        return jnp.sum(hit * low.astype(jnp.float32), axis=0, keepdims=True)

    refreshed = lookup(refreshed_map, table_high, table_low) > 0.5
    row_out[:, :plane_rows] = jnp.where(refreshed, -1, table_ids).astype(jnp.float32)
    row_out[:, plane_rows:] = plane_ids.astype(jnp.float32)
    own_ids = (outer * owners_plane + inner) * rows_dev + lax.broadcasted_iota(jnp.int32, (1, rows_dev), 1)
    own_out[...] = (lookup(refreshed_map, *split_one_hot(own_ids, high_count)) > 0.5).astype(jnp.int32)

    for group in range(planes):
        one_map = bitmap(neg[group : group + 1, :], high_count).astype(jnp.bfloat16)
        in_list = lookup(one_map, table_high, table_low) > 0.5
        lw_out[group : group + 1, :plane_rows] = jnp.where(in_list & ~refreshed, log_weight[...], MASKED)
        in_list = lookup(one_map, fresh_high, fresh_low) > 0.5
        lw_out[group : group + 1, plane_rows:] = jnp.where(in_list, 0.0, MASKED)

    share = cap // replicas
    earlier = jnp.where(
        lax.broadcasted_iota(jnp.int32, (plane_refresh, plane_refresh), 0)
        < lax.broadcasted_iota(jnp.int32, (plane_refresh, plane_refresh), 1),
        1.0,
        0.0,
    ).astype(jnp.bfloat16)
    plane_owner = plane_ids // rows_dev
    target_plane = lax.broadcasted_iota(jnp.int32, (planes, plane_refresh), 0)
    send_match = plane_owner == target_plane * owners_plane + inner
    take_match = (ref_ids[...] // rows_dev) == outer * owners_plane + inner

    def ranked(match):
        ones = jnp.where(match, 1.0, 0.0)
        rank = lax.dot_general(ones.astype(jnp.bfloat16), earlier, NN, preferred_element_type=jnp.float32)
        return jnp.where(match, rank.astype(jnp.int32), -1)

    send_rank = ranked(send_match) - core * share
    send_rank = jnp.where(send_match, send_rank, -1)
    take_rank = ranked(take_match)
    take_row = ref_ids[...] - (outer * owners_plane + inner) * rows_dev
    for plane in range(planes):
        pack_out[plane * share : (plane + 1) * share, :] = one_hot(send_rank[plane : plane + 1, :], share)
        slot = one_hot(take_rank[plane : plane + 1, :], cap)
        row = one_hot(take_row[plane : plane + 1, :], rows_dev)
        where_to = lax.dot_general(row, slot, NT, preferred_element_type=jnp.float32)
        for replica in range(replicas):
            first = (replica * planes + plane) * share
            apply_out[:, first : first + share] = where_to[:, replica * share : (replica + 1) * share]


def pack_kernel(select, rows, out):
    out[...] = lax.dot_general(select[...], rows[...], NN, preferred_element_type=jnp.float32).astype(jnp.bfloat16)


def apply_kernel(select, arrived, table, out):
    chosen = select[...]
    fresh = lax.dot_general(chosen.astype(jnp.bfloat16), arrived[...], NN, preferred_element_type=jnp.float32)
    hit = jnp.sum(chosen, axis=1, keepdims=True) > 0.5
    out[...] = jnp.where(hit, fresh, table[...].astype(jnp.float32)).astype(jnp.bfloat16)


def to_lanes(row):
    return jnp.broadcast_to(row, (LANES, LANES)).T


def score_kernel(
    queries, table, fresh, log_weight, row_ids, scale, positive, out, q_scale, pos_b, total, pos_total, *, table_steps, groups
):
    step = pl.program_id(0)
    count, width = queries.shape
    per_group = count // groups

    @pl.when(step == 0)
    def _():
        for block in range(count // LANES):
            part = pl.ds(block * LANES, LANES)
            values = queries[part, :].astype(jnp.float32)
            squares = jnp.sum(values * values, axis=1, keepdims=True)
            q_scale[part, :] = jnp.broadcast_to(lax.rsqrt(squares / width + epsilon), (LANES, LANES))
            pos_b[part, :] = to_lanes(positive[block : block + 1, :])
        total[...] = jnp.zeros_like(total)
        pos_total[...] = jnp.zeros_like(pos_total)

    def add(rows):
        block = rows.shape[0]
        for group in range(groups):
            part = pl.ds(group * per_group, per_group)
            raw = lax.dot_general(queries[part, :], rows[...], NT, preferred_element_type=jnp.float32)
            sums = total[part, :]
            positives = pos_total[part, :]
            for chunk in range(block // LANES):
                cols = slice(chunk * LANES, (chunk + 1) * LANES)
                powers = raw[:, cols] * q_scale[part, :] * scale[:, cols] + log_weight[group : group + 1, cols]
                sums = sums + jnp.exp2(powers)
                positives = positives + jnp.where(pos_b[part, :] == row_ids[:, cols], powers, 0.0)
            total[part, :] = sums
            pos_total[part, :] = positives

    @pl.when(step < table_steps)
    def _():
        add(table)

    @pl.when(step >= table_steps)
    def _():
        add(fresh)

    @pl.when(step == pl.num_programs(0) - 1)
    def _():
        for block in range(count // LANES):
            part = pl.ds(block * LANES, LANES)
            out[0, block : block + 1, :] = jnp.sum(total[part, :].T, axis=0, keepdims=True)
            out[1, block : block + 1, :] = jnp.sum(pos_total[part, :].T, axis=0, keepdims=True)


def whole(memory=pltpu.VMEM):
    return pl.BlockSpec(memory_space=memory)


def params():
    return pltpu.CompilerParams(vmem_limit_bytes=VMEM_LIMIT)


def on_device(table, ages, refresh_ids, fresh_rows, neg_ids, queries, pos_ids):
    rows_dev, width = table.shape
    refresh_dev = refresh_ids.shape[0]
    planes = lax.axis_size("outer")
    owners_plane = lax.axis_size("inner")
    replicas = lax.axis_size("query")
    owners = planes * owners_plane
    query_count = queries.shape[0]
    list_size = neg_ids.shape[1]
    outer, inner, core = lax.axis_index("outer"), lax.axis_index("inner"), lax.axis_index("query")
    plane_rows = owners_plane * rows_dev
    plane_refresh = owners_plane * refresh_dev
    cap = owners_plane * max(2, (2 * refresh_dev + owners - 1) // owners)

    table_half = lax.dynamic_slice_in_dim(table, core * (rows_dev // replicas), rows_dev // replicas, 0)
    fresh_half = lax.dynamic_slice_in_dim(fresh_rows, core * (refresh_dev // replicas), refresh_dev // replicas, 0)
    fresh_plane = lax.all_gather(fresh_half, ("inner", "query"), axis=0, tiled=True)
    table_plane = lax.all_gather(table_half, ("inner", "query"), axis=0, tiled=True)
    queries_line = lax.all_gather(queries, "outer", axis=0, tiled=True)

    def row_scale(rows):
        values = rows.astype(jnp.float32)
        squares = jnp.sum(values * values, axis=1)
        return lax.rsqrt(squares / width + epsilon) * (score_scale / width * LOG2E)

    weight = jnp.exp(-ages.astype(jnp.float32) / age_scale).astype(jnp.bfloat16).astype(jnp.float32)
    meta = jnp.concatenate(
        [
            refresh_ids.astype(jnp.float32),
            neg_ids[0].astype(jnp.float32),
            pos_ids.astype(jnp.float32),
            jnp.log2(weight),
            row_scale(table),
            row_scale(fresh_rows),
        ]
    )
    meta_all = lax.all_gather(meta, ("outer", "inner"), axis=0).reshape(planes, owners_plane, -1)
    cuts = [refresh_dev, list_size, query_count, rows_dev, rows_dev, refresh_dev]
    ends = [sum(cuts[: i + 1]) for i in range(len(cuts))]

    def piece(values, i):
        return values[..., ends[i] - cuts[i] : ends[i]]

    line = lax.dynamic_index_in_dim(meta_all, inner, 1, keepdims=False)
    plane = lax.dynamic_index_in_dim(meta_all, outer, 0, keepdims=False)
    ref_all = piece(meta_all, 0).reshape(planes, plane_refresh).astype(jnp.int32)
    neg_line = piece(line, 1).astype(jnp.int32)
    positive = piece(line, 2).reshape(-1, LANES)
    log_weight_plane = piece(plane, 3).reshape(1, plane_rows)
    scale_plane = jnp.concatenate([piece(plane, 4).reshape(1, -1), piece(plane, 5).reshape(1, -1)], axis=1)

    share = cap // replicas
    all_rows = plane_rows + plane_refresh
    lw, row_ids, pack, apply_to, own = pl.pallas_call(
        functools.partial(meta_kernel, rows_dev=rows_dev, cap=cap, replicas=replicas),
        out_shape=(
            jax.ShapeDtypeStruct((planes, all_rows), jnp.float32),
            jax.ShapeDtypeStruct((1, all_rows), jnp.float32),
            jax.ShapeDtypeStruct((planes * share, plane_refresh), jnp.bfloat16),
            jax.ShapeDtypeStruct((rows_dev, planes * cap), jnp.float32),
            jax.ShapeDtypeStruct((1, rows_dev), jnp.int32),
        ),
        in_specs=[whole(pltpu.SMEM)] + [whole()] * 3,
        out_specs=[whole()] * 5,
        compiler_params=params(),
        name="meta",
    )(jnp.stack([outer, inner, core]).astype(jnp.int32), ref_all, neg_line, log_weight_plane)
    new_ages = jnp.where(own.reshape(rows_dev) > 0, 0, ages)

    packed = pl.pallas_call(
        pack_kernel,
        out_shape=jax.ShapeDtypeStruct((planes * share, width), jnp.bfloat16),
        in_specs=[whole()] * 2,
        out_specs=whole(),
        compiler_params=params(),
        name="pack",
    )(pack, fresh_plane)
    arrived = lax.all_to_all(packed.reshape(planes, share, width), "outer", split_axis=0, concat_axis=0, tiled=True)
    arrived = lax.all_gather(arrived.reshape(planes * share, width), "query", axis=0, tiled=True)
    new_table = pl.pallas_call(
        apply_kernel,
        out_shape=jax.ShapeDtypeStruct(table.shape, jnp.bfloat16),
        in_specs=[whole()] * 3,
        out_specs=whole(),
        compiler_params=params(),
        name="apply",
    )(apply_to, arrived, table)

    block = min(512, plane_refresh)
    table_steps, fresh_steps = plane_rows // block, plane_refresh // block
    all_queries = planes * query_count
    partial = pl.pallas_call(
        functools.partial(score_kernel, table_steps=table_steps, groups=planes),
        out_shape=jax.ShapeDtypeStruct((2, all_queries // LANES, LANES), jnp.float32),
        grid=(table_steps + fresh_steps,),
        in_specs=[
            pl.BlockSpec((all_queries, width), lambda i: (0, 0)),
            pl.BlockSpec((block, width), lambda i: (jnp.minimum(i, table_steps - 1), 0)),
            pl.BlockSpec((block, width), lambda i: (jnp.maximum(i - table_steps, 0), 0)),
            pl.BlockSpec((planes, block), lambda i: (0, i)),
            pl.BlockSpec((1, block), lambda i: (0, i)),
            pl.BlockSpec((1, block), lambda i: (0, i)),
            pl.BlockSpec((all_queries // LANES, LANES), lambda i: (0, 0)),
        ],
        out_specs=pl.BlockSpec((2, all_queries // LANES, LANES), lambda i: (0, 0, 0)),
        scratch_shapes=[pltpu.VMEM((all_queries, LANES), jnp.float32)] * 4,
        compiler_params=params(),
        name="score",
    )(queries_line, table_plane, fresh_plane, lw, row_ids, scale_plane, positive)

    partial = partial.reshape(2, planes, query_count)
    mine = lax.dynamic_index_in_dim(partial, outer, 1, keepdims=False)
    for shift in range(1, planes):
        target = lax.rem(outer + shift, planes)
        sent = lax.dynamic_index_in_dim(partial, target, 1, keepdims=False)
        mine = mine + lax.ppermute(sent, "outer", [(i, (i + shift) % planes) for i in range(planes)])
    loss = (jnp.log2(mine[0]) - mine[1]) * math.log(2.0)
    return new_table, new_ages, loss


def solution(mesh):
    owners, replicas = mesh.shape["index"], mesh.shape["query"]
    inner = 1 << (int(math.log2(owners)) // 2)
    split = Mesh(mesh.devices.reshape(owners // inner, inner, replicas), ("outer", "inner", "query"))
    index = ("outer", "inner")
    placed = (
        P(index, None),
        P(index),
        P(index),
        P(index, None),
        P(index, None),
        P(("outer", "inner", "query"), None),
        P(("outer", "inner", "query")),
    )
    return jax.shard_map(
        on_device,
        mesh=split,
        in_specs=placed,
        out_specs=(P(index, None), P(index), P(("outer", "inner", "query"))),
        check_vma=False,
    )
```

```python
import functools
import math

import jax
import jax.numpy as jnp
from jax import lax
from jax.experimental import pallas as pl
from jax.experimental.pallas import tpu as pltpu
from jax.sharding import Mesh, PartitionSpec as P

score_scale = 20.0
age_scale = 16.0
epsilon = 1e-06
LOG2E = math.log2(math.e)
MASKED = -1e30
LANES = 128
VMEM_LIMIT = 48 * 1024 * 1024

NT = (((1,), (1,)), ((), ()))
NN = (((1,), (0,)), ((), ()))


def one_hot(ids, count):
    rows = lax.broadcasted_iota(jnp.int32, (count, ids.shape[1]), 0)
    return jnp.where(rows == ids, 1.0, 0.0).astype(jnp.bfloat16)


def split_one_hot(ids, high_count):
    return one_hot(ids >> 7, high_count), one_hot(ids & 127, LANES)


def bitmap(ids, high_count):
    high, low = split_one_hot(ids, high_count)
    return lax.dot_general(low, high, NT, preferred_element_type=jnp.float32)


def prep_kernel(place, table, fresh, ages, ref_ids, rows_out, meta_out, *, replicas):
    core = place[2]
    row = 0
    for source in (table, fresh):
        half = source.shape[0] // replicas
        rows_out[row : row + half, :] = source[pl.ds(pl.multiple_of(core * half, half), half), :]
        row += half
    width = table.shape[1]
    ref_rows, age_rows = ref_ids.shape[0], ages.shape[0]
    meta_out[:ref_rows, :] = ref_ids[...].astype(jnp.float32)
    weight = jnp.exp(-ages[...].astype(jnp.float32) / age_scale).astype(jnp.bfloat16).astype(jnp.float32)
    meta_out[ref_rows : ref_rows + age_rows, :] = jnp.log2(weight)
    line = ref_rows + age_rows
    for source in (table, fresh):
        for block in range(source.shape[0] // LANES):
            squares = jnp.zeros((LANES, LANES), jnp.float32)
            for chunk in range(width // LANES):
                values = source[block * LANES : (block + 1) * LANES, chunk * LANES : (chunk + 1) * LANES]
                values = values.astype(jnp.float32)
                squares += values * values
            mean = jnp.sum(squares.T, axis=0, keepdims=True) / width
            meta_out[line : line + 1, :] = lax.rsqrt(mean + epsilon) * (score_scale / width * LOG2E)
            line += 1


def meta_kernel(
    place, ref_ids, neg, log_weight, lw_out, row_out, pack_out, apply_out, own_out, *, rows_dev, refresh_dev, cap, replicas
):
    outer, inner, core = place[0], place[1], place[2]
    planes, plane_refresh = ref_ids.shape
    plane_rows = log_weight.shape[1]
    owners_plane = plane_rows // rows_dev
    high_count = planes * plane_rows // LANES
    own_owner = outer * owners_plane + inner
    plane_ids = ref_ids[0:1, :]
    column = lax.broadcasted_iota(jnp.int32, (1, plane_rows), 1)
    table_ids = (outer * owners_plane + (inner ^ (column // rows_dev))) * rows_dev + column % rows_dev

    refreshed_map = jnp.zeros((LANES, high_count), jnp.float32)
    for plane in range(planes):
        refreshed_map += bitmap(ref_ids[plane : plane + 1, :], high_count)
    refreshed_map = refreshed_map.astype(jnp.bfloat16)

    table_high, table_low = split_one_hot(table_ids, high_count)
    fresh_high, fresh_low = split_one_hot(plane_ids, high_count)

    def lookup(one_map, high, low):
        hit = lax.dot_general(one_map, high, NN, preferred_element_type=jnp.float32)
        return jnp.sum(hit * low.astype(jnp.float32), axis=0, keepdims=True)

    refreshed = lookup(refreshed_map, table_high, table_low) > 0.5
    row_out[:, :plane_rows] = jnp.where(refreshed, -1, table_ids).astype(jnp.float32)
    row_out[:, plane_rows:] = plane_ids.astype(jnp.float32)
    own_out[...] = refreshed[:, :rows_dev].astype(jnp.int32)

    for group in range(planes):
        one_map = bitmap(neg[group : group + 1, :], high_count).astype(jnp.bfloat16)
        in_list = lookup(one_map, table_high, table_low) > 0.5
        lw_out[group : group + 1, :plane_rows] = jnp.where(in_list & ~refreshed, log_weight[...], MASKED)
        in_list = lookup(one_map, fresh_high, fresh_low) > 0.5
        lw_out[group : group + 1, plane_rows:] = jnp.where(in_list, 0.0, MASKED)

    share = cap // replicas
    earlier = jnp.where(
        lax.broadcasted_iota(jnp.int32, (plane_refresh, plane_refresh), 0)
        < lax.broadcasted_iota(jnp.int32, (plane_refresh, plane_refresh), 1),
        1.0,
        0.0,
    ).astype(jnp.bfloat16)
    target_plane = outer ^ lax.broadcasted_iota(jnp.int32, (planes, plane_refresh), 0)
    send_match = plane_ids // rows_dev == target_plane * owners_plane + inner
    take_match = ref_ids[...] // rows_dev == own_owner

    def ranked(match):
        ones = jnp.where(match, 1.0, 0.0)
        rank = lax.dot_general(ones.astype(jnp.bfloat16), earlier, NN, preferred_element_type=jnp.float32)
        return jnp.where(match, rank.astype(jnp.int32), -cap)

    send_rank, take_rank = ranked(send_match), ranked(take_match)
    take_row = ref_ids[...] - own_owner * rows_dev
    pack_out[:cap, :] = one_hot(send_rank[0:1, :], cap)
    for plane in range(1, planes):
        first = cap + (plane - 1) * share
        pack_out[first : first + share, :] = one_hot(send_rank[plane : plane + 1, :] - core * share, share)
    for plane in range(planes):
        row = one_hot(take_row[plane : plane + 1, :], rows_dev)
        for part in range(1 if plane == 0 else replicas):
            size = cap if plane == 0 else share
            skip = 0 if plane == 0 else (core ^ part) * share
            slot = one_hot(take_rank[plane : plane + 1, :] - skip, size)
            first = plane * cap + part * share
            apply_out[:, first : first + size] = lax.dot_general(row, slot, NT, preferred_element_type=jnp.float32)


def piece_offset(place, piece):
    column, size, flip = piece
    if flip is None:
        return column
    return pl.multiple_of(column + (place[2] ^ flip) * size, size)


def pack_kernel(place, select, *refs, pieces):
    out = refs[-1]
    total = jnp.zeros(out.shape, jnp.float32)
    for source, start, size, column in pieces:
        columns = pl.ds(piece_offset(place, column), size)
        total += lax.dot_general(
            select[:, columns], refs[source][start : start + size, :], NN, preferred_element_type=jnp.float32
        )
    out[...] = total.astype(jnp.bfloat16)


def apply_kernel(select, table, *refs):
    out = refs[-1]
    fresh = jnp.zeros(out.shape, jnp.float32)
    first = 0
    for arrived in refs[:-1]:
        part = select[:, first : first + arrived.shape[0]].astype(jnp.bfloat16)
        fresh += lax.dot_general(part, arrived[...], NN, preferred_element_type=jnp.float32)
        first += arrived.shape[0]
    hit = jnp.sum(select[...], axis=1, keepdims=True) > 0.5
    out[...] = jnp.where(hit, fresh, table[...].astype(jnp.float32)).astype(jnp.bfloat16)


def to_lanes(row):
    return jnp.broadcast_to(row, (LANES, LANES)).T


def score_kernel(place, queries, positive, log_weight, row_ids, scale, *refs, pieces):
    out, total, pos_total, q_scale, pos_b = refs[-5:]
    count, width = queries.shape
    for block in range(count // LANES):
        part = slice(block * LANES, (block + 1) * LANES)
        values = queries[part, :].astype(jnp.float32)
        squares = jnp.sum(values * values, axis=1, keepdims=True)
        q_scale[part, :] = jnp.broadcast_to(lax.rsqrt(squares / width + epsilon), (LANES, LANES))
        pos_b[part, :] = to_lanes(positive[block : block + 1, :])
    total[...] = jnp.zeros_like(total)
    pos_total[...] = jnp.zeros_like(pos_total)
    for source, start, size, column in pieces:
        first = piece_offset(place, column)
        raw = lax.dot_general(
            queries[...], refs[source][start : start + size, :], NT, preferred_element_type=jnp.float32
        )
        sums = total[...]
        positives = pos_total[...]
        for chunk in range(size // LANES):
            cols = pl.ds(first + chunk * LANES, LANES)
            part = raw[:, chunk * LANES : (chunk + 1) * LANES]
            powers = part * q_scale[...] * scale[:, cols] + log_weight[:, cols]
            sums = sums + jnp.exp2(powers)
            positives = positives + jnp.where(pos_b[...] == row_ids[:, cols], powers, 0.0)
        total[...] = sums
        pos_total[...] = positives
    for block in range(count // LANES):
        part = slice(block * LANES, (block + 1) * LANES)
        out[0, block : block + 1, :] = jnp.sum(total[part, :].T, axis=0, keepdims=True)
        out[1, block : block + 1, :] = jnp.sum(pos_total[part, :].T, axis=0, keepdims=True)


def whole(memory=pltpu.VMEM):
    return pl.BlockSpec(memory_space=memory)


def call(kernel, name, outs, place, *operands, scratch=(), flops=0, **options):
    specs = [whole()] * len(operands)
    if place is not None:
        specs = [whole(pltpu.SMEM)] + specs
        operands = (place, *operands)
    moved = sum(math.prod(x.shape) * x.dtype.itemsize for x in (*operands, *outs))
    return pl.pallas_call(
        functools.partial(kernel, **options),
        out_shape=tuple(outs),
        in_specs=specs,
        out_specs=tuple(whole() for _ in outs),
        scratch_shapes=list(scratch),
        compiler_params=pltpu.CompilerParams(vmem_limit_bytes=VMEM_LIMIT),
        cost_estimate=pl.CostEstimate(flops=flops, bytes_accessed=moved, transcendentals=0),
        name=name,
    )(*operands)


def swap(values, axis, flip):
    return lax.ppermute(values, axis, [(i, i ^ flip) for i in range(lax.axis_size(axis))])


def on_device(table, ages, refresh_ids, fresh_rows, neg_ids, queries, pos_ids):
    rows_dev, width = table.shape
    refresh_dev = refresh_ids.shape[0]
    planes = lax.axis_size("outer")
    owners_plane = lax.axis_size("inner")
    replicas = lax.axis_size("query")
    owners = planes * owners_plane
    query_count = queries.shape[0]
    list_size = neg_ids.shape[1]
    place = jnp.stack([lax.axis_index(name) for name in ("outer", "inner", "query")]).astype(jnp.int32)
    plane_rows = owners_plane * rows_dev
    plane_refresh = owners_plane * refresh_dev
    all_rows = plane_rows + plane_refresh
    cap = owners_plane * max(2, (2 * refresh_dev + owners - 1) // owners)
    share = cap // replicas
    table_half, fresh_half = rows_dev // replicas, refresh_dev // replicas
    bf16, f32 = jnp.bfloat16, jnp.float32

    meta_lines = (2 * refresh_dev + 2 * rows_dev) // LANES
    rows_half, meta = call(
        prep_kernel,
        "prep",
        [jax.ShapeDtypeStruct((table_half + fresh_half, width), bf16), jax.ShapeDtypeStruct((meta_lines, LANES), f32)],
        place,
        table,
        fresh_rows,
        ages.reshape(-1, LANES),
        refresh_ids.reshape(-1, LANES),
        replicas=replicas,
    )
    metas = jnp.stack([meta] + [swap(meta, "inner", s) for s in range(1, owners_plane)])
    got_queries = [queries] + [swap(queries, "outer", s) for s in range(1, planes)]
    got_rows = [swap(rows_half, "inner", s) for s in range(1, owners_plane)]
    cuts = [refresh_dev, rows_dev, rows_dev, refresh_dev]
    ends = [sum(cuts[: i + 1]) // LANES for i in range(len(cuts))]

    def piece(i):
        return metas[:, ends[i] - cuts[i] // LANES : ends[i]].reshape(1, -1)

    ref_plane, log_weight_plane = piece(0), piece(1)
    scale_plane = jnp.concatenate([piece(2), piece(3)], axis=1)
    line = jnp.concatenate([ref_plane[0], neg_ids[0].astype(f32), pos_ids.astype(f32)])
    lines = jnp.stack([line] + [swap(line, "outer", s) for s in range(1, planes)])
    ref_all = lines[:, :plane_refresh].astype(jnp.int32)
    neg_line = lines[:, plane_refresh : plane_refresh + list_size].astype(jnp.int32)
    positive = lines[:, plane_refresh + list_size :].reshape(planes, -1, LANES)

    lw, row_ids, pack, apply_to, own = call(
        meta_kernel,
        "meta",
        [
            jax.ShapeDtypeStruct((planes, all_rows), f32),
            jax.ShapeDtypeStruct((1, all_rows), f32),
            jax.ShapeDtypeStruct((cap + (planes - 1) * share, plane_refresh), bf16),
            jax.ShapeDtypeStruct((rows_dev, planes * cap), f32),
            jax.ShapeDtypeStruct((1, rows_dev), jnp.int32),
        ],
        place,
        ref_all,
        neg_line,
        log_weight_plane,
        rows_dev=rows_dev,
        refresh_dev=refresh_dev,
        cap=cap,
        replicas=replicas,
    )
    new_ages = jnp.where(own.reshape(rows_dev) > 0, 0, ages)

    if replicas == 2:
        buffers = [table, fresh_rows]
        table_pieces = [(0, 0, rows_dev, (0, rows_dev, None))]
        fresh_pieces = [(1, 0, refresh_dev, (0, refresh_dev, None))]
        for s in range(1, owners_plane):
            for flip, rows in enumerate((got_rows[s - 1], swap(got_rows[s - 1], "query", 1))):
                table_pieces.append((len(buffers), 0, table_half, (s * rows_dev, table_half, flip)))
                fresh_pieces.append((len(buffers), table_half, fresh_half, (s * refresh_dev, fresh_half, flip)))
                buffers.append(rows)
    else:
        gathered = lax.all_gather(jnp.stack([rows_half] + got_rows), "query", axis=0)
        gathered = jnp.swapaxes(gathered, 0, 1)
        buffers = [
            gathered[:, :, :table_half].reshape(plane_rows, width),
            gathered[:, :, table_half:].reshape(plane_refresh, width),
        ]
        table_pieces = [(0, i * 512, 512, (i * 512, 512, None)) for i in range(plane_rows // 512)]
        fresh_pieces = [(1, i * 512, 512, (i * 512, 512, None)) for i in range(plane_refresh // 512)]

    def shift(pieces, columns):
        return [(a, b, c, (d[0] + columns, *d[1:])) for a, b, c, d in pieces]

    (packed,) = call(
        pack_kernel, "pack", [jax.ShapeDtypeStruct((pack.shape[0], width), bf16)], place, pack, *buffers, pieces=fresh_pieces
    )
    arrived = [packed[:cap]]
    for s in range(1, planes):
        first = cap + (s - 1) * share
        part = swap(packed[first : first + share], "outer", s)
        arrived += [part] + [swap(part, "query", flip) for flip in range(1, replicas)]

    pieces = table_pieces + shift(fresh_pieces, plane_rows)
    mine = None
    for s in [*range(1, planes), 0]:
        (partial,) = call(
            score_kernel,
            "score",
            [jax.ShapeDtypeStruct((2, query_count // LANES, LANES), f32)],
            place,
            got_queries[s],
            positive[s],
            lw[s : s + 1],
            row_ids,
            scale_plane,
            *buffers,
            scratch=[pltpu.VMEM((query_count, LANES), f32)] * 4,
            flops=2 * query_count * all_rows * width,
            pieces=pieces,
        )
        if s:
            partial = swap(partial, "outer", s)
        mine = partial if mine is None else mine + partial
    (new_table,) = call(
        apply_kernel, "apply", [jax.ShapeDtypeStruct(table.shape, bf16)], None, apply_to, table, *arrived
    )
    loss = (jnp.log2(mine[0]) - mine[1]) * math.log(2.0)
    return new_table, new_ages, loss.reshape(query_count)


def solution(mesh):
    owners, replicas = mesh.shape["index"], mesh.shape["query"]
    inner = 1 << (int(math.log2(owners)) // 2)
    split = Mesh(mesh.devices.reshape(owners // inner, inner, replicas), ("outer", "inner", "query"))
    index = ("outer", "inner")
    placed = (
        P(index, None),
        P(index),
        P(index),
        P(index, None),
        P(index, None),
        P(("outer", "inner", "query"), None),
        P(("outer", "inner", "query")),
    )
    return jax.shard_map(
        on_device,
        mesh=split,
        in_specs=placed,
        out_specs=(P(index, None), P(index), P(("outer", "inner", "query"))),
        check_vma=False,
    )
```

```python
import functools
import math

import jax
import jax.numpy as jnp
from jax import lax
from jax.experimental import pallas as pl
from jax.experimental.pallas import tpu as pltpu
from jax.sharding import Mesh, PartitionSpec as P

score_scale = 20.0
age_scale = 16.0
epsilon = 1e-06
LOG2E = math.log2(math.e)
MASKED = -1e30
LANES = 128
VMEM_LIMIT = 48 * 1024 * 1024

NT = (((1,), (1,)), ((), ()))
NN = (((1,), (0,)), ((), ()))


def one_hot(ids, count):
    rows = lax.broadcasted_iota(jnp.int32, (count, ids.shape[1]), 0)
    return jnp.where(rows == ids, 1.0, 0.0).astype(jnp.bfloat16)


def split_one_hot(ids, high_count):
    return one_hot(ids >> 7, high_count), one_hot(ids & 127, LANES)


def bitmap(ids, high_count):
    high, low = split_one_hot(ids, high_count)
    return lax.dot_general(low, high, NT, preferred_element_type=jnp.float32)


def prep_kernel(place, table, fresh, ages, ref_ids, rows_out, meta_out, *, replicas):
    core = place[2]
    row = 0
    for source in (table, fresh):
        half = source.shape[0] // replicas
        rows_out[row : row + half, :] = source[pl.ds(pl.multiple_of(core * half, half), half), :]
        row += half
    width = table.shape[1]
    ref_rows, age_rows = ref_ids.shape[0], ages.shape[0]
    meta_out[:ref_rows, :] = ref_ids[...].astype(jnp.float32)
    weight = jnp.exp(-ages[...].astype(jnp.float32) / age_scale).astype(jnp.bfloat16).astype(jnp.float32)
    meta_out[ref_rows : ref_rows + age_rows, :] = jnp.log2(weight)
    line = ref_rows + age_rows
    for source in (table, fresh):
        for block in range(source.shape[0] // LANES):
            squares = jnp.zeros((LANES, LANES), jnp.float32)
            for chunk in range(width // LANES):
                values = source[block * LANES : (block + 1) * LANES, chunk * LANES : (chunk + 1) * LANES]
                values = values.astype(jnp.float32)
                squares += values * values
            mean = jnp.sum(squares.T, axis=0, keepdims=True) / width
            meta_out[line : line + 1, :] = lax.rsqrt(mean + epsilon) * (score_scale / width * LOG2E)
            line += 1


def meta_kernel(
    place, ref_ids, neg, log_weight, lw_out, row_out, pack_out, apply_out, own_out, *, rows_dev, refresh_dev, cap, replicas
):
    outer, inner, core = place[0], place[1], place[2]
    planes, plane_refresh = ref_ids.shape
    plane_rows = log_weight.shape[1]
    owners_plane = plane_rows // rows_dev
    high_count = planes * plane_rows // LANES
    own_owner = outer * owners_plane + inner
    plane_ids = ref_ids[0:1, :]
    column = lax.broadcasted_iota(jnp.int32, (1, plane_rows), 1)
    table_ids = (outer * owners_plane + (inner ^ (column // rows_dev))) * rows_dev + column % rows_dev

    refreshed_map = jnp.zeros((LANES, high_count), jnp.float32)
    for plane in range(planes):
        refreshed_map += bitmap(ref_ids[plane : plane + 1, :], high_count)
    refreshed_map = refreshed_map.astype(jnp.bfloat16)

    table_high, table_low = split_one_hot(table_ids, high_count)
    fresh_high, fresh_low = split_one_hot(plane_ids, high_count)

    def lookup(one_map, high, low):
        hit = lax.dot_general(one_map, high, NN, preferred_element_type=jnp.float32)
        return jnp.sum(hit * low.astype(jnp.float32), axis=0, keepdims=True)

    refreshed = lookup(refreshed_map, table_high, table_low) > 0.5
    row_out[:, :plane_rows] = jnp.where(refreshed, -1, table_ids).astype(jnp.float32)
    row_out[:, plane_rows:] = plane_ids.astype(jnp.float32)
    own_out[...] = refreshed[:, :rows_dev].astype(jnp.int32)

    for group in range(planes):
        one_map = bitmap(neg[group : group + 1, :], high_count).astype(jnp.bfloat16)
        in_list = lookup(one_map, table_high, table_low) > 0.5
        lw_out[group : group + 1, :plane_rows] = jnp.where(in_list & ~refreshed, log_weight[...], MASKED)
        in_list = lookup(one_map, fresh_high, fresh_low) > 0.5
        lw_out[group : group + 1, plane_rows:] = jnp.where(in_list, 0.0, MASKED)

    share = cap // replicas
    earlier = jnp.where(
        lax.broadcasted_iota(jnp.int32, (plane_refresh, plane_refresh), 0)
        < lax.broadcasted_iota(jnp.int32, (plane_refresh, plane_refresh), 1),
        1.0,
        0.0,
    ).astype(jnp.bfloat16)
    target_plane = outer ^ lax.broadcasted_iota(jnp.int32, (planes, plane_refresh), 0)
    send_match = plane_ids // rows_dev == target_plane * owners_plane + inner
    take_match = ref_ids[...] // rows_dev == own_owner

    def ranked(match):
        ones = jnp.where(match, 1.0, 0.0)
        rank = lax.dot_general(ones.astype(jnp.bfloat16), earlier, NN, preferred_element_type=jnp.float32)
        return jnp.where(match, rank.astype(jnp.int32), -cap)

    send_rank, take_rank = ranked(send_match), ranked(take_match)
    take_row = ref_ids[...] - own_owner * rows_dev
    pack_out[:cap, :] = one_hot(send_rank[0:1, :], cap)
    for plane in range(1, planes):
        first = cap + (plane - 1) * share
        pack_out[first : first + share, :] = one_hot(send_rank[plane : plane + 1, :] - core * share, share)
    for plane in range(planes):
        row = one_hot(take_row[plane : plane + 1, :], rows_dev)
        for part in range(1 if plane == 0 else replicas):
            size = cap if plane == 0 else share
            skip = 0 if plane == 0 else (core ^ part) * share
            slot = one_hot(take_rank[plane : plane + 1, :] - skip, size)
            first = plane and cap + (part * (planes - 1) + plane - 1) * share
            apply_out[:, first : first + size] = lax.dot_general(row, slot, NT, preferred_element_type=jnp.float32)


def piece_offset(place, piece):
    column, size, flip, by_core = piece
    if flip is None:
        return column
    column += (place[2] ^ flip) * size
    if by_core is not None:
        column += (place[2] ^ by_core) * size * 2
    return pl.multiple_of(column, size)


def pack_kernel(place, select, *refs, pieces):
    out = refs[-1]
    total = jnp.zeros(out.shape, jnp.float32)
    for source, start, size, column in pieces:
        columns = pl.ds(piece_offset(place, column), size)
        total += lax.dot_general(
            select[:, columns], refs[source][start : start + size, :], NN, preferred_element_type=jnp.float32
        )
    out[...] = total.astype(jnp.bfloat16)


def apply_kernel(select, table, *refs):
    out = refs[-1]
    fresh = jnp.zeros(out.shape, jnp.float32)
    first = 0
    for arrived in refs[:-1]:
        part = select[:, first : first + arrived.shape[0]].astype(jnp.bfloat16)
        fresh += lax.dot_general(part, arrived[...], NN, preferred_element_type=jnp.float32)
        first += arrived.shape[0]
    hit = jnp.sum(select[...], axis=1, keepdims=True) > 0.5
    out[...] = jnp.where(hit, fresh, table[...].astype(jnp.float32)).astype(jnp.bfloat16)


def to_lanes(row):
    return jnp.broadcast_to(row, (LANES, LANES)).T


def score_kernel(place, *refs, pieces, sources):
    positive, log_weight, row_ids, scale = refs[sources : sources + 4]
    out, total, pos_total, q_scale, pos_b, chosen = refs[-6:]
    queries = refs[0]
    count, width = queries.shape
    if sources == 2:
        at_end = (place[0] == 0) | (place[0] == 3)
        chosen[...] = jnp.where(at_end, refs[0][...], refs[1][...])
        queries = chosen
    for block in range(count // LANES):
        part = slice(block * LANES, (block + 1) * LANES)
        values = queries[part, :].astype(jnp.float32)
        squares = jnp.sum(values * values, axis=1, keepdims=True)
        q_scale[part, :] = jnp.broadcast_to(lax.rsqrt(squares / width + epsilon), (LANES, LANES))
        pos_b[part, :] = to_lanes(positive[block : block + 1, :])
    total[...] = jnp.zeros_like(total)
    pos_total[...] = jnp.zeros_like(pos_total)
    for source, start, size, column in pieces:
        first = piece_offset(place, column)
        raw = lax.dot_general(
            queries[...], refs[sources + 4 + source][start : start + size, :], NT, preferred_element_type=jnp.float32
        )
        sums = total[...]
        positives = pos_total[...]
        for chunk in range(size // LANES):
            cols = pl.ds(first + chunk * LANES, LANES)
            part = raw[:, chunk * LANES : (chunk + 1) * LANES]
            powers = part * q_scale[...] * scale[:, cols] + log_weight[:, cols]
            sums = sums + jnp.exp2(powers)
            positives = positives + jnp.where(pos_b[...] == row_ids[:, cols], powers, 0.0)
        total[...] = sums
        pos_total[...] = positives
    for block in range(count // LANES):
        part = slice(block * LANES, (block + 1) * LANES)
        out[0, block : block + 1, :] = jnp.sum(total[part, :].T, axis=0, keepdims=True)
        out[1, block : block + 1, :] = jnp.sum(pos_total[part, :].T, axis=0, keepdims=True)


def whole(memory=pltpu.VMEM):
    return pl.BlockSpec(memory_space=memory)


def call(kernel, name, outs, place, *operands, scratch=(), **options):
    specs = [whole()] * len(operands)
    if place is not None:
        specs = [whole(pltpu.SMEM)] + specs
        operands = (place, *operands)
    return pl.pallas_call(
        functools.partial(kernel, **options),
        out_shape=tuple(outs),
        in_specs=specs,
        out_specs=tuple(whole() for _ in outs),
        scratch_shapes=list(scratch),
        compiler_params=pltpu.CompilerParams(vmem_limit_bytes=VMEM_LIMIT),
        cost_estimate=pl.CostEstimate(flops=1, bytes_accessed=1, transcendentals=0),
        name=name,
    )(*operands)


def swap(values, axis, flip):
    return lax.ppermute(values, axis, [(i, i ^ flip) for i in range(lax.axis_size(axis))])


def gather_line(values, small):
    planes = lax.axis_size("outer")
    if planes != 4:
        return [(swap(values, "outer", s),) for s in range(1, planes)], small
    middle, outward = [(1, 2), (2, 1)], [(1, 0), (2, 3)]
    beside = swap(values, "outer", 1)
    across = lax.ppermute(values, "outer", middle)
    beside, across, small = lax.optimization_barrier((beside, across, small))
    from_end = lax.ppermute(beside, "outer", middle)
    to_end = lax.ppermute(across, "outer", outward)
    last = lax.ppermute(from_end, "outer", outward)
    return [(beside,), (to_end, from_end), (last, across)], small


def on_device(table, ages, refresh_ids, fresh_rows, neg_ids, queries, pos_ids):
    rows_dev, width = table.shape
    refresh_dev = refresh_ids.shape[0]
    planes = lax.axis_size("outer")
    owners_plane = lax.axis_size("inner")
    replicas = lax.axis_size("query")
    owners = planes * owners_plane
    query_count = queries.shape[0]
    list_size = neg_ids.shape[1]
    place = jnp.stack([lax.axis_index(name) for name in ("outer", "inner", "query")]).astype(jnp.int32)
    plane_rows = owners_plane * rows_dev
    plane_refresh = owners_plane * refresh_dev
    all_rows = plane_rows + plane_refresh
    cap = owners_plane * max(2, (2 * refresh_dev + owners - 1) // owners)
    share = cap // replicas
    table_half, fresh_half = rows_dev // replicas, refresh_dev // replicas
    bf16, f32 = jnp.bfloat16, jnp.float32

    meta_lines = (2 * refresh_dev + 2 * rows_dev) // LANES
    rows_half, meta = call(
        prep_kernel,
        "prep",
        [jax.ShapeDtypeStruct((table_half + fresh_half, width), bf16), jax.ShapeDtypeStruct((meta_lines, LANES), f32)],
        place,
        table,
        fresh_rows,
        ages.reshape(-1, LANES),
        refresh_ids.reshape(-1, LANES),
        replicas=replicas,
    )
    metas = jnp.stack([meta] + [swap(meta, "inner", s) for s in range(1, owners_plane)])
    cuts = [refresh_dev, rows_dev, rows_dev, refresh_dev]
    ends = [sum(cuts[: i + 1]) // LANES for i in range(len(cuts))]

    def piece(i):
        return metas[:, ends[i] - cuts[i] // LANES : ends[i]].reshape(1, -1)

    ref_plane, log_weight_plane = piece(0), piece(1)
    scale_plane = jnp.concatenate([piece(2), piece(3)], axis=1)
    line = jnp.concatenate([ref_plane[0], neg_ids[0].astype(f32), pos_ids.astype(f32)])
    got_queries, line = gather_line(queries, line)
    got_queries = [(queries,)] + got_queries
    lines = jnp.stack([line] + [swap(line, "outer", s) for s in range(1, planes)])
    ref_all = lines[:, :plane_refresh].astype(jnp.int32)
    neg_line = lines[:, plane_refresh : plane_refresh + list_size].astype(jnp.int32)
    positive = lines[:, plane_refresh + list_size :].reshape(planes, -1, LANES)

    lw, row_ids, pack, apply_to, own = call(
        meta_kernel,
        "meta",
        [
            jax.ShapeDtypeStruct((planes, all_rows), f32),
            jax.ShapeDtypeStruct((1, all_rows), f32),
            jax.ShapeDtypeStruct((cap + (planes - 1) * share, plane_refresh), bf16),
            jax.ShapeDtypeStruct((rows_dev, planes * cap), f32),
            jax.ShapeDtypeStruct((1, rows_dev), jnp.int32),
        ],
        place,
        ref_all,
        neg_line,
        log_weight_plane,
        rows_dev=rows_dev,
        refresh_dev=refresh_dev,
        cap=cap,
        replicas=replicas,
    )
    new_ages = jnp.where(own.reshape(rows_dev) > 0, 0, ages)

    if replicas == 2 and owners_plane == 4:
        axes = ("inner", "query")
        first = [(2 * i + c, 2 * (i ^ (1 + c)) + c) for i in range(4) for c in range(2)]
        second = [(2 * i + c, 2 * (i ^ (2 - c)) + c) for i in range(4) for c in range(2)]
        near = lax.ppermute(rows_half, axes, first)
        side = lax.ppermute(rows_half, axes, second)
        far = lax.ppermute(near, axes, second)
        buffers = [table, fresh_rows]
        table_pieces = [(0, 0, rows_dev, (0, rows_dev, None, None))]
        fresh_pieces = [(1, 0, refresh_dev, (0, refresh_dev, None, None))]
        for slot, by_core, mine in ((1, 0, near), (1, 1, side), (3, None, far)):
            for flip, rows in enumerate((mine, swap(mine, "query", 1))):
                by = None if by_core is None else by_core ^ flip
                table_pieces.append((len(buffers), 0, table_half, (slot * rows_dev, table_half, flip, by)))
                fresh_pieces.append((len(buffers), table_half, fresh_half, (slot * refresh_dev, fresh_half, flip, by)))
                buffers.append(rows)
    else:
        got_rows = [rows_half] + [swap(rows_half, "inner", s) for s in range(1, owners_plane)]
        gathered = lax.all_gather(jnp.stack(got_rows), "query", axis=0)
        gathered = jnp.swapaxes(gathered, 0, 1)
        buffers = [
            gathered[:, :, :table_half].reshape(plane_rows, width),
            gathered[:, :, table_half:].reshape(plane_refresh, width),
        ]
        table_pieces = [(0, i * 512, 512, (i * 512, 512, None, None)) for i in range(plane_rows // 512)]
        fresh_pieces = [(1, i * 512, 512, (i * 512, 512, None, None)) for i in range(plane_refresh // 512)]

    def shift(pieces, columns):
        return [(a, b, c, (d[0] + columns, *d[1:])) for a, b, c, d in pieces]

    (packed,) = call(
        pack_kernel, "pack", [jax.ShapeDtypeStruct((pack.shape[0], width), bf16)], place, pack, *buffers, pieces=fresh_pieces
    )
    parts = []
    for s in range(1, planes):
        first = cap + (s - 1) * share
        parts.append(swap(packed[first : first + share], "outer", s))
    parts = jnp.concatenate(parts)
    arrived = [packed[:cap], parts] + [swap(parts, "query", flip) for flip in range(1, replicas)]

    pieces = table_pieces + shift(fresh_pieces, plane_rows)
    mine = None
    for s in [*range(1, planes), 0]:
        (partial,) = call(
            score_kernel,
            "score",
            [jax.ShapeDtypeStruct((2, query_count // LANES, LANES), f32)],
            place,
            *got_queries[s],
            positive[s],
            lw[s : s + 1],
            row_ids,
            scale_plane,
            *buffers,
            scratch=[pltpu.VMEM((query_count, LANES), f32)] * 4 + [pltpu.VMEM((query_count, width), bf16)],
            pieces=pieces,
            sources=len(got_queries[s]),
        )
        if s:
            partial = swap(partial, "outer", s)
        mine = partial if mine is None else mine + partial
    (new_table,) = call(
        apply_kernel, "apply", [jax.ShapeDtypeStruct(table.shape, bf16)], None, apply_to, table, *arrived
    )
    loss = (jnp.log2(mine[0]) - mine[1]) * math.log(2.0)
    return new_table, new_ages, loss.reshape(query_count)


def solution(mesh):
    owners, replicas = mesh.shape["index"], mesh.shape["query"]
    inner = 1 << (int(math.log2(owners)) // 2)
    split = Mesh(mesh.devices.reshape(owners // inner, inner, replicas), ("outer", "inner", "query"))
    index = ("outer", "inner")
    placed = (
        P(index, None),
        P(index),
        P(index),
        P(index, None),
        P(index, None),
        P(("outer", "inner", "query"), None),
        P(("outer", "inner", "query")),
    )
    return jax.shard_map(
        on_device,
        mesh=split,
        in_specs=placed,
        out_specs=(P(index, None), P(index), P(("outer", "inner", "query"))),
        check_vma=False,
    )
```

```python
import functools
import math

import jax
import jax.numpy as jnp
from jax import lax
from jax.experimental import pallas as pl
from jax.experimental.pallas import tpu as pltpu
from jax.sharding import Mesh, PartitionSpec as P

score_scale = 20.0
age_scale = 16.0
epsilon = 1e-06
LOG2E = math.log2(math.e)
MASKED = -1e30
LANES = 128
VMEM_LIMIT = 48 * 1024 * 1024

NT = (((1,), (1,)), ((), ()))
NN = (((1,), (0,)), ((), ()))


def one_hot(ids, count):
    rows = lax.broadcasted_iota(jnp.int32, (count, ids.shape[1]), 0)
    return jnp.where(rows == ids, 1.0, 0.0).astype(jnp.bfloat16)


def split_one_hot(ids, high_count):
    return one_hot(ids >> 7, high_count), one_hot(ids & 127, LANES)


def bitmap(ids, high_count):
    high, low = split_one_hot(ids, high_count)
    return lax.dot_general(low, high, NT, preferred_element_type=jnp.float32)


def as_row(lines):
    return jnp.concatenate([lines[i : i + 1, :] for i in range(lines.shape[0])], axis=1)


def split_terms(values):
    terms = []
    for _ in range(3):
        terms.append(values.astype(jnp.bfloat16))
        values = values - terms[-1].astype(jnp.float32)
    return terms


def prep_kernel(place, table, fresh, rows_out, scale_out, table_in, fresh_in, arrived, *, replicas, encode):
    core = place[2]
    copies = [
        pltpu.make_async_copy(table, table_in, arrived.at[0]),
        pltpu.make_async_copy(fresh, fresh_in, arrived.at[1]),
    ]
    for copy in copies:
        copy.start()
    line, row = 0, 0
    halves = []
    for copy, source in zip(copies, (table_in, fresh_in)):
        copy.wait()
        rows, width = source.shape
        half = rows // replicas
        rows_out[row : row + half, :] = source[pl.ds(pl.multiple_of(core * half, half), half), :]
        row += half
        for block in range(rows // LANES):
            squares = jnp.zeros((LANES, LANES), jnp.float32)
            for chunk in range(width // LANES):
                values = source[block * LANES : (block + 1) * LANES, chunk * LANES : (chunk + 1) * LANES]
                values = values.astype(jnp.float32)
                squares += values * values
            mean = jnp.sum(squares.T, axis=0, keepdims=True) / width
            scale_out[line + block : line + block + 1, :] = lax.rsqrt(mean + epsilon) * (score_scale / width * LOG2E)
        if encode:
            lines = half // LANES
            halves += [(line, i, lines) for i in range(lines)]
        line += rows // LANES
    if encode:
        rows_out[row:, :] = jnp.zeros((16, width), jnp.bfloat16)
        terms = []
        for first, i, lines in halves:
            terms += split_terms(scale_out[pl.ds(first + core * lines + i, 1), :])
        for i, term in enumerate(terms):
            rows_out[row + i : row + i + 1, :LANES] = term


def meta_kernel(place, meta, lw_out, row_out, pack_out, apply_out, own_out, *, planes, cuts, cap, replicas):
    outer, inner, core = place[0], place[1], place[2]
    owners_plane = meta.shape[0] // planes
    refresh_lines, age_lines, neg_lines = (cut // LANES for cut in cuts[:3])
    refresh_dev, rows_dev = cuts[:2]
    plane_rows = owners_plane * rows_dev
    plane_refresh = owners_plane * refresh_dev
    high_count = planes * plane_rows // LANES
    own_owner = outer * owners_plane + inner
    column = lax.broadcasted_iota(jnp.int32, (1, plane_rows), 1)
    table_ids = (outer * owners_plane + (inner ^ (column // rows_dev))) * rows_dev + column % rows_dev

    ref_planes = []
    for plane in range(planes):
        owners = range(plane * owners_plane, (plane + 1) * owners_plane)
        ref_planes.append(jnp.concatenate([as_row(meta[owner, :refresh_lines, :]) for owner in owners], axis=1))
    beside = [outer * owners_plane + (inner ^ s) for s in range(owners_plane)]
    plane_ids = jnp.concatenate([as_row(meta[owner, :refresh_lines, :]) for owner in beside], axis=1)
    first, last = refresh_lines, refresh_lines + age_lines
    plane_ages = jnp.concatenate([as_row(meta[owner, first:last, :]) for owner in beside], axis=1)
    weight = jnp.exp(-plane_ages.astype(jnp.float32) / age_scale).astype(jnp.bfloat16).astype(jnp.float32)
    log_weight = jnp.log2(weight)

    refreshed_map = jnp.zeros((LANES, high_count), jnp.float32)
    for ids in ref_planes:
        refreshed_map += bitmap(ids, high_count)
    refreshed_map = refreshed_map.astype(jnp.bfloat16)

    table_high, table_low = split_one_hot(table_ids, high_count)
    fresh_high, fresh_low = split_one_hot(plane_ids, high_count)

    def lookup(one_map, high, low):
        hit = lax.dot_general(one_map, high, NN, preferred_element_type=jnp.float32)
        return jnp.sum(hit * low.astype(jnp.float32), axis=0, keepdims=True)

    refreshed = lookup(refreshed_map, table_high, table_low) > 0.5
    row_out[:, :plane_rows] = jnp.where(refreshed, -1, table_ids)
    row_out[:, plane_rows:] = plane_ids
    own_out[...] = refreshed[:, :rows_dev].astype(jnp.int32)

    first, last = last, last + neg_lines
    for group in range(planes):
        neg = as_row(meta[(outer ^ group) * owners_plane + inner, first:last, :])
        one_map = bitmap(neg, high_count).astype(jnp.bfloat16)
        in_list = lookup(one_map, table_high, table_low) > 0.5
        lw_out[group : group + 1, :plane_rows] = jnp.where(in_list & ~refreshed, log_weight, MASKED)
        in_list = lookup(one_map, fresh_high, fresh_low) > 0.5
        lw_out[group : group + 1, plane_rows:] = jnp.where(in_list, 0.0, MASKED)

    share = cap // replicas
    before = lax.broadcasted_iota(jnp.int32, (plane_refresh, plane_refresh), 0)
    after = lax.broadcasted_iota(jnp.int32, (plane_refresh, plane_refresh), 1)
    earlier = jnp.where(before < after, 1.0, 0.0).astype(jnp.bfloat16)
    block = refresh_dev
    before_own = (inner ^ (before // block)) * block + before % block
    after_own = (inner ^ (after // block)) * block + after % block
    earlier_own = jnp.where(before_own < after_own, 1.0, 0.0).astype(jnp.bfloat16)
    target_plane = lax.broadcasted_iota(jnp.int32, (planes, plane_refresh), 0)
    send_match = plane_ids // rows_dev == target_plane * owners_plane + inner
    ref_all = jnp.concatenate(ref_planes, axis=0)
    take_match = ref_all // rows_dev == own_owner

    def ranked(match, order):
        ones = jnp.where(match, 1.0, 0.0)
        rank = lax.dot_general(ones.astype(jnp.bfloat16), order, NN, preferred_element_type=jnp.float32)
        return jnp.where(match, rank.astype(jnp.int32), -cap)

    send_rank, take_rank = ranked(send_match, earlier_own), ranked(take_match, earlier)
    take_row = ref_all - own_owner * rows_dev
    for plane in range(planes):
        pack_out[plane * share : (plane + 1) * share, :] = one_hot(send_rank[plane : plane + 1, :] - core * share, share)
        row = one_hot(take_row[plane : plane + 1, :], rows_dev)
        for part in range(replicas):
            slot = one_hot(take_rank[plane : plane + 1, :] - (core ^ part) * share, share)
            first = (part * planes + plane) * share
            apply_out[:, first : first + share] = lax.dot_general(row, slot, NT, preferred_element_type=jnp.float32)


def piece_offset(place, piece):
    column, size, flip, by_core = piece
    if flip is None:
        return column
    column += (place[2] ^ flip) * size
    if by_core is not None:
        column += (place[2] ^ by_core) * size * 2
    return pl.multiple_of(column, size)


def pack_kernel(place, select, *refs, pieces):
    out = refs[-1]
    total = jnp.zeros(out.shape, jnp.float32)
    for source, start, size, column, _ in pieces:
        columns = pl.ds(piece_offset(place, column), size)
        total += lax.dot_general(
            select[:, columns], refs[source][start : start + size, :], NN, preferred_element_type=jnp.float32
        )
    out[...] = total.astype(jnp.bfloat16)


def apply_kernel(select, table, *refs):
    out = refs[-1]
    fresh = jnp.zeros(out.shape, jnp.float32)
    first = 0
    for arrived in refs[:-1]:
        part = select[:, first : first + arrived.shape[0]].astype(jnp.bfloat16)
        fresh += lax.dot_general(part, arrived[...], NN, preferred_element_type=jnp.float32)
        first += arrived.shape[0]
    hit = jnp.sum(select[...], axis=1, keepdims=True) > 0.5
    out[...] = jnp.where(hit, fresh, table[...].astype(jnp.float32)).astype(jnp.bfloat16)


def to_lanes(row):
    return jnp.broadcast_to(row, (LANES, LANES)).T


def score_kernel(place, meta, *refs, pieces, flip, slot, owners_plane, given):
    out, total, pos_total, q_scale, pos_b, chosen = refs[-6:]
    queries = refs[0]
    if given == 2:
        at_end = (place[0] == 0) | (place[0] == 3)
        chosen[...] = jnp.where(at_end, refs[0][...], refs[1][...])
        queries = chosen
    log_weight, row_ids, scale, *refs = refs[given:-6]
    count, width = queries.shape
    owner = (place[0] ^ flip) * owners_plane + place[1]
    for block in range(count // LANES):
        part = slice(block * LANES, (block + 1) * LANES)
        values = queries[part, :].astype(jnp.float32)
        squares = jnp.sum(values * values, axis=1, keepdims=True)
        q_scale[part, :] = jnp.broadcast_to(lax.rsqrt(squares / width + epsilon), (LANES, LANES))
        pos_b[part, :] = to_lanes(meta[owner, slot + block : slot + block + 1, :].astype(jnp.float32))
    total[...] = jnp.zeros_like(total)
    pos_total[...] = jnp.zeros_like(pos_total)
    for source, start, size, column, scale_at in pieces:
        first = piece_offset(place, column)
        raw = lax.dot_general(
            queries[...], refs[source][start : start + size, :], NT, preferred_element_type=jnp.float32
        )
        sums = total[...]
        positives = pos_total[...]
        for chunk in range(size // LANES):
            cols = pl.ds(first + chunk * LANES, LANES)
            part = raw[:, chunk * LANES : (chunk + 1) * LANES]
            if scale_at < 0:
                line = -1 - scale_at + chunk
                row_scale = scale[line : line + 1, :]
            else:
                line = scale_at + 3 * chunk
                row_scale = jnp.sum(refs[source][line : line + 3, :LANES].astype(jnp.float32), axis=0, keepdims=True)
            powers = part * q_scale[...] * row_scale + log_weight[flip : flip + 1, cols]
            sums = sums + jnp.exp2(powers)
            positives = positives + jnp.where(pos_b[...] == row_ids[:, cols].astype(jnp.float32), powers, 0.0)
        total[...] = sums
        pos_total[...] = positives
    for block in range(count // LANES):
        part = slice(block * LANES, (block + 1) * LANES)
        out[0, block : block + 1, :] = jnp.sum(total[part, :].T, axis=0, keepdims=True)
        out[1, block : block + 1, :] = jnp.sum(pos_total[part, :].T, axis=0, keepdims=True)


def whole(memory=pltpu.VMEM):
    return pl.BlockSpec(memory_space=memory)


def call(kernel, name, outs, place, *operands, scratch=(), in_place=False, **options):
    specs = [whole(pl.ANY if in_place else pltpu.VMEM)] * len(operands)
    if place is not None:
        specs = [whole(pltpu.SMEM)] + specs
        operands = (place, *operands)
    return pl.pallas_call(
        functools.partial(kernel, **options),
        out_shape=tuple(outs),
        in_specs=specs,
        out_specs=tuple(whole() for _ in outs),
        scratch_shapes=list(scratch),
        compiler_params=pltpu.CompilerParams(vmem_limit_bytes=VMEM_LIMIT),
        cost_estimate=pl.CostEstimate(flops=1, bytes_accessed=1, transcendentals=0),
        name=name,
    )(*operands)


def swap(values, axis, flip):
    return lax.ppermute(values, axis, [(i, i ^ flip) for i in range(lax.axis_size(axis))])


def on_device(table, ages, refresh_ids, fresh_rows, neg_ids, queries, pos_ids):
    rows_dev, width = table.shape
    refresh_dev = refresh_ids.shape[0]
    planes = lax.axis_size("outer")
    owners_plane = lax.axis_size("inner")
    replicas = lax.axis_size("query")
    owners = planes * owners_plane
    query_count = queries.shape[0]
    list_size = neg_ids.shape[1]
    place = jnp.stack([lax.axis_index(name) for name in ("outer", "inner", "query")]).astype(jnp.int32)
    plane_rows = owners_plane * rows_dev
    plane_refresh = owners_plane * refresh_dev
    all_rows = plane_rows + plane_refresh
    cap = owners_plane * max(2, (2 * refresh_dev + owners - 1) // owners)
    share = cap // replicas
    table_half, fresh_half = rows_dev // replicas, refresh_dev // replicas
    bf16, f32 = jnp.bfloat16, jnp.float32

    meta = jnp.concatenate([refresh_ids, ages, neg_ids[0], pos_ids]).reshape(-1, LANES)
    meta_all = lax.all_to_all(
        jnp.broadcast_to(meta, (owners, *meta.shape)), ("outer", "inner"), split_axis=0, concat_axis=0, tiled=True
    )
    fast = replicas == 2 and owners_plane == 4 and planes == 4
    extra = 16 if fast else 0
    rows_half, scales = call(
        prep_kernel,
        "prep",
        [
            jax.ShapeDtypeStruct((table_half + fresh_half + extra, width), bf16),
            jax.ShapeDtypeStruct(((rows_dev + refresh_dev) // LANES, LANES), f32),
        ],
        place,
        table,
        fresh_rows,
        scratch=[
            pltpu.VMEM(table.shape, bf16),
            pltpu.VMEM(fresh_rows.shape, bf16),
            pltpu.SemaphoreType.DMA((2,)),
        ],
        in_place=True,
        replicas=replicas,
        encode=fast,
    )
    cuts = (refresh_dev, rows_dev, list_size, query_count)
    if fast:
        axes = ("inner", "query")
        first = [(2 * i + c, 2 * (i ^ (1 + c)) + c) for i in range(4) for c in range(2)]
        second = [(2 * i + c, 2 * (i ^ (2 - c)) + c) for i in range(4) for c in range(2)]
        near = lax.ppermute(rows_half, axes, first)
        side = lax.ppermute(rows_half, axes, second)
        middle, outward = [(1, 2), (2, 1)], [(1, 0), (2, 3)]
        beside = swap(queries, "outer", 1)
        across = lax.ppermute(queries, "outer", middle)
        near, meta_all, beside, across = lax.optimization_barrier((near, meta_all, beside, across))
        from_end = lax.ppermute(beside, "outer", middle)
        to_end = lax.ppermute(across, "outer", outward)
        far = lax.ppermute(near, axes, second)
        far, from_end, to_end = lax.optimization_barrier((far, from_end, to_end))
        last = lax.ppermute(from_end, "outer", outward)
        got_queries = [(queries,), (beside,), (to_end, from_end), (last, across)]
        buffers = [table, fresh_rows]
        table_pieces = [(0, 0, rows_dev, (0, rows_dev, None, None), -1)]
        fresh_pieces = [(1, 0, refresh_dev, (0, refresh_dev, None, None), -1 - rows_dev // LANES)]
        for slot, by_core, mine in ((1, 0, near), (1, 1, side), (3, None, far)):
            for flip, rows in enumerate((mine, swap(mine, "query", 1))):
                by = None if by_core is None else by_core ^ flip
                data = table_half + fresh_half
                fresh_at = data + 3 * (table_half // LANES)
                table_pieces.append((len(buffers), 0, table_half, (slot * rows_dev, table_half, flip, by), data))
                fresh_pieces.append(
                    (len(buffers), table_half, fresh_half, (slot * refresh_dev, fresh_half, flip, by), fresh_at)
                )
                buffers.append(rows)
    else:
        got_queries = [(queries,)] + [(swap(queries, "outer", s),) for s in range(1, planes)]
        got_rows = [rows_half] + [swap(rows_half, "inner", s) for s in range(1, owners_plane)]
        gathered = lax.all_gather(jnp.stack(got_rows), "query", axis=0)
        gathered = jnp.swapaxes(gathered, 0, 1)
        buffers = [
            gathered[:, :, :table_half].reshape(plane_rows, width),
            gathered[:, :, table_half:].reshape(plane_refresh, width),
        ]
        scales = []
        for rows in buffers:
            values = rows.astype(f32)
            mean = jnp.sum(values * values, axis=1) / width
            scales.append((lax.rsqrt(mean + epsilon) * (score_scale / width * LOG2E)).reshape(-1, LANES))
        scales = jnp.concatenate(scales)

        def blocks(buffer, count, line):
            starts = range(0, count, 512)
            return [(buffer, i, 512, (i, 512, None, None), -1 - line - i // LANES) for i in starts]

        table_pieces = blocks(0, plane_rows, 0)
        fresh_pieces = blocks(1, plane_refresh, plane_rows // LANES)

    lw, row_ids, pack, apply_to, own = call(
        meta_kernel,
        "meta",
        [
            jax.ShapeDtypeStruct((planes, all_rows), f32),
            jax.ShapeDtypeStruct((1, all_rows), jnp.int32),
            jax.ShapeDtypeStruct((planes * share, plane_refresh), bf16),
            jax.ShapeDtypeStruct((rows_dev, planes * cap), f32),
            jax.ShapeDtypeStruct((1, rows_dev), jnp.int32),
        ],
        place,
        meta_all,
        planes=planes,
        cuts=cuts,
        cap=cap,
        replicas=replicas,
    )
    new_ages = jnp.where(own.reshape(rows_dev) > 0, 0, ages)

    def shift(pieces, columns):
        return [(a, b, c, (d[0] + columns, *d[1:]), e) for a, b, c, d, e in pieces]

    (packed,) = call(
        pack_kernel, "pack", [jax.ShapeDtypeStruct((pack.shape[0], width), bf16)], place, pack, *buffers, pieces=fresh_pieces
    )
    packed, lw = lax.optimization_barrier((packed, lw))
    came = lax.all_to_all(packed.reshape(planes, share, width), "outer", split_axis=0, concat_axis=0, tiled=True)
    came = came.reshape(planes * share, width)
    arrived = [came] + [swap(came, "query", flip) for flip in range(1, replicas)]

    pieces = table_pieces + shift(fresh_pieces, plane_rows)
    mine = None
    for s in [*range(1, planes), 0]:
        (partial,) = call(
            score_kernel,
            "score",
            [jax.ShapeDtypeStruct((2, query_count // LANES, LANES), f32)],
            place,
            meta_all,
            *got_queries[s],
            lw,
            row_ids,
            scales,
            *buffers,
            scratch=[pltpu.VMEM((query_count, LANES), f32)] * 4 + [pltpu.VMEM(queries.shape, bf16)],
            pieces=pieces,
            flip=s,
            slot=sum(cuts[:3]) // LANES,
            owners_plane=owners_plane,
            given=len(got_queries[s]),
        )
        if s:
            partial = swap(partial, "outer", s)
        mine = partial if mine is None else mine + partial
    (new_table,) = call(
        apply_kernel, "apply", [jax.ShapeDtypeStruct(table.shape, bf16)], None, apply_to, table, *arrived
    )
    loss = (jnp.log2(mine[0]) - mine[1]) * math.log(2.0)
    return new_table, new_ages, loss.reshape(query_count)


def solution(mesh):
    owners, replicas = mesh.shape["index"], mesh.shape["query"]
    inner = 1 << (int(math.log2(owners)) // 2)
    split = Mesh(mesh.devices.reshape(owners // inner, inner, replicas), ("outer", "inner", "query"))
    index = ("outer", "inner")
    placed = (
        P(index, None),
        P(index),
        P(index),
        P(index, None),
        P(index, None),
        P(("outer", "inner", "query"), None),
        P(("outer", "inner", "query")),
    )
    return jax.shard_map(
        on_device,
        mesh=split,
        in_specs=placed,
        out_specs=(P(index, None), P(index), P(("outer", "inner", "query"))),
        check_vma=False,
    )
```

```python
import functools
import math

import jax
import jax.numpy as jnp
from jax import lax
from jax.experimental import pallas as pl
from jax.experimental.pallas import tpu as pltpu
from jax.sharding import Mesh, PartitionSpec as P

score_scale = 20.0
age_scale = 16.0
epsilon = 1e-06
LOG2E = math.log2(math.e)
MASKED = -1e30
LANES = 128

NT = (((1,), (1,)), ((), ()))
NN = (((1,), (0,)), ((), ()))


def one_hot(ids, count):
    rows = lax.broadcasted_iota(jnp.int32, (count, ids.shape[1]), 0)
    return jnp.where(rows == ids, 1.0, 0.0).astype(jnp.bfloat16)


def split_terms(values):
    terms = []
    for _ in range(3):
        terms.append(values.astype(jnp.bfloat16))
        values = values - terms[-1].astype(jnp.float32)
    return terms


def counted(hits):
    count = hits.shape[1]
    before = lax.broadcasted_iota(jnp.int32, (count, count), 0)
    after = lax.broadcasted_iota(jnp.int32, (count, count), 1)
    earlier = jnp.where(before < after, 1.0, 0.0).astype(jnp.bfloat16)
    return lax.dot_general(hits.astype(jnp.bfloat16), earlier, NN, preferred_element_type=jnp.float32)


def small(values):
    return values.astype(jnp.float32).astype(jnp.bfloat16)


def number(values):
    return values.astype(jnp.float32).astype(jnp.int32)


def prep_kernel(
    place, table, fresh, ref_ids, ages, neg, pos, mail, rows_out, scale_out, table_in, fresh_in, arrived,
    *, owners, cap, replicas, encode
):
    core = place[2]
    copies = [
        pltpu.make_async_copy(fresh, fresh_in, arrived.at[0]),
        pltpu.make_async_copy(table, table_in, arrived.at[1]),
    ]
    for copy in copies:
        copy.start()
    rows_dev, width = table.shape
    refresh_dev, list_size = ref_ids.shape[1], neg.shape[1]
    share = cap // replicas

    mail[...] = jnp.zeros_like(mail)
    ids = ref_ids[...]
    lines = [
        jnp.concatenate([small(ids >> 7), small(ids & 127), small(pos[...] >> 7)], axis=1),
        jnp.concatenate([small(pos[...] & 127), small(ages[...])], axis=1),
    ]
    for digits in (neg[...] >> 7, neg[...] & 127):
        for first in range(0, list_size, width):
            lines.append(small(digits[:, first : first + width]))
    for owner in range(owners):
        for i, line in enumerate(lines):
            mail[owner, share + i : share + i + 1, : line.shape[1]] = line

    owner_of = ids // rows_dev
    hits = one_hot(owner_of, owners).astype(jnp.float32)
    rank = jnp.sum(hits * counted(hits), axis=0, keepdims=True).astype(jnp.int32) - core * share
    code = jnp.where((rank >= 0) & (rank < share), owner_of * share + rank, -1)
    select = one_hot(code, owners * share)
    copies[0].wait()
    packed = lax.dot_general(select, fresh_in[...], NN, preferred_element_type=jnp.float32).astype(jnp.bfloat16)
    for owner in range(owners):
        mail[owner, :share, :] = packed[owner * share : (owner + 1) * share, :]

    copies[1].wait()
    line, row = 0, 0
    halves = []
    for source in (table_in, fresh_in):
        rows = source.shape[0]
        half = rows // replicas
        rows_out[row : row + half, :] = source[pl.ds(pl.multiple_of(core * half, half), half), :]
        row += half
        for block in range(rows // LANES):
            squares = jnp.zeros((LANES, LANES), jnp.float32)
            for chunk in range(width // LANES):
                values = source[block * LANES : (block + 1) * LANES, chunk * LANES : (chunk + 1) * LANES]
                values = values.astype(jnp.float32)
                squares += values * values
            mean = jnp.sum(squares.T, axis=0, keepdims=True) / width
            scale_out[line + block : line + block + 1, :] = lax.rsqrt(mean + epsilon) * (score_scale / width * LOG2E)
        if encode:
            halves += [(line, i, half // LANES) for i in range(half // LANES)]
        line += rows // LANES
    if encode:
        rows_out[row:, :] = jnp.zeros((16, width), jnp.bfloat16)
        terms = []
        for first, i, count in halves:
            terms += split_terms(scale_out[pl.ds(first + core * count + i, 1), :])
        for i, term in enumerate(terms):
            rows_out[row + i : row + i + 1, :LANES] = term


def meta_kernel(place, mail, lw_out, row_out, target_out, own_out, *, planes, sizes, cap, replicas):
    outer, inner, core = place[0], place[1], place[2]
    owners, _, width = mail.shape
    owners_plane = owners // planes
    refresh_dev, rows_dev, list_size = sizes
    share = cap // replicas
    plane_rows = owners_plane * rows_dev
    high_count = planes * plane_rows // LANES
    own_owner = outer * owners_plane + inner

    def ref_digits(owner):
        line = number(mail[owner, share : share + 1, : 2 * refresh_dev])
        return line[:, :refresh_dev], line[:, refresh_dev:]

    def joined(pairs):
        return tuple(jnp.concatenate(part, axis=1) for part in zip(*pairs))

    def one_hots(pair):
        return one_hot(pair[0], high_count), one_hot(pair[1], LANES)

    def bitmap(pair):
        high, low = one_hots(pair)
        return lax.dot_general(low, high, NT, preferred_element_type=jnp.float32)

    def lookup(one_map, pair):
        hit = lax.dot_general(one_map.astype(jnp.bfloat16), pair[0], NN, preferred_element_type=jnp.float32)
        return jnp.sum(hit * pair[1].astype(jnp.float32), axis=0, keepdims=True) > 0.5

    beside = [outer * owners_plane + (inner ^ s) for s in range(owners_plane)]
    all_digits = [ref_digits(owner) for owner in range(owners)]
    refreshed_map = bitmap(joined(all_digits))
    plane_digits = joined([ref_digits(owner) for owner in beside])
    column = lax.broadcasted_iota(jnp.int32, (1, plane_rows), 1)
    table_ids = (outer * owners_plane + (inner ^ (column // rows_dev))) * rows_dev + column % rows_dev
    table_hots = one_hots((table_ids >> 7, table_ids & 127))
    fresh_hots = one_hots(plane_digits)

    ages = [number(mail[owner, share + 1 : share + 2, width - rows_dev :]) for owner in beside]
    ages = jnp.concatenate(ages, axis=1).astype(jnp.float32)
    weight = jnp.exp(-ages / age_scale).astype(jnp.bfloat16).astype(jnp.float32)
    refreshed = lookup(refreshed_map, table_hots)
    row_out[:, :plane_rows] = jnp.where(refreshed, -1, table_ids)
    row_out[:, plane_rows:] = plane_digits[0] * LANES + plane_digits[1]
    own_out[...] = refreshed[:, :rows_dev].astype(jnp.int32)
    log_weight = jnp.where(refreshed, MASKED, jnp.log2(weight))

    lines = -(-list_size // width)
    for group in range(planes):
        owner = (outer ^ group) * owners_plane + inner
        digits = []
        for first in (share + 2, share + 2 + lines):
            parts = [mail[owner, first + i : first + i + 1, :] for i in range(lines)]
            digits.append(number(jnp.concatenate(parts, axis=1)[:, :list_size]))
        one_map = bitmap(digits)
        lw_out[group : group + 1, :plane_rows] = jnp.where(lookup(one_map, table_hots), log_weight, MASKED)
        lw_out[group : group + 1, plane_rows:] = jnp.where(lookup(one_map, fresh_hots), 0.0, MASKED)

    local = [high * LANES + low - own_owner * rows_dev for high, low in all_digits]
    local = jnp.concatenate(local, axis=0)
    match = (local >= 0) & (local < rows_dev)
    rank = counted(jnp.where(match, 1.0, 0.0)).astype(jnp.int32)
    slot = jnp.where(match, ((rank // share) ^ core) * share + rank % share, -1)
    for owner in range(owners):
        row = jnp.where(match, local, 0)[owner : owner + 1, :]
        kinds = lax.broadcasted_iota(jnp.int32, (8, refresh_dev), 0)
        digits = jnp.where(kinds == 0, row // 16, jnp.where(kinds == 1, row % 16, 1))
        hits = one_hot(slot[owner : owner + 1, :], cap)
        found = lax.dot_general(small(digits), hits, NT, preferred_element_type=jnp.float32).astype(jnp.int32)
        target = jnp.where(found[2:3, :] > 0, found[0:1, :] * 16 + found[1:2, :], -1)
        for part in range(replicas):
            first = (part * owners + owner) * share
            target_out[:, first : first + share] = target[:, part * share : (part + 1) * share]


def piece_offset(place, piece):
    column, size, flip, by_core = piece
    if flip is None:
        return column
    column += (place[2] ^ flip) * size
    if by_core is not None:
        column += (place[2] ^ by_core) * size * 2
    return pl.multiple_of(column, size)


def apply_kernel(target, table, *refs):
    out = refs[-1]
    rows = lax.broadcasted_iota(jnp.int32, (table.shape[0], target.shape[1]), 0)
    chosen = jnp.where(rows == target[...], 1.0, 0.0)
    share = target.shape[1] // len(refs[:-1]) // refs[0].shape[0]
    arrived = [part[owner, :share, :] for part in refs[:-1] for owner in range(part.shape[0])]
    arrived = jnp.concatenate(arrived, axis=0)
    fresh = lax.dot_general(chosen.astype(jnp.bfloat16), arrived, NN, preferred_element_type=jnp.float32)
    hit = jnp.sum(chosen, axis=1, keepdims=True) > 0.5
    out[...] = jnp.where(hit, fresh, table[...].astype(jnp.float32)).astype(jnp.bfloat16)


def to_lanes(row):
    return jnp.broadcast_to(row, (LANES, LANES)).T


def score_kernel(place, mail, *refs, pieces, flip, share, owners_plane, given):
    out, total, pos_total, q_scale, pos_b, chosen = refs[-6:]
    queries = refs[0]
    if given == 2:
        at_end = (place[0] == 0) | (place[0] == 3)
        chosen[...] = jnp.where(at_end, refs[0][...], refs[1][...])
        queries = chosen
    log_weight, row_ids, scale, *refs = refs[given:-6]
    count, width = queries.shape
    owner = (place[0] ^ flip) * owners_plane + place[1]
    positive = number(mail[owner, share : share + 1, width - count :]) * LANES
    positive = (positive + number(mail[owner, share + 1 : share + 2, :count])).astype(jnp.float32)
    for block in range(count // LANES):
        part = slice(block * LANES, (block + 1) * LANES)
        values = queries[part, :].astype(jnp.float32)
        squares = jnp.sum(values * values, axis=1, keepdims=True)
        q_scale[part, :] = jnp.broadcast_to(lax.rsqrt(squares / width + epsilon), (LANES, LANES))
        pos_b[part, :] = to_lanes(positive[:, part])
    total[...] = jnp.zeros_like(total)
    pos_total[...] = jnp.zeros_like(pos_total)
    for source, start, size, column, scale_at in pieces:
        first = piece_offset(place, column)
        raw = lax.dot_general(
            queries[...], refs[source][start : start + size, :], NT, preferred_element_type=jnp.float32
        )
        sums = total[...]
        positives = pos_total[...]
        for chunk in range(size // LANES):
            cols = pl.ds(first + chunk * LANES, LANES)
            part = raw[:, chunk * LANES : (chunk + 1) * LANES]
            if scale_at < 0:
                line = -1 - scale_at + chunk
                row_scale = scale[line : line + 1, :]
            else:
                line = scale_at + 3 * chunk
                row_scale = jnp.sum(refs[source][line : line + 3, :LANES].astype(jnp.float32), axis=0, keepdims=True)
            powers = part * q_scale[...] * row_scale + log_weight[flip : flip + 1, cols]
            sums = sums + jnp.exp2(powers)
            positives = positives + jnp.where(pos_b[...] == row_ids[:, cols].astype(jnp.float32), powers, 0.0)
        total[...] = sums
        pos_total[...] = positives
    for block in range(count // LANES):
        part = slice(block * LANES, (block + 1) * LANES)
        out[0, block : block + 1, :] = jnp.sum(total[part, :].T, axis=0, keepdims=True)
        out[1, block : block + 1, :] = jnp.sum(pos_total[part, :].T, axis=0, keepdims=True)


def whole(memory=pltpu.VMEM):
    return pl.BlockSpec(memory_space=memory)


def call(kernel, name, outs, place, *operands, scratch=(), in_place=0, vmem=16, **options):
    specs = [whole(pltpu.HBM)] * in_place + [whole()] * (len(operands) - in_place)
    if place is not None:
        specs = [whole(pltpu.SMEM)] + specs
        operands = (place, *operands)
    return pl.pallas_call(
        functools.partial(kernel, **options),
        out_shape=tuple(outs),
        in_specs=specs,
        out_specs=tuple(whole() for _ in outs),
        scratch_shapes=list(scratch),
        compiler_params=pltpu.CompilerParams(vmem_limit_bytes=vmem << 20),
        cost_estimate=pl.CostEstimate(flops=1, bytes_accessed=1, transcendentals=0),
        name=name,
    )(*operands)


def swap(values, axis, flip):
    return lax.ppermute(values, axis, [(i, i ^ flip) for i in range(lax.axis_size(axis))])


def on_device(table, ages, refresh_ids, fresh_rows, neg_ids, queries, pos_ids):
    rows_dev, width = table.shape
    refresh_dev = refresh_ids.shape[0]
    planes = lax.axis_size("outer")
    owners_plane = lax.axis_size("inner")
    replicas = lax.axis_size("query")
    owners = planes * owners_plane
    query_count = queries.shape[0]
    list_size = neg_ids.shape[1]
    place = jnp.stack([lax.axis_index(name) for name in ("outer", "inner", "query")]).astype(jnp.int32)
    plane_rows = owners_plane * rows_dev
    plane_refresh = owners_plane * refresh_dev
    all_rows = plane_rows + plane_refresh
    cap = max(2, (2 * refresh_dev + owners - 1) // owners)
    share = cap // replicas
    table_half, fresh_half = rows_dev // replicas, refresh_dev // replicas
    bf16, f32 = jnp.bfloat16, jnp.float32

    assert 3 * refresh_dev == width and query_count + rows_dev == width and query_count == refresh_dev
    fast = replicas == 2 and owners_plane == 4 and planes == 4
    extra = 16 if fast else 0
    vmem = 16 if fast else 48
    mail, rows_half, scales = call(
        prep_kernel,
        "prep",
        [
            jax.ShapeDtypeStruct((owners, share + 8, width), bf16),
            jax.ShapeDtypeStruct((table_half + fresh_half + extra, width), bf16),
            jax.ShapeDtypeStruct(((rows_dev + refresh_dev) // LANES, LANES), f32),
        ],
        place,
        table,
        fresh_rows,
        refresh_ids.reshape(1, -1),
        ages.reshape(1, -1),
        neg_ids,
        pos_ids.reshape(1, -1),
        scratch=[
            pltpu.VMEM(table.shape, bf16),
            pltpu.VMEM(fresh_rows.shape, bf16),
            pltpu.SemaphoreType.DMA((2,)),
        ],
        in_place=2,
        vmem=vmem,
        owners=owners,
        cap=cap,
        replicas=replicas,
        encode=fast,
    )
    mail = lax.all_to_all(mail, ("outer", "inner"), split_axis=0, concat_axis=0, tiled=True)

    if fast:
        axes = ("inner", "query")
        first = [(2 * i + c, 2 * (i ^ (1 + c)) + c) for i in range(4) for c in range(2)]
        second = [(2 * i + c, 2 * (i ^ (2 - c)) + c) for i in range(4) for c in range(2)]
        near = lax.ppermute(rows_half, axes, first)
        side = lax.ppermute(rows_half, axes, second)
        middle, outward = [(1, 2), (2, 1)], [(1, 0), (2, 3)]
        beside = swap(queries, "outer", 1)
        across = lax.ppermute(queries, "outer", middle)
        near, beside, across = lax.optimization_barrier((near, beside, across))
        from_end = lax.ppermute(beside, "outer", middle)
        to_end = lax.ppermute(across, "outer", outward)
        far = lax.ppermute(near, axes, second)
        far, mail = lax.optimization_barrier((far, mail))
        last = lax.ppermute(from_end, "outer", outward)
        got_queries = [(queries,), (beside,), (to_end, from_end), (last, across)]
        buffers = [table, fresh_rows]
        table_pieces = [(0, 0, rows_dev, (0, rows_dev, None, None), -1)]
        fresh_pieces = [(1, 0, refresh_dev, (0, refresh_dev, None, None), -1 - rows_dev // LANES)]
        for slot, by_core, mine in ((1, 0, near), (1, 1, side), (3, None, far)):
            for flip, rows in enumerate((mine, swap(mine, "query", 1))):
                by = None if by_core is None else by_core ^ flip
                data = table_half + fresh_half
                fresh_at = data + 3 * (table_half // LANES)
                table_pieces.append((len(buffers), 0, table_half, (slot * rows_dev, table_half, flip, by), data))
                fresh_pieces.append(
                    (len(buffers), table_half, fresh_half, (slot * refresh_dev, fresh_half, flip, by), fresh_at)
                )
                buffers.append(rows)
    else:
        got_queries = [(queries,)] + [(swap(queries, "outer", s),) for s in range(1, planes)]
        got_rows = [rows_half] + [swap(rows_half, "inner", s) for s in range(1, owners_plane)]
        gathered = lax.all_gather(jnp.stack(got_rows), "query", axis=0)
        gathered = jnp.swapaxes(gathered, 0, 1)
        buffers = [
            gathered[:, :, :table_half].reshape(plane_rows, width),
            gathered[:, :, table_half:].reshape(plane_refresh, width),
        ]
        scales = []
        for rows in buffers:
            values = rows.astype(f32)
            mean = jnp.sum(values * values, axis=1) / width
            scales.append((lax.rsqrt(mean + epsilon) * (score_scale / width * LOG2E)).reshape(-1, LANES))
        scales = jnp.concatenate(scales)

        def blocks(buffer, count, line):
            starts = range(0, count, 512)
            return [(buffer, i, 512, (i, 512, None, None), -1 - line - i // LANES) for i in starts]

        table_pieces = blocks(0, plane_rows, 0)
        fresh_pieces = blocks(1, plane_refresh, plane_rows // LANES)

    lw, row_ids, target, own = call(
        meta_kernel,
        "meta",
        [
            jax.ShapeDtypeStruct((planes, all_rows), f32),
            jax.ShapeDtypeStruct((1, all_rows), jnp.int32),
            jax.ShapeDtypeStruct((1, owners * cap), jnp.int32),
            jax.ShapeDtypeStruct((1, rows_dev), jnp.int32),
        ],
        place,
        mail,
        vmem=vmem,
        planes=planes,
        sizes=(refresh_dev, rows_dev, list_size),
        cap=cap,
        replicas=replicas,
    )
    new_ages = jnp.where(own.reshape(rows_dev) > 0, 0, ages)
    mails = [mail] + [swap(mail, "query", flip) for flip in range(1, replicas)]

    def shift(pieces, columns):
        return [(a, b, c, (d[0] + columns, *d[1:]), e) for a, b, c, d, e in pieces]

    pieces = table_pieces + shift(fresh_pieces, plane_rows)
    mine = None
    for s in [*range(1, planes), 0]:
        (partial,) = call(
            score_kernel,
            "score",
            [jax.ShapeDtypeStruct((2, query_count // LANES, LANES), f32)],
            place,
            mail,
            *got_queries[s],
            lw,
            row_ids,
            scales,
            *buffers,
            scratch=[pltpu.VMEM((query_count, LANES), f32)] * 4 + [pltpu.VMEM(queries.shape, bf16)],
            vmem=vmem,
            pieces=pieces,
            flip=s,
            share=share,
            owners_plane=owners_plane,
            given=len(got_queries[s]),
        )
        if s:
            partial = swap(partial, "outer", s)
        mine = partial if mine is None else mine + partial
    (new_table,) = call(
        apply_kernel, "apply", [jax.ShapeDtypeStruct(table.shape, bf16)], None, target, table, *mails
    )
    loss = (jnp.log2(mine[0]) - mine[1]) * math.log(2.0)
    return new_table, new_ages, loss.reshape(query_count)


def solution(mesh):
    owners, replicas = mesh.shape["index"], mesh.shape["query"]
    inner = 1 << (int(math.log2(owners)) // 2)
    split = Mesh(mesh.devices.reshape(owners // inner, inner, replicas), ("outer", "inner", "query"))
    index = ("outer", "inner")
    placed = (
        P(index, None),
        P(index),
        P(index),
        P(index, None),
        P(index, None),
        P(("outer", "inner", "query"), None),
        P(("outer", "inner", "query")),
    )
    return jax.shard_map(
        on_device,
        mesh=split,
        in_specs=placed,
        out_specs=(P(index, None), P(index), P(("outer", "inner", "query"))),
        check_vma=False,
    )
```

```python
import functools
import math

import jax
import jax.numpy as jnp
from jax import lax
from jax.experimental import pallas as pl
from jax.experimental.pallas import tpu as pltpu
from jax.sharding import Mesh, PartitionSpec as P

score_scale = 20.0
age_scale = 16.0
epsilon = 1e-06
LOG2E = math.log2(math.e)
MASKED = -1e30
VMEM_LIMIT = 48 * 1024 * 1024
LANES = 128

NT = (((1,), (1,)), ((), ()))
NN = (((1,), (0,)), ((), ()))


def one_hot(ids, count):
    rows = lax.broadcasted_iota(jnp.int32, (count, ids.shape[1]), 0)
    return jnp.where(rows == ids, 1.0, 0.0).astype(jnp.bfloat16)


def split_terms(values):
    terms = []
    for _ in range(3):
        terms.append(values.astype(jnp.bfloat16))
        values = values - terms[-1].astype(jnp.float32)
    return terms


def counted(hits):
    count = hits.shape[1]
    before = lax.broadcasted_iota(jnp.int32, (count, count), 0)
    after = lax.broadcasted_iota(jnp.int32, (count, count), 1)
    earlier = jnp.where(before < after, 1.0, 0.0).astype(jnp.bfloat16)
    return lax.dot_general(hits.astype(jnp.bfloat16), earlier, NN, preferred_element_type=jnp.float32)


def small(values):
    return values.astype(jnp.float32).astype(jnp.bfloat16)


def prep_kernel(place, table, fresh, rows_out, scale_out, *, replicas, encode):
    core = place[2]
    width = table.shape[1]
    line, row = 0, 0
    halves = []
    for source in (table, fresh):
        rows = source.shape[0]
        half = rows // replicas
        rows_out[row : row + half, :] = source[pl.ds(pl.multiple_of(core * half, half), half), :]
        row += half
        for block in range(rows // LANES):
            squares = jnp.zeros((LANES, LANES), jnp.float32)
            for chunk in range(width // LANES):
                values = source[block * LANES : (block + 1) * LANES, chunk * LANES : (chunk + 1) * LANES]
                values = values.astype(jnp.float32)
                squares += values * values
            mean = jnp.sum(squares.T, axis=0, keepdims=True) / width
            scale_out[line + block : line + block + 1, :] = lax.rsqrt(mean + epsilon) * (score_scale / width * LOG2E)
        if encode:
            halves += [(line, i, half // LANES) for i in range(half // LANES)]
        line += rows // LANES
    if encode:
        rows_out[row:, :] = jnp.zeros((16, width), jnp.bfloat16)
        terms = []
        for first, i, count in halves:
            terms += split_terms(scale_out[pl.ds(first + core * count + i, 1), :])
        for i, term in enumerate(terms):
            rows_out[row + i : row + i + 1, :LANES] = term


def meta_kernel(place, *refs, planes, owners_plane, sizes, cap, replicas):
    outer, inner, core = place[0], place[1], place[2]
    lines, sides = refs[:planes], refs[planes : planes + owners_plane]
    lw_out, row_out, code_out, own_target_out, target_out, own_out = refs[planes + owners_plane :]
    refresh_dev, rows_dev, list_size = sizes
    share = cap // replicas
    plane_rows = owners_plane * rows_dev
    high_count = planes * plane_rows // LANES
    own_owner = outer * owners_plane + inner

    def one_hots(ids):
        return one_hot(ids >> 7, high_count), one_hot(ids & 127, LANES)

    def bitmap(ids):
        high, low = one_hots(ids)
        return lax.dot_general(low, high, NT, preferred_element_type=jnp.float32)

    def lookup(one_map, pair):
        hit = lax.dot_general(one_map.astype(jnp.bfloat16), pair[0], NN, preferred_element_type=jnp.float32)
        return jnp.sum(hit * pair[1].astype(jnp.float32), axis=0, keepdims=True) > 0.5

    def ref_ids(plane, side):
        return sides[side][:, plane * refresh_dev : (plane + 1) * refresh_dev]

    all_refs = planes * refresh_dev
    plane_ids = jnp.concatenate([ref_ids(0, side) for side in range(owners_plane)], axis=1)
    refreshed_map = bitmap(jnp.concatenate([side[:, :all_refs] for side in sides], axis=1))
    column = lax.broadcasted_iota(jnp.int32, (1, plane_rows), 1)
    table_ids = (outer * owners_plane + (inner ^ (column // rows_dev))) * rows_dev + column % rows_dev
    table_hots, fresh_hots = one_hots(table_ids), one_hots(plane_ids)

    ages = jnp.concatenate([side[:, all_refs:] for side in sides], axis=1).astype(jnp.float32)
    weight = jnp.exp(-ages / age_scale).astype(jnp.bfloat16).astype(jnp.float32)
    refreshed = lookup(refreshed_map, table_hots)
    row_out[:, :plane_rows] = jnp.where(refreshed, -1, table_ids).astype(jnp.float32)
    row_out[:, plane_rows:] = plane_ids.astype(jnp.float32)
    own_out[...] = refreshed[:, :rows_dev].astype(jnp.int32)
    log_weight = jnp.where(refreshed, MASKED, jnp.log2(weight))
    for group in range(planes):
        one_map = bitmap(lines[group][:, refresh_dev : refresh_dev + list_size])
        lw_out[group : group + 1, :plane_rows] = jnp.where(lookup(one_map, table_hots), log_weight, MASKED)
        lw_out[group : group + 1, plane_rows:] = jnp.where(lookup(one_map, fresh_hots), 0.0, MASKED)

    pairs = [(plane, side) for plane in range(planes) for side in range(owners_plane)]
    sent_owner = [ref_ids(0, side) // rows_dev - ((outer ^ plane) * owners_plane + inner) for plane, side in pairs]
    taken_owner = [ref_ids(plane, side) // rows_dev - own_owner for plane, side in pairs]
    match = jnp.concatenate(sent_owner + taken_owner, axis=0) == 0
    rank = counted(jnp.where(match, 1.0, 0.0)).astype(jnp.int32)
    rank = jnp.where(match, rank, -cap)
    own_target_out[...] = plane_ids - own_owner * rows_dev
    for i, (plane, side) in enumerate(pairs):
        if plane == 0:
            code_out[:, side * refresh_dev : (side + 1) * refresh_dev] = jnp.full((1, refresh_dev), -1, jnp.int32)
            continue
        base = ((plane - 1) * owners_plane + side) * share
        sent_rank = rank[i : i + 1, :] - core * share
        columns = slice(side * refresh_dev, (side + 1) * refresh_dev)
        here = (sent_rank >= 0) & (sent_rank < share)
        code_out[:, columns] = jnp.where(here, base + sent_rank, code_out[:, columns])
        take_rank = rank[len(pairs) + i : len(pairs) + i + 1, :]
        slot = jnp.where(take_rank < 0, -1, ((take_rank // share) ^ core) * share + take_rank % share)
        row = jnp.where(take_rank < 0, 0, ref_ids(plane, side) - own_owner * rows_dev)
        kinds = lax.broadcasted_iota(jnp.int32, (8, refresh_dev), 0)
        digits = jnp.where(kinds == 0, row // 16, jnp.where(kinds == 1, row % 16, 1))
        found = lax.dot_general(small(digits), one_hot(slot, cap), NT, preferred_element_type=jnp.float32)
        found = found.astype(jnp.int32)
        target = jnp.where(found[2:3, :] > 0, found[0:1, :] * 16 + found[1:2, :], -1)
        for part in range(replicas):
            first = part * (planes - 1) * owners_plane * share + base
            target_out[:, first : first + share] = target[:, part * share : (part + 1) * share]


def piece_offset(place, piece):
    column, size, flip, by_core = piece
    if flip is None:
        return column
    column += (place[2] ^ flip) * size
    if by_core is not None:
        column += (place[2] ^ by_core) * size * 2
    return pl.multiple_of(column, size)


def pack_kernel(place, code, scale, *refs, pieces, all_pieces):
    *buffers, out, scale_out = refs
    total = jnp.zeros(out.shape, jnp.float32)
    for source, start, size, column, _ in pieces:
        select = one_hot(code[:, pl.ds(piece_offset(place, column), size)], out.shape[0])
        total += lax.dot_general(select, buffers[source][start : start + size, :], NN, preferred_element_type=jnp.float32)
    out[...] = total.astype(jnp.bfloat16)
    for source, start, size, column, scale_at in all_pieces:
        first = piece_offset(place, column)
        for chunk in range(size // LANES):
            if scale_at < 0:
                line = -1 - scale_at + chunk
                row = scale[line : line + 1, :]
            else:
                line = scale_at + 3 * chunk
                row = jnp.sum(buffers[source][line : line + 3, :LANES].astype(jnp.float32), axis=0, keepdims=True)
            scale_out[:, pl.ds(first + chunk * LANES, LANES)] = row


def apply_kernel(place, own_target, target, table, *refs, pieces, arrivals):
    out = refs[-1]
    buffers, arrived = refs[: -1 - arrivals], refs[-1 - arrivals : -1]
    parts = [
        (own_target[:, pl.ds(piece_offset(place, column), size)], buffers[source][start : start + size, :])
        for source, start, size, column, _ in pieces
    ]
    first = 0
    for block in arrived:
        parts.append((target[:, first : first + block.shape[0]], block[...]))
        first += block.shape[0]
    fresh = jnp.zeros(out.shape, jnp.float32)
    hit = jnp.zeros((out.shape[0], 1), jnp.float32)
    for to_row, values in parts:
        rows = lax.broadcasted_iota(jnp.int32, (out.shape[0], to_row.shape[1]), 0)
        chosen = jnp.where(rows == to_row, 1.0, 0.0)
        hit += jnp.sum(chosen, axis=1, keepdims=True)
        fresh += lax.dot_general(chosen.astype(jnp.bfloat16), values, NN, preferred_element_type=jnp.float32)
    out[...] = jnp.where(hit > 0.5, fresh, table[...].astype(jnp.float32)).astype(jnp.bfloat16)


def to_lanes(row):
    return jnp.broadcast_to(row, (LANES, LANES)).T


def score_kernel(place, positive, *refs, pieces, flip, given):
    out, total, pos_total, q_scale, pos_b, chosen = refs[-6:]
    queries = refs[0]
    if given == 2:
        at_end = (place[0] == 0) | (place[0] == 3)
        chosen[...] = jnp.where(at_end, refs[0][...], refs[1][...])
        queries = chosen
    log_weight, row_ids, scale, *refs = refs[given:-6]
    count, width = queries.shape
    for block in range(count // LANES):
        part = slice(block * LANES, (block + 1) * LANES)
        values = queries[part, :].astype(jnp.float32)
        squares = jnp.sum(values * values, axis=1, keepdims=True)
        q_scale[part, :] = jnp.broadcast_to(lax.rsqrt(squares / width + epsilon), (LANES, LANES))
        pos_b[part, :] = to_lanes(positive[:, part].astype(jnp.float32))
    total[...] = jnp.zeros_like(total)
    pos_total[...] = jnp.zeros_like(pos_total)
    for source, start, size, column, _ in pieces:
        first = piece_offset(place, column)
        raw = lax.dot_general(
            queries[...], refs[source][start : start + size, :], NT, preferred_element_type=jnp.float32
        )
        for top in range(0, count, 64):
            part = slice(top, top + 64)
            sums, positives = total[part, :], pos_total[part, :]
            for chunk in range(size // LANES):
                cols = pl.ds(first + chunk * LANES, LANES)
                powers = raw[part, chunk * LANES : (chunk + 1) * LANES] * q_scale[part, :]
                powers = powers * scale[:, cols] + log_weight[flip : flip + 1, cols]
                sums = sums + jnp.exp2(powers)
                positives = positives + jnp.where(pos_b[part, :] == row_ids[:, cols], powers, 0.0)
            total[part, :] = sums
            pos_total[part, :] = positives
    for block in range(count // LANES):
        part = slice(block * LANES, (block + 1) * LANES)
        out[0, block : block + 1, :] = jnp.sum(total[part, :].T, axis=0, keepdims=True)
        out[1, block : block + 1, :] = jnp.sum(pos_total[part, :].T, axis=0, keepdims=True)


def whole(memory=pltpu.VMEM):
    return pl.BlockSpec(memory_space=memory)


def call(kernel, name, outs, place, *operands, scratch=(), **options):
    specs = [whole()] * len(operands)
    if place is not None:
        specs = [whole(pltpu.SMEM)] + specs
        operands = (place, *operands)
    return pl.pallas_call(
        functools.partial(kernel, **options),
        out_shape=tuple(outs),
        in_specs=specs,
        out_specs=tuple(whole() for _ in outs),
        scratch_shapes=list(scratch),
        compiler_params=pltpu.CompilerParams(vmem_limit_bytes=VMEM_LIMIT),
        cost_estimate=pl.CostEstimate(flops=1, bytes_accessed=1, transcendentals=0),
        name=name,
    )(*operands)


def swap(values, axis, flip):
    return lax.ppermute(values, axis, [(i, i ^ flip) for i in range(lax.axis_size(axis))])


def on_device(table, ages, refresh_ids, fresh_rows, neg_ids, queries, pos_ids):
    rows_dev, width = table.shape
    refresh_dev = refresh_ids.shape[0]
    planes = lax.axis_size("outer")
    owners_plane = lax.axis_size("inner")
    replicas = lax.axis_size("query")
    owners = planes * owners_plane
    query_count = queries.shape[0]
    list_size = neg_ids.shape[1]
    place = jnp.stack([lax.axis_index(name) for name in ("outer", "inner", "query")]).astype(jnp.int32)
    plane_rows = owners_plane * rows_dev
    plane_refresh = owners_plane * refresh_dev
    all_rows = plane_rows + plane_refresh
    cap = max(2, (2 * refresh_dev + owners - 1) // owners)
    share = cap // replicas
    table_half, fresh_half = rows_dev // replicas, refresh_dev // replicas
    bf16, f32 = jnp.bfloat16, jnp.float32

    line = jnp.concatenate([refresh_ids, neg_ids[0], pos_ids])
    lines = [line] + [swap(line, "outer", s) for s in range(1, planes)]
    side = jnp.concatenate([one[:refresh_dev] for one in lines] + [ages])
    sides = [side] + [swap(side, "inner", s) for s in range(1, owners_plane)]
    positive = [one[refresh_dev + list_size :].reshape(1, -1) for one in lines]

    fast = replicas == 2 and owners_plane == 4 and planes == 4
    extra = 16 if fast else 0
    rows_half, scales = call(
        prep_kernel,
        "prep",
        [
            jax.ShapeDtypeStruct((table_half + fresh_half + extra, width), bf16),
            jax.ShapeDtypeStruct(((rows_dev + refresh_dev) // LANES, LANES), f32),
        ],
        place,
        table,
        fresh_rows,
        replicas=replicas,
        encode=fast,
    )
    rows_half, *sides = lax.optimization_barrier((rows_half, *sides))

    others = (planes - 1) * owners_plane
    lw, row_ids, code, own_target, target, own = call(
        meta_kernel,
        "meta",
        [
            jax.ShapeDtypeStruct((planes, all_rows), f32),
            jax.ShapeDtypeStruct((1, all_rows), f32),
            jax.ShapeDtypeStruct((1, plane_refresh), jnp.int32),
            jax.ShapeDtypeStruct((1, plane_refresh), jnp.int32),
            jax.ShapeDtypeStruct((1, others * cap), jnp.int32),
            jax.ShapeDtypeStruct((1, rows_dev), jnp.int32),
        ],
        place,
        *[one.reshape(1, -1) for one in lines],
        *[one.reshape(1, -1) for one in sides],
        planes=planes,
        owners_plane=owners_plane,
        sizes=(refresh_dev, rows_dev, list_size),
        cap=cap,
        replicas=replicas,
    )
    new_ages = jnp.where(own.reshape(rows_dev) > 0, 0, ages)

    if fast:
        axes = ("inner", "query")
        first = [(2 * i + c, 2 * (i ^ (1 + c)) + c) for i in range(4) for c in range(2)]
        second = [(2 * i + c, 2 * (i ^ (2 - c)) + c) for i in range(4) for c in range(2)]
        near = lax.ppermute(rows_half, axes, first)
        side = lax.ppermute(rows_half, axes, second)
        middle, outward = [(1, 2), (2, 1)], [(1, 0), (2, 3)]
        beside = swap(queries, "outer", 1)
        across = lax.ppermute(queries, "outer", middle)
        near, beside, across, lw = lax.optimization_barrier((near, beside, across, lw))
        from_end = lax.ppermute(beside, "outer", middle)
        to_end = lax.ppermute(across, "outer", outward)
        far = lax.ppermute(near, axes, second)
        far, from_end, to_end = lax.optimization_barrier((far, from_end, to_end))
        last = lax.ppermute(from_end, "outer", outward)
        got_queries = [(queries,), (beside,), (to_end, from_end), (last, across)]
        buffers = [table, fresh_rows]
        table_pieces = [(0, 0, rows_dev, (0, rows_dev, None, None), -1)]
        fresh_pieces = [(1, 0, refresh_dev, (0, refresh_dev, None, None), -1 - rows_dev // LANES)]
        for slot, by_core, mine in ((1, 0, near), (1, 1, side), (3, None, far)):
            for flip, rows in enumerate((mine, swap(mine, "query", 1))):
                by = None if by_core is None else by_core ^ flip
                data = table_half + fresh_half
                fresh_at = data + 3 * (table_half // LANES)
                table_pieces.append((len(buffers), 0, table_half, (slot * rows_dev, table_half, flip, by), data))
                fresh_pieces.append(
                    (len(buffers), table_half, fresh_half, (slot * refresh_dev, fresh_half, flip, by), fresh_at)
                )
                buffers.append(rows)
    else:
        got_queries = [(queries,)] + [(swap(queries, "outer", s),) for s in range(1, planes)]
        got_rows = [rows_half] + [swap(rows_half, "inner", s) for s in range(1, owners_plane)]
        gathered = lax.all_gather(jnp.stack(got_rows), "query", axis=0)
        gathered = jnp.swapaxes(gathered, 0, 1)
        buffers = [
            gathered[:, :, :table_half].reshape(plane_rows, width),
            gathered[:, :, table_half:].reshape(plane_refresh, width),
        ]
        scales = []
        for rows in buffers:
            values = rows.astype(f32)
            mean = jnp.sum(values * values, axis=1) / width
            scales.append((lax.rsqrt(mean + epsilon) * (score_scale / width * LOG2E)).reshape(-1, LANES))
        scales = jnp.concatenate(scales)

        def blocks(buffer, count, line):
            starts = range(0, count, 512)
            return [(buffer, i, 512, (i, 512, None, None), -1 - line - i // LANES) for i in starts]

        table_pieces = blocks(0, plane_rows, 0)
        fresh_pieces = blocks(1, plane_refresh, plane_rows // LANES)

    def shift(pieces, columns):
        return [(a, b, c, (d[0] + columns, *d[1:]), e) for a, b, c, d, e in pieces]

    pieces = table_pieces + shift(fresh_pieces, plane_rows)
    packed, scale_plane = call(
        pack_kernel,
        "pack",
        [jax.ShapeDtypeStruct((others * share, width), bf16), jax.ShapeDtypeStruct((1, all_rows), f32)],
        place,
        code,
        scales,
        *buffers,
        pieces=fresh_pieces,
        all_pieces=pieces,
    )
    size = owners_plane * share
    came = jnp.concatenate([swap(packed[(s - 1) * size : s * size], "outer", s) for s in range(1, planes)])
    arrived = [came] + [swap(came, "query", flip) for flip in range(1, replicas)]
    mine = None
    for s in [*range(1, planes), 0]:
        (partial,) = call(
            score_kernel,
            "score",
            [jax.ShapeDtypeStruct((2, query_count // LANES, LANES), f32)],
            place,
            positive[s],
            *got_queries[s],
            lw,
            row_ids,
            scale_plane,
            *buffers,
            scratch=[pltpu.VMEM((query_count, LANES), f32)] * 4 + [pltpu.VMEM(queries.shape, bf16)],
            pieces=pieces,
            flip=s,
            given=len(got_queries[s]),
        )
        if s:
            partial = swap(partial, "outer", s)
        mine = partial if mine is None else mine + partial
    (new_table,) = call(
        apply_kernel,
        "apply",
        [jax.ShapeDtypeStruct(table.shape, bf16)],
        place,
        own_target,
        target,
        table,
        *buffers,
        *arrived,
        pieces=fresh_pieces,
        arrivals=len(arrived),
    )
    loss = (jnp.log2(mine[0]) - mine[1]) * math.log(2.0)
    return new_table, new_ages, loss.reshape(query_count)


def solution(mesh):
    owners, replicas = mesh.shape["index"], mesh.shape["query"]
    inner = 1 << (int(math.log2(owners)) // 2)
    split = Mesh(mesh.devices.reshape(owners // inner, inner, replicas), ("outer", "inner", "query"))
    index = ("outer", "inner")
    placed = (
        P(index, None),
        P(index),
        P(index),
        P(index, None),
        P(index, None),
        P(("outer", "inner", "query"), None),
        P(("outer", "inner", "query")),
    )
    return jax.shard_map(
        on_device,
        mesh=split,
        in_specs=placed,
        out_specs=(P(index, None), P(index), P(("outer", "inner", "query"))),
        check_vma=False,
    )
```

```python
import functools
import math

import jax
import jax.numpy as jnp
from jax import lax
from jax.experimental import pallas as pl
from jax.experimental.pallas import tpu as pltpu
from jax.sharding import Mesh, PartitionSpec as P

score_scale = 20.0
age_scale = 16.0
epsilon = 1e-06
LOG2E = math.log2(math.e)
MASKED = -1e30
VMEM_LIMIT = 48 * 1024 * 1024
LANES = 128

NT = (((1,), (1,)), ((), ()))
NN = (((1,), (0,)), ((), ()))


def one_hot(ids, count):
    rows = lax.broadcasted_iota(jnp.int32, (count, ids.shape[1]), 0)
    return jnp.where(rows == ids, 1.0, 0.0).astype(jnp.bfloat16)


def split_terms(values):
    terms = []
    for _ in range(3):
        terms.append(values.astype(jnp.bfloat16))
        values = values - terms[-1].astype(jnp.float32)
    return terms


def counted(hits):
    count = hits.shape[1]
    before = lax.broadcasted_iota(jnp.int32, (count, count), 0)
    after = lax.broadcasted_iota(jnp.int32, (count, count), 1)
    earlier = jnp.where(before < after, 1.0, 0.0).astype(jnp.bfloat16)
    return lax.dot_general(hits.astype(jnp.bfloat16), earlier, NN, preferred_element_type=jnp.float32)


def small(values):
    return values.astype(jnp.float32).astype(jnp.bfloat16)


def prep_kernel(place, table, fresh, rows_out, scale_out, *, replicas, encode):
    core = place[2]
    width = table.shape[1]
    line, row = 0, 0
    halves = []
    for source in (table, fresh):
        rows = source.shape[0]
        half = rows // replicas
        rows_out[row : row + half, :] = source[pl.ds(pl.multiple_of(core * half, half), half), :]
        row += half
        for block in range(rows // LANES):
            squares = jnp.zeros((LANES, LANES), jnp.float32)
            for chunk in range(width // LANES):
                values = source[block * LANES : (block + 1) * LANES, chunk * LANES : (chunk + 1) * LANES]
                values = values.astype(jnp.float32)
                squares += values * values
            mean = jnp.sum(squares.T, axis=0, keepdims=True) / width
            scale_out[line + block : line + block + 1, :] = lax.rsqrt(mean + epsilon) * (score_scale / width * LOG2E)
        if encode:
            halves += [(line, i, half // LANES) for i in range(half // LANES)]
        line += rows // LANES
    if encode:
        rows_out[row:, :] = jnp.zeros((16, width), jnp.bfloat16)
        terms = []
        for first, i, count in halves:
            terms += split_terms(scale_out[pl.ds(first + core * count + i, 1), :])
        for i, term in enumerate(terms):
            rows_out[row + i : row + i + 1, :LANES] = term


def meta_kernel(place, *refs, planes, owners_plane, sizes, cap, replicas):
    outer, inner, core = place[0], place[1], place[2]
    lines, sides = refs[:planes], refs[planes : planes + owners_plane]
    lw_out, row_out, code_out, own_target_out, target_out, own_out = refs[planes + owners_plane :]
    refresh_dev, rows_dev, list_size = sizes
    share = cap // replicas
    plane_rows = owners_plane * rows_dev
    high_count = planes * plane_rows // LANES
    own_owner = outer * owners_plane + inner

    def one_hots(ids):
        return one_hot(ids >> 7, high_count), one_hot(ids & 127, LANES)

    def bitmap(ids):
        high, low = one_hots(ids)
        return lax.dot_general(low, high, NT, preferred_element_type=jnp.float32)

    def lookup(one_map, pair):
        hit = lax.dot_general(one_map.astype(jnp.bfloat16), pair[0], NN, preferred_element_type=jnp.float32)
        return jnp.sum(hit * pair[1].astype(jnp.float32), axis=0, keepdims=True) > 0.5

    def ref_ids(plane, side):
        return sides[side][:, plane * refresh_dev : (plane + 1) * refresh_dev]

    all_refs = planes * refresh_dev
    plane_ids = jnp.concatenate([ref_ids(0, side) for side in range(owners_plane)], axis=1)
    refreshed_map = bitmap(jnp.concatenate([side[:, :all_refs] for side in sides], axis=1))
    column = lax.broadcasted_iota(jnp.int32, (1, plane_rows), 1)
    table_ids = (outer * owners_plane + (inner ^ (column // rows_dev))) * rows_dev + column % rows_dev
    table_hots, fresh_hots = one_hots(table_ids), one_hots(plane_ids)

    ages = jnp.concatenate([side[:, all_refs:] for side in sides], axis=1).astype(jnp.float32)
    weight = jnp.exp(-ages / age_scale).astype(jnp.bfloat16).astype(jnp.float32)
    refreshed = lookup(refreshed_map, table_hots)
    row_out[:, :plane_rows] = jnp.where(refreshed, -1, table_ids).astype(jnp.float32)
    row_out[:, plane_rows:] = plane_ids.astype(jnp.float32)
    own_out[...] = refreshed[:, :rows_dev].astype(jnp.int32)
    log_weight = jnp.where(refreshed, MASKED, jnp.log2(weight))
    for group in range(planes):
        one_map = bitmap(lines[group][:, refresh_dev : refresh_dev + list_size])
        lw_out[group : group + 1, :plane_rows] = jnp.where(lookup(one_map, table_hots), log_weight, MASKED)
        lw_out[group : group + 1, plane_rows:] = jnp.where(lookup(one_map, fresh_hots), 0.0, MASKED)

    pairs = [(plane, side) for plane in range(planes) for side in range(owners_plane)]
    sent_owner = [ref_ids(0, side) // rows_dev - ((outer ^ plane) * owners_plane + inner) for plane, side in pairs]
    taken_owner = [ref_ids(plane, side) // rows_dev - own_owner for plane, side in pairs]
    match = jnp.concatenate(sent_owner + taken_owner, axis=0) == 0
    rank = counted(jnp.where(match, 1.0, 0.0)).astype(jnp.int32)
    rank = jnp.where(match, rank, -cap)
    own_target_out[...] = plane_ids - own_owner * rows_dev
    for i, (plane, side) in enumerate(pairs):
        if plane == 0:
            code_out[:, side * refresh_dev : (side + 1) * refresh_dev] = jnp.full((1, refresh_dev), -1, jnp.int32)
            continue
        base = ((plane - 1) * owners_plane + side) * share
        sent_rank = rank[i : i + 1, :] - core * share
        columns = slice(side * refresh_dev, (side + 1) * refresh_dev)
        here = (sent_rank >= 0) & (sent_rank < share)
        code_out[:, columns] = jnp.where(here, base + sent_rank, code_out[:, columns])
        take_rank = rank[len(pairs) + i : len(pairs) + i + 1, :]
        slot = jnp.where(take_rank < 0, -1, ((take_rank // share) ^ core) * share + take_rank % share)
        row = jnp.where(take_rank < 0, 0, ref_ids(plane, side) - own_owner * rows_dev)
        kinds = lax.broadcasted_iota(jnp.int32, (8, refresh_dev), 0)
        digits = jnp.where(kinds == 0, row // 16, jnp.where(kinds == 1, row % 16, 1))
        found = lax.dot_general(small(digits), one_hot(slot, cap), NT, preferred_element_type=jnp.float32)
        found = found.astype(jnp.int32)
        target = jnp.where(found[2:3, :] > 0, found[0:1, :] * 16 + found[1:2, :], -1)
        for part in range(replicas):
            first = part * (planes - 1) * owners_plane * share + base
            target_out[:, first : first + share] = target[:, part * share : (part + 1) * share]


def piece_offset(place, piece):
    column, size, flip, by_core = piece
    if flip is None:
        return column
    column += (place[2] ^ flip) * size
    if by_core is not None:
        column += (place[2] ^ by_core) * size * 2
    return pl.multiple_of(column, size)


def pack_kernel(place, code, scale, *refs, pieces, all_pieces):
    *buffers, out, scale_out = refs
    total = jnp.zeros(out.shape, jnp.float32)
    for source, start, size, column, _ in pieces:
        select = one_hot(code[:, pl.ds(piece_offset(place, column), size)], out.shape[0])
        total += lax.dot_general(select, buffers[source][start : start + size, :], NN, preferred_element_type=jnp.float32)
    out[...] = total.astype(jnp.bfloat16)
    for source, start, size, column, scale_at in all_pieces:
        first = piece_offset(place, column)
        for chunk in range(size // LANES):
            if scale_at < 0:
                line = -1 - scale_at + chunk
                row = scale[line : line + 1, :]
            else:
                line = scale_at + 3 * chunk
                row = jnp.sum(buffers[source][line : line + 3, :LANES].astype(jnp.float32), axis=0, keepdims=True)
            scale_out[:, pl.ds(first + chunk * LANES, LANES)] = row


def apply_kernel(place, own_target, target, refreshed, table, *refs, pieces, arrivals):
    out = refs[-1]
    buffers, arrived = refs[: -1 - arrivals], refs[-1 - arrivals : -1]
    parts = [
        (own_target[:, pl.ds(piece_offset(place, column), size)], buffers[source][start : start + size, :])
        for source, start, size, column, _ in pieces
    ]
    first = 0
    for block in arrived:
        parts.append((target[:, first : first + block.shape[0]], block[...]))
        first += block.shape[0]
    fresh = jnp.zeros(out.shape, jnp.float32)
    for to_row, values in parts:
        rows = lax.broadcasted_iota(jnp.int32, (out.shape[0], to_row.shape[1]), 0)
        chosen = jnp.where(rows == to_row, 1.0, 0.0).astype(jnp.bfloat16)
        fresh += lax.dot_general(chosen, values, NN, preferred_element_type=jnp.float32)
    for top in range(0, out.shape[0], LANES):
        part = slice(top, top + LANES)
        hit = to_lanes(refreshed[:, part].astype(jnp.float32)) > 0.5
        for left in range(0, out.shape[1], LANES):
            cols = slice(left, left + LANES)
            out[part, cols] = jnp.where(hit, fresh[part, cols], table[part, cols].astype(jnp.float32)).astype(jnp.bfloat16)


def to_lanes(row):
    return jnp.broadcast_to(row, (LANES, LANES)).T


def score_kernel(place, positive, *refs, pieces, flip, given):
    out, total, pos_total, q_scale, pos_b, chosen = refs[-6:]
    queries = refs[0]
    if given == 2:
        at_end = (place[0] == 0) | (place[0] == 3)
        chosen[...] = jnp.where(at_end, refs[0][...], refs[1][...])
        queries = chosen
    log_weight, row_ids, scale, *refs = refs[given:-6]
    count, width = queries.shape
    for block in range(count // LANES):
        part = slice(block * LANES, (block + 1) * LANES)
        values = queries[part, :].astype(jnp.float32)
        squares = jnp.sum(values * values, axis=1, keepdims=True)
        q_scale[part, :] = jnp.broadcast_to(lax.rsqrt(squares / width + epsilon), (LANES, LANES))
        pos_b[part, :] = to_lanes(positive[:, part].astype(jnp.float32))
    total[...] = jnp.zeros_like(total)
    pos_total[...] = jnp.zeros_like(pos_total)

    def product(piece):
        source, start, size = piece[:3]
        rows = refs[source][start : start + size, :]
        return lax.dot_general(queries[...], rows, NT, preferred_element_type=jnp.float32)

    following = product(pieces[0])
    for i, (_, _, size, column, _) in enumerate(pieces):
        raw = following
        if i + 1 < len(pieces):
            following = product(pieces[i + 1])
        first = piece_offset(place, column)
        for top in range(0, count, 64):
            part = slice(top, top + 64)
            sums, positives = total[part, :], pos_total[part, :]
            query_scale, wanted = q_scale[part, :], pos_b[part, :]
            for chunk in range(size // LANES):
                cols = pl.ds(first + chunk * LANES, LANES)
                powers = raw[part, chunk * LANES : (chunk + 1) * LANES] * query_scale
                powers = powers * scale[:, cols] + log_weight[flip : flip + 1, cols]
                sums = sums + jnp.exp2(powers)
                positives = positives + jnp.where(wanted == row_ids[:, cols], powers, 0.0)
            total[part, :] = sums
            pos_total[part, :] = positives
    for block in range(count // LANES):
        part = slice(block * LANES, (block + 1) * LANES)
        out[0, block : block + 1, :] = jnp.sum(total[part, :].T, axis=0, keepdims=True)
        out[1, block : block + 1, :] = jnp.sum(pos_total[part, :].T, axis=0, keepdims=True)


def whole(memory=pltpu.VMEM):
    return pl.BlockSpec(memory_space=memory)


def call(kernel, name, outs, place, *operands, scratch=(), **options):
    specs = [whole()] * len(operands)
    if place is not None:
        specs = [whole(pltpu.SMEM)] + specs
        operands = (place, *operands)
    return pl.pallas_call(
        functools.partial(kernel, **options),
        out_shape=tuple(outs),
        in_specs=specs,
        out_specs=tuple(whole() for _ in outs),
        scratch_shapes=list(scratch),
        compiler_params=pltpu.CompilerParams(vmem_limit_bytes=VMEM_LIMIT),
        cost_estimate=pl.CostEstimate(flops=1, bytes_accessed=1, transcendentals=0),
        name=name,
    )(*operands)


def swap(values, axis, flip):
    return lax.ppermute(values, axis, [(i, i ^ flip) for i in range(lax.axis_size(axis))])


def on_device(table, ages, refresh_ids, fresh_rows, neg_ids, queries, pos_ids):
    rows_dev, width = table.shape
    refresh_dev = refresh_ids.shape[0]
    planes = lax.axis_size("outer")
    owners_plane = lax.axis_size("inner")
    replicas = lax.axis_size("query")
    owners = planes * owners_plane
    query_count = queries.shape[0]
    list_size = neg_ids.shape[1]
    place = jnp.stack([lax.axis_index(name) for name in ("outer", "inner", "query")]).astype(jnp.int32)
    plane_rows = owners_plane * rows_dev
    plane_refresh = owners_plane * refresh_dev
    all_rows = plane_rows + plane_refresh
    cap = max(2, (2 * refresh_dev + owners - 1) // owners)
    share = cap // replicas
    table_half, fresh_half = rows_dev // replicas, refresh_dev // replicas
    bf16, f32 = jnp.bfloat16, jnp.float32

    line = jnp.concatenate([refresh_ids, neg_ids[0], pos_ids])
    lines = [line] + [swap(line, "outer", s) for s in range(1, planes)]
    side = jnp.concatenate([one[:refresh_dev] for one in lines] + [ages])
    sides = [side] + [swap(side, "inner", s) for s in range(1, owners_plane)]
    positive = [one[refresh_dev + list_size :].reshape(1, -1) for one in lines]

    fast = replicas == 2 and owners_plane == 4 and planes == 4
    extra = 16 if fast else 0
    rows_half, scales = call(
        prep_kernel,
        "prep",
        [
            jax.ShapeDtypeStruct((table_half + fresh_half + extra, width), bf16),
            jax.ShapeDtypeStruct(((rows_dev + refresh_dev) // LANES, LANES), f32),
        ],
        place,
        table,
        fresh_rows,
        replicas=replicas,
        encode=fast,
    )

    others = (planes - 1) * owners_plane
    lw, row_ids, code, own_target, target, own = call(
        meta_kernel,
        "meta",
        [
            jax.ShapeDtypeStruct((planes, all_rows), f32),
            jax.ShapeDtypeStruct((1, all_rows), f32),
            jax.ShapeDtypeStruct((1, plane_refresh), jnp.int32),
            jax.ShapeDtypeStruct((1, plane_refresh), jnp.int32),
            jax.ShapeDtypeStruct((1, others * cap), jnp.int32),
            jax.ShapeDtypeStruct((1, rows_dev), jnp.int32),
        ],
        place,
        *[one.reshape(1, -1) for one in lines],
        *[one.reshape(1, -1) for one in sides],
        planes=planes,
        owners_plane=owners_plane,
        sizes=(refresh_dev, rows_dev, list_size),
        cap=cap,
        replicas=replicas,
    )
    new_ages = jnp.where(own.reshape(rows_dev) > 0, 0, ages)

    if fast:
        axes = ("inner", "query")
        first = [(2 * i + c, 2 * (i ^ (1 + c)) + c) for i in range(4) for c in range(2)]
        second = [(2 * i + c, 2 * (i ^ (2 - c)) + c) for i in range(4) for c in range(2)]
        near = lax.ppermute(rows_half, axes, first)
        side_rows = lax.ppermute(rows_half, axes, second)
        middle, outward = [(1, 2), (2, 1)], [(1, 0), (2, 3)]
        beside = swap(queries, "outer", 1)
        across = lax.ppermute(queries, "outer", middle)
        near, side_rows, beside, across, *lines = lax.optimization_barrier((near, side_rows, beside, across, *lines))
        from_end = lax.ppermute(beside, "outer", middle)
        to_end = lax.ppermute(across, "outer", outward)
        far = lax.ppermute(near, axes, second)
        far, from_end, to_end, lw = lax.optimization_barrier((far, from_end, to_end, lw))
        last = lax.ppermute(from_end, "outer", outward)
        got_queries = [(queries,), (beside,), (to_end, from_end), (last, across)]
        buffers = [table, fresh_rows]
        table_pieces = [(0, 0, rows_dev, (0, rows_dev, None, None), -1)]
        fresh_pieces = [(1, 0, refresh_dev, (0, refresh_dev, None, None), -1 - rows_dev // LANES)]
        for slot, by_core, mine in ((1, 0, near), (1, 1, side_rows), (3, None, far)):
            for flip, rows in enumerate((mine, swap(mine, "query", 1))):
                by = None if by_core is None else by_core ^ flip
                data = table_half + fresh_half
                fresh_at = data + 3 * (table_half // LANES)
                table_pieces.append((len(buffers), 0, table_half, (slot * rows_dev, table_half, flip, by), data))
                fresh_pieces.append(
                    (len(buffers), table_half, fresh_half, (slot * refresh_dev, fresh_half, flip, by), fresh_at)
                )
                buffers.append(rows)
    else:
        got_queries = [(queries,)] + [(swap(queries, "outer", s),) for s in range(1, planes)]
        got_rows = [rows_half] + [swap(rows_half, "inner", s) for s in range(1, owners_plane)]
        gathered = lax.all_gather(jnp.stack(got_rows), "query", axis=0)
        gathered = jnp.swapaxes(gathered, 0, 1)
        buffers = [
            gathered[:, :, :table_half].reshape(plane_rows, width),
            gathered[:, :, table_half:].reshape(plane_refresh, width),
        ]
        scales = []
        for rows in buffers:
            values = rows.astype(f32)
            mean = jnp.sum(values * values, axis=1) / width
            scales.append((lax.rsqrt(mean + epsilon) * (score_scale / width * LOG2E)).reshape(-1, LANES))
        scales = jnp.concatenate(scales)

        def blocks(buffer, count, line):
            starts = range(0, count, 512)
            return [(buffer, i, 512, (i, 512, None, None), -1 - line - i // LANES) for i in starts]

        table_pieces = blocks(0, plane_rows, 0)
        fresh_pieces = blocks(1, plane_refresh, plane_rows // LANES)

    def shift(pieces, columns):
        return [(a, b, c, (d[0] + columns, *d[1:]), e) for a, b, c, d, e in pieces]

    pieces = table_pieces + shift(fresh_pieces, plane_rows)
    packed, scale_plane = call(
        pack_kernel,
        "pack",
        [jax.ShapeDtypeStruct((others * share, width), bf16), jax.ShapeDtypeStruct((1, all_rows), f32)],
        place,
        code,
        scales,
        *buffers,
        pieces=fresh_pieces,
        all_pieces=pieces,
    )
    size = owners_plane * share
    came = jnp.concatenate([swap(packed[(s - 1) * size : s * size], "outer", s) for s in range(1, planes)])

    def score(s, given):
        (partial,) = call(
            score_kernel,
            "score",
            [jax.ShapeDtypeStruct((2, query_count // LANES, LANES), f32)],
            place,
            positive[s],
            *given,
            lw,
            row_ids,
            scale_plane,
            *buffers,
            scratch=[pltpu.VMEM((query_count, LANES), f32)] * 4 + [pltpu.VMEM(queries.shape, bf16)],
            pieces=pieces,
            flip=s,
            given=len(given),
        )
        return partial

    first = score(1, got_queries[1])
    late = [one for group in got_queries[2:] for one in group]
    came, first, *late = lax.optimization_barrier((came, first, *late))
    arrived = [came] + [swap(came, "query", flip) for flip in range(1, replicas)]
    mine = swap(first, "outer", 1)
    each = len(late) // (planes - 2)
    for s in range(2, planes):
        mine = mine + swap(score(s, late[(s - 2) * each : (s - 1) * each]), "outer", s)
    own_queries, *arrived = lax.optimization_barrier((queries, *arrived))
    mine = mine + score(0, [own_queries])
    (new_table,) = call(
        apply_kernel,
        "apply",
        [jax.ShapeDtypeStruct(table.shape, bf16)],
        place,
        own_target,
        target,
        own,
        table,
        *buffers,
        *arrived,
        pieces=fresh_pieces,
        arrivals=len(arrived),
    )
    loss = (jnp.log2(mine[0]) - mine[1]) * math.log(2.0)
    return new_table, new_ages, loss.reshape(query_count)


def solution(mesh):
    owners, replicas = mesh.shape["index"], mesh.shape["query"]
    inner = 1 << (int(math.log2(owners)) // 2)
    split = Mesh(mesh.devices.reshape(owners // inner, inner, replicas), ("outer", "inner", "query"))
    index = ("outer", "inner")
    placed = (
        P(index, None),
        P(index),
        P(index),
        P(index, None),
        P(index, None),
        P(("outer", "inner", "query"), None),
        P(("outer", "inner", "query")),
    )
    return jax.shard_map(
        on_device,
        mesh=split,
        in_specs=placed,
        out_specs=(P(index, None), P(index), P(("outer", "inner", "query"))),
        check_vma=False,
    )
```

```python
import functools
import math

import jax
import jax.numpy as jnp
from jax import lax
from jax.experimental import pallas as pl
from jax.experimental.pallas import tpu as pltpu
from jax.sharding import Mesh, PartitionSpec as P

score_scale = 20.0
age_scale = 16.0
epsilon = 1e-06
LOG2E = math.log2(math.e)
MASKED = -1e30
VMEM_LIMIT = 48 * 1024 * 1024
LANES = 128

NT = (((1,), (1,)), ((), ()))
NN = (((1,), (0,)), ((), ()))


def one_hot(ids, count):
    rows = lax.broadcasted_iota(jnp.int32, (count, ids.shape[1]), 0)
    return jnp.where(rows == ids, 1.0, 0.0).astype(jnp.bfloat16)


def split_terms(values):
    terms = []
    for _ in range(3):
        terms.append(values.astype(jnp.bfloat16))
        values = values - terms[-1].astype(jnp.float32)
    return terms


def counted(hits):
    count = hits.shape[1]
    before = lax.broadcasted_iota(jnp.int32, (count, count), 0)
    after = lax.broadcasted_iota(jnp.int32, (count, count), 1)
    earlier = jnp.where(before < after, 1.0, 0.0).astype(jnp.bfloat16)
    return lax.dot_general(hits.astype(jnp.bfloat16), earlier, NN, preferred_element_type=jnp.float32)


def small(values):
    return values.astype(jnp.float32).astype(jnp.bfloat16)


def prep_kernel(place, table, fresh, *refs, replicas, encode):
    core = place[2]
    rows_out, scale_out = refs[-2:]
    width = table.shape[1]
    line, row = 0, 0
    halves = []
    for source in (table, fresh):
        rows = source.shape[0]
        half = rows // replicas
        rows_out[row : row + half, :] = source[pl.ds(pl.multiple_of(core * half, half), half), :]
        row += half
        for block in range(rows // LANES):
            squares = jnp.zeros((LANES, LANES), jnp.float32)
            for chunk in range(width // LANES):
                values = source[block * LANES : (block + 1) * LANES, chunk * LANES : (chunk + 1) * LANES]
                values = values.astype(jnp.float32)
                squares += values * values
            mean = jnp.sum(squares.T, axis=0, keepdims=True) / width
            scale_out[line + block : line + block + 1, :] = lax.rsqrt(mean + epsilon) * (score_scale / width * LOG2E)
        if encode:
            halves += [(line, i, half // LANES) for i in range(half // LANES)]
        line += rows // LANES
    if encode:
        rows_out[row:, :] = jnp.zeros((16, width), jnp.bfloat16)
        terms = []
        for first, i, count in halves:
            terms += split_terms(scale_out[pl.ds(first + core * count + i, 1), :])
        for i, term in enumerate(terms):
            rows_out[row + i : row + i + 1, :LANES] = term
        *ids, ages = refs[:-2]
        ids = jnp.concatenate([one[...] for one in ids], axis=1)
        for at, values in ((9, ids >> 7), (11, ids & 127), (13, ages[...])):
            for i, left in enumerate(range(0, values.shape[1], width)):
                part = small(values[:, left : left + width])
                rows_out[row + at + i : row + at + i + 1, : part.shape[1]] = part


def unpacked(rows, first, id_count, age_count):
    width = rows.shape[1]

    def read(at, count):
        parts = [number(rows[first + at + i : first + at + i + 1, :]) for i in range(-(-count // width))]
        return jnp.concatenate(parts, axis=1)[:, :count]

    return read(9, id_count) * LANES + read(11, id_count), read(13, age_count)


def number(values):
    return values.astype(jnp.float32).astype(jnp.int32)


def meta_kernel(place, *refs, planes, owners_plane, sizes, cap, replicas, extra):
    outer, inner, core = place[0], place[1], place[2]
    refresh_dev, rows_dev, list_size = sizes
    all_refs = planes * refresh_dev
    lines, own_ages = refs[:planes], refs[planes]
    sides = refs[planes + 1 : planes + owners_plane]
    lw_out, row_out, code_out, own_target_out, target_out, own_out, ages_out = refs[planes + owners_plane :]
    if extra:
        near, beside, far = [unpacked(side, extra, all_refs, rows_dev) for side in sides]
        swapped = [(jnp.where(core == 0, a, b), jnp.where(core == 0, b, a)) for a, b in zip(near, beside)]
        sides = [tuple(pair[0] for pair in swapped), tuple(pair[1] for pair in swapped), far]
    else:
        sides = [(side[:, :all_refs], side[:, all_refs:]) for side in sides]
    own_ids = jnp.concatenate([line[:, :refresh_dev] for line in lines], axis=1)
    sides = [(own_ids, own_ages[...]), *sides]
    share = cap // replicas
    plane_rows = owners_plane * rows_dev
    high_count = planes * plane_rows // LANES
    own_owner = outer * owners_plane + inner

    def one_hots(ids):
        return one_hot(ids >> 7, high_count), one_hot(ids & 127, LANES)

    def bitmap(ids):
        high, low = one_hots(ids)
        return lax.dot_general(low, high, NT, preferred_element_type=jnp.float32)

    def lookup(one_map, pair):
        hit = lax.dot_general(one_map.astype(jnp.bfloat16), pair[0], NN, preferred_element_type=jnp.float32)
        return jnp.sum(hit * pair[1].astype(jnp.float32), axis=0, keepdims=True) > 0.5

    def ref_ids(plane, side):
        return sides[side][0][:, plane * refresh_dev : (plane + 1) * refresh_dev]

    plane_ids = jnp.concatenate([ref_ids(0, side) for side in range(owners_plane)], axis=1)
    refreshed_map = bitmap(jnp.concatenate([side[0] for side in sides], axis=1))
    column = lax.broadcasted_iota(jnp.int32, (1, plane_rows), 1)
    table_ids = (outer * owners_plane + (inner ^ (column // rows_dev))) * rows_dev + column % rows_dev
    table_hots, fresh_hots = one_hots(table_ids), one_hots(plane_ids)

    ages = jnp.concatenate([side[1] for side in sides], axis=1).astype(jnp.float32)
    weight = jnp.exp(-ages / age_scale).astype(jnp.bfloat16).astype(jnp.float32)
    refreshed = lookup(refreshed_map, table_hots)
    row_out[:, :plane_rows] = jnp.where(refreshed, -1, table_ids).astype(jnp.float32)
    row_out[:, plane_rows:] = plane_ids.astype(jnp.float32)
    own_out[...] = refreshed[:, :rows_dev].astype(jnp.int32)
    ages_out[...] = jnp.where(refreshed[:, :rows_dev], 0, own_ages[...])
    log_weight = jnp.where(refreshed, MASKED, jnp.log2(weight))
    for group in range(planes):
        one_map = bitmap(lines[group][:, refresh_dev : refresh_dev + list_size])
        lw_out[group : group + 1, :plane_rows] = jnp.where(lookup(one_map, table_hots), log_weight, MASKED)
        lw_out[group : group + 1, plane_rows:] = jnp.where(lookup(one_map, fresh_hots), 0.0, MASKED)

    pairs = [(plane, side) for plane in range(planes) for side in range(owners_plane)]
    sent_owner = [ref_ids(0, side) // rows_dev - ((outer ^ plane) * owners_plane + inner) for plane, side in pairs]
    taken_owner = [ref_ids(plane, side) // rows_dev - own_owner for plane, side in pairs]
    match = jnp.concatenate(sent_owner + taken_owner, axis=0) == 0
    rank = counted(jnp.where(match, 1.0, 0.0)).astype(jnp.int32)
    rank = jnp.where(match, rank, -cap)
    own_target_out[...] = plane_ids - own_owner * rows_dev
    for i, (plane, side) in enumerate(pairs):
        if plane == 0:
            code_out[:, side * refresh_dev : (side + 1) * refresh_dev] = jnp.full((1, refresh_dev), -1, jnp.int32)
            continue
        base = ((plane - 1) * owners_plane + side) * share
        sent_rank = rank[i : i + 1, :] - core * share
        columns = slice(side * refresh_dev, (side + 1) * refresh_dev)
        here = (sent_rank >= 0) & (sent_rank < share)
        code_out[:, columns] = jnp.where(here, base + sent_rank, code_out[:, columns])
        take_rank = rank[len(pairs) + i : len(pairs) + i + 1, :]
        slot = jnp.where(take_rank < 0, -1, ((take_rank // share) ^ core) * share + take_rank % share)
        row = jnp.where(take_rank < 0, 0, ref_ids(plane, side) - own_owner * rows_dev)
        kinds = lax.broadcasted_iota(jnp.int32, (8, refresh_dev), 0)
        digits = jnp.where(kinds == 0, row // 16, jnp.where(kinds == 1, row % 16, 1))
        found = lax.dot_general(small(digits), one_hot(slot, cap), NT, preferred_element_type=jnp.float32)
        found = found.astype(jnp.int32)
        target = jnp.where(found[2:3, :] > 0, found[0:1, :] * 16 + found[1:2, :], -1)
        for part in range(replicas):
            first = part * (planes - 1) * owners_plane * share + base
            target_out[:, first : first + share] = target[:, part * share : (part + 1) * share]


def piece_offset(place, piece):
    column, size, flip, by_core = piece
    if flip is None:
        return column
    column += (place[2] ^ flip) * size
    if by_core is not None:
        column += (place[2] ^ by_core) * size * 2
    return pl.multiple_of(column, size)


def pack_kernel(place, code, scale, *refs, pieces, all_pieces):
    *buffers, out, scale_out = refs
    selects = [
        one_hot(code[:, pl.ds(piece_offset(place, column), size)], out.shape[0]) for _, _, size, column, _ in pieces
    ]
    values = [buffers[source][start : start + size, :] for source, start, size, _, _ in pieces]
    select, values = jnp.concatenate(selects, axis=1), jnp.concatenate(values, axis=0)
    out[...] = lax.dot_general(select, values, NN, preferred_element_type=jnp.float32).astype(jnp.bfloat16)
    for source, start, size, column, scale_at in all_pieces:
        first = piece_offset(place, column)
        for chunk in range(size // LANES):
            if scale_at < 0:
                line = -1 - scale_at + chunk
                row = scale[line : line + 1, :]
            else:
                line = scale_at + 3 * chunk
                row = jnp.sum(buffers[source][line : line + 3, :LANES].astype(jnp.float32), axis=0, keepdims=True)
            scale_out[:, pl.ds(first + chunk * LANES, LANES)] = row


def apply_kernel(place, own_target, target, refreshed, table, *refs, pieces, arrivals):
    out = refs[-1]
    buffers, arrived = refs[: -1 - arrivals], refs[-1 - arrivals : -1]
    to_rows = [own_target[:, pl.ds(piece_offset(place, column), size)] for _, _, size, column, _ in pieces]
    values = [buffers[source][start : start + size, :] for source, start, size, _, _ in pieces]
    to_row = jnp.concatenate([*to_rows, target[...]], axis=1)
    values = jnp.concatenate([*values, *[block[...] for block in arrived]], axis=0)
    rows = lax.broadcasted_iota(jnp.int32, (out.shape[0], to_row.shape[1]), 0)
    chosen = jnp.where(rows == to_row, 1.0, 0.0).astype(jnp.bfloat16)
    fresh = lax.dot_general(chosen, values, NN, preferred_element_type=jnp.float32)
    for top in range(0, out.shape[0], LANES):
        part = slice(top, top + LANES)
        hit = to_lanes(refreshed[:, part].astype(jnp.float32)) > 0.5
        for left in range(0, out.shape[1], LANES):
            cols = slice(left, left + LANES)
            out[part, cols] = jnp.where(hit, fresh[part, cols], table[part, cols].astype(jnp.float32)).astype(jnp.bfloat16)


def to_lanes(row):
    return jnp.broadcast_to(row, (LANES, LANES)).T


def score_kernel(place, positive, *refs, pieces, flip, given):
    out, total, pos_total, q_scale, pos_b, chosen = refs[-6:]
    queries = refs[0]
    if given == 2:
        at_end = (place[0] == 0) | (place[0] == 3)
        chosen[...] = jnp.where(at_end, refs[0][...], refs[1][...])
        queries = chosen
    log_weight, row_ids, scale, *refs = refs[given:-6]
    count, width = queries.shape
    for block in range(count // LANES):
        part = slice(block * LANES, (block + 1) * LANES)
        values = queries[part, :].astype(jnp.float32)
        squares = jnp.sum(values * values, axis=1, keepdims=True)
        q_scale[part, :] = jnp.broadcast_to(lax.rsqrt(squares / width + epsilon), (LANES, LANES))
        pos_b[part, :] = to_lanes(positive[:, part].astype(jnp.float32))
    total[...] = jnp.zeros_like(total)
    pos_total[...] = jnp.zeros_like(pos_total)

    def product(piece):
        source, start, size = piece[:3]
        rows = refs[source][start : start + size, :]
        return lax.dot_general(queries[...], rows, NT, preferred_element_type=jnp.float32)

    following = product(pieces[0])
    for i, (_, _, size, column, _) in enumerate(pieces):
        raw = following
        if i + 1 < len(pieces):
            following = product(pieces[i + 1])
        first = piece_offset(place, column)
        for top in range(0, count, 64):
            part = slice(top, top + 64)
            sums, positives = total[part, :], pos_total[part, :]
            query_scale, wanted = q_scale[part, :], pos_b[part, :]
            for chunk in range(size // LANES):
                cols = pl.ds(first + chunk * LANES, LANES)
                powers = raw[part, chunk * LANES : (chunk + 1) * LANES] * query_scale
                powers = powers * scale[:, cols] + log_weight[flip : flip + 1, cols]
                sums = sums + jnp.exp2(powers)
                positives = positives + jnp.where(wanted == row_ids[:, cols], powers, 0.0)
            total[part, :] = sums
            pos_total[part, :] = positives
    for block in range(count // LANES):
        part = slice(block * LANES, (block + 1) * LANES)
        out[0, block : block + 1, :] = jnp.sum(total[part, :].T, axis=0, keepdims=True)
        out[1, block : block + 1, :] = jnp.sum(pos_total[part, :].T, axis=0, keepdims=True)


def whole(memory=pltpu.VMEM):
    return pl.BlockSpec(memory_space=memory)


def call(kernel, name, outs, place, *operands, scratch=(), **options):
    specs = [whole()] * len(operands)
    if place is not None:
        specs = [whole(pltpu.SMEM)] + specs
        operands = (place, *operands)
    return pl.pallas_call(
        functools.partial(kernel, **options),
        out_shape=tuple(outs),
        in_specs=specs,
        out_specs=tuple(whole() for _ in outs),
        scratch_shapes=list(scratch),
        compiler_params=pltpu.CompilerParams(vmem_limit_bytes=VMEM_LIMIT),
        cost_estimate=pl.CostEstimate(flops=1, bytes_accessed=1, transcendentals=0),
        name=name,
    )(*operands)


def swap(values, axis, flip):
    return lax.ppermute(values, axis, [(i, i ^ flip) for i in range(lax.axis_size(axis))])


def on_device(table, ages, refresh_ids, fresh_rows, neg_ids, queries, pos_ids):
    rows_dev, width = table.shape
    refresh_dev = refresh_ids.shape[0]
    planes = lax.axis_size("outer")
    owners_plane = lax.axis_size("inner")
    replicas = lax.axis_size("query")
    owners = planes * owners_plane
    query_count = queries.shape[0]
    list_size = neg_ids.shape[1]
    place = jnp.stack([lax.axis_index(name) for name in ("outer", "inner", "query")]).astype(jnp.int32)
    plane_rows = owners_plane * rows_dev
    plane_refresh = owners_plane * refresh_dev
    all_rows = plane_rows + plane_refresh
    cap = max(2, (2 * refresh_dev + owners - 1) // owners)
    share = cap // replicas
    table_half, fresh_half = rows_dev // replicas, refresh_dev // replicas
    bf16, f32 = jnp.bfloat16, jnp.float32

    line = jnp.concatenate([refresh_ids, neg_ids[0], pos_ids])
    lines = [line] + [swap(line, "outer", s) for s in range(1, planes)]
    positive = [one[refresh_dev + list_size :].reshape(1, -1) for one in lines]
    ref_lines = [one[:refresh_dev].reshape(1, -1) for one in lines]
    own_ages = ages.reshape(1, -1)

    fast = replicas == 2 and owners_plane == 4 and planes == 4
    extra = 16 if fast else 0
    rows_half, scales = call(
        prep_kernel,
        "prep",
        [
            jax.ShapeDtypeStruct((table_half + fresh_half + extra, width), bf16),
            jax.ShapeDtypeStruct(((rows_dev + refresh_dev) // LANES, LANES), f32),
        ],
        place,
        table,
        fresh_rows,
        *(ref_lines if fast else []),
        own_ages,
        replicas=replicas,
        encode=fast,
    )

    others = (planes - 1) * owners_plane
    if fast:
        axes = ("inner", "query")
        first = [(2 * i + c, 2 * (i ^ (1 + c)) + c) for i in range(4) for c in range(2)]
        second = [(2 * i + c, 2 * (i ^ (2 - c)) + c) for i in range(4) for c in range(2)]
        near = lax.ppermute(rows_half, axes, first)
        side_rows = lax.ppermute(rows_half, axes, second)
        middle, outward = [(1, 2), (2, 1)], [(1, 0), (2, 3)]
        beside = swap(queries, "outer", 1)
        across = lax.ppermute(queries, "outer", middle)
        near, side_rows, beside, across = lax.optimization_barrier((near, side_rows, beside, across))
        from_end = lax.ppermute(beside, "outer", middle)
        to_end = lax.ppermute(across, "outer", outward)
        far = lax.ppermute(near, axes, second)
        far, from_end, to_end = lax.optimization_barrier((far, from_end, to_end))
        sides = [near, side_rows, far]
        last = lax.ppermute(from_end, "outer", outward)
        got_queries = [(queries,), (beside,), (to_end, from_end), (last, across)]
        buffers = [table, fresh_rows]
        table_pieces = [(0, 0, rows_dev, (0, rows_dev, None, None), -1)]
        fresh_pieces = [(1, 0, refresh_dev, (0, refresh_dev, None, None), -1 - rows_dev // LANES)]
        for slot, by_core, mine in ((1, 0, near), (1, 1, side_rows), (3, None, far)):
            for flip, rows in enumerate((mine, swap(mine, "query", 1))):
                by = None if by_core is None else by_core ^ flip
                data = table_half + fresh_half
                fresh_at = data + 3 * (table_half // LANES)
                table_pieces.append((len(buffers), 0, table_half, (slot * rows_dev, table_half, flip, by), data))
                fresh_pieces.append(
                    (len(buffers), table_half, fresh_half, (slot * refresh_dev, fresh_half, flip, by), fresh_at)
                )
                buffers.append(rows)
    else:
        got_queries = [(queries,)] + [(swap(queries, "outer", s),) for s in range(1, planes)]
        side = jnp.concatenate([*[one[0] for one in ref_lines], ages])
        sides = [swap(side, "inner", s).reshape(1, -1) for s in range(1, owners_plane)]
        got_rows = [rows_half] + [swap(rows_half, "inner", s) for s in range(1, owners_plane)]
        gathered = lax.all_gather(jnp.stack(got_rows), "query", axis=0)
        gathered = jnp.swapaxes(gathered, 0, 1)
        buffers = [
            gathered[:, :, :table_half].reshape(plane_rows, width),
            gathered[:, :, table_half:].reshape(plane_refresh, width),
        ]
        scales = []
        for rows in buffers:
            values = rows.astype(f32)
            mean = jnp.sum(values * values, axis=1) / width
            scales.append((lax.rsqrt(mean + epsilon) * (score_scale / width * LOG2E)).reshape(-1, LANES))
        scales = jnp.concatenate(scales)

        def blocks(buffer, count, line):
            starts = range(0, count, 512)
            return [(buffer, i, 512, (i, 512, None, None), -1 - line - i // LANES) for i in starts]

        table_pieces = blocks(0, plane_rows, 0)
        fresh_pieces = blocks(1, plane_refresh, plane_rows // LANES)

    lw, row_ids, code, own_target, target, own, new_ages = call(
        meta_kernel,
        "meta",
        [
            jax.ShapeDtypeStruct((planes, all_rows), f32),
            jax.ShapeDtypeStruct((1, all_rows), f32),
            jax.ShapeDtypeStruct((1, plane_refresh), jnp.int32),
            jax.ShapeDtypeStruct((1, plane_refresh), jnp.int32),
            jax.ShapeDtypeStruct((1, others * cap), jnp.int32),
            jax.ShapeDtypeStruct((1, rows_dev), jnp.int32),
            jax.ShapeDtypeStruct((1, rows_dev), jnp.int32),
        ],
        place,
        *[one.reshape(1, -1) for one in lines],
        own_ages,
        *sides,
        planes=planes,
        owners_plane=owners_plane,
        sizes=(refresh_dev, rows_dev, list_size),
        cap=cap,
        replicas=replicas,
        extra=table_half + fresh_half if fast else 0,
    )
    new_ages = new_ages.reshape(rows_dev)

    def shift(pieces, columns):
        return [(a, b, c, (d[0] + columns, *d[1:]), e) for a, b, c, d, e in pieces]

    pieces = table_pieces + shift(fresh_pieces, plane_rows)
    packed, scale_plane = call(
        pack_kernel,
        "pack",
        [jax.ShapeDtypeStruct((others * share, width), bf16), jax.ShapeDtypeStruct((1, all_rows), f32)],
        place,
        code,
        scales,
        *buffers,
        pieces=fresh_pieces,
        all_pieces=pieces,
    )
    size = owners_plane * share
    came = jnp.concatenate([swap(packed[(s - 1) * size : s * size], "outer", s) for s in range(1, planes)])

    def score(s, given):
        (partial,) = call(
            score_kernel,
            "score",
            [jax.ShapeDtypeStruct((2, query_count // LANES, LANES), f32)],
            place,
            positive[s],
            *given,
            lw,
            row_ids,
            scale_plane,
            *buffers,
            scratch=[pltpu.VMEM((query_count, LANES), f32)] * 4 + [pltpu.VMEM(queries.shape, bf16)],
            pieces=pieces,
            flip=s,
            given=len(given),
        )
        return partial

    first, own_part = score(1, got_queries[1]), score(0, got_queries[0])
    late = [one for group in got_queries[2:] for one in group]
    came, first, own_part, *late = lax.optimization_barrier((came, first, own_part, *late))
    arrived = [came] + [swap(came, "query", flip) for flip in range(1, replicas)]
    mine = own_part + swap(first, "outer", 1)
    each = len(late) // (planes - 2)
    for s in range(2, planes):
        mine = mine + swap(score(s, late[(s - 2) * each : (s - 1) * each]), "outer", s)
    (new_table,) = call(
        apply_kernel,
        "apply",
        [jax.ShapeDtypeStruct(table.shape, bf16)],
        place,
        own_target,
        target,
        own,
        table,
        *buffers,
        *arrived,
        pieces=fresh_pieces,
        arrivals=len(arrived),
    )
    mine, new_table = lax.optimization_barrier((mine, new_table))
    loss = (jnp.log2(mine[0]) - mine[1]) * math.log(2.0)
    return new_table, new_ages, loss.reshape(query_count)


def solution(mesh):
    owners, replicas = mesh.shape["index"], mesh.shape["query"]
    inner = 1 << (int(math.log2(owners)) // 2)
    split = Mesh(mesh.devices.reshape(owners // inner, inner, replicas), ("outer", "inner", "query"))
    index = ("outer", "inner")
    placed = (
        P(index, None),
        P(index),
        P(index),
        P(index, None),
        P(index, None),
        P(("outer", "inner", "query"), None),
        P(("outer", "inner", "query")),
    )
    return jax.shard_map(
        on_device,
        mesh=split,
        in_specs=placed,
        out_specs=(P(index, None), P(index), P(("outer", "inner", "query"))),
        check_vma=False,
    )
```

```python
import functools
import math

import jax
import jax.numpy as jnp
from jax import lax
from jax.experimental import pallas as pl
from jax.experimental.pallas import tpu as pltpu
from jax.sharding import Mesh, PartitionSpec as P

score_scale = 20.0
age_scale = 16.0
epsilon = 1e-06
LOG2E = math.log2(math.e)
MASKED = -1e30
VMEM_LIMIT = 48 * 1024 * 1024
EXTRA = 16
IDS_ROW = 9
AGES_ROW = 11
LANES = 128

NT = (((1,), (1,)), ((), ()))
NN = (((1,), (0,)), ((), ()))


def one_hot(ids, count):
    rows = lax.broadcasted_iota(jnp.int32, (count, ids.shape[1]), 0)
    return jnp.where(rows == ids, 1.0, 0.0).astype(jnp.bfloat16)


def split_terms(values):
    terms = []
    for _ in range(3):
        terms.append(values.astype(jnp.bfloat16))
        values = values - terms[-1].astype(jnp.float32)
    return terms


def counted(hits):
    count = hits.shape[1]
    before = lax.broadcasted_iota(jnp.int32, (count, count), 0)
    after = lax.broadcasted_iota(jnp.int32, (count, count), 1)
    earlier = jnp.where(before < after, 1.0, 0.0).astype(jnp.bfloat16)
    return lax.dot_general(hits.astype(jnp.bfloat16), earlier, NN, preferred_element_type=jnp.float32)


def small(values):
    return values.astype(jnp.float32).astype(jnp.bfloat16)


def number(values):
    return values.astype(jnp.float32).astype(jnp.int32)


def put(out, row, values):
    width = out.shape[1]
    for i, left in enumerate(range(0, values.shape[1], width)):
        part = small(values[:, left : left + width])
        out[row + i : row + i + 1, : part.shape[1]] = part


def take(rows, row, count):
    width = rows.shape[1]
    parts = [number(rows[row + i : row + i + 1, :]) for i in range(-(-count // width))]
    return jnp.concatenate(parts, axis=1)[:, :count]


def put_ids(out, row, ids):
    lines = -(-ids.shape[1] // out.shape[1])
    put(out, row, ids >> 7)
    put(out, row + lines, ids & 127)


def take_ids(rows, row, count):
    lines = -(-count // rows.shape[1])
    return take(rows, row, count) * LANES + take(rows, row + lines, count)


def prep_kernel(
    place, queries, table, fresh, ref_ids, ages, neg, pos, queries_out, rows_out, scale_out, *, replicas, encode
):
    core = place[2]
    count, width = queries.shape
    queries_out[:count, :] = queries[...]
    queries_out[count:, :] = jnp.zeros((EXTRA, width), jnp.bfloat16)
    put_ids(queries_out, count, neg[...])
    put_ids(queries_out, count + 2 * -(-neg.shape[1] // width), pos[...])
    line, row = 0, 0
    halves = []
    for source in (table, fresh):
        rows = source.shape[0]
        half = rows // replicas
        rows_out[row : row + half, :] = source[pl.ds(pl.multiple_of(core * half, half), half), :]
        row += half
        for block in range(rows // LANES):
            squares = jnp.zeros((LANES, LANES), jnp.float32)
            for chunk in range(width // LANES):
                values = source[block * LANES : (block + 1) * LANES, chunk * LANES : (chunk + 1) * LANES]
                values = values.astype(jnp.float32)
                squares += values * values
            mean = jnp.sum(squares.T, axis=0, keepdims=True) / width
            scale_out[line + block : line + block + 1, :] = lax.rsqrt(mean + epsilon) * (score_scale / width * LOG2E)
        halves += [(line, i, half // LANES) for i in range(half // LANES)]
        line += rows // LANES
    rows_out[row:, :] = jnp.zeros((EXTRA, width), jnp.bfloat16)
    if encode:
        terms = []
        for first, i, count in halves:
            terms += split_terms(scale_out[pl.ds(first + core * count + i, 1), :])
        for i, term in enumerate(terms):
            rows_out[row + i : row + i + 1, :LANES] = term
    put_ids(rows_out, row + IDS_ROW, ref_ids[...])
    put(rows_out, row + AGES_ROW, ages[...])


def in_order(place, values, fast):
    if not fast:
        return values
    own, near, side, far = values
    core = place[2]
    return [own, jnp.where(core == 0, near, side), jnp.where(core == 0, side, near), far]


def owner_ranks(rows, refresh_dev, cap):
    match = jnp.concatenate(rows, axis=0) == 0
    rank = counted(jnp.where(match, 1.0, 0.0)).astype(jnp.int32)
    return jnp.where(match, rank, -cap)


def pack_kernel(
    place, ref_ids, scale, *refs, sides, pieces, all_pieces, planes, rows_dev, cap, replicas, fast
):
    outer, inner, core = place[0], place[1], place[2]
    buffers, outs = refs[: -planes - 1], refs[-planes - 1 : -2]
    scale_out, ids_out = refs[-2:]
    refresh_dev = ref_ids.shape[1]
    owners_plane = len(sides) + 1
    share = cap // replicas
    ids = [ref_ids[...]] + [take_ids(buffers[i], row + IDS_ROW, refresh_dev) for i, row in sides]
    ids = in_order(place, ids, fast)
    pairs = [(plane, side) for plane in range(1, planes) for side in range(owners_plane)]
    rank = owner_ranks(
        [ids[side] // rows_dev - ((outer ^ plane) * owners_plane + inner) for plane, side in pairs], refresh_dev, cap
    )
    rank = rank - core * share
    codes = [jnp.full((1, refresh_dev), -1, jnp.int32)] * owners_plane
    for i, (plane, side) in enumerate(pairs):
        here = (rank[i : i + 1, :] >= 0) & (rank[i : i + 1, :] < share)
        base = ((plane - 1) * owners_plane + side) * share
        codes[side] = jnp.where(here, base + rank[i : i + 1, :], codes[side])
    code = jnp.concatenate(codes, axis=1)
    plane_ids = jnp.concatenate(ids, axis=1)
    ids_out[...] = plane_ids

    selects = []
    for _, _, size, column, _ in pieces:
        if column[2] is None:
            part = code[:, column[0] : column[0] + size]
        else:
            part = None
            for option in range(2):
                at = column[0] + (option ^ column[2]) * size
                at += 0 if column[3] is None else (option ^ column[3]) * size * 2
                one = code[:, at : at + size]
                part = one if part is None else jnp.where(core == 0, part, one)
        selects.append(one_hot(part, len(outs) * owners_plane * share))
    values = [buffers[source][start : start + size, :] for source, start, size, _, _ in pieces]
    select, values = jnp.concatenate(selects, axis=1), jnp.concatenate(values, axis=0)
    packed = lax.dot_general(select, values, NN, preferred_element_type=jnp.float32).astype(jnp.bfloat16)
    size = owners_plane * share
    for i, out in enumerate(outs):
        out[:size, :] = packed[i * size : (i + 1) * size, :]
        out[size:, :] = jnp.zeros((EXTRA, out.shape[1]), jnp.bfloat16)
        put_ids(out, size, plane_ids)
    for source, start, size, column, scale_at in all_pieces:
        first = piece_offset(place, column)
        for chunk in range(size // LANES):
            if scale_at < 0:
                line = -1 - scale_at + chunk
                row = scale[line : line + 1, :]
            else:
                line = scale_at + 3 * chunk
                row = jnp.sum(buffers[source][line : line + 3, :LANES].astype(jnp.float32), axis=0, keepdims=True)
            scale_out[:, pl.ds(first + chunk * LANES, LANES)] = row


def one_hots(ids, high_count):
    return one_hot(ids >> 7, high_count), one_hot(ids & 127, LANES)


def bitmap(ids, high_count):
    high, low = one_hots(ids, high_count)
    return lax.dot_general(low, high, NT, preferred_element_type=jnp.float32).astype(jnp.bfloat16)


def lookup(one_map, pair):
    hit = lax.dot_general(one_map, pair[0], NN, preferred_element_type=jnp.float32)
    return jnp.sum(hit * pair[1].astype(jnp.float32), axis=0, keepdims=True)


def column_ids(place, owners_plane, rows_dev):
    column = lax.broadcasted_iota(jnp.int32, (1, owners_plane * rows_dev), 1)
    return (place[0] * owners_plane + (place[1] ^ (column // rows_dev))) * rows_dev + column % rows_dev


def list_row(place, blocks, count, list_size):
    lists = [take_ids(block, count, list_size) for block in blocks]
    if len(lists) == 1:
        return lists[0]
    return jnp.where((place[0] == 0) | (place[0] == 3), lists[0], lists[1])


def lists_kernel(place, plane_ids, neg, *refs, given, planes, owners_plane, rows_dev, count):
    out = refs[-1]
    high_count = planes * owners_plane * rows_dev // LANES
    pair = one_hots(jnp.concatenate([column_ids(place, owners_plane, rows_dev), plane_ids[...]], axis=1), high_count)
    first = 0
    out[0:1, :] = lookup(bitmap(neg[...], high_count), pair)
    for i, number_of in enumerate(given):
        ids = list_row(place, refs[first : first + number_of], count, neg.shape[1])
        out[i + 1 : i + 2, :] = lookup(bitmap(ids, high_count), pair)
        first += number_of


def meta_kernel(
    place, plane_ids, ages, hits, *refs, arrivals, given, sides, planes, owners_plane, rows_dev, list_size, count, cap,
    replicas, fast
):
    outer, inner, core = place[0], place[1], place[2]
    lw_out, row_out, own_target_out, target_out, own_out, ages_out = refs[-6:]
    came, blocks, buffers = refs[:arrivals], refs[arrivals : arrivals + given], refs[arrivals + given : -6]
    share = cap // replicas
    plane_rows = owners_plane * rows_dev
    plane_refresh = plane_ids.shape[1]
    refresh_dev = plane_refresh // owners_plane
    high_count = planes * plane_rows // LANES
    own_owner = outer * owners_plane + inner

    ids = [plane_ids[...]] + [take_ids(block, owners_plane * share, plane_refresh) for block in came]
    table_ids = column_ids(place, owners_plane, rows_dev)
    pair = one_hots(jnp.concatenate([table_ids, ids[0]], axis=1), high_count)
    refreshed = lookup(bitmap(jnp.concatenate(ids, axis=1), high_count), (pair[0][:, :plane_rows], pair[1][:, :plane_rows]))
    refreshed = refreshed > 0.5
    row_out[:, :plane_rows] = jnp.where(refreshed, -1, table_ids).astype(jnp.float32)
    row_out[:, plane_rows:] = ids[0].astype(jnp.float32)
    own_out[...] = refreshed[:, :rows_dev].astype(jnp.int32)
    ages_out[...] = jnp.where(refreshed[:, :rows_dev], 0, ages[...])

    all_ages = [ages[...]] + [take(buffers[i], row + AGES_ROW, rows_dev) for i, row in sides]
    all_ages = jnp.concatenate(in_order(place, all_ages, fast), axis=1).astype(jnp.float32)
    weight = jnp.exp(-all_ages / age_scale).astype(jnp.bfloat16).astype(jnp.float32)
    log_weight = jnp.where(refreshed, MASKED, jnp.log2(weight))
    log_weight = jnp.concatenate([log_weight, jnp.zeros((1, plane_refresh), jnp.float32)], axis=1)
    for group in range(planes):
        if group < planes - 1:
            hit = hits[group : group + 1, :]
        else:
            hit = lookup(bitmap(list_row(place, blocks, count, list_size), high_count), pair)
        lw_out[group : group + 1, :] = jnp.where(hit > 0.5, log_weight, MASKED)

    own_target_out[...] = ids[0] - own_owner * rows_dev
    pairs = [(plane, side) for plane in range(1, planes) for side in range(owners_plane)]
    part_ids = [ids[plane][:, side * refresh_dev : (side + 1) * refresh_dev] for plane, side in pairs]
    rank = owner_ranks([one // rows_dev - own_owner for one in part_ids], refresh_dev, cap)
    for i, (plane, side) in enumerate(pairs):
        base = ((plane - 1) * owners_plane + side) * share
        took = rank[i : i + 1, :]
        slot = jnp.where(took < 0, -1, ((took // share) ^ core) * share + took % share)
        row = jnp.where(took < 0, 0, part_ids[i] - own_owner * rows_dev)
        kinds = lax.broadcasted_iota(jnp.int32, (8, refresh_dev), 0)
        digits = jnp.where(kinds == 0, row // 16, jnp.where(kinds == 1, row % 16, 1))
        found = lax.dot_general(small(digits), one_hot(slot, cap), NT, preferred_element_type=jnp.float32)
        found = found.astype(jnp.int32)
        target = jnp.where(found[2:3, :] > 0, found[0:1, :] * 16 + found[1:2, :], -1)
        for part in range(replicas):
            first = part * (planes - 1) * owners_plane * share + base
            target_out[:, first : first + share] = target[:, part * share : (part + 1) * share]


def piece_offset(place, piece):
    column, size, flip, by_core = piece
    if flip is None:
        return column
    column += (place[2] ^ flip) * size
    if by_core is not None:
        column += (place[2] ^ by_core) * size * 2
    return pl.multiple_of(column, size)


def apply_kernel(place, own_target, target, refreshed, table, *refs, pieces, arrivals):
    out = refs[-1]
    buffers, arrived = refs[: -1 - arrivals], refs[-1 - arrivals : -1]
    to_rows = [own_target[:, pl.ds(piece_offset(place, column), size)] for _, _, size, column, _ in pieces]
    values = [buffers[source][start : start + size, :] for source, start, size, _, _ in pieces]
    to_row = jnp.concatenate([*to_rows, target[...]], axis=1)
    values = jnp.concatenate([*values, *[block[...] for block in arrived]], axis=0)
    rows = lax.broadcasted_iota(jnp.int32, (out.shape[0], to_row.shape[1]), 0)
    chosen = jnp.where(rows == to_row, 1.0, 0.0).astype(jnp.bfloat16)
    fresh = lax.dot_general(chosen, values, NN, preferred_element_type=jnp.float32)
    for top in range(0, out.shape[0], LANES):
        part = slice(top, top + LANES)
        hit = to_lanes(refreshed[:, part].astype(jnp.float32)) > 0.5
        for left in range(0, out.shape[1], LANES):
            cols = slice(left, left + LANES)
            out[part, cols] = jnp.where(hit, fresh[part, cols], table[part, cols].astype(jnp.float32)).astype(jnp.bfloat16)


def to_lanes(row):
    return jnp.broadcast_to(row, (LANES, LANES)).T


def score_kernel(place, *refs, pieces, flip, given, list_size):
    out, total, pos_total, q_scale, pos_b, chosen = refs[-6:]
    count, width = chosen.shape
    log_weight, row_ids, scale = refs[given : given + 3]
    row = count + 2 * -(-list_size // width)
    positive = [take_ids(block, row, count) for block in refs[:given]]
    if given == 2:
        at_end = (place[0] == 0) | (place[0] == 3)
        chosen[...] = jnp.where(at_end, refs[0][:count, :], refs[1][:count, :])
        queries, positive = chosen, jnp.where(at_end, *positive)
    else:
        queries, positive = refs[0].at[:count, :], positive[0]
    refs = refs[given + 3 : -6]
    for block in range(count // LANES):
        part = slice(block * LANES, (block + 1) * LANES)
        values = queries[part, :].astype(jnp.float32)
        squares = jnp.sum(values * values, axis=1, keepdims=True)
        q_scale[part, :] = jnp.broadcast_to(lax.rsqrt(squares / width + epsilon), (LANES, LANES))
        pos_b[part, :] = to_lanes(positive[:, part].astype(jnp.float32))
    total[...] = jnp.zeros_like(total)
    pos_total[...] = jnp.zeros_like(pos_total)

    def product(piece):
        source, start, size = piece[:3]
        rows = refs[source][start : start + size, :]
        return lax.dot_general(queries[...], rows, NT, preferred_element_type=jnp.float32)

    following = product(pieces[0])
    for i, (_, _, size, column, _) in enumerate(pieces):
        raw = following
        if i + 1 < len(pieces):
            following = product(pieces[i + 1])
        first = piece_offset(place, column)
        for top in range(0, count, 64):
            part = slice(top, top + 64)
            sums, positives = total[part, :], pos_total[part, :]
            query_scale, wanted = q_scale[part, :], pos_b[part, :]
            for chunk in range(size // LANES):
                cols = pl.ds(first + chunk * LANES, LANES)
                powers = raw[part, chunk * LANES : (chunk + 1) * LANES] * query_scale
                powers = powers * scale[:, cols] + log_weight[flip : flip + 1, cols]
                sums = sums + jnp.exp2(powers)
                positives = positives + jnp.where(wanted == row_ids[:, cols], powers, 0.0)
            total[part, :] = sums
            pos_total[part, :] = positives
    for block in range(count // LANES):
        part = slice(block * LANES, (block + 1) * LANES)
        out[0, block : block + 1, :] = jnp.sum(total[part, :].T, axis=0, keepdims=True)
        out[1, block : block + 1, :] = jnp.sum(pos_total[part, :].T, axis=0, keepdims=True)


def whole(memory=pltpu.VMEM):
    return pl.BlockSpec(memory_space=memory)


def call(kernel, name, outs, place, *operands, scratch=(), **options):
    specs = [whole()] * len(operands)
    if place is not None:
        specs = [whole(pltpu.SMEM)] + specs
        operands = (place, *operands)
    return pl.pallas_call(
        functools.partial(kernel, **options),
        out_shape=tuple(outs),
        in_specs=specs,
        out_specs=tuple(whole() for _ in outs),
        scratch_shapes=list(scratch),
        compiler_params=pltpu.CompilerParams(vmem_limit_bytes=VMEM_LIMIT),
        cost_estimate=pl.CostEstimate(flops=1, bytes_accessed=1, transcendentals=0),
        name=name,
    )(*operands)


def swap(values, axis, flip):
    return lax.ppermute(values, axis, [(i, i ^ flip) for i in range(lax.axis_size(axis))])


def on_device(table, ages, refresh_ids, fresh_rows, neg_ids, queries, pos_ids):
    rows_dev, width = table.shape
    refresh_dev = refresh_ids.shape[0]
    planes = lax.axis_size("outer")
    owners_plane = lax.axis_size("inner")
    replicas = lax.axis_size("query")
    owners = planes * owners_plane
    query_count = queries.shape[0]
    list_size = neg_ids.shape[1]
    place = jnp.stack([lax.axis_index(name) for name in ("outer", "inner", "query")]).astype(jnp.int32)
    plane_rows = owners_plane * rows_dev
    plane_refresh = owners_plane * refresh_dev
    all_rows = plane_rows + plane_refresh
    cap = max(2, (2 * refresh_dev + owners - 1) // owners)
    share = cap // replicas
    table_half, fresh_half = rows_dev // replicas, refresh_dev // replicas
    bf16, f32 = jnp.bfloat16, jnp.float32

    fast = replicas == 2 and owners_plane == 4 and planes == 4
    own_ids, own_ages = refresh_ids.reshape(1, -1), ages.reshape(1, -1)
    query_block, rows_half, scales = call(
        prep_kernel,
        "prep",
        [
            jax.ShapeDtypeStruct((query_count + EXTRA, width), bf16),
            jax.ShapeDtypeStruct((table_half + fresh_half + EXTRA, width), bf16),
            jax.ShapeDtypeStruct(((rows_dev + refresh_dev) // LANES, LANES), f32),
        ],
        place,
        queries,
        table,
        fresh_rows,
        own_ids,
        own_ages,
        neg_ids,
        pos_ids.reshape(1, -1),
        replicas=replicas,
        encode=fast,
    )
    others = (planes - 1) * owners_plane

    if fast:
        axes = ("inner", "query")
        first = [(2 * i + c, 2 * (i ^ (1 + c)) + c) for i in range(4) for c in range(2)]
        second = [(2 * i + c, 2 * (i ^ (2 - c)) + c) for i in range(4) for c in range(2)]
        near = lax.ppermute(rows_half, axes, first)
        side_rows = lax.ppermute(rows_half, axes, second)
        middle, outward = [(1, 2), (2, 1)], [(1, 0), (2, 3)]
        beside = swap(query_block, "outer", 1)
        across = lax.ppermute(query_block, "outer", middle)
        near, beside, across = lax.optimization_barrier((near, beside, across))
        from_end = lax.ppermute(beside, "outer", middle)
        to_end = lax.ppermute(across, "outer", outward)
        far = lax.ppermute(near, axes, second)
        far, from_end, to_end = lax.optimization_barrier((far, from_end, to_end))
        last = lax.ppermute(from_end, "outer", outward)
        got_queries = [(query_block,), (beside,), (to_end, from_end), (last, across)]
        sides = [(i, table_half + fresh_half) for i in (2, 4, 6)]
        buffers = [table, fresh_rows]
        table_pieces = [(0, 0, rows_dev, (0, rows_dev, None, None), -1)]
        fresh_pieces = [(1, 0, refresh_dev, (0, refresh_dev, None, None), -1 - rows_dev // LANES)]
        for slot, by_core, mine in ((1, 0, near), (1, 1, side_rows), (3, None, far)):
            for flip, rows in enumerate((mine, swap(mine, "query", 1))):
                by = None if by_core is None else by_core ^ flip
                data = table_half + fresh_half
                fresh_at = data + 3 * (table_half // LANES)
                table_pieces.append((len(buffers), 0, table_half, (slot * rows_dev, table_half, flip, by), data))
                fresh_pieces.append(
                    (len(buffers), table_half, fresh_half, (slot * refresh_dev, fresh_half, flip, by), fresh_at)
                )
                buffers.append(rows)
    else:
        got_queries = [(query_block,)] + [(swap(query_block, "outer", s),) for s in range(1, planes)]
        got_rows = [rows_half] + [swap(rows_half, "inner", s) for s in range(1, owners_plane)]
        data = table_half + fresh_half
        gathered = lax.all_gather(jnp.stack(got_rows), "query", axis=0)
        gathered = jnp.swapaxes(gathered, 0, 1)
        buffers = [
            gathered[:, :, :table_half].reshape(plane_rows, width),
            gathered[:, :, table_half:data].reshape(plane_refresh, width),
            *[one[data:] for one in got_rows[1:]],
        ]
        sides = [(i + 1, 0) for i in range(1, owners_plane)]
        scales = []
        for rows in buffers[:2]:
            values = rows.astype(f32)
            mean = jnp.sum(values * values, axis=1) / width
            scales.append((lax.rsqrt(mean + epsilon) * (score_scale / width * LOG2E)).reshape(-1, LANES))
        scales = jnp.concatenate(scales)

        def blocks(buffer, count, line):
            starts = range(0, count, 512)
            return [(buffer, i, 512, (i, 512, None, None), -1 - line - i // LANES) for i in starts]

        table_pieces = blocks(0, plane_rows, 0)
        fresh_pieces = blocks(1, plane_refresh, plane_rows // LANES)

    def shift(pieces, columns):
        return [(a, b, c, (d[0] + columns, *d[1:]), e) for a, b, c, d, e in pieces]

    pieces = table_pieces + shift(fresh_pieces, plane_rows)
    size = owners_plane * share
    *packed, scale_plane, plane_ids = call(
        pack_kernel,
        "pack",
        [jax.ShapeDtypeStruct((size + EXTRA, width), bf16)] * (planes - 1)
        + [jax.ShapeDtypeStruct((1, all_rows), f32), jax.ShapeDtypeStruct((1, plane_refresh), jnp.int32)],
        place,
        own_ids,
        scales,
        *buffers,
        sides=sides,
        pieces=fresh_pieces,
        all_pieces=pieces,
        planes=planes,
        rows_dev=rows_dev,
        cap=cap,
        replicas=replicas,
        fast=fast,
    )
    came = [swap(packed[s - 1], "outer", s) for s in range(1, planes)]
    early = [one for group in got_queries[1:-1] for one in group]
    plane_ids, *packed = lax.optimization_barrier((plane_ids, *packed))
    (hits,) = call(
        lists_kernel,
        "lists",
        [jax.ShapeDtypeStruct((planes - 1, all_rows), f32)],
        place,
        plane_ids,
        neg_ids,
        *early,
        given=[len(group) for group in got_queries[1:-1]],
        planes=planes,
        owners_plane=owners_plane,
        rows_dev=rows_dev,
        count=query_count,
    )
    hits, *came = lax.optimization_barrier((hits, *came))
    lw, row_ids, own_target, target, own, new_ages = call(
        meta_kernel,
        "meta",
        [
            jax.ShapeDtypeStruct((planes, all_rows), f32),
            jax.ShapeDtypeStruct((1, all_rows), f32),
            jax.ShapeDtypeStruct((1, plane_refresh), jnp.int32),
            jax.ShapeDtypeStruct((1, others * cap), jnp.int32),
            jax.ShapeDtypeStruct((1, rows_dev), jnp.int32),
            jax.ShapeDtypeStruct((1, rows_dev), jnp.int32),
        ],
        place,
        plane_ids,
        own_ages,
        hits,
        *came,
        *got_queries[-1],
        *buffers,
        arrivals=planes - 1,
        given=len(got_queries[-1]),
        sides=sides,
        planes=planes,
        owners_plane=owners_plane,
        rows_dev=rows_dev,
        list_size=list_size,
        count=query_count,
        cap=cap,
        replicas=replicas,
        fast=fast,
    )
    new_ages = new_ages.reshape(rows_dev)
    came = jnp.concatenate([one[:size] for one in came])
    arrived = [came] + [swap(came, "query", flip) for flip in range(1, replicas)]

    def score(s, given):
        (partial,) = call(
            score_kernel,
            "score",
            [jax.ShapeDtypeStruct((2, query_count // LANES, LANES), f32)],
            place,
            *given,
            lw,
            row_ids,
            scale_plane,
            *buffers,
            scratch=[pltpu.VMEM((query_count, LANES), f32)] * 4 + [pltpu.VMEM(queries.shape, bf16)],
            pieces=pieces,
            flip=s,
            given=len(given),
            list_size=list_size,
        )
        return partial

    mine = None
    for s in [*range(1, planes), 0]:
        partial = score(s, got_queries[s])
        if s:
            partial = swap(partial, "outer", s)
        mine = partial if mine is None else mine + partial
    (new_table,) = call(
        apply_kernel,
        "apply",
        [jax.ShapeDtypeStruct(table.shape, bf16)],
        place,
        own_target,
        target,
        own,
        table,
        *buffers,
        *arrived,
        pieces=fresh_pieces,
        arrivals=len(arrived),
    )
    mine, new_table = lax.optimization_barrier((mine, new_table))
    loss = (jnp.log2(mine[0]) - mine[1]) * math.log(2.0)
    return new_table, new_ages, loss.reshape(query_count)


def solution(mesh):
    owners, replicas = mesh.shape["index"], mesh.shape["query"]
    inner = 1 << (int(math.log2(owners)) // 2)
    split = Mesh(mesh.devices.reshape(owners // inner, inner, replicas), ("outer", "inner", "query"))
    index = ("outer", "inner")
    placed = (
        P(index, None),
        P(index),
        P(index),
        P(index, None),
        P(index, None),
        P(("outer", "inner", "query"), None),
        P(("outer", "inner", "query")),
    )
    return jax.shard_map(
        on_device,
        mesh=split,
        in_specs=placed,
        out_specs=(P(index, None), P(index), P(("outer", "inner", "query"))),
        check_vma=False,
    )
```

```python
import functools
import math

import jax
import jax.numpy as jnp
from jax import lax
from jax.experimental import pallas as pl
from jax.experimental.pallas import tpu as pltpu
from jax.sharding import Mesh, PartitionSpec as P

score_scale = 20.0
age_scale = 16.0
epsilon = 1e-06
LOG2E = math.log2(math.e)
MASKED = -1e30
VMEM_LIMIT = 48 * 1024 * 1024
EXTRA = 16
AGES_ROW = 9
LANES = 128

NT = (((1,), (1,)), ((), ()))
NN = (((1,), (0,)), ((), ()))


def one_hot(ids, count):
    rows = lax.broadcasted_iota(jnp.int32, (count, ids.shape[1]), 0)
    return jnp.where(rows == ids, 1.0, 0.0).astype(jnp.bfloat16)


def split_terms(values):
    terms = []
    for _ in range(3):
        terms.append(values.astype(jnp.bfloat16))
        values = values - terms[-1].astype(jnp.float32)
    return terms


def counted(hits):
    count = hits.shape[1]
    before = lax.broadcasted_iota(jnp.int32, (count, count), 0)
    after = lax.broadcasted_iota(jnp.int32, (count, count), 1)
    earlier = jnp.where(before < after, 1.0, 0.0).astype(jnp.bfloat16)
    return lax.dot_general(hits.astype(jnp.bfloat16), earlier, NN, preferred_element_type=jnp.float32)


def small(values):
    return values.astype(jnp.float32).astype(jnp.bfloat16)


def number(values):
    return values.astype(jnp.float32).astype(jnp.int32)


def put(out, row, values):
    width = out.shape[1]
    for i, left in enumerate(range(0, values.shape[1], width)):
        part = small(values[:, left : left + width])
        out[row + i : row + i + 1, : part.shape[1]] = part


def take(rows, row, count):
    width = rows.shape[1]
    parts = [number(rows[row + i : row + i + 1, :]) for i in range(-(-count // width))]
    return jnp.concatenate(parts, axis=1)[:, :count]


def put_ids(out, row, ids):
    lines = -(-ids.shape[1] // out.shape[1])
    put(out, row, ids >> 7)
    put(out, row + lines, ids & 127)


def take_ids(rows, row, count):
    lines = -(-count // rows.shape[1])
    return take(rows, row, count) * LANES + take(rows, row + lines, count)


def prep_kernel(
    place, table, fresh, ref_ids, ages, neg, pos, rows_out, scale_out, *mail, owners_plane, cap, replicas, encode
):
    outer, inner, core = place[0], place[1], place[2]
    width = table.shape[1]
    refresh_dev, rows_dev = fresh.shape[0], table.shape[0]
    planes, share = len(mail), cap // replicas
    pairs = [(plane, side) for plane in range(planes) for side in range(owners_plane)]
    ids = ref_ids[...]
    owner_of = ids // rows_dev
    rank = owner_ranks(
        [owner_of - ((outer ^ plane) * owners_plane + (inner ^ side)) for plane, side in pairs], refresh_dev, cap
    )
    rank = rank - core * share
    code = jnp.full((1, refresh_dev), -1, jnp.int32)
    for i in range(len(pairs)):
        here = (rank[i : i + 1, :] >= 0) & (rank[i : i + 1, :] < share)
        code = jnp.where(here, i * share + rank[i : i + 1, :], code)
    select = one_hot(code, len(pairs) * share)
    packed = lax.dot_general(select, fresh[...], NN, preferred_element_type=jnp.float32).astype(jnp.bfloat16)
    size = owners_plane * share
    for i, out in enumerate(mail):
        out[:size, :] = packed[i * size : (i + 1) * size, :]
        out[size:, :] = jnp.zeros((EXTRA, width), jnp.bfloat16)
        row = size
        for values in (neg[...], pos[...], ids):
            put_ids(out, row, values)
            row += 2 * -(-values.shape[1] // width)

    line, row = 0, 0
    halves = []
    for source in (table, fresh):
        rows = source.shape[0]
        half = rows // replicas
        rows_out[row : row + half, :] = source[pl.ds(pl.multiple_of(core * half, half), half), :]
        row += half
        for block in range(rows // LANES):
            squares = jnp.zeros((LANES, LANES), jnp.float32)
            for chunk in range(width // LANES):
                values = source[block * LANES : (block + 1) * LANES, chunk * LANES : (chunk + 1) * LANES]
                values = values.astype(jnp.float32)
                squares += values * values
            mean = jnp.sum(squares.T, axis=0, keepdims=True) / width
            scale_out[line + block : line + block + 1, :] = lax.rsqrt(mean + epsilon) * (score_scale / width * LOG2E)
        halves += [(line, i, half // LANES) for i in range(half // LANES)]
        line += rows // LANES
    rows_out[row:, :] = jnp.zeros((EXTRA, width), jnp.bfloat16)
    if encode:
        terms = []
        for first, i, count in halves:
            terms += split_terms(scale_out[pl.ds(first + core * count + i, 1), :])
        for i, term in enumerate(terms):
            rows_out[row + i : row + i + 1, :LANES] = term
    put(rows_out, row + AGES_ROW, ages[...])


def relay_kernel(*refs, planes, owners_plane, share, list_size, count, refresh_dev):
    mail, outs = refs[:planes], refs[planes:]
    size = owners_plane * share
    width = mail[0].shape[1]
    row = size + 2 * (-(-list_size // width) + -(-count // width))
    ids = jnp.concatenate([take_ids(block, row, refresh_dev) for block in mail], axis=1)
    for side, out in enumerate(outs):
        for plane, block in enumerate(mail):
            out[plane * share : (plane + 1) * share, :] = block[side * share : (side + 1) * share, :]
        out[planes * share :, :] = jnp.zeros((EXTRA, width), jnp.bfloat16)
        put_ids(out, planes * share, ids)


def in_order(place, values, fast):
    if not fast:
        return values
    own, near, side, far = values
    core = place[2]
    return [own, jnp.where(core == 0, near, side), jnp.where(core == 0, side, near), far]


def owner_ranks(rows, refresh_dev, cap):
    match = jnp.concatenate(rows, axis=0) == 0
    rank = counted(jnp.where(match, 1.0, 0.0)).astype(jnp.int32)
    return jnp.where(match, rank, -cap)


def one_hots(ids, high_count):
    return one_hot(ids >> 7, high_count), one_hot(ids & 127, LANES)


def bitmap(ids, high_count):
    high, low = one_hots(ids, high_count)
    return lax.dot_general(low, high, NT, preferred_element_type=jnp.float32).astype(jnp.bfloat16)


def lookup(one_map, pair):
    hit = lax.dot_general(one_map, pair[0], NN, preferred_element_type=jnp.float32)
    return jnp.sum(hit * pair[1].astype(jnp.float32), axis=0, keepdims=True)


def column_ids(place, owners_plane, rows_dev):
    column = lax.broadcasted_iota(jnp.int32, (1, owners_plane * rows_dev), 1)
    return (place[0] * owners_plane + (place[1] ^ (column // rows_dev))) * rows_dev + column % rows_dev


def meta_kernel(
    place, ages, scale, *refs, sides, pieces, planes, owners_plane, rows_dev, refresh_dev, list_size, count, cap, replicas,
    fast
):
    outer, inner, core = place[0], place[1], place[2]
    lw_out, row_out, scale_out, pos_out, target_out, own_out, ages_out = refs[-7:]
    mail, relayed, buffers = refs[:planes], refs[planes : planes + owners_plane], refs[planes + owners_plane : -7]
    share = cap // replicas
    plane_rows = owners_plane * rows_dev
    high_count = planes * plane_rows // LANES
    own_owner = outer * owners_plane + inner

    ids = [take_ids(block, planes * share, planes * refresh_dev) for block in relayed]
    plane_ids = jnp.concatenate([one[:, :refresh_dev] for one in ids], axis=1)
    table_ids = column_ids(place, owners_plane, rows_dev)
    pair = one_hots(jnp.concatenate([table_ids, plane_ids], axis=1), high_count)
    refreshed = lookup(bitmap(jnp.concatenate(ids, axis=1), high_count), (pair[0][:, :plane_rows], pair[1][:, :plane_rows]))
    refreshed = refreshed > 0.5
    row_out[:, :plane_rows] = jnp.where(refreshed, -1, table_ids).astype(jnp.float32)
    row_out[:, plane_rows:] = plane_ids.astype(jnp.float32)
    own_out[...] = refreshed[:, :rows_dev].astype(jnp.int32)
    ages_out[...] = jnp.where(refreshed[:, :rows_dev], 0, ages[...])

    all_ages = [ages[...]] + [take(buffers[i], row + AGES_ROW, rows_dev) for i, row in sides]
    all_ages = jnp.concatenate(in_order(place, all_ages, fast), axis=1).astype(jnp.float32)
    weight = jnp.exp(-all_ages / age_scale).astype(jnp.bfloat16).astype(jnp.float32)
    log_weight = jnp.where(refreshed, MASKED, jnp.log2(weight))
    log_weight = jnp.concatenate([log_weight, jnp.zeros((1, plane_ids.shape[1]), jnp.float32)], axis=1)
    for group, block in enumerate(mail):
        row = owners_plane * share
        hit = lookup(bitmap(take_ids(block, row, list_size), high_count), pair)
        lw_out[group : group + 1, :] = jnp.where(hit > 0.5, log_weight, MASKED)
        row += 2 * -(-list_size // block.shape[1])
        pos_out[group : group + 1, :] = take_ids(block, row, count).astype(jnp.float32)

    pairs = [(side, plane) for side in range(owners_plane) for plane in range(planes)]
    part_ids = [ids[side][:, plane * refresh_dev : (plane + 1) * refresh_dev] for side, plane in pairs]
    rank = owner_ranks([one // rows_dev - own_owner for one in part_ids], refresh_dev, cap)
    for i in range(len(pairs)):
        took = rank[i : i + 1, :]
        slot = jnp.where(took < 0, -1, ((took // share) ^ core) * share + took % share)
        row = jnp.where(took < 0, 0, part_ids[i] - own_owner * rows_dev)
        kinds = lax.broadcasted_iota(jnp.int32, (8, refresh_dev), 0)
        digits = jnp.where(kinds == 0, row // 16, jnp.where(kinds == 1, row % 16, 1))
        found = lax.dot_general(small(digits), one_hot(slot, cap), NT, preferred_element_type=jnp.float32)
        found = found.astype(jnp.int32)
        target = jnp.where(found[2:3, :] > 0, found[0:1, :] * 16 + found[1:2, :], -1)
        for part in range(replicas):
            first = (part * len(pairs) + i) * share
            target_out[:, first : first + share] = target[:, part * share : (part + 1) * share]

    for source, start, size, column, scale_at in pieces:
        first = piece_offset(place, column)
        for chunk in range(size // LANES):
            if scale_at < 0:
                line = -1 - scale_at + chunk
                row = scale[line : line + 1, :]
            else:
                line = scale_at + 3 * chunk
                row = jnp.sum(buffers[source][line : line + 3, :LANES].astype(jnp.float32), axis=0, keepdims=True)
            scale_out[:, pl.ds(first + chunk * LANES, LANES)] = row


def piece_offset(place, piece):
    column, size, flip, by_core = piece
    if flip is None:
        return column
    column += (place[2] ^ flip) * size
    if by_core is not None:
        column += (place[2] ^ by_core) * size * 2
    return pl.multiple_of(column, size)


def apply_kernel(target, refreshed, table, *refs):
    *arrived, out = refs
    values = jnp.concatenate([block[...] for block in arrived], axis=0)
    rows = lax.broadcasted_iota(jnp.int32, (out.shape[0], values.shape[0]), 0)
    chosen = jnp.where(rows == target[...], 1.0, 0.0).astype(jnp.bfloat16)
    fresh = lax.dot_general(chosen, values, NN, preferred_element_type=jnp.float32)
    for top in range(0, out.shape[0], LANES):
        part = slice(top, top + LANES)
        hit = to_lanes(refreshed[:, part].astype(jnp.float32)) > 0.5
        for left in range(0, out.shape[1], LANES):
            cols = slice(left, left + LANES)
            out[part, cols] = jnp.where(hit, fresh[part, cols], table[part, cols].astype(jnp.float32)).astype(jnp.bfloat16)


def to_lanes(row):
    return jnp.broadcast_to(row, (LANES, LANES)).T


def score_kernel(place, *refs, pieces, flip, given):
    out, total, pos_total, q_scale, pos_b, chosen = refs[-6:]
    positives_row, log_weight, row_ids, scale = refs[given : given + 4]
    positive = positives_row[flip : flip + 1, :]
    queries = refs[0]
    count, width = queries.shape
    if given == 2:
        at_end = (place[0] == 0) | (place[0] == 3)
        chosen[...] = jnp.where(at_end, refs[0][...], refs[1][...])
        queries = chosen
    refs = refs[given + 4 : -6]
    for block in range(count // LANES):
        part = slice(block * LANES, (block + 1) * LANES)
        values = queries[part, :].astype(jnp.float32)
        squares = jnp.sum(values * values, axis=1, keepdims=True)
        q_scale[part, :] = jnp.broadcast_to(lax.rsqrt(squares / width + epsilon), (LANES, LANES))
        pos_b[part, :] = to_lanes(positive[:, part])
    total[...] = jnp.zeros_like(total)
    pos_total[...] = jnp.zeros_like(pos_total)

    def product(piece):
        source, start, size = piece[:3]
        rows = refs[source][start : start + size, :]
        return lax.dot_general(queries[...], rows, NT, preferred_element_type=jnp.float32)

    following = product(pieces[0])
    for i, (_, _, size, column, _) in enumerate(pieces):
        raw = following
        if i + 1 < len(pieces):
            following = product(pieces[i + 1])
        first = piece_offset(place, column)
        for top in range(0, count, 64):
            part = slice(top, top + 64)
            sums, positives = total[part, :], pos_total[part, :]
            query_scale, wanted = q_scale[part, :], pos_b[part, :]
            for chunk in range(size // LANES):
                cols = pl.ds(first + chunk * LANES, LANES)
                powers = raw[part, chunk * LANES : (chunk + 1) * LANES] * query_scale
                powers = powers * scale[:, cols] + log_weight[flip : flip + 1, cols]
                sums = sums + jnp.exp2(powers)
                positives = positives + jnp.where(wanted == row_ids[:, cols], powers, 0.0)
            total[part, :] = sums
            pos_total[part, :] = positives
    for block in range(count // LANES):
        part = slice(block * LANES, (block + 1) * LANES)
        out[0, block : block + 1, :] = jnp.sum(total[part, :].T, axis=0, keepdims=True)
        out[1, block : block + 1, :] = jnp.sum(pos_total[part, :].T, axis=0, keepdims=True)


def whole(memory=pltpu.VMEM):
    return pl.BlockSpec(memory_space=memory)


def call(kernel, name, outs, place, *operands, scratch=(), **options):
    specs = [whole()] * len(operands)
    if place is not None:
        specs = [whole(pltpu.SMEM)] + specs
        operands = (place, *operands)
    return pl.pallas_call(
        functools.partial(kernel, **options),
        out_shape=tuple(outs),
        in_specs=specs,
        out_specs=tuple(whole() for _ in outs),
        scratch_shapes=list(scratch),
        compiler_params=pltpu.CompilerParams(vmem_limit_bytes=VMEM_LIMIT),
        cost_estimate=pl.CostEstimate(flops=1, bytes_accessed=1, transcendentals=0),
        name=name,
    )(*operands)


def swap(values, axis, flip):
    return lax.ppermute(values, axis, [(i, i ^ flip) for i in range(lax.axis_size(axis))])


def on_device(table, ages, refresh_ids, fresh_rows, neg_ids, queries, pos_ids):
    rows_dev, width = table.shape
    refresh_dev = refresh_ids.shape[0]
    planes = lax.axis_size("outer")
    owners_plane = lax.axis_size("inner")
    replicas = lax.axis_size("query")
    owners = planes * owners_plane
    query_count = queries.shape[0]
    list_size = neg_ids.shape[1]
    place = jnp.stack([lax.axis_index(name) for name in ("outer", "inner", "query")]).astype(jnp.int32)
    plane_rows = owners_plane * rows_dev
    plane_refresh = owners_plane * refresh_dev
    all_rows = plane_rows + plane_refresh
    cap = max(2, (2 * refresh_dev + owners - 1) // owners)
    share = cap // replicas
    table_half, fresh_half = rows_dev // replicas, refresh_dev // replicas
    bf16, f32 = jnp.bfloat16, jnp.float32

    fast = replicas == 2 and owners_plane == 4 and planes == 4
    own_ages = ages.reshape(1, -1)
    size = owners_plane * share
    rows_half, scales, *mail = call(
        prep_kernel,
        "prep",
        [
            jax.ShapeDtypeStruct((table_half + fresh_half + EXTRA, width), bf16),
            jax.ShapeDtypeStruct(((rows_dev + refresh_dev) // LANES, LANES), f32),
        ]
        + [jax.ShapeDtypeStruct((size + EXTRA, width), bf16)] * planes,
        place,
        table,
        fresh_rows,
        refresh_ids.reshape(1, -1),
        own_ages,
        neg_ids,
        pos_ids.reshape(1, -1),
        owners_plane=owners_plane,
        cap=cap,
        replicas=replicas,
        encode=fast,
    )
    mail = [mail[0]] + [swap(mail[s], "outer", s) for s in range(1, planes)]

    if fast:
        axes = ("inner", "query")
        first = [(2 * i + c, 2 * (i ^ (1 + c)) + c) for i in range(4) for c in range(2)]
        second = [(2 * i + c, 2 * (i ^ (2 - c)) + c) for i in range(4) for c in range(2)]
        near = lax.ppermute(rows_half, axes, first)
        side_rows = lax.ppermute(rows_half, axes, second)
        middle, outward = [(1, 2), (2, 1)], [(1, 0), (2, 3)]
        beside = swap(queries, "outer", 1)
        across = lax.ppermute(queries, "outer", middle)
        beside, across, *mail = lax.optimization_barrier((beside, across, *mail))
        from_end = lax.ppermute(beside, "outer", middle)
        to_end = lax.ppermute(across, "outer", outward)
        far = lax.ppermute(near, axes, second)
        far, from_end, to_end = lax.optimization_barrier((far, from_end, to_end))
        last = lax.ppermute(from_end, "outer", outward)
        got_queries = [(queries,), (beside,), (to_end, from_end), (last, across)]
        sides = [(i, table_half + fresh_half) for i in (2, 4, 6)]
        buffers = [table, fresh_rows]
        table_pieces = [(0, 0, rows_dev, (0, rows_dev, None, None), -1)]
        fresh_pieces = [(1, 0, refresh_dev, (0, refresh_dev, None, None), -1 - rows_dev // LANES)]
        for slot, by_core, mine in ((1, 0, near), (1, 1, side_rows), (3, None, far)):
            for flip, rows in enumerate((mine, swap(mine, "query", 1))):
                by = None if by_core is None else by_core ^ flip
                data = table_half + fresh_half
                fresh_at = data + 3 * (table_half // LANES)
                table_pieces.append((len(buffers), 0, table_half, (slot * rows_dev, table_half, flip, by), data))
                fresh_pieces.append(
                    (len(buffers), table_half, fresh_half, (slot * refresh_dev, fresh_half, flip, by), fresh_at)
                )
                buffers.append(rows)
    else:
        got_queries = [(queries,)] + [(swap(queries, "outer", s),) for s in range(1, planes)]
        got_rows = [rows_half] + [swap(rows_half, "inner", s) for s in range(1, owners_plane)]
        data = table_half + fresh_half
        gathered = lax.all_gather(jnp.stack(got_rows), "query", axis=0)
        gathered = jnp.swapaxes(gathered, 0, 1)
        buffers = [
            gathered[:, :, :table_half].reshape(plane_rows, width),
            gathered[:, :, table_half:data].reshape(plane_refresh, width),
            *[one[data:] for one in got_rows[1:]],
        ]
        sides = [(i + 1, 0) for i in range(1, owners_plane)]
        scales = []
        for rows in buffers[:2]:
            values = rows.astype(f32)
            mean = jnp.sum(values * values, axis=1) / width
            scales.append((lax.rsqrt(mean + epsilon) * (score_scale / width * LOG2E)).reshape(-1, LANES))
        scales = jnp.concatenate(scales)

        def blocks(buffer, count, line):
            starts = range(0, count, 512)
            return [(buffer, i, 512, (i, 512, None, None), -1 - line - i // LANES) for i in starts]

        table_pieces = blocks(0, plane_rows, 0)
        fresh_pieces = blocks(1, plane_refresh, plane_rows // LANES)

    def shift(pieces, columns):
        return [(a, b, c, (d[0] + columns, *d[1:]), e) for a, b, c, d, e in pieces]

    pieces = table_pieces + shift(fresh_pieces, plane_rows)
    relayed = call(
        relay_kernel,
        "relay",
        [jax.ShapeDtypeStruct((planes * share + EXTRA, width), bf16)] * owners_plane,
        None,
        *mail,
        planes=planes,
        owners_plane=owners_plane,
        share=share,
        list_size=list_size,
        count=query_count,
        refresh_dev=refresh_dev,
    )
    relayed = [relayed[0]] + [swap(relayed[s], "inner", s) for s in range(1, owners_plane)]
    lw, row_ids, scale_plane, positive, target, own, new_ages = call(
        meta_kernel,
        "meta",
        [
            jax.ShapeDtypeStruct((planes, all_rows), f32),
            jax.ShapeDtypeStruct((1, all_rows), f32),
            jax.ShapeDtypeStruct((1, all_rows), f32),
            jax.ShapeDtypeStruct((planes, query_count), f32),
            jax.ShapeDtypeStruct((1, owners * cap), jnp.int32),
            jax.ShapeDtypeStruct((1, rows_dev), jnp.int32),
            jax.ShapeDtypeStruct((1, rows_dev), jnp.int32),
        ],
        place,
        own_ages,
        scales,
        *mail,
        *relayed,
        *buffers,
        sides=sides,
        pieces=pieces,
        planes=planes,
        owners_plane=owners_plane,
        rows_dev=rows_dev,
        refresh_dev=refresh_dev,
        list_size=list_size,
        count=query_count,
        cap=cap,
        replicas=replicas,
        fast=fast,
    )
    new_ages = new_ages.reshape(rows_dev)
    came = jnp.concatenate([one[: planes * share] for one in relayed])
    arrived = [came] + [swap(came, "query", flip) for flip in range(1, replicas)]

    def score(s, given):
        (partial,) = call(
            score_kernel,
            "score",
            [jax.ShapeDtypeStruct((2, query_count // LANES, LANES), f32)],
            place,
            *given,
            positive,
            lw,
            row_ids,
            scale_plane,
            *buffers,
            scratch=[pltpu.VMEM((query_count, LANES), f32)] * 4 + [pltpu.VMEM(queries.shape, bf16)],
            pieces=pieces,
            flip=s,
            given=len(given),
        )
        return partial

    (new_table,) = call(
        apply_kernel, "apply", [jax.ShapeDtypeStruct(table.shape, bf16)], None, target, own, table, *arrived
    )
    partials = [swap(score(s, got_queries[s]), "outer", s) for s in range(1, planes - 1)] + [score(0, got_queries[0])]
    new_table, *tied = lax.optimization_barrier((new_table, *partials, *got_queries[-1]))
    partials, last_queries = tied[: planes - 1], tied[planes - 1 :]
    mine = sum(partials[1:], partials[0])
    mine = mine + swap(score(planes - 1, last_queries), "outer", planes - 1)
    loss = (jnp.log2(mine[0]) - mine[1]) * math.log(2.0)
    return new_table, new_ages, loss.reshape(query_count)


def solution(mesh):
    owners, replicas = mesh.shape["index"], mesh.shape["query"]
    inner = 1 << (int(math.log2(owners)) // 2)
    split = Mesh(mesh.devices.reshape(owners // inner, inner, replicas), ("outer", "inner", "query"))
    index = ("outer", "inner")
    placed = (
        P(index, None),
        P(index),
        P(index),
        P(index, None),
        P(index, None),
        P(("outer", "inner", "query"), None),
        P(("outer", "inner", "query")),
    )
    return jax.shard_map(
        on_device,
        mesh=split,
        in_specs=placed,
        out_specs=(P(index, None), P(index), P(("outer", "inner", "query"))),
        check_vma=False,
    )
```

```python
import functools
import math

import jax
import jax.numpy as jnp
from jax import lax
from jax.experimental import pallas as pl
from jax.experimental.pallas import tpu as pltpu
from jax.sharding import Mesh, PartitionSpec as P

score_scale = 20.0
age_scale = 16.0
epsilon = 1e-06
LOG2E = math.log2(math.e)
MASKED = -1e30
VMEM_LIMIT = 48 * 1024 * 1024
EXTRA = 16
AGES_ROW = 9
LANES = 128

NT = (((1,), (1,)), ((), ()))
NN = (((1,), (0,)), ((), ()))


def one_hot(ids, count):
    rows = lax.broadcasted_iota(jnp.int32, (count, ids.shape[1]), 0)
    if count <= 256:
        ids = jnp.where((ids < 0) | (ids >= count), -1, ids)
        rows, ids = rows.astype(jnp.float32).astype(jnp.bfloat16), ids.astype(jnp.float32).astype(jnp.bfloat16)
        return jnp.where(rows == ids, jnp.bfloat16(1), jnp.bfloat16(0))
    return jnp.where(rows == ids, 1.0, 0.0).astype(jnp.bfloat16)


def split_terms(values):
    terms = []
    for _ in range(3):
        terms.append(values.astype(jnp.bfloat16))
        values = values - terms[-1].astype(jnp.float32)
    return terms


def counted(hits):
    count = hits.shape[1]
    before = lax.broadcasted_iota(jnp.int32, (count, count), 0)
    after = lax.broadcasted_iota(jnp.int32, (count, count), 1)
    earlier = jnp.where(before < after, 1.0, 0.0).astype(jnp.bfloat16)
    return lax.dot_general(hits.astype(jnp.bfloat16), earlier, NN, preferred_element_type=jnp.float32)


def small(values):
    return values.astype(jnp.float32).astype(jnp.bfloat16)


def number(values):
    return values.astype(jnp.float32).astype(jnp.int32)


def put(out, row, values):
    width = out.shape[1]
    for i, left in enumerate(range(0, values.shape[1], width)):
        part = small(values[:, left : left + width])
        out[row + i : row + i + 1, : part.shape[1]] = part


def take(rows, row, count):
    width = rows.shape[1]
    parts = [number(rows[row + i : row + i + 1, :]) for i in range(-(-count // width))]
    return jnp.concatenate(parts, axis=1)[:, :count]


def put_ids(out, row, ids):
    lines = -(-ids.shape[1] // out.shape[1])
    put(out, row, ids >> 7)
    put(out, row + lines, ids & 127)


def take_ids(rows, row, count):
    lines = -(-count // rows.shape[1])
    return take(rows, row, count) * LANES + take(rows, row + lines, count)


def prep_kernel(
    place, table, fresh, ref_ids, ages, neg, pos, rows_out, scale_out, *mail, owners_plane, cap, replicas, encode
):
    outer, inner, core = place[0], place[1], place[2]
    width = table.shape[1]
    refresh_dev, rows_dev = fresh.shape[0], table.shape[0]
    planes, share = len(mail), cap // replicas
    pairs = [(plane, side) for plane in range(planes) for side in range(owners_plane)]
    ids = ref_ids[...]
    owner_of = ids // rows_dev
    rank = owner_ranks(
        [owner_of - ((outer ^ plane) * owners_plane + (inner ^ side)) for plane, side in pairs], refresh_dev, cap
    )
    rank = rank - core * share
    code = jnp.full((1, refresh_dev), -1, jnp.int32)
    for i in range(len(pairs)):
        here = (rank[i : i + 1, :] >= 0) & (rank[i : i + 1, :] < share)
        code = jnp.where(here, i * share + rank[i : i + 1, :], code)
    select = one_hot(code, len(pairs) * share)
    packed = lax.dot_general(select, fresh[...], NN, preferred_element_type=jnp.float32).astype(jnp.bfloat16)
    size = owners_plane * share
    for i, out in enumerate(mail):
        out[:size, :] = packed[i * size : (i + 1) * size, :]
        out[size:, :] = jnp.zeros((EXTRA, width), jnp.bfloat16)
        row = size
        for values in (neg[...], pos[...], ids):
            put_ids(out, row, values)
            row += 2 * -(-values.shape[1] // width)

    line, row = 0, 0
    halves = []
    for source in (table, fresh):
        rows = source.shape[0]
        half = rows // replicas
        rows_out[row : row + half, :] = source[pl.ds(pl.multiple_of(core * half, half), half), :]
        row += half
        for block in range(rows // LANES):
            squares = jnp.zeros((LANES, LANES), jnp.float32)
            for chunk in range(width // LANES):
                values = source[block * LANES : (block + 1) * LANES, chunk * LANES : (chunk + 1) * LANES]
                values = values.astype(jnp.float32)
                squares += values * values
            mean = jnp.sum(squares.T, axis=0, keepdims=True) / width
            scale_out[line + block : line + block + 1, :] = lax.rsqrt(mean + epsilon) * (score_scale / width * LOG2E)
        halves += [(line, i, half // LANES) for i in range(half // LANES)]
        line += rows // LANES
    rows_out[row:, :] = jnp.zeros((EXTRA, width), jnp.bfloat16)
    if encode:
        terms = []
        for first, i, count in halves:
            terms += split_terms(scale_out[pl.ds(first + core * count + i, 1), :])
        for i, term in enumerate(terms):
            rows_out[row + i : row + i + 1, :LANES] = term
    put(rows_out, row + AGES_ROW, ages[...])


def relay_kernel(*refs, planes, owners_plane, share, list_size, count, refresh_dev):
    mail, outs = refs[:planes], refs[planes:]
    size = owners_plane * share
    width = mail[0].shape[1]
    row = size + 2 * (-(-list_size // width) + -(-count // width))
    ids = jnp.concatenate([take_ids(block, row, refresh_dev) for block in mail], axis=1)
    for side, out in enumerate(outs):
        for plane, block in enumerate(mail):
            out[plane * share : (plane + 1) * share, :] = block[side * share : (side + 1) * share, :]
        out[planes * share :, :] = jnp.zeros((EXTRA, width), jnp.bfloat16)
        put_ids(out, planes * share, ids)


def in_order(place, values, fast):
    if not fast:
        return values
    own, near, side, far = values
    core = place[2]
    return [own, jnp.where(core == 0, near, side), jnp.where(core == 0, side, near), far]


def owner_ranks(rows, refresh_dev, cap):
    match = jnp.concatenate(rows, axis=0) == 0
    rank = counted(jnp.where(match, 1.0, 0.0)).astype(jnp.int32)
    return jnp.where(match, rank, -cap)


def one_hots(ids, high_count):
    return one_hot(ids >> 7, high_count), one_hot(ids & 127, LANES)


def bitmap(ids, high_count):
    high, low = one_hots(ids, high_count)
    return lax.dot_general(low, high, NT, preferred_element_type=jnp.float32).astype(jnp.bfloat16)


def lookup(one_map, pair):
    hit = lax.dot_general(one_map, pair[0], NN, preferred_element_type=jnp.float32)
    return jnp.sum(hit * pair[1].astype(jnp.float32), axis=0, keepdims=True)


def column_ids(place, owners_plane, rows_dev):
    column = lax.broadcasted_iota(jnp.int32, (1, owners_plane * rows_dev), 1)
    return (place[0] * owners_plane + (place[1] ^ (column // rows_dev))) * rows_dev + column % rows_dev


def lists_kernel(*refs, first, list_size, high_count):
    *mail, out = refs
    for group, block in enumerate(mail):
        out[group, :, :] = bitmap(take_ids(block, first, list_size), high_count)


def meta_kernel(
    place, maps, ages, scale, *refs, sides, pieces, planes, owners_plane, rows_dev, refresh_dev, list_size, count, cap, replicas,
    fast
):
    outer, inner, core = place[0], place[1], place[2]
    lw_out, row_out, scale_out, pos_out, target_out, own_out, ages_out = refs[-7:]
    mail, relayed, buffers = refs[:planes], refs[planes : planes + owners_plane], refs[planes + owners_plane : -7]
    share = cap // replicas
    plane_rows = owners_plane * rows_dev
    high_count = planes * plane_rows // LANES
    own_owner = outer * owners_plane + inner

    ids = [take_ids(block, planes * share, planes * refresh_dev) for block in relayed]
    plane_ids = jnp.concatenate([one[:, :refresh_dev] for one in ids], axis=1)
    table_ids = column_ids(place, owners_plane, rows_dev)
    pair = one_hots(jnp.concatenate([table_ids, plane_ids], axis=1), high_count)
    refreshed = lookup(bitmap(jnp.concatenate(ids, axis=1), high_count), (pair[0][:, :plane_rows], pair[1][:, :plane_rows]))
    refreshed = refreshed > 0.5
    row_out[:, :plane_rows] = jnp.where(refreshed, -1, table_ids).astype(jnp.float32)
    row_out[:, plane_rows:] = plane_ids.astype(jnp.float32)
    own_out[...] = refreshed[:, :rows_dev].astype(jnp.int32)
    ages_out[...] = jnp.where(refreshed[:, :rows_dev], 0, ages[...])

    all_ages = [ages[...]] + [take(buffers[i], row + AGES_ROW, rows_dev) for i, row in sides]
    all_ages = jnp.concatenate(in_order(place, all_ages, fast), axis=1).astype(jnp.float32)
    weight = jnp.exp(-all_ages / age_scale).astype(jnp.bfloat16).astype(jnp.float32)
    log_weight = jnp.where(refreshed, MASKED, jnp.log2(weight))
    log_weight = jnp.concatenate([log_weight, jnp.zeros((1, plane_ids.shape[1]), jnp.float32)], axis=1)
    for group, block in enumerate(mail):
        row = owners_plane * share
        hit = lookup(maps[group, :, :], pair)
        lw_out[group : group + 1, :] = jnp.where(hit > 0.5, log_weight, MASKED)
        row += 2 * -(-list_size // block.shape[1])
        pos_out[group : group + 1, :] = take_ids(block, row, count).astype(jnp.float32)

    pairs = [(side, plane) for side in range(owners_plane) for plane in range(planes)]
    part_ids = [ids[side][:, plane * refresh_dev : (plane + 1) * refresh_dev] for side, plane in pairs]
    rank = owner_ranks([one // rows_dev - own_owner for one in part_ids], refresh_dev, cap)
    for i in range(len(pairs)):
        took = rank[i : i + 1, :]
        slot = jnp.where(took < 0, -1, ((took // share) ^ core) * share + took % share)
        row = jnp.where(took < 0, 0, part_ids[i] - own_owner * rows_dev)
        kinds = lax.broadcasted_iota(jnp.int32, (8, refresh_dev), 0)
        digits = jnp.where(kinds == 0, row // 16, jnp.where(kinds == 1, row % 16, 1))
        found = lax.dot_general(small(digits), one_hot(slot, cap), NT, preferred_element_type=jnp.float32)
        found = found.astype(jnp.int32)
        target = jnp.where(found[2:3, :] > 0, found[0:1, :] * 16 + found[1:2, :], -1)
        for part in range(replicas):
            first = (part * len(pairs) + i) * share
            target_out[:, first : first + share] = target[:, part * share : (part + 1) * share]

    for source, start, size, column, scale_at in pieces:
        first = piece_offset(place, column)
        for chunk in range(size // LANES):
            if scale_at < 0:
                line = -1 - scale_at + chunk
                row = scale[line : line + 1, :]
            else:
                line = scale_at + 3 * chunk
                row = jnp.sum(buffers[source][line : line + 3, :LANES].astype(jnp.float32), axis=0, keepdims=True)
            scale_out[:, pl.ds(first + chunk * LANES, LANES)] = row


def piece_offset(place, piece):
    column, size, flip, by_core = piece
    if flip is None:
        return column
    column += (place[2] ^ flip) * size
    if by_core is not None:
        column += (place[2] ^ by_core) * size * 2
    return pl.multiple_of(column, size)


def apply_kernel(target, refreshed, table, *refs):
    *arrived, out = refs
    values = jnp.concatenate([block[...] for block in arrived], axis=0)
    rows = lax.broadcasted_iota(jnp.int32, (out.shape[0], values.shape[0]), 0)
    chosen = jnp.where(rows == target[...], 1.0, 0.0).astype(jnp.bfloat16)
    fresh = lax.dot_general(chosen, values, NN, preferred_element_type=jnp.float32)
    for top in range(0, out.shape[0], LANES):
        part = slice(top, top + LANES)
        hit = to_lanes(refreshed[:, part].astype(jnp.float32)) > 0.5
        for left in range(0, out.shape[1], LANES):
            cols = slice(left, left + LANES)
            out[part, cols] = jnp.where(hit, fresh[part, cols], table[part, cols].astype(jnp.float32)).astype(jnp.bfloat16)


def to_lanes(row):
    return jnp.broadcast_to(row, (LANES, LANES)).T


def score_kernel(place, *refs, pieces, flip, given):
    out, total, pos_total, q_scale, pos_b, chosen = refs[-6:]
    positives_row, log_weight, row_ids, scale = refs[given : given + 4]
    positive = positives_row[flip : flip + 1, :]
    queries = refs[0]
    count, width = queries.shape
    if given == 2:
        at_end = (place[0] == 0) | (place[0] == 3)
        chosen[...] = jnp.where(at_end, refs[0][...], refs[1][...])
        queries = chosen
    refs = refs[given + 4 : -6]
    for block in range(count // LANES):
        part = slice(block * LANES, (block + 1) * LANES)
        values = queries[part, :].astype(jnp.float32)
        squares = jnp.sum(values * values, axis=1, keepdims=True)
        q_scale[part, :] = jnp.broadcast_to(lax.rsqrt(squares / width + epsilon), (LANES, LANES))
        pos_b[part, :] = to_lanes(positive[:, part])
    total[...] = jnp.zeros_like(total)
    pos_total[...] = jnp.zeros_like(pos_total)

    def product(group):
        rows = [refs[source][start : start + size, :] for source, start, size, _, _ in group]
        rows = rows[0] if len(rows) == 1 else jnp.concatenate(rows, axis=0)
        return lax.dot_general(queries[...], rows, NT, preferred_element_type=jnp.float32)

    narrow = [piece for piece in pieces if piece[2] < 256]
    groups = [[piece] for piece in pieces if piece[2] >= 256] + [narrow[i : i + 2] for i in range(0, len(narrow), 2)]
    following = product(groups[0])
    for i, group in enumerate(groups):
        raw = following
        if i + 1 < len(groups):
            following = product(groups[i + 1])
        columns = []
        for _, _, size, column, _ in group:
            columns += [piece_offset(place, column) + chunk * LANES for chunk in range(size // LANES)]
        for top in range(0, count, 64):
            part = slice(top, top + 64)
            sums, positives = total[part, :], pos_total[part, :]
            query_scale, wanted = q_scale[part, :], pos_b[part, :]
            for chunk, first in enumerate(columns):
                cols = pl.ds(first, LANES)
                powers = raw[part, chunk * LANES : (chunk + 1) * LANES] * query_scale
                powers = powers * scale[:, cols] + log_weight[flip : flip + 1, cols]
                sums = sums + jnp.exp2(powers)
                positives = positives + jnp.where(wanted == row_ids[:, cols], powers, 0.0)
            total[part, :] = sums
            pos_total[part, :] = positives
    for block in range(count // LANES):
        part = slice(block * LANES, (block + 1) * LANES)
        out[0, block : block + 1, :] = jnp.sum(total[part, :].T, axis=0, keepdims=True)
        out[1, block : block + 1, :] = jnp.sum(pos_total[part, :].T, axis=0, keepdims=True)


def whole(memory=pltpu.VMEM):
    return pl.BlockSpec(memory_space=memory)


def call(kernel, name, outs, place, *operands, scratch=(), **options):
    specs = [whole()] * len(operands)
    if place is not None:
        specs = [whole(pltpu.SMEM)] + specs
        operands = (place, *operands)
    return pl.pallas_call(
        functools.partial(kernel, **options),
        out_shape=tuple(outs),
        in_specs=specs,
        out_specs=tuple(whole() for _ in outs),
        scratch_shapes=list(scratch),
        compiler_params=pltpu.CompilerParams(vmem_limit_bytes=VMEM_LIMIT),
        cost_estimate=pl.CostEstimate(flops=1, bytes_accessed=1, transcendentals=0),
        name=name,
    )(*operands)


def swap(values, axis, flip):
    return lax.ppermute(values, axis, [(i, i ^ flip) for i in range(lax.axis_size(axis))])


def on_device(table, ages, refresh_ids, fresh_rows, neg_ids, queries, pos_ids):
    rows_dev, width = table.shape
    refresh_dev = refresh_ids.shape[0]
    planes = lax.axis_size("outer")
    owners_plane = lax.axis_size("inner")
    replicas = lax.axis_size("query")
    owners = planes * owners_plane
    query_count = queries.shape[0]
    list_size = neg_ids.shape[1]
    place = jnp.stack([lax.axis_index(name) for name in ("outer", "inner", "query")]).astype(jnp.int32)
    plane_rows = owners_plane * rows_dev
    plane_refresh = owners_plane * refresh_dev
    all_rows = plane_rows + plane_refresh
    cap = max(2, (2 * refresh_dev + owners - 1) // owners)
    share = cap // replicas
    table_half, fresh_half = rows_dev // replicas, refresh_dev // replicas
    bf16, f32 = jnp.bfloat16, jnp.float32

    fast = replicas == 2 and owners_plane == 4 and planes == 4
    own_ages = ages.reshape(1, -1)
    size = owners_plane * share
    rows_half, scales, *mail = call(
        prep_kernel,
        "prep",
        [
            jax.ShapeDtypeStruct((table_half + fresh_half + EXTRA, width), bf16),
            jax.ShapeDtypeStruct(((rows_dev + refresh_dev) // LANES, LANES), f32),
        ]
        + [jax.ShapeDtypeStruct((size + EXTRA, width), bf16)] * planes,
        place,
        table,
        fresh_rows,
        refresh_ids.reshape(1, -1),
        own_ages,
        neg_ids,
        pos_ids.reshape(1, -1),
        owners_plane=owners_plane,
        cap=cap,
        replicas=replicas,
        encode=fast,
    )
    mail = [mail[0]] + [swap(mail[s], "outer", s) for s in range(1, planes)]

    high_count = owners * rows_dev // LANES
    (maps,) = call(
        lists_kernel,
        "lists",
        [jax.ShapeDtypeStruct((planes, LANES, high_count), bf16)],
        None,
        *mail,
        first=size,
        list_size=list_size,
        high_count=high_count,
    )

    if fast:
        axes = ("inner", "query")
        first = [(2 * i + c, 2 * (i ^ (1 + c)) + c) for i in range(4) for c in range(2)]
        second = [(2 * i + c, 2 * (i ^ (2 - c)) + c) for i in range(4) for c in range(2)]
        near = lax.ppermute(rows_half, axes, first)
        side_rows = lax.ppermute(rows_half, axes, second)
        middle, outward = [(1, 2), (2, 1)], [(1, 0), (2, 3)]
        beside, across = swap(queries, "outer", 1), swap(queries, "outer", 3)
        beside, across, near, maps, *mail = lax.optimization_barrier((beside, across, near, maps, *mail))
        from_end = lax.ppermute(beside, "outer", middle)
        to_end = lax.ppermute(across, "outer", outward)
        far = lax.ppermute(near, axes, second)
        far, from_end, to_end = lax.optimization_barrier((far, from_end, to_end))
        got_queries = [(queries,), (beside,), (across,), (to_end, from_end)]
        flips = [0, 1, 3, 2]
        sides = [(i, table_half + fresh_half) for i in (2, 4, 6)]
        buffers = [table, fresh_rows]
        table_pieces = [(0, 0, rows_dev, (0, rows_dev, None, None), -1)]
        fresh_pieces = [(1, 0, refresh_dev, (0, refresh_dev, None, None), -1 - rows_dev // LANES)]
        for slot, by_core, mine in ((1, 0, near), (1, 1, side_rows), (3, None, far)):
            for flip, rows in enumerate((mine, swap(mine, "query", 1))):
                by = None if by_core is None else by_core ^ flip
                data = table_half + fresh_half
                fresh_at = data + 3 * (table_half // LANES)
                table_pieces.append((len(buffers), 0, table_half, (slot * rows_dev, table_half, flip, by), data))
                fresh_pieces.append(
                    (len(buffers), table_half, fresh_half, (slot * refresh_dev, fresh_half, flip, by), fresh_at)
                )
                buffers.append(rows)
    else:
        got_queries = [(queries,)] + [(swap(queries, "outer", s),) for s in range(1, planes)]
        flips = range(planes)
        got_rows = [rows_half] + [swap(rows_half, "inner", s) for s in range(1, owners_plane)]
        data = table_half + fresh_half
        gathered = lax.all_gather(jnp.stack(got_rows), "query", axis=0)
        gathered = jnp.swapaxes(gathered, 0, 1)
        buffers = [
            gathered[:, :, :table_half].reshape(plane_rows, width),
            gathered[:, :, table_half:data].reshape(plane_refresh, width),
            *[one[data:] for one in got_rows[1:]],
        ]
        sides = [(i + 1, 0) for i in range(1, owners_plane)]
        scales = []
        for rows in buffers[:2]:
            values = rows.astype(f32)
            mean = jnp.sum(values * values, axis=1) / width
            scales.append((lax.rsqrt(mean + epsilon) * (score_scale / width * LOG2E)).reshape(-1, LANES))
        scales = jnp.concatenate(scales)

        def blocks(buffer, count, line):
            starts = range(0, count, 512)
            return [(buffer, i, 512, (i, 512, None, None), -1 - line - i // LANES) for i in starts]

        table_pieces = blocks(0, plane_rows, 0)
        fresh_pieces = blocks(1, plane_refresh, plane_rows // LANES)

    def shift(pieces, columns):
        return [(a, b, c, (d[0] + columns, *d[1:]), e) for a, b, c, d, e in pieces]

    pieces = table_pieces + shift(fresh_pieces, plane_rows)
    relayed = call(
        relay_kernel,
        "relay",
        [jax.ShapeDtypeStruct((planes * share + EXTRA, width), bf16)] * owners_plane,
        None,
        *mail,
        planes=planes,
        owners_plane=owners_plane,
        share=share,
        list_size=list_size,
        count=query_count,
        refresh_dev=refresh_dev,
    )
    relayed = [relayed[0]] + [swap(relayed[s], "inner", s) for s in range(1, owners_plane)]
    lw, row_ids, scale_plane, positive, target, own, new_ages = call(
        meta_kernel,
        "meta",
        [
            jax.ShapeDtypeStruct((planes, all_rows), f32),
            jax.ShapeDtypeStruct((1, all_rows), f32),
            jax.ShapeDtypeStruct((1, all_rows), f32),
            jax.ShapeDtypeStruct((planes, query_count), f32),
            jax.ShapeDtypeStruct((1, owners * cap), jnp.int32),
            jax.ShapeDtypeStruct((1, rows_dev), jnp.int32),
            jax.ShapeDtypeStruct((1, rows_dev), jnp.int32),
        ],
        place,
        maps,
        own_ages,
        scales,
        *mail,
        *relayed,
        *buffers,
        sides=sides,
        pieces=pieces,
        planes=planes,
        owners_plane=owners_plane,
        rows_dev=rows_dev,
        refresh_dev=refresh_dev,
        list_size=list_size,
        count=query_count,
        cap=cap,
        replicas=replicas,
        fast=fast,
    )
    new_ages = new_ages.reshape(rows_dev)
    came = jnp.concatenate([one[: planes * share] for one in relayed])
    arrived = [came] + [swap(came, "query", flip) for flip in range(1, replicas)]

    def score(i, given):
        s = flips[i]
        (partial,) = call(
            score_kernel,
            "score",
            [jax.ShapeDtypeStruct((2, query_count // LANES, LANES), f32)],
            place,
            *given,
            positive,
            lw,
            row_ids,
            scale_plane,
            *buffers,
            scratch=[pltpu.VMEM((query_count, LANES), f32)] * 4 + [pltpu.VMEM(queries.shape, bf16)],
            pieces=pieces,
            flip=s,
            given=len(given),
        )
        return partial

    (new_table,) = call(
        apply_kernel, "apply", [jax.ShapeDtypeStruct(table.shape, bf16)], None, target, own, table, *arrived
    )
    partials = [swap(score(i, got_queries[i]), "outer", flips[i]) for i in range(1, planes - 1)]
    partials.append(score(0, got_queries[0]))
    new_table, *tied = lax.optimization_barrier((new_table, *partials, *got_queries[-1]))
    partials, last_queries = tied[: planes - 1], tied[planes - 1 :]
    mine = sum(partials[1:], partials[0])
    mine = mine + swap(score(planes - 1, last_queries), "outer", flips[-1])
    loss = (jnp.log2(mine[0]) - mine[1]) * math.log(2.0)
    return new_table, new_ages, loss.reshape(query_count)


def solution(mesh):
    owners, replicas = mesh.shape["index"], mesh.shape["query"]
    inner = 1 << (int(math.log2(owners)) // 2)
    split = Mesh(mesh.devices.reshape(owners // inner, inner, replicas), ("outer", "inner", "query"))
    index = ("outer", "inner")
    placed = (
        P(index, None),
        P(index),
        P(index),
        P(index, None),
        P(index, None),
        P(("outer", "inner", "query"), None),
        P(("outer", "inner", "query")),
    )
    return jax.shard_map(
        on_device,
        mesh=split,
        in_specs=placed,
        out_specs=(P(index, None), P(index), P(("outer", "inner", "query"))),
        check_vma=False,
    )
```

```python
import functools
import math

import jax
import jax.numpy as jnp
from jax import lax
from jax.experimental import pallas as pl
from jax.experimental.pallas import tpu as pltpu
from jax.sharding import Mesh, PartitionSpec as P

score_scale = 20.0
age_scale = 16.0
epsilon = 1e-06
LOG2E = math.log2(math.e)
MASKED = -1e30
VMEM_LIMIT = 48 * 1024 * 1024
EXTRA = 16
AGES_ROW = 9
LANES = 128

NT = (((1,), (1,)), ((), ()))
NN = (((1,), (0,)), ((), ()))


def one_hot(ids, count):
    rows = lax.broadcasted_iota(jnp.int32, (count, ids.shape[1]), 0)
    if count <= 256:
        ids = jnp.where((ids < 0) | (ids >= count), -1, ids)
        rows, ids = rows.astype(jnp.float32).astype(jnp.bfloat16), ids.astype(jnp.float32).astype(jnp.bfloat16)
        return jnp.where(rows == ids, jnp.bfloat16(1), jnp.bfloat16(0))
    return jnp.where(rows == ids, 1.0, 0.0).astype(jnp.bfloat16)


def split_terms(values):
    terms = []
    for _ in range(3):
        terms.append(values.astype(jnp.bfloat16))
        values = values - terms[-1].astype(jnp.float32)
    return terms


def counted(hits):
    count = hits.shape[1]
    before = lax.broadcasted_iota(jnp.int32, (count, count), 0)
    after = lax.broadcasted_iota(jnp.int32, (count, count), 1)
    earlier = jnp.where(before < after, 1.0, 0.0).astype(jnp.bfloat16)
    return lax.dot_general(hits.astype(jnp.bfloat16), earlier, NN, preferred_element_type=jnp.float32)


def small(values):
    return values.astype(jnp.float32).astype(jnp.bfloat16)


def number(values):
    return values.astype(jnp.float32).astype(jnp.int32)


def put(out, row, values):
    width = out.shape[1]
    for i, left in enumerate(range(0, values.shape[1], width)):
        part = small(values[:, left : left + width])
        out[row + i : row + i + 1, : part.shape[1]] = part


def take(rows, row, count):
    width = rows.shape[1]
    parts = [number(rows[row + i : row + i + 1, :]) for i in range(-(-count // width))]
    return jnp.concatenate(parts, axis=1)[:, :count]


def put_ids(out, row, ids):
    lines = -(-ids.shape[1] // out.shape[1])
    put(out, row, ids >> 7)
    put(out, row + lines, ids & 127)


def take_ids(rows, row, count):
    lines = -(-count // rows.shape[1])
    return take(rows, row, count) * LANES + take(rows, row + lines, count)


def prep_kernel(
    place, table, fresh, ref_ids, neg, pos, rows_out, scale_out, *mail, owners_plane, cap, replicas, encode
):
    outer, inner, core = place[0], place[1], place[2]
    width = table.shape[1]
    refresh_dev, rows_dev = fresh.shape[0], table.shape[0]
    planes, share = len(mail), cap // replicas
    pairs = [(plane, side) for plane in range(planes) for side in range(owners_plane)]
    ids = ref_ids[...]
    owner_of = ids // rows_dev
    rank = owner_ranks(
        [owner_of - ((outer ^ plane) * owners_plane + (inner ^ side)) for plane, side in pairs], refresh_dev, cap
    )
    rank = rank - core * share
    code = jnp.full((1, refresh_dev), -1, jnp.int32)
    for i in range(len(pairs)):
        here = (rank[i : i + 1, :] >= 0) & (rank[i : i + 1, :] < share)
        code = jnp.where(here, i * share + rank[i : i + 1, :], code)
    select = one_hot(code, len(pairs) * share)
    packed = lax.dot_general(select, fresh[...], NN, preferred_element_type=jnp.float32).astype(jnp.bfloat16)
    size = owners_plane * share
    for i, out in enumerate(mail):
        out[:size, :] = packed[i * size : (i + 1) * size, :]
        out[size:, :] = jnp.zeros((EXTRA, width), jnp.bfloat16)
        row = size
        for values in (neg[...], pos[...], ids):
            put_ids(out, row, values)
            row += 2 * -(-values.shape[1] // width)

    line, row = 0, 0
    halves = []
    for source in (table, fresh):
        rows = source.shape[0]
        half = rows // replicas
        rows_out[row : row + half, :] = source[pl.ds(pl.multiple_of(core * half, half), half), :]
        row += half
        for block in range(rows // LANES):
            squares = jnp.zeros((LANES, LANES), jnp.float32)
            for chunk in range(width // LANES):
                values = source[block * LANES : (block + 1) * LANES, chunk * LANES : (chunk + 1) * LANES]
                values = values.astype(jnp.float32)
                squares += values * values
            mean = jnp.sum(squares.T, axis=0, keepdims=True) / width
            scale_out[line + block : line + block + 1, :] = lax.rsqrt(mean + epsilon) * (score_scale / width * LOG2E)
        halves += [(line, i, half // LANES) for i in range(half // LANES)]
        line += rows // LANES
    rows_out[row:, :] = jnp.zeros((EXTRA, width), jnp.bfloat16)
    if encode:
        terms = []
        for first, i, count in halves:
            terms += split_terms(scale_out[pl.ds(first + core * count + i, 1), :])
        for i, term in enumerate(terms):
            rows_out[row + i : row + i + 1, :LANES] = term


def relay_kernel(ages, *refs, planes, owners_plane, share, list_size, count, refresh_dev):
    mail, outs = refs[:planes], refs[planes:]
    size = owners_plane * share
    width = mail[0].shape[1]
    row = size + 2 * (-(-list_size // width) + -(-count // width))
    ids = jnp.concatenate([take_ids(block, row, refresh_dev) for block in mail], axis=1)
    for side, out in enumerate(outs):
        for plane, block in enumerate(mail):
            out[plane * share : (plane + 1) * share, :] = block[side * share : (side + 1) * share, :]
        out[planes * share :, :] = jnp.zeros((EXTRA, width), jnp.bfloat16)
        put_ids(out, planes * share, ids)
        put(out, planes * share + AGES_ROW, ages[...])


def owner_ranks(rows, refresh_dev, cap):
    match = jnp.concatenate(rows, axis=0) == 0
    rank = counted(jnp.where(match, 1.0, 0.0)).astype(jnp.int32)
    return jnp.where(match, rank, -cap)


def one_hots(ids, high_count):
    return one_hot(ids >> 7, high_count), one_hot(ids & 127, LANES)


def bitmap(ids, high_count):
    high, low = one_hots(ids, high_count)
    return lax.dot_general(low, high, NT, preferred_element_type=jnp.float32).astype(jnp.bfloat16)


def lookup(one_map, pair):
    hit = lax.dot_general(one_map, pair[0], NN, preferred_element_type=jnp.float32)
    return jnp.sum(hit * pair[1].astype(jnp.float32), axis=0, keepdims=True)


def column_ids(place, owners_plane, rows_dev):
    column = lax.broadcasted_iota(jnp.int32, (1, owners_plane * rows_dev), 1)
    return (place[0] * owners_plane + (place[1] ^ (column // rows_dev))) * rows_dev + column % rows_dev


def lists_kernel(*refs, first, list_size, high_count):
    *mail, out = refs
    for group, block in enumerate(mail):
        out[group, :, :] = bitmap(take_ids(block, first, list_size), high_count)


def meta_kernel(
    place, maps, ages, *refs, planes, owners_plane, rows_dev, refresh_dev, list_size, count, cap, replicas
):
    outer, inner, core = place[0], place[1], place[2]
    lw_out, row_out, pos_out, target_out, own_out, ages_out = refs[-6:]
    mail, relayed = refs[:planes], refs[planes:-6]
    share = cap // replicas
    plane_rows = owners_plane * rows_dev
    high_count = planes * plane_rows // LANES
    own_owner = outer * owners_plane + inner

    ids = [take_ids(block, planes * share, planes * refresh_dev) for block in relayed]
    plane_ids = jnp.concatenate([one[:, :refresh_dev] for one in ids], axis=1)
    table_ids = column_ids(place, owners_plane, rows_dev)
    pair = one_hots(jnp.concatenate([table_ids, plane_ids], axis=1), high_count)
    refreshed = lookup(bitmap(jnp.concatenate(ids, axis=1), high_count), (pair[0][:, :plane_rows], pair[1][:, :plane_rows]))
    refreshed = refreshed > 0.5
    row_out[:, :plane_rows] = jnp.where(refreshed, -1, table_ids).astype(jnp.float32)
    row_out[:, plane_rows:] = plane_ids.astype(jnp.float32)
    own_out[...] = refreshed[:, :rows_dev].astype(jnp.int32)
    ages_out[...] = jnp.where(refreshed[:, :rows_dev], 0, ages[...])

    all_ages = [take(block, planes * share + AGES_ROW, rows_dev) for block in relayed]
    all_ages = jnp.concatenate(all_ages, axis=1).astype(jnp.float32)
    weight = jnp.exp(-all_ages / age_scale).astype(jnp.bfloat16).astype(jnp.float32)
    log_weight = jnp.where(refreshed, MASKED, jnp.log2(weight))
    log_weight = jnp.concatenate([log_weight, jnp.zeros((1, plane_ids.shape[1]), jnp.float32)], axis=1)
    for group, block in enumerate(mail):
        row = owners_plane * share
        hit = lookup(maps[group, :, :], pair)
        lw_out[group : group + 1, :] = jnp.where(hit > 0.5, log_weight, MASKED)
        row += 2 * -(-list_size // block.shape[1])
        pos_out[group : group + 1, :] = take_ids(block, row, count).astype(jnp.float32)

    pairs = [(side, plane) for side in range(owners_plane) for plane in range(planes)]
    part_ids = [ids[side][:, plane * refresh_dev : (plane + 1) * refresh_dev] for side, plane in pairs]
    rank = owner_ranks([one // rows_dev - own_owner for one in part_ids], refresh_dev, cap)
    for i in range(len(pairs)):
        took = rank[i : i + 1, :]
        slot = jnp.where(took < 0, -1, ((took // share) ^ core) * share + took % share)
        row = jnp.where(took < 0, 0, part_ids[i] - own_owner * rows_dev)
        kinds = lax.broadcasted_iota(jnp.int32, (8, refresh_dev), 0)
        digits = jnp.where(kinds == 0, row // 16, jnp.where(kinds == 1, row % 16, 1))
        found = lax.dot_general(small(digits), one_hot(slot, cap), NT, preferred_element_type=jnp.float32)
        found = found.astype(jnp.int32)
        target = jnp.where(found[2:3, :] > 0, found[0:1, :] * 16 + found[1:2, :], -1)
        for part in range(replicas):
            first = (part * len(pairs) + i) * share
            target_out[:, first : first + share] = target[:, part * share : (part + 1) * share]


def piece_offset(place, piece):
    column, size, flip, by_core = piece
    if flip is None:
        return column
    column += (place[2] ^ flip) * size
    if by_core is not None:
        column += (place[2] ^ by_core) * size * 2
    return pl.multiple_of(column, size)


def apply_kernel(target, refreshed, table, *refs):
    *arrived, out = refs
    values = jnp.concatenate([block[...] for block in arrived], axis=0)
    rows = lax.broadcasted_iota(jnp.int32, (out.shape[0], values.shape[0]), 0)
    chosen = jnp.where(rows == target[...], 1.0, 0.0).astype(jnp.bfloat16)
    fresh = lax.dot_general(chosen, values, NN, preferred_element_type=jnp.float32)
    for top in range(0, out.shape[0], LANES):
        part = slice(top, top + LANES)
        hit = to_lanes(refreshed[:, part].astype(jnp.float32)) > 0.5
        for left in range(0, out.shape[1], LANES):
            cols = slice(left, left + LANES)
            out[part, cols] = jnp.where(hit, fresh[part, cols], table[part, cols].astype(jnp.float32)).astype(jnp.bfloat16)


def to_lanes(row):
    return jnp.broadcast_to(row, (LANES, LANES)).T


def score_kernel(place, *refs, pieces, flip, given, follows):
    out, total, pos_total, q_scale, pos_b, chosen = refs[-6:]
    before, refs = (refs[0], refs[1:]) if follows else (None, refs)
    positives_row, log_weight, row_ids, scale = refs[given : given + 4]
    positive = positives_row[flip : flip + 1, :]
    queries = refs[0]
    count, width = queries.shape
    if given == 2:
        at_end = (place[0] == 0) | (place[0] == 3)
        chosen[...] = jnp.where(at_end, refs[0][...], refs[1][...])
        queries = chosen
    refs = refs[given + 4 : -6]
    for block in range(count // LANES):
        part = slice(block * LANES, (block + 1) * LANES)
        values = queries[part, :].astype(jnp.float32)
        squares = jnp.sum(values * values, axis=1, keepdims=True)
        q_scale[part, :] = jnp.broadcast_to(lax.rsqrt(squares / width + epsilon), (LANES, LANES))
        pos_b[part, :] = to_lanes(positive[:, part])
    total[...] = jnp.zeros_like(total)
    pos_total[...] = jnp.zeros_like(pos_total)

    def product(group):
        rows = [refs[source][start : start + size, :] for source, start, size, _, _ in group]
        rows = rows[0] if len(rows) == 1 else jnp.concatenate(rows, axis=0)
        return lax.dot_general(queries[...], rows, NT, preferred_element_type=jnp.float32)

    narrow = [piece for piece in pieces if piece[2] < 256]
    groups = [[piece] for piece in pieces if piece[2] >= 256] + [narrow[i : i + 2] for i in range(0, len(narrow), 2)]
    following = product(groups[0])
    for i, group in enumerate(groups):
        raw = following
        if i + 1 < len(groups):
            following = product(groups[i + 1])
        columns = []
        for source, _, size, column, scale_at in group:
            for chunk in range(size // LANES):
                if scale_at < 0:
                    line = -1 - scale_at + chunk
                    row_scale = scale[line : line + 1, :]
                else:
                    line = scale_at + 3 * chunk
                    row_scale = refs[source][line : line + 3, :LANES].astype(jnp.float32)
                    row_scale = jnp.sum(row_scale, axis=0, keepdims=True)
                columns.append((piece_offset(place, column) + chunk * LANES, row_scale))
        for top in range(0, count, 64):
            part = slice(top, top + 64)
            sums, positives = total[part, :], pos_total[part, :]
            query_scale, wanted = q_scale[part, :], pos_b[part, :]
            for chunk, (first, row_scale) in enumerate(columns):
                cols = pl.ds(first, LANES)
                powers = raw[part, chunk * LANES : (chunk + 1) * LANES] * query_scale
                powers = powers * row_scale + log_weight[flip : flip + 1, cols]
                sums = sums + jnp.exp2(powers)
                positives = positives + jnp.where(wanted == row_ids[:, cols], powers, 0.0)
            total[part, :] = sums
            pos_total[part, :] = positives
    for block in range(count // LANES):
        part = slice(block * LANES, (block + 1) * LANES)
        for i, sums in enumerate((total, pos_total)):
            row = jnp.sum(sums[part, :].T, axis=0, keepdims=True)
            out[i, block : block + 1, :] = row + before[i, block : block + 1, :] if follows else row


def whole(memory=pltpu.VMEM):
    return pl.BlockSpec(memory_space=memory)


def call(kernel, name, outs, place, *operands, scratch=(), **options):
    specs = [whole()] * len(operands)
    if place is not None:
        specs = [whole(pltpu.SMEM)] + specs
        operands = (place, *operands)
    return pl.pallas_call(
        functools.partial(kernel, **options),
        out_shape=tuple(outs),
        in_specs=specs,
        out_specs=tuple(whole() for _ in outs),
        scratch_shapes=list(scratch),
        compiler_params=pltpu.CompilerParams(vmem_limit_bytes=VMEM_LIMIT),
        cost_estimate=pl.CostEstimate(flops=1, bytes_accessed=1, transcendentals=0),
        name=name,
    )(*operands)


def swap(values, axis, flip):
    return lax.ppermute(values, axis, [(i, i ^ flip) for i in range(lax.axis_size(axis))])


def on_device(table, ages, refresh_ids, fresh_rows, neg_ids, queries, pos_ids):
    rows_dev, width = table.shape
    refresh_dev = refresh_ids.shape[0]
    planes = lax.axis_size("outer")
    owners_plane = lax.axis_size("inner")
    replicas = lax.axis_size("query")
    owners = planes * owners_plane
    query_count = queries.shape[0]
    list_size = neg_ids.shape[1]
    place = jnp.stack([lax.axis_index(name) for name in ("outer", "inner", "query")]).astype(jnp.int32)
    plane_rows = owners_plane * rows_dev
    plane_refresh = owners_plane * refresh_dev
    all_rows = plane_rows + plane_refresh
    cap = max(2, (2 * refresh_dev + owners - 1) // owners)
    share = cap // replicas
    table_half, fresh_half = rows_dev // replicas, refresh_dev // replicas
    bf16, f32 = jnp.bfloat16, jnp.float32

    fast = replicas == 2 and owners_plane == 4 and planes == 4
    own_ages = ages.reshape(1, -1)
    size = owners_plane * share
    rows_half, scales, *mail = call(
        prep_kernel,
        "prep",
        [
            jax.ShapeDtypeStruct((table_half + fresh_half + EXTRA, width), bf16),
            jax.ShapeDtypeStruct(((rows_dev + refresh_dev) // LANES, LANES), f32),
        ]
        + [jax.ShapeDtypeStruct((size + EXTRA, width), bf16)] * planes,
        place,
        table,
        fresh_rows,
        refresh_ids.reshape(1, -1),
        neg_ids,
        pos_ids.reshape(1, -1),
        owners_plane=owners_plane,
        cap=cap,
        replicas=replicas,
        encode=fast,
    )
    mail = [mail[0]] + [swap(mail[s], "outer", s) for s in range(1, planes)]
    bare = queries
    queries, *mail = lax.optimization_barrier((queries, *mail))

    high_count = owners * rows_dev // LANES
    (maps,) = call(
        lists_kernel,
        "lists",
        [jax.ShapeDtypeStruct((planes, LANES, high_count), bf16)],
        None,
        *mail,
        first=size,
        list_size=list_size,
        high_count=high_count,
    )

    relayed = call(
        relay_kernel,
        "relay",
        [jax.ShapeDtypeStruct((planes * share + EXTRA, width), bf16)] * owners_plane,
        None,
        own_ages,
        *mail,
        planes=planes,
        owners_plane=owners_plane,
        share=share,
        list_size=list_size,
        count=query_count,
        refresh_dev=refresh_dev,
    )
    relayed = [relayed[0]] + [swap(relayed[s], "inner", s) for s in range(1, owners_plane)]
    lw, row_ids, positive, target, own, new_ages = call(
        meta_kernel,
        "meta",
        [
            jax.ShapeDtypeStruct((planes, all_rows), f32),
            jax.ShapeDtypeStruct((1, all_rows), f32),
            jax.ShapeDtypeStruct((planes, query_count), f32),
            jax.ShapeDtypeStruct((1, owners * cap), jnp.int32),
            jax.ShapeDtypeStruct((1, rows_dev), jnp.int32),
            jax.ShapeDtypeStruct((1, rows_dev), jnp.int32),
        ],
        place,
        maps,
        own_ages,
        *mail,
        *relayed,
        planes=planes,
        owners_plane=owners_plane,
        rows_dev=rows_dev,
        refresh_dev=refresh_dev,
        list_size=list_size,
        count=query_count,
        cap=cap,
        replicas=replicas,
    )

    def shift(pieces, columns):
        return [(a, b, c, (d[0] + columns, *d[1:]), e) for a, b, c, d, e in pieces]

    def score(i, given, buffers, pieces, before=()):
        (partial,) = call(
            score_kernel,
            "score",
            [jax.ShapeDtypeStruct((2, query_count // LANES, LANES), f32)],
            place,
            *before,
            *given,
            positive,
            lw,
            row_ids,
            scales,
            *buffers,
            scratch=[pltpu.VMEM((query_count, LANES), f32)] * 4 + [pltpu.VMEM(queries.shape, bf16)],
            pieces=pieces,
            flip=flips[i],
            given=len(given),
            follows=len(before),
        )
        return partial

    if fast:
        axes = ("inner", "query")
        first = [(2 * i + c, 2 * (i ^ (1 + c)) + c) for i in range(4) for c in range(2)]
        second = [(2 * i + c, 2 * (i ^ (2 - c)) + c) for i in range(4) for c in range(2)]
        near = lax.ppermute(rows_half, axes, first)
        behind, *_ = lax.optimization_barrier((rows_half, *relayed))
        side_rows = lax.ppermute(behind, axes, second)
        middle, outward = [(1, 2), (2, 1)], [(1, 0), (2, 3)]
        beside, across = swap(queries, "outer", 1), swap(queries, "outer", 3)
        near, beside, across, lw = lax.optimization_barrier((near, beside, across, lw))
        from_end = lax.ppermute(beside, "outer", middle)
        to_end = lax.ppermute(across, "outer", outward)
        far = lax.ppermute(near, axes, second)
        got_queries = [(bare,), (beside,), (across,)]
        flips = [0, 1, 3, 2]
        buffers = [table, fresh_rows]
        table_pieces = [(0, 0, rows_dev, (0, rows_dev, None, None), -1)]
        fresh_pieces = [(1, 0, refresh_dev, (0, refresh_dev, None, None), -1 - rows_dev // LANES)]

        def add_pieces(slot, by_core, mine):
            data = table_half + fresh_half
            fresh_at = data + 3 * (table_half // LANES)
            for flip, rows in enumerate((mine, swap(mine, "query", 1))):
                by = None if by_core is None else by_core ^ flip
                table_pieces.append((len(buffers), 0, table_half, (slot * rows_dev, table_half, flip, by), data))
                fresh_pieces.append(
                    (len(buffers), table_half, fresh_half, (slot * refresh_dev, fresh_half, flip, by), fresh_at)
                )
                buffers.append(rows)

        add_pieces(1, 0, near)
        add_pieces(1, 1, side_rows)
        early = table_pieces + shift(fresh_pieces, plane_rows)
        partials = [score(i, got_queries[i], list(buffers), early) for i in range(planes - 1)]
        far, from_end, to_end, *partials = lax.optimization_barrier((far, from_end, to_end, *partials))
        got_queries.append((to_end, from_end))
        add_pieces(3, None, far)
        pieces = table_pieces + shift(fresh_pieces, plane_rows)
        late = [piece for piece in pieces if piece not in early]
        partials = [score(i, got_queries[i], buffers, late, [partials[i]]) for i in range(planes - 1)]
    else:
        got_queries = [(queries,)] + [(swap(queries, "outer", s),) for s in range(1, planes)]
        flips = range(planes)
        got_rows = [rows_half] + [swap(rows_half, "inner", s) for s in range(1, owners_plane)]
        data = table_half + fresh_half
        gathered = lax.all_gather(jnp.stack(got_rows), "query", axis=0)
        gathered = jnp.swapaxes(gathered, 0, 1)
        buffers = [
            gathered[:, :, :table_half].reshape(plane_rows, width),
            gathered[:, :, table_half:data].reshape(plane_refresh, width),
        ]
        scales = []
        for rows in buffers:
            values = rows.astype(f32)
            mean = jnp.sum(values * values, axis=1) / width
            scales.append((lax.rsqrt(mean + epsilon) * (score_scale / width * LOG2E)).reshape(-1, LANES))
        scales = jnp.concatenate(scales)

        def blocks(buffer, count, line):
            starts = range(0, count, 512)
            return [(buffer, i, 512, (i, 512, None, None), -1 - line - i // LANES) for i in starts]

        table_pieces = blocks(0, plane_rows, 0)
        fresh_pieces = blocks(1, plane_refresh, plane_rows // LANES)
        pieces = table_pieces + shift(fresh_pieces, plane_rows)
        partials = [score(i, got_queries[i], buffers, pieces) for i in range(planes - 1)]

    pieces = table_pieces + shift(fresh_pieces, plane_rows)
    new_ages = new_ages.reshape(rows_dev)
    came = jnp.concatenate([one[: planes * share] for one in relayed])
    arrived = [came] + [swap(came, "query", flip) for flip in range(1, replicas)]

    (new_table,) = call(
        apply_kernel, "apply", [jax.ShapeDtypeStruct(table.shape, bf16)], None, target, own, table, *arrived
    )
    partials = [partials[0]] + [swap(partials[i], "outer", flips[i]) for i in range(1, planes - 1)]
    new_table, *tied = lax.optimization_barrier((new_table, *partials, *got_queries[-1]))
    partials, last_queries = tied[: planes - 1], tied[planes - 1 :]
    mine = sum(partials[1:], partials[0])
    mine = mine + swap(score(planes - 1, last_queries, buffers, pieces), "outer", flips[-1])
    loss = (jnp.log2(mine[0]) - mine[1]) * math.log(2.0)
    return new_table, new_ages, loss.reshape(query_count)


def solution(mesh):
    owners, replicas = mesh.shape["index"], mesh.shape["query"]
    inner = 1 << (int(math.log2(owners)) // 2)
    split = Mesh(mesh.devices.reshape(owners // inner, inner, replicas), ("outer", "inner", "query"))
    index = ("outer", "inner")
    placed = (
        P(index, None),
        P(index),
        P(index),
        P(index, None),
        P(index, None),
        P(("outer", "inner", "query"), None),
        P(("outer", "inner", "query")),
    )
    return jax.shard_map(
        on_device,
        mesh=split,
        in_specs=placed,
        out_specs=(P(index, None), P(index), P(("outer", "inner", "query"))),
        check_vma=False,
    )
```

```python
import functools
import math

import jax
import jax.numpy as jnp
from jax import lax
from jax.experimental import pallas as pl
from jax.experimental.pallas import tpu as pltpu
from jax.sharding import Mesh, PartitionSpec as P

score_scale = 20.0
age_scale = 16.0
epsilon = 1e-06
LOG2E = math.log2(math.e)
MASKED = -1e30
VMEM_LIMIT = 48 * 1024 * 1024
EXTRA = 16
AGES_ROW = 9
LANES = 128

NT = (((1,), (1,)), ((), ()))
NN = (((1,), (0,)), ((), ()))


def one_hot(ids, count):
    rows = lax.broadcasted_iota(jnp.int32, (count, ids.shape[1]), 0)
    if count <= 256:
        ids = jnp.where((ids < 0) | (ids >= count), -1, ids)
        rows, ids = rows.astype(jnp.float32).astype(jnp.bfloat16), ids.astype(jnp.float32).astype(jnp.bfloat16)
        return jnp.where(rows == ids, jnp.bfloat16(1), jnp.bfloat16(0))
    return jnp.where(rows == ids, 1.0, 0.0).astype(jnp.bfloat16)


def split_terms(values):
    terms = []
    for _ in range(3):
        terms.append(values.astype(jnp.bfloat16))
        values = values - terms[-1].astype(jnp.float32)
    return terms


def counted(hits):
    count = hits.shape[1]
    before = lax.broadcasted_iota(jnp.int32, (count, count), 0)
    after = lax.broadcasted_iota(jnp.int32, (count, count), 1)
    earlier = jnp.where(before < after, 1.0, 0.0).astype(jnp.bfloat16)
    return lax.dot_general(hits.astype(jnp.bfloat16), earlier, NN, preferred_element_type=jnp.float32)


def small(values):
    return values.astype(jnp.float32).astype(jnp.bfloat16)


def number(values):
    return values.astype(jnp.float32).astype(jnp.int32)


def put(out, row, values):
    width = out.shape[1]
    for i, left in enumerate(range(0, values.shape[1], width)):
        part = small(values[:, left : left + width])
        out[row + i : row + i + 1, : part.shape[1]] = part


def take(rows, row, count):
    width = rows.shape[1]
    parts = [number(rows[row + i : row + i + 1, :]) for i in range(-(-count // width))]
    return jnp.concatenate(parts, axis=1)[:, :count]


def put_ids(out, row, ids):
    lines = -(-ids.shape[1] // out.shape[1])
    put(out, row, ids >> 7)
    put(out, row + lines, ids & 127)


def take_ids(rows, row, count):
    lines = -(-count // rows.shape[1])
    return take(rows, row, count) * LANES + take(rows, row + lines, count)


def prep_kernel(
    place, table, fresh, ref_ids, neg, pos, rows_out, scale_out, *mail, owners_plane, cap, replicas, encode
):
    outer, inner, core = place[0], place[1], place[2]
    width = table.shape[1]
    refresh_dev, rows_dev = fresh.shape[0], table.shape[0]
    planes, share = len(mail), cap // replicas
    pairs = [(plane, side) for plane in range(planes) for side in range(owners_plane)]
    ids = ref_ids[...]
    owner_of = ids // rows_dev
    rank = owner_ranks(
        [owner_of - ((outer ^ plane) * owners_plane + (inner ^ side)) for plane, side in pairs], refresh_dev, cap
    )
    rank = rank - core * share
    code = jnp.full((1, refresh_dev), -1, jnp.int32)
    for i in range(len(pairs)):
        here = (rank[i : i + 1, :] >= 0) & (rank[i : i + 1, :] < share)
        code = jnp.where(here, i * share + rank[i : i + 1, :], code)
    select = one_hot(code, len(pairs) * share)
    packed = lax.dot_general(select, fresh[...], NN, preferred_element_type=jnp.float32).astype(jnp.bfloat16)
    size = owners_plane * share
    for i, out in enumerate(mail):
        out[:size, :] = packed[i * size : (i + 1) * size, :]
        out[size:, :] = jnp.zeros((EXTRA, width), jnp.bfloat16)
        row = size
        for values in (neg[...], pos[...], ids):
            put_ids(out, row, values)
            row += 2 * -(-values.shape[1] // width)

    line, row = 0, 0
    halves = []
    for source in (table, fresh):
        rows = source.shape[0]
        half = rows // replicas
        rows_out[row : row + half, :] = source[pl.ds(pl.multiple_of(core * half, half), half), :]
        row += half
        for block in range(rows // LANES):
            squares = jnp.zeros((LANES, LANES), jnp.float32)
            for chunk in range(width // LANES):
                values = source[block * LANES : (block + 1) * LANES, chunk * LANES : (chunk + 1) * LANES]
                values = values.astype(jnp.float32)
                squares += values * values
            mean = jnp.sum(squares.T, axis=0, keepdims=True) / width
            scale_out[line + block : line + block + 1, :] = lax.rsqrt(mean + epsilon) * (score_scale / width * LOG2E)
        halves += [(line, i, half // LANES) for i in range(half // LANES)]
        line += rows // LANES
    rows_out[row:, :] = jnp.zeros((EXTRA, width), jnp.bfloat16)
    if encode:
        terms = []
        for first, i, count in halves:
            terms += split_terms(scale_out[pl.ds(first + core * count + i, 1), :])
        for i, term in enumerate(terms):
            rows_out[row + i : row + i + 1, :LANES] = term


def relay_kernel(ages, *refs, planes, owners_plane, share, list_size, count, refresh_dev):
    mail, outs = refs[:planes], refs[planes:]
    size = owners_plane * share
    width = mail[0].shape[1]
    row = size + 2 * (-(-list_size // width) + -(-count // width))
    ids = jnp.concatenate([take_ids(block, row, refresh_dev) for block in mail], axis=1)
    for side, out in enumerate(outs):
        for plane, block in enumerate(mail):
            out[plane * share : (plane + 1) * share, :] = block[side * share : (side + 1) * share, :]
        out[planes * share :, :] = jnp.zeros((EXTRA, width), jnp.bfloat16)
        put_ids(out, planes * share, ids)
        put(out, planes * share + AGES_ROW, ages[...])


def owner_ranks(rows, refresh_dev, cap):
    match = jnp.concatenate(rows, axis=0) == 0
    rank = counted(jnp.where(match, 1.0, 0.0)).astype(jnp.int32)
    return jnp.where(match, rank, -cap)


def one_hots(ids, high_count):
    return one_hot(ids >> 7, high_count), one_hot(ids & 127, LANES)


def bitmap(ids, high_count):
    high, low = one_hots(ids, high_count)
    return lax.dot_general(low, high, NT, preferred_element_type=jnp.float32).astype(jnp.bfloat16)


def lookup(one_map, pair):
    hit = lax.dot_general(one_map, pair[0], NN, preferred_element_type=jnp.float32)
    return jnp.sum(hit * pair[1].astype(jnp.float32), axis=0, keepdims=True)


def column_ids(place, owners_plane, rows_dev):
    column = lax.broadcasted_iota(jnp.int32, (1, owners_plane * rows_dev), 1)
    return (place[0] * owners_plane + (place[1] ^ (column // rows_dev))) * rows_dev + column % rows_dev


def lists_kernel(*refs, first, list_size, high_count):
    *mail, out = refs
    for group, block in enumerate(mail):
        out[group, :, :] = bitmap(take_ids(block, first, list_size), high_count)


def meta_kernel(
    place, maps, ages, *refs, planes, owners_plane, rows_dev, refresh_dev, list_size, count, cap, replicas
):
    outer, inner, core = place[0], place[1], place[2]
    lw_out, row_out, pos_out, target_out, own_out, ages_out = refs[-6:]
    mail, relayed = refs[:planes], refs[planes:-6]
    share = cap // replicas
    plane_rows = owners_plane * rows_dev
    high_count = planes * plane_rows // LANES
    own_owner = outer * owners_plane + inner

    ids = [take_ids(block, planes * share, planes * refresh_dev) for block in relayed]
    plane_ids = jnp.concatenate([one[:, :refresh_dev] for one in ids], axis=1)
    table_ids = column_ids(place, owners_plane, rows_dev)
    pair = one_hots(jnp.concatenate([table_ids, plane_ids], axis=1), high_count)
    refreshed = lookup(bitmap(jnp.concatenate(ids, axis=1), high_count), (pair[0][:, :plane_rows], pair[1][:, :plane_rows]))
    refreshed = refreshed > 0.5
    row_out[:, :plane_rows] = jnp.where(refreshed, -1, table_ids).astype(jnp.float32)
    row_out[:, plane_rows:] = plane_ids.astype(jnp.float32)
    own_out[...] = refreshed[:, :rows_dev].astype(jnp.int32)
    ages_out[...] = jnp.where(refreshed[:, :rows_dev], 0, ages[...])

    all_ages = [take(block, planes * share + AGES_ROW, rows_dev) for block in relayed]
    all_ages = jnp.concatenate(all_ages, axis=1).astype(jnp.float32)
    weight = jnp.exp(-all_ages / age_scale).astype(jnp.bfloat16).astype(jnp.float32)
    log_weight = jnp.where(refreshed, MASKED, jnp.log2(weight))
    log_weight = jnp.concatenate([log_weight, jnp.zeros((1, plane_ids.shape[1]), jnp.float32)], axis=1)
    for group, block in enumerate(mail):
        row = owners_plane * share
        hit = lookup(maps[group, :, :], pair)
        lw_out[group : group + 1, :] = jnp.where(hit > 0.5, log_weight, MASKED)
        row += 2 * -(-list_size // block.shape[1])
        pos_out[group : group + 1, :] = take_ids(block, row, count).astype(jnp.float32)

    pairs = [(side, plane) for side in range(owners_plane) for plane in range(planes)]
    part_ids = [ids[side][:, plane * refresh_dev : (plane + 1) * refresh_dev] for side, plane in pairs]
    rank = owner_ranks([one // rows_dev - own_owner for one in part_ids], refresh_dev, cap)
    for i in range(len(pairs)):
        took = rank[i : i + 1, :]
        slot = jnp.where(took < 0, -1, ((took // share) ^ core) * share + took % share)
        row = jnp.where(took < 0, 0, part_ids[i] - own_owner * rows_dev)
        kinds = lax.broadcasted_iota(jnp.int32, (8, refresh_dev), 0)
        digits = jnp.where(kinds == 0, row // 16, jnp.where(kinds == 1, row % 16, 1))
        found = lax.dot_general(small(digits), one_hot(slot, cap), NT, preferred_element_type=jnp.float32)
        found = found.astype(jnp.int32)
        target = jnp.where(found[2:3, :] > 0, found[0:1, :] * 16 + found[1:2, :], -1)
        for part in range(replicas):
            first = (part * len(pairs) + i) * share
            target_out[:, first : first + share] = target[:, part * share : (part + 1) * share]


def piece_offset(place, piece):
    column, size, flip, by_core = piece
    if flip is None:
        return column
    column += (place[2] ^ flip) * size
    if by_core is not None:
        column += (place[2] ^ by_core) * size * 2
    return pl.multiple_of(column, size)


def apply_kernel(target, refreshed, table, *refs):
    *arrived, out = refs
    values = jnp.concatenate([block[...] for block in arrived], axis=0)
    rows = lax.broadcasted_iota(jnp.int32, (out.shape[0], values.shape[0]), 0)
    chosen = jnp.where(rows == target[...], 1.0, 0.0).astype(jnp.bfloat16)
    fresh = lax.dot_general(chosen, values, NN, preferred_element_type=jnp.float32)
    for top in range(0, out.shape[0], LANES):
        part = slice(top, top + LANES)
        hit = to_lanes(refreshed[:, part].astype(jnp.float32)) > 0.5
        for left in range(0, out.shape[1], LANES):
            cols = slice(left, left + LANES)
            out[part, cols] = jnp.where(hit, fresh[part, cols], table[part, cols].astype(jnp.float32)).astype(jnp.bfloat16)


def to_lanes(row):
    return jnp.broadcast_to(row, (LANES, LANES)).T


def score_kernel(place, *refs, pieces, flip, given, follows):
    out, total, pos_total, q_scale, pos_b, chosen = refs[-6:]
    before, refs = (refs[0], refs[1:]) if follows else (None, refs)
    positives_row, log_weight, row_ids, scale = refs[given : given + 4]
    positive = positives_row[flip : flip + 1, :]
    queries = refs[0]
    count, width = queries.shape
    if given == 2:
        at_end = (place[0] == 0) | (place[0] == 3)
        chosen[...] = jnp.where(at_end, refs[0][...], refs[1][...])
        queries = chosen
    refs = refs[given + 4 : -6]
    for block in range(count // LANES):
        part = slice(block * LANES, (block + 1) * LANES)
        values = queries[part, :].astype(jnp.float32)
        squares = jnp.sum(values * values, axis=1, keepdims=True)
        q_scale[part, :] = jnp.broadcast_to(lax.rsqrt(squares / width + epsilon), (LANES, LANES))
        pos_b[part, :] = to_lanes(positive[:, part])
    total[...] = jnp.zeros_like(total)
    pos_total[...] = jnp.zeros_like(pos_total)

    def product(group):
        rows = [refs[source][start : start + size, :] for source, start, size, _, _ in group]
        rows = rows[0] if len(rows) == 1 else jnp.concatenate(rows, axis=0)
        return lax.dot_general(queries[...], rows, NT, preferred_element_type=jnp.float32)

    narrow = [piece for piece in pieces if piece[2] < 256]
    groups = [[piece] for piece in pieces if piece[2] >= 256] + [narrow[i : i + 2] for i in range(0, len(narrow), 2)]
    following = product(groups[0])
    for i, group in enumerate(groups):
        raw = following
        if i + 1 < len(groups):
            following = product(groups[i + 1])
        columns = []
        for source, _, size, column, scale_at in group:
            for chunk in range(size // LANES):
                if scale_at < 0:
                    line = -1 - scale_at + chunk
                    row_scale = scale[line : line + 1, :]
                else:
                    line = scale_at + 3 * chunk
                    row_scale = refs[source][line : line + 3, :LANES].astype(jnp.float32)
                    row_scale = jnp.sum(row_scale, axis=0, keepdims=True)
                columns.append((piece_offset(place, column) + chunk * LANES, row_scale))
        for top in range(0, count, 64):
            part = slice(top, top + 64)
            sums, positives = total[part, :], pos_total[part, :]
            query_scale, wanted = q_scale[part, :], pos_b[part, :]
            for chunk, (first, row_scale) in enumerate(columns):
                cols = pl.ds(first, LANES)
                powers = raw[part, chunk * LANES : (chunk + 1) * LANES] * query_scale
                powers = powers * row_scale + log_weight[flip : flip + 1, cols]
                sums = sums + jnp.exp2(powers)
                positives = positives + jnp.where(wanted == row_ids[:, cols], powers, 0.0)
            total[part, :] = sums
            pos_total[part, :] = positives
    for block in range(count // LANES):
        part = slice(block * LANES, (block + 1) * LANES)
        for i, sums in enumerate((total, pos_total)):
            row = jnp.sum(sums[part, :].T, axis=0, keepdims=True)
            out[i, block : block + 1, :] = row + before[i, block : block + 1, :] if follows else row


def whole(memory=pltpu.VMEM):
    return pl.BlockSpec(memory_space=memory)


def call(kernel, name, outs, place, *operands, scratch=(), **options):
    specs = [whole()] * len(operands)
    if place is not None:
        specs = [whole(pltpu.SMEM)] + specs
        operands = (place, *operands)
    return pl.pallas_call(
        functools.partial(kernel, **options),
        out_shape=tuple(outs),
        in_specs=specs,
        out_specs=tuple(whole() for _ in outs),
        scratch_shapes=list(scratch),
        compiler_params=pltpu.CompilerParams(vmem_limit_bytes=VMEM_LIMIT),
        cost_estimate=pl.CostEstimate(flops=1, bytes_accessed=1, transcendentals=0),
        name=name,
    )(*operands)


def swap(values, axis, flip):
    return lax.ppermute(values, axis, [(i, i ^ flip) for i in range(lax.axis_size(axis))])


def on_device(table, ages, refresh_ids, fresh_rows, neg_ids, queries, pos_ids):
    rows_dev, width = table.shape
    refresh_dev = refresh_ids.shape[0]
    planes = lax.axis_size("outer")
    owners_plane = lax.axis_size("inner")
    replicas = lax.axis_size("query")
    owners = planes * owners_plane
    query_count = queries.shape[0]
    list_size = neg_ids.shape[1]
    place = jnp.stack([lax.axis_index(name) for name in ("outer", "inner", "query")]).astype(jnp.int32)
    plane_rows = owners_plane * rows_dev
    plane_refresh = owners_plane * refresh_dev
    all_rows = plane_rows + plane_refresh
    cap = max(2, (2 * refresh_dev + owners - 1) // owners)
    share = cap // replicas
    table_half, fresh_half = rows_dev // replicas, refresh_dev // replicas
    bf16, f32 = jnp.bfloat16, jnp.float32

    fast = replicas == 2 and owners_plane == 4 and planes == 4
    own_ages = ages.reshape(1, -1)
    size = owners_plane * share
    rows_half, scales, *mail = call(
        prep_kernel,
        "prep",
        [
            jax.ShapeDtypeStruct((table_half + fresh_half + EXTRA, width), bf16),
            jax.ShapeDtypeStruct(((rows_dev + refresh_dev) // LANES, LANES), f32),
        ]
        + [jax.ShapeDtypeStruct((size + EXTRA, width), bf16)] * planes,
        place,
        table,
        fresh_rows,
        refresh_ids.reshape(1, -1),
        neg_ids,
        pos_ids.reshape(1, -1),
        owners_plane=owners_plane,
        cap=cap,
        replicas=replicas,
        encode=fast,
    )
    mail = [mail[0]] + [swap(mail[s], "outer", s) for s in range(1, planes)]
    bare = queries
    queries, mail[1] = lax.optimization_barrier((queries, mail[1]))

    high_count = owners * rows_dev // LANES
    (maps,) = call(
        lists_kernel,
        "lists",
        [jax.ShapeDtypeStruct((planes, LANES, high_count), bf16)],
        None,
        *mail,
        first=size,
        list_size=list_size,
        high_count=high_count,
    )

    relayed = call(
        relay_kernel,
        "relay",
        [jax.ShapeDtypeStruct((planes * share + EXTRA, width), bf16)] * owners_plane,
        None,
        own_ages,
        *mail,
        planes=planes,
        owners_plane=owners_plane,
        share=share,
        list_size=list_size,
        count=query_count,
        refresh_dev=refresh_dev,
    )
    relayed = [relayed[0]] + [swap(relayed[s], "inner", s) for s in range(1, owners_plane)]
    lw, row_ids, positive, target, own, new_ages = call(
        meta_kernel,
        "meta",
        [
            jax.ShapeDtypeStruct((planes, all_rows), f32),
            jax.ShapeDtypeStruct((1, all_rows), f32),
            jax.ShapeDtypeStruct((planes, query_count), f32),
            jax.ShapeDtypeStruct((1, owners * cap), jnp.int32),
            jax.ShapeDtypeStruct((1, rows_dev), jnp.int32),
            jax.ShapeDtypeStruct((1, rows_dev), jnp.int32),
        ],
        place,
        maps,
        own_ages,
        *mail,
        *relayed,
        planes=planes,
        owners_plane=owners_plane,
        rows_dev=rows_dev,
        refresh_dev=refresh_dev,
        list_size=list_size,
        count=query_count,
        cap=cap,
        replicas=replicas,
    )

    new_ages = new_ages.reshape(rows_dev)
    came = jnp.concatenate([one[: planes * share] for one in relayed])
    arrived = [came] + [swap(came, "query", flip) for flip in range(1, replicas)]
    (new_table,) = call(
        apply_kernel, "apply", [jax.ShapeDtypeStruct(table.shape, bf16)], None, target, own, table, *arrived
    )

    def shift(pieces, columns):
        return [(a, b, c, (d[0] + columns, *d[1:]), e) for a, b, c, d, e in pieces]

    def score(i, given, buffers, pieces, before=()):
        (partial,) = call(
            score_kernel,
            "score",
            [jax.ShapeDtypeStruct((2, query_count // LANES, LANES), f32)],
            place,
            *before,
            *given,
            positive,
            lw,
            row_ids,
            scales,
            *buffers,
            scratch=[pltpu.VMEM((query_count, LANES), f32)] * 4 + [pltpu.VMEM(queries.shape, bf16)],
            pieces=pieces,
            flip=flips[i],
            given=len(given),
            follows=len(before),
        )
        return partial

    if fast:
        axes = ("inner", "query")
        first = [(2 * i + c, 2 * (i ^ (1 + c)) + c) for i in range(4) for c in range(2)]
        second = [(2 * i + c, 2 * (i ^ (2 - c)) + c) for i in range(4) for c in range(2)]
        near = lax.ppermute(rows_half, axes, first)
        side_rows = lax.ppermute(rows_half, axes, second)
        middle, outward = [(1, 2), (2, 1)], [(1, 0), (2, 3)]
        beside, across = swap(queries, "outer", 1), swap(queries, "outer", 3)
        near, beside, across, lw = lax.optimization_barrier((near, beside, across, lw))
        from_end = lax.ppermute(beside, "outer", middle)
        to_end = lax.ppermute(across, "outer", outward)
        far = lax.ppermute(near, axes, second)
        got_queries = [(bare,), (beside,), (across,)]
        flips = [0, 1, 3, 2]
        buffers = [table, fresh_rows]
        table_pieces = [(0, 0, rows_dev, (0, rows_dev, None, None), -1)]
        fresh_pieces = [(1, 0, refresh_dev, (0, refresh_dev, None, None), -1 - rows_dev // LANES)]

        def add_pieces(slot, by_core, mine):
            data = table_half + fresh_half
            fresh_at = data + 3 * (table_half // LANES)
            for flip, rows in enumerate((mine, swap(mine, "query", 1))):
                by = None if by_core is None else by_core ^ flip
                table_pieces.append((len(buffers), 0, table_half, (slot * rows_dev, table_half, flip, by), data))
                fresh_pieces.append(
                    (len(buffers), table_half, fresh_half, (slot * refresh_dev, fresh_half, flip, by), fresh_at)
                )
                buffers.append(rows)

        add_pieces(1, 0, near)
        add_pieces(1, 1, side_rows)
        early = table_pieces + shift(fresh_pieces, plane_rows)
        partials = [score(i, got_queries[i], list(buffers), early) for i in range(planes - 1)]
        far, from_end, to_end, new_table, *partials = lax.optimization_barrier((far, from_end, to_end, new_table, *partials))
        got_queries.append((to_end, from_end))
        add_pieces(3, None, far)
        pieces = table_pieces + shift(fresh_pieces, plane_rows)
        late = [piece for piece in pieces if piece not in early]
        partials = [score(i, got_queries[i], buffers, late, [partials[i]]) for i in range(planes - 1)]
    else:
        got_queries = [(queries,)] + [(swap(queries, "outer", s),) for s in range(1, planes)]
        flips = range(planes)
        got_rows = [rows_half] + [swap(rows_half, "inner", s) for s in range(1, owners_plane)]
        data = table_half + fresh_half
        gathered = lax.all_gather(jnp.stack(got_rows), "query", axis=0)
        gathered = jnp.swapaxes(gathered, 0, 1)
        buffers = [
            gathered[:, :, :table_half].reshape(plane_rows, width),
            gathered[:, :, table_half:data].reshape(plane_refresh, width),
        ]
        scales = []
        for rows in buffers:
            values = rows.astype(f32)
            mean = jnp.sum(values * values, axis=1) / width
            scales.append((lax.rsqrt(mean + epsilon) * (score_scale / width * LOG2E)).reshape(-1, LANES))
        scales = jnp.concatenate(scales)

        def blocks(buffer, count, line):
            starts = range(0, count, 512)
            return [(buffer, i, 512, (i, 512, None, None), -1 - line - i // LANES) for i in starts]

        table_pieces = blocks(0, plane_rows, 0)
        fresh_pieces = blocks(1, plane_refresh, plane_rows // LANES)
        pieces = table_pieces + shift(fresh_pieces, plane_rows)
        partials = [score(i, got_queries[i], buffers, pieces) for i in range(planes - 1)]

    pieces = table_pieces + shift(fresh_pieces, plane_rows)
    partials = [partials[0]] + [swap(partials[i], "outer", flips[i]) for i in range(1, planes - 1)]
    new_table, *tied = lax.optimization_barrier((new_table, *partials, *got_queries[-1]))
    partials, last_queries = tied[: planes - 1], tied[planes - 1 :]
    mine = sum(partials[1:], partials[0])
    mine = mine + swap(score(planes - 1, last_queries, buffers, pieces), "outer", flips[-1])
    loss = (jnp.log2(mine[0]) - mine[1]) * math.log(2.0)
    return new_table, new_ages, loss.reshape(query_count)


def solution(mesh):
    owners, replicas = mesh.shape["index"], mesh.shape["query"]
    inner = 1 << (int(math.log2(owners)) // 2)
    split = Mesh(mesh.devices.reshape(owners // inner, inner, replicas), ("outer", "inner", "query"))
    index = ("outer", "inner")
    placed = (
        P(index, None),
        P(index),
        P(index),
        P(index, None),
        P(index, None),
        P(("outer", "inner", "query"), None),
        P(("outer", "inner", "query")),
    )
    return jax.shard_map(
        on_device,
        mesh=split,
        in_specs=placed,
        out_specs=(P(index, None), P(index), P(("outer", "inner", "query"))),
        check_vma=False,
    )
```

```python
import functools
import math

import jax
import jax.numpy as jnp
from jax import lax
from jax.experimental import pallas as pl
from jax.experimental.pallas import tpu as pltpu
from jax.sharding import Mesh, PartitionSpec as P

score_scale = 20.0
age_scale = 16.0
epsilon = 1e-06
LOG2E = math.log2(math.e)
MASKED = -1e30
VMEM_LIMIT = 48 * 1024 * 1024
EXTRA = 16
AGES_ROW = 9
LANES = 128

NT = (((1,), (1,)), ((), ()))
NN = (((1,), (0,)), ((), ()))


def one_hot(ids, count):
    rows = lax.broadcasted_iota(jnp.int32, (count, ids.shape[1]), 0)
    if count <= 256:
        ids = jnp.where((ids < 0) | (ids >= count), -1, ids)
        rows, ids = rows.astype(jnp.float32).astype(jnp.bfloat16), ids.astype(jnp.float32).astype(jnp.bfloat16)
        return jnp.where(rows == ids, jnp.bfloat16(1), jnp.bfloat16(0))
    return jnp.where(rows == ids, 1.0, 0.0).astype(jnp.bfloat16)


def split_terms(values):
    terms = []
    for _ in range(3):
        terms.append(values.astype(jnp.bfloat16))
        values = values - terms[-1].astype(jnp.float32)
    return terms


def counted(hits):
    count = hits.shape[1]
    before = lax.broadcasted_iota(jnp.int32, (count, count), 0)
    after = lax.broadcasted_iota(jnp.int32, (count, count), 1)
    earlier = jnp.where(before < after, 1.0, 0.0).astype(jnp.bfloat16)
    return lax.dot_general(hits.astype(jnp.bfloat16), earlier, NN, preferred_element_type=jnp.float32)


def small(values):
    return values.astype(jnp.float32).astype(jnp.bfloat16)


def number(values):
    return values.astype(jnp.float32).astype(jnp.int32)


def put(out, row, values):
    width = out.shape[1]
    for i, left in enumerate(range(0, values.shape[1], width)):
        part = small(values[:, left : left + width])
        out[row + i : row + i + 1, : part.shape[1]] = part


def take(rows, row, count):
    width = rows.shape[1]
    parts = [number(rows[row + i : row + i + 1, :]) for i in range(-(-count // width))]
    return jnp.concatenate(parts, axis=1)[:, :count]


def put_ids(out, row, ids):
    lines = -(-ids.shape[1] // out.shape[1])
    put(out, row, ids >> 7)
    put(out, row + lines, ids & 127)


def take_ids(rows, row, count):
    lines = -(-count // rows.shape[1])
    return take(rows, row, count) * LANES + take(rows, row + lines, count)


def prep_kernel(
    place, queries, table, fresh, ref_ids, neg, pos, rows_out, scale_out, *mail, owners_plane, cap, replicas, encode
):
    outer, inner, core = place[0], place[1], place[2]
    width = table.shape[1]
    refresh_dev, rows_dev = fresh.shape[0], table.shape[0]
    planes, share = len(mail), cap // replicas
    pairs = [(plane, side) for plane in range(planes) for side in range(owners_plane)]
    ids = ref_ids[...]
    owner_of = ids // rows_dev
    rank = owner_ranks(
        [owner_of - ((outer ^ plane) * owners_plane + (inner ^ side)) for plane, side in pairs], refresh_dev, cap
    )
    rank = rank - core * share
    code = jnp.full((1, refresh_dev), -1, jnp.int32)
    for i in range(len(pairs)):
        here = (rank[i : i + 1, :] >= 0) & (rank[i : i + 1, :] < share)
        code = jnp.where(here, i * share + rank[i : i + 1, :], code)
    select = one_hot(code, len(pairs) * share)
    packed = lax.dot_general(select, fresh[...], NN, preferred_element_type=jnp.float32).astype(jnp.bfloat16)
    size = owners_plane * share
    for i, out in enumerate(mail):
        lead = out.shape[0] - size - EXTRA
        if lead:
            out[:lead, :] = queries[...]
        row = lead + size
        out[lead:row, :] = packed[i * size : (i + 1) * size, :]
        out[row:, :] = jnp.zeros((EXTRA, width), jnp.bfloat16)
        for values in (neg[...], pos[...], ids):
            put_ids(out, row, values)
            row += 2 * -(-values.shape[1] // width)

    line, row = 0, 0
    halves = []
    for source in (table, fresh):
        rows = source.shape[0]
        half = rows // replicas
        rows_out[row : row + half, :] = source[pl.ds(pl.multiple_of(core * half, half), half), :]
        row += half
        for block in range(rows // LANES):
            squares = jnp.zeros((LANES, LANES), jnp.float32)
            for chunk in range(width // LANES):
                values = source[block * LANES : (block + 1) * LANES, chunk * LANES : (chunk + 1) * LANES]
                values = values.astype(jnp.float32)
                squares += values * values
            mean = jnp.sum(squares.T, axis=0, keepdims=True) / width
            scale_out[line + block : line + block + 1, :] = lax.rsqrt(mean + epsilon) * (score_scale / width * LOG2E)
        halves += [(line, i, half // LANES) for i in range(half // LANES)]
        line += rows // LANES
    rows_out[row:, :] = jnp.zeros((EXTRA, width), jnp.bfloat16)
    if encode:
        terms = []
        for first, i, count in halves:
            terms += split_terms(scale_out[pl.ds(first + core * count + i, 1), :])
        for i, term in enumerate(terms):
            rows_out[row + i : row + i + 1, :LANES] = term


def relay_kernel(place, ages, *refs, planes, owners_plane, share, list_size, count, refresh_dev):
    *mail, whole_out = refs
    size = owners_plane * share
    width = mail[0].shape[1]
    row = size + 2 * (-(-list_size // width) + -(-count // width))
    ids = jnp.concatenate([take_ids(block, row, refresh_dev) for block in mail], axis=1)
    for side in range(owners_plane):
        out = whole_out.at[place[1] ^ side]
        for plane, block in enumerate(mail):
            out[plane * share : (plane + 1) * share, :] = block[side * share : (side + 1) * share, :]
        out[planes * share :, :] = jnp.zeros((EXTRA, width), jnp.bfloat16)
        put_ids(out, planes * share, ids)
        put(out, planes * share + AGES_ROW, ages[...])


def owner_ranks(rows, refresh_dev, cap):
    match = jnp.concatenate(rows, axis=0) == 0
    rank = counted(jnp.where(match, 1.0, 0.0)).astype(jnp.int32)
    return jnp.where(match, rank, -cap)


def one_hots(ids, high_count):
    return one_hot(ids >> 7, high_count), one_hot(ids & 127, LANES)


def bitmap(ids, high_count):
    high, low = one_hots(ids, high_count)
    return lax.dot_general(low, high, NT, preferred_element_type=jnp.float32).astype(jnp.bfloat16)


def lookup(one_map, pair):
    hit = lax.dot_general(one_map, pair[0], NN, preferred_element_type=jnp.float32)
    return jnp.sum(hit * pair[1].astype(jnp.float32), axis=0, keepdims=True)


def column_ids(place, owners_plane, rows_dev):
    column = lax.broadcasted_iota(jnp.int32, (1, owners_plane * rows_dev), 1)
    return (place[0] * owners_plane + (place[1] ^ (column // rows_dev))) * rows_dev + column % rows_dev


def lists_kernel(*refs, first, list_size, high_count):
    *mail, out = refs
    for group, block in enumerate(mail):
        out[group, :, :] = bitmap(take_ids(block, first, list_size), high_count)


def meta_kernel(
    place, maps, ages, *refs, planes, owners_plane, rows_dev, refresh_dev, list_size, count, cap, replicas
):
    outer, inner, core = place[0], place[1], place[2]
    lw_out, row_out, pos_out, target_out, own_out, ages_out = refs[-6:]
    mail, relayed = refs[:planes], [refs[planes].at[inner ^ side] for side in range(owners_plane)]
    share = cap // replicas
    plane_rows = owners_plane * rows_dev
    high_count = planes * plane_rows // LANES
    own_owner = outer * owners_plane + inner

    ids = [take_ids(block, planes * share, planes * refresh_dev) for block in relayed]
    plane_ids = jnp.concatenate([one[:, :refresh_dev] for one in ids], axis=1)
    table_ids = column_ids(place, owners_plane, rows_dev)
    pair = one_hots(jnp.concatenate([table_ids, plane_ids], axis=1), high_count)
    refreshed = lookup(bitmap(jnp.concatenate(ids, axis=1), high_count), (pair[0][:, :plane_rows], pair[1][:, :plane_rows]))
    refreshed = refreshed > 0.5
    row_out[:, :plane_rows] = jnp.where(refreshed, -1, table_ids).astype(jnp.float32)
    row_out[:, plane_rows:] = plane_ids.astype(jnp.float32)
    own_out[...] = refreshed[:, :rows_dev].astype(jnp.int32)
    ages_out[...] = jnp.where(refreshed[:, :rows_dev], 0, ages[...])

    all_ages = [take(block, planes * share + AGES_ROW, rows_dev) for block in relayed]
    all_ages = jnp.concatenate(all_ages, axis=1).astype(jnp.float32)
    weight = jnp.exp(-all_ages / age_scale).astype(jnp.bfloat16).astype(jnp.float32)
    log_weight = jnp.where(refreshed, MASKED, jnp.log2(weight))
    log_weight = jnp.concatenate([log_weight, jnp.zeros((1, plane_ids.shape[1]), jnp.float32)], axis=1)
    for group, block in enumerate(mail):
        row = owners_plane * share
        hit = lookup(maps[group, :, :], pair)
        lw_out[group : group + 1, :] = jnp.where(hit > 0.5, log_weight, MASKED)
        row += 2 * -(-list_size // block.shape[1])
        pos_out[group : group + 1, :] = take_ids(block, row, count).astype(jnp.float32)

    pairs = [(side, plane) for side in range(owners_plane) for plane in range(planes)]
    part_ids = [ids[side][:, plane * refresh_dev : (plane + 1) * refresh_dev] for side, plane in pairs]
    rank = owner_ranks([one // rows_dev - own_owner for one in part_ids], refresh_dev, cap)
    for i in range(len(pairs)):
        took = rank[i : i + 1, :]
        slot = jnp.where(took < 0, -1, ((took // share) ^ core) * share + took % share)
        row = jnp.where(took < 0, 0, part_ids[i] - own_owner * rows_dev)
        kinds = lax.broadcasted_iota(jnp.int32, (8, refresh_dev), 0)
        digits = jnp.where(kinds == 0, row // 16, jnp.where(kinds == 1, row % 16, 1))
        found = lax.dot_general(small(digits), one_hot(slot, cap), NT, preferred_element_type=jnp.float32)
        found = found.astype(jnp.int32)
        target = jnp.where(found[2:3, :] > 0, found[0:1, :] * 16 + found[1:2, :], -1)
        for part in range(replicas):
            first = (part * len(pairs) + i) * share
            target_out[:, first : first + share] = target[:, part * share : (part + 1) * share]


def piece_offset(place, piece):
    column, size, flip, by_core = piece
    if flip is None:
        return column
    column += (place[2] ^ flip) * size
    if by_core is not None:
        column += (place[2] ^ by_core) * size * 2
    return pl.multiple_of(column, size)


def apply_kernel(place, target, refreshed, table, *refs, size):
    *arrived, out = refs
    blocks = [block[place[1] ^ side, :size, :] for block in arrived for side in range(block.shape[0])]
    values = jnp.concatenate(blocks, axis=0)
    rows = lax.broadcasted_iota(jnp.int32, (out.shape[0], values.shape[0]), 0)
    chosen = jnp.where(rows == target[...], 1.0, 0.0).astype(jnp.bfloat16)
    fresh = lax.dot_general(chosen, values, NN, preferred_element_type=jnp.float32)
    for top in range(0, out.shape[0], LANES):
        part = slice(top, top + LANES)
        hit = to_lanes(refreshed[:, part].astype(jnp.float32)) > 0.5
        for left in range(0, out.shape[1], LANES):
            cols = slice(left, left + LANES)
            out[part, cols] = jnp.where(hit, fresh[part, cols], table[part, cols].astype(jnp.float32)).astype(jnp.bfloat16)


def to_lanes(row):
    return jnp.broadcast_to(row, (LANES, LANES)).T


def score_kernel(place, *refs, pieces, flip, given):
    out, total, pos_total, q_scale, pos_b, chosen = refs[-6:]
    positives_row, log_weight, row_ids, scale = refs[given : given + 4]
    positive = positives_row[flip : flip + 1, :]
    queries = refs[0]
    count, width = queries.shape
    if given == 2:
        at_end = (place[0] == 0) | (place[0] == 3)
        chosen[...] = jnp.where(at_end, refs[0][...], refs[1][...])
        queries = chosen
    refs = refs[given + 4 : -6]
    for block in range(count // LANES):
        part = slice(block * LANES, (block + 1) * LANES)
        values = queries[part, :].astype(jnp.float32)
        squares = jnp.sum(values * values, axis=1, keepdims=True)
        q_scale[part, :] = jnp.broadcast_to(lax.rsqrt(squares / width + epsilon), (LANES, LANES))
        pos_b[part, :] = to_lanes(positive[:, part])
    total[...] = jnp.zeros_like(total)
    pos_total[...] = jnp.zeros_like(pos_total)

    def product(group):
        rows = [refs[source][start : start + size, :] for source, start, size, _, _ in group]
        rows = rows[0] if len(rows) == 1 else jnp.concatenate(rows, axis=0)
        return lax.dot_general(queries[...], rows, NT, preferred_element_type=jnp.float32)

    narrow = [piece for piece in pieces if piece[2] < 256]
    groups = [[piece] for piece in pieces if piece[2] >= 256] + [narrow[i : i + 2] for i in range(0, len(narrow), 2)]
    following = product(groups[0])
    for i, group in enumerate(groups):
        raw = following
        if i + 1 < len(groups):
            following = product(groups[i + 1])
        columns = []
        for source, _, size, column, scale_at in group:
            for chunk in range(size // LANES):
                if scale_at < 0:
                    line = -1 - scale_at + chunk
                    row_scale = scale[line : line + 1, :]
                else:
                    line = scale_at + 3 * chunk
                    row_scale = refs[source][line : line + 3, :LANES].astype(jnp.float32)
                    row_scale = jnp.sum(row_scale, axis=0, keepdims=True)
                columns.append((piece_offset(place, column) + chunk * LANES, row_scale))
        for top in range(0, count, 64):
            part = slice(top, top + 64)
            sums, positives = total[part, :], pos_total[part, :]
            query_scale, wanted = q_scale[part, :], pos_b[part, :]
            for chunk, (first, row_scale) in enumerate(columns):
                cols = pl.ds(first, LANES)
                powers = raw[part, chunk * LANES : (chunk + 1) * LANES] * query_scale
                powers = powers * row_scale + log_weight[flip : flip + 1, cols]
                sums = sums + jnp.exp2(powers)
                positives = positives + jnp.where(wanted == row_ids[:, cols], powers, 0.0)
            total[part, :] = sums
            pos_total[part, :] = positives
    for block in range(count // LANES):
        part = slice(block * LANES, (block + 1) * LANES)
        for i, sums in enumerate((total, pos_total)):
            row = jnp.sum(sums[part, :].T, axis=0, keepdims=True)
            out[i, block : block + 1, :] = row


def whole(memory=pltpu.VMEM):
    return pl.BlockSpec(memory_space=memory)


def call(kernel, name, outs, place, *operands, scratch=(), **options):
    specs = [whole()] * len(operands)
    if place is not None:
        specs = [whole(pltpu.SMEM)] + specs
        operands = (place, *operands)
    return pl.pallas_call(
        functools.partial(kernel, **options),
        out_shape=tuple(outs),
        in_specs=specs,
        out_specs=tuple(whole() for _ in outs),
        scratch_shapes=list(scratch),
        compiler_params=pltpu.CompilerParams(vmem_limit_bytes=VMEM_LIMIT),
        cost_estimate=pl.CostEstimate(flops=1, bytes_accessed=1, transcendentals=0),
        name=name,
    )(*operands)


def swap(values, axis, flip):
    return lax.ppermute(values, axis, [(i, i ^ flip) for i in range(lax.axis_size(axis))])


def on_device(table, ages, refresh_ids, fresh_rows, neg_ids, queries, pos_ids):
    rows_dev, width = table.shape
    refresh_dev = refresh_ids.shape[0]
    planes = lax.axis_size("outer")
    owners_plane = lax.axis_size("inner")
    replicas = lax.axis_size("query")
    owners = planes * owners_plane
    query_count = queries.shape[0]
    list_size = neg_ids.shape[1]
    place = jnp.stack([lax.axis_index(name) for name in ("outer", "inner", "query")]).astype(jnp.int32)
    plane_rows = owners_plane * rows_dev
    plane_refresh = owners_plane * refresh_dev
    all_rows = plane_rows + plane_refresh
    cap = max(2, (2 * refresh_dev + owners - 1) // owners)
    share = cap // replicas
    table_half, fresh_half = rows_dev // replicas, refresh_dev // replicas
    bf16, f32 = jnp.bfloat16, jnp.float32

    fast = replicas == 2 and owners_plane == 4 and planes == 4
    own_ages = ages.reshape(1, -1)
    size = owners_plane * share
    rows_half, scales, *mail = call(
        prep_kernel,
        "prep",
        [
            jax.ShapeDtypeStruct((table_half + fresh_half + EXTRA, width), bf16),
            jax.ShapeDtypeStruct(((rows_dev + refresh_dev) // LANES, LANES), f32),
        ]
        + [
            jax.ShapeDtypeStruct((size + EXTRA + query_count * (fast and s in (1, 3)), width), bf16)
            for s in range(planes)
        ],
        place,
        queries,
        table,
        fresh_rows,
        refresh_ids.reshape(1, -1),
        neg_ids,
        pos_ids.reshape(1, -1),
        owners_plane=owners_plane,
        cap=cap,
        replicas=replicas,
        encode=fast,
    )
    mail = [mail[0]] + [swap(mail[s], "outer", s) for s in range(1, planes)]
    if fast:
        axes = ("inner", "query")
        first = [(2 * i + c, 2 * (i ^ (1 + c)) + c) for i in range(4) for c in range(2)]
        second = [(2 * i + c, 2 * (i ^ (2 - c)) + c) for i in range(4) for c in range(2)]
        near = lax.ppermute(rows_half, axes, first)
        side_rows = lax.ppermute(rows_half, axes, second)
        near, side_rows, *mail = lax.optimization_barrier((near, side_rows, *mail))
        far = lax.ppermute(near, axes, second)
        near_other, side_other = swap(near, "query", 1), swap(side_rows, "query", 1)
        beside, mail[1] = mail[1][:query_count], mail[1][query_count:]
        across, mail[3] = mail[3][:query_count], mail[3][query_count:]

    high_count = owners * rows_dev // LANES
    (maps,) = call(
        lists_kernel,
        "lists",
        [jax.ShapeDtypeStruct((planes, LANES, high_count), bf16)],
        None,
        *mail,
        first=size,
        list_size=list_size,
        high_count=high_count,
    )

    (relayed,) = call(
        relay_kernel,
        "relay",
        [jax.ShapeDtypeStruct((owners_plane, planes * share + EXTRA, width), bf16)],
        place,
        own_ages,
        *mail,
        planes=planes,
        owners_plane=owners_plane,
        share=share,
        list_size=list_size,
        count=query_count,
        refresh_dev=refresh_dev,
    )
    relayed = lax.all_to_all(relayed, "inner", split_axis=0, concat_axis=0, tiled=True)
    lw, row_ids, positive, target, own, new_ages = call(
        meta_kernel,
        "meta",
        [
            jax.ShapeDtypeStruct((planes, all_rows), f32),
            jax.ShapeDtypeStruct((1, all_rows), f32),
            jax.ShapeDtypeStruct((planes, query_count), f32),
            jax.ShapeDtypeStruct((1, owners * cap), jnp.int32),
            jax.ShapeDtypeStruct((1, rows_dev), jnp.int32),
            jax.ShapeDtypeStruct((1, rows_dev), jnp.int32),
        ],
        place,
        maps,
        own_ages,
        *mail,
        relayed,
        planes=planes,
        owners_plane=owners_plane,
        rows_dev=rows_dev,
        refresh_dev=refresh_dev,
        list_size=list_size,
        count=query_count,
        cap=cap,
        replicas=replicas,
    )

    new_ages = new_ages.reshape(rows_dev)
    arrived = [relayed] + [swap(relayed, "query", flip) for flip in range(1, replicas)]
    (new_table,) = call(
        apply_kernel,
        "apply",
        [jax.ShapeDtypeStruct(table.shape, bf16)],
        place,
        target,
        own,
        table,
        *arrived,
        size=planes * share,
    )

    def shift(pieces, columns):
        return [(a, b, c, (d[0] + columns, *d[1:]), e) for a, b, c, d, e in pieces]

    def score(i, given, buffers, pieces):
        (partial,) = call(
            score_kernel,
            "score",
            [jax.ShapeDtypeStruct((2, query_count // LANES, LANES), f32)],
            place,
            *given,
            positive,
            lw,
            row_ids,
            scales,
            *buffers,
            scratch=[pltpu.VMEM((query_count, LANES), f32)] * 4 + [pltpu.VMEM(queries.shape, bf16)],
            pieces=pieces,
            flip=flips[i],
            given=len(given),
        )
        return partial

    if fast:
        middle, outward = [(1, 2), (2, 1)], [(1, 0), (2, 3)]
        from_end = lax.ppermute(beside, "outer", middle)
        to_end = lax.ppermute(across, "outer", outward)
        got_queries = [(queries,), (beside,), (across,), (to_end, from_end)]
        flips = [0, 1, 3, 2]
        buffers = [table, fresh_rows]
        table_pieces = [(0, 0, rows_dev, (0, rows_dev, None, None), -1)]
        fresh_pieces = [(1, 0, refresh_dev, (0, refresh_dev, None, None), -1 - rows_dev // LANES)]

        def add_pieces(slot, by_core, *both):
            data = table_half + fresh_half
            fresh_at = data + 3 * (table_half // LANES)
            for flip, rows in enumerate(both):
                by = None if by_core is None else by_core ^ flip
                table_pieces.append((len(buffers), 0, table_half, (slot * rows_dev, table_half, flip, by), data))
                fresh_pieces.append(
                    (len(buffers), table_half, fresh_half, (slot * refresh_dev, fresh_half, flip, by), fresh_at)
                )
                buffers.append(rows)

        add_pieces(1, 0, near, near_other)
        add_pieces(1, 1, side_rows, side_other)
        add_pieces(3, None, far, swap(far, "query", 1))
    else:
        got_queries = [(queries,)] + [(swap(queries, "outer", s),) for s in range(1, planes)]
        flips = range(planes)
        got_rows = [rows_half] + [swap(rows_half, "inner", s) for s in range(1, owners_plane)]
        data = table_half + fresh_half
        gathered = lax.all_gather(jnp.stack(got_rows), "query", axis=0)
        gathered = jnp.swapaxes(gathered, 0, 1)
        buffers = [
            gathered[:, :, :table_half].reshape(plane_rows, width),
            gathered[:, :, table_half:data].reshape(plane_refresh, width),
        ]
        scales = []
        for rows in buffers:
            values = rows.astype(f32)
            mean = jnp.sum(values * values, axis=1) / width
            scales.append((lax.rsqrt(mean + epsilon) * (score_scale / width * LOG2E)).reshape(-1, LANES))
        scales = jnp.concatenate(scales)

        def blocks(buffer, count, line):
            starts = range(0, count, 512)
            return [(buffer, i, 512, (i, 512, None, None), -1 - line - i // LANES) for i in starts]

        table_pieces = blocks(0, plane_rows, 0)
        fresh_pieces = blocks(1, plane_refresh, plane_rows // LANES)

    pieces = table_pieces + shift(fresh_pieces, plane_rows)
    pieces = table_pieces + shift(fresh_pieces, plane_rows)
    partials = [score(i, got_queries[i], buffers, pieces) for i in range(2)]
    *partials, given = lax.optimization_barrier((*partials, tuple(got_queries[-1])))
    got_queries[-1] = given
    partials += [score(i, got_queries[i], buffers, pieces) for i in range(2, planes - 1)]
    partials = [partials[0]] + [swap(partials[i], "outer", flips[i]) for i in range(1, planes - 1)]
    new_table, *tied = lax.optimization_barrier((new_table, *partials, *got_queries[-1]))
    partials, last_queries = tied[: planes - 1], tied[planes - 1 :]
    mine = sum(partials[1:], partials[0])
    mine = mine + swap(score(planes - 1, last_queries, buffers, pieces), "outer", flips[-1])
    loss = (jnp.log2(mine[0]) - mine[1]) * math.log(2.0)
    return new_table, new_ages, loss.reshape(query_count)


def solution(mesh):
    owners, replicas = mesh.shape["index"], mesh.shape["query"]
    inner = 1 << (int(math.log2(owners)) // 2)
    split = Mesh(mesh.devices.reshape(owners // inner, inner, replicas), ("outer", "inner", "query"))
    index = ("outer", "inner")
    placed = (
        P(index, None),
        P(index),
        P(index),
        P(index, None),
        P(index, None),
        P(("outer", "inner", "query"), None),
        P(("outer", "inner", "query")),
    )
    return jax.shard_map(
        on_device,
        mesh=split,
        in_specs=placed,
        out_specs=(P(index, None), P(index), P(("outer", "inner", "query"))),
        check_vma=False,
    )
```

```python
import functools
import math

import jax
import jax.numpy as jnp
from jax import lax
from jax.experimental import pallas as pl
from jax.experimental.pallas import tpu as pltpu
from jax.sharding import Mesh, PartitionSpec as P

score_scale = 20.0
age_scale = 16.0
epsilon = 1e-06
LOG2E = math.log2(math.e)
MASKED = -1e30
LANES = 128
VMEM_LIMIT = 48 * 1024 * 1024

NT = (((1,), (1,)), ((), ()))
NN = (((1,), (0,)), ((), ()))


def one_hot(ids, count):
    rows = lax.broadcasted_iota(jnp.int32, (count, ids.shape[1]), 0)
    if count <= 256:
        ids = jnp.where((ids < 0) | (ids >= count), -1, ids)
        rows, ids = rows.astype(jnp.float32).astype(jnp.bfloat16), ids.astype(jnp.float32).astype(jnp.bfloat16)
        return jnp.where(rows == ids, jnp.bfloat16(1), jnp.bfloat16(0))
    return jnp.where(rows == ids, 1.0, 0.0).astype(jnp.bfloat16)


def counted(hits):
    count = hits.shape[1]
    before = lax.broadcasted_iota(jnp.int32, (count, count), 0)
    after = lax.broadcasted_iota(jnp.int32, (count, count), 1)
    earlier = jnp.where(before < after, 1.0, 0.0).astype(jnp.bfloat16)
    return lax.dot_general(hits.astype(jnp.bfloat16), earlier, NN, preferred_element_type=jnp.float32)


def small(values):
    return values.astype(jnp.float32).astype(jnp.bfloat16)


def owner_ranks(rows, refresh_dev, cap):
    match = jnp.concatenate(rows, axis=0) == 0
    rank = counted(jnp.where(match, 1.0, 0.0)).astype(jnp.int32)
    return jnp.where(match, rank, -cap)


def one_hots(ids, high_count):
    return one_hot(ids >> 7, high_count), one_hot(ids & 127, LANES)


def bitmap(ids, high_count):
    high, low = one_hots(ids, high_count)
    return lax.dot_general(low, high, NT, preferred_element_type=jnp.float32).astype(jnp.bfloat16)


def lookup(one_map, pair):
    hit = lax.dot_general(one_map, pair[0], NN, preferred_element_type=jnp.float32)
    return jnp.sum(hit * pair[1].astype(jnp.float32), axis=0, keepdims=True)


def prep_kernel(place, table, fresh, ages, ref_ids, rows_out, meta_out, *, replicas):
    core = place[2]
    row = 0
    for source in (table, fresh):
        half = source.shape[0] // replicas
        rows_out[row : row + half, :] = source[pl.ds(pl.multiple_of(core * half, half), half), :]
        row += half
    width = table.shape[1]
    ref_rows, age_rows = ref_ids.shape[0], ages.shape[0]
    meta_out[:ref_rows, :] = ref_ids[...].astype(jnp.float32)
    weight = jnp.exp(-ages[...].astype(jnp.float32) / age_scale).astype(jnp.bfloat16).astype(jnp.float32)
    meta_out[ref_rows : ref_rows + age_rows, :] = jnp.log2(weight)
    line = ref_rows + age_rows
    for source in (table, fresh):
        for block in range(source.shape[0] // LANES):
            squares = jnp.zeros((LANES, LANES), jnp.float32)
            for chunk in range(width // LANES):
                values = source[block * LANES : (block + 1) * LANES, chunk * LANES : (chunk + 1) * LANES]
                values = values.astype(jnp.float32)
                squares += values * values
            mean = jnp.sum(squares.T, axis=0, keepdims=True) / width
            meta_out[line : line + 1, :] = lax.rsqrt(mean + epsilon) * (score_scale / width * LOG2E)
            line += 1


def meta_kernel(
    place, ref_ids, neg, log_weight, ages, lw_out, row_out, code_out, target_out, own_out, ages_out,
    *, rows_dev, refresh_dev, cap, replicas
):
    outer, inner, core = place[0], place[1], place[2]
    planes, plane_refresh = ref_ids.shape
    plane_rows = log_weight.shape[1]
    owners_plane = plane_rows // rows_dev
    high_count = planes * plane_rows // LANES
    own_owner = outer * owners_plane + inner
    share = cap // replicas
    plane_ids = ref_ids[0:1, :]
    column = lax.broadcasted_iota(jnp.int32, (1, plane_rows), 1)
    table_ids = (outer * owners_plane + (inner ^ (column // rows_dev))) * rows_dev + column % rows_dev

    pair = one_hots(jnp.concatenate([table_ids, plane_ids], axis=1), high_count)
    all_ids = jnp.concatenate([ref_ids[plane : plane + 1, :] for plane in range(planes)], axis=1)
    refreshed = lookup(bitmap(all_ids, high_count), (pair[0][:, :plane_rows], pair[1][:, :plane_rows])) > 0.5
    row_out[:, :plane_rows] = jnp.where(refreshed, -1, table_ids).astype(jnp.float32)
    row_out[:, plane_rows:] = plane_ids.astype(jnp.float32)
    own_out[...] = refreshed[:, :rows_dev].astype(jnp.int32)
    ages_out[...] = jnp.where(refreshed[:, :rows_dev], 0, ages[...])
    weights = jnp.where(refreshed, MASKED, log_weight[...])
    weights = jnp.concatenate([weights, jnp.zeros((1, plane_refresh), jnp.float32)], axis=1)
    for group in range(planes):
        hit = lookup(bitmap(neg[group : group + 1, :], high_count), pair)
        lw_out[group : group + 1, :] = jnp.where(hit > 0.5, weights, MASKED)

    pairs = [(plane, side) for plane in range(planes) for side in range(owners_plane)]

    def ids_of(plane, side):
        return ref_ids[plane : plane + 1, side * refresh_dev : (side + 1) * refresh_dev]

    sent = [ids_of(0, side) // rows_dev - ((outer ^ plane) * owners_plane + inner) for plane, side in pairs]
    taken = [ids_of(plane, side) // rows_dev - own_owner for plane, side in pairs]
    rank = owner_ranks(sent + taken, refresh_dev, cap)
    own_slots = owners_plane * cap
    codes = [jnp.full((1, refresh_dev), -1, jnp.int32)] * owners_plane
    for i, (plane, side) in enumerate(pairs):
        size = share if plane else cap
        base = own_slots + ((plane - 1) * owners_plane + side) * share if plane else side * cap
        sends = rank[i : i + 1, :] - (core * share if plane else 0)
        codes[side] = jnp.where((sends >= 0) & (sends < size), base + sends, codes[side])
        took = rank[len(pairs) + i : len(pairs) + i + 1, :]
        slot = jnp.where(took < 0, -1, ((took // share) ^ core) * share + took % share if plane else took)
        row = jnp.where(took < 0, 0, ids_of(plane, side) - own_owner * rows_dev)
        kinds = lax.broadcasted_iota(jnp.int32, (8, refresh_dev), 0)
        digits = jnp.where(kinds == 0, row // 16, jnp.where(kinds == 1, row % 16, 1))
        found = lax.dot_general(small(digits), one_hot(slot, cap), NT, preferred_element_type=jnp.float32)
        found = found.astype(jnp.int32)
        target = jnp.where(found[2:3, :] > 0, found[0:1, :] * 16 + found[1:2, :], -1)
        if plane == 0:
            target_out[:, base : base + cap] = target
            continue
        for part in range(replicas):
            first = base + part * (planes - 1) * owners_plane * share
            target_out[:, first : first + share] = target[:, part * share : (part + 1) * share]
    code_out[...] = jnp.concatenate(codes, axis=1)


def piece_offset(place, piece):
    column, size, flip, by_core = piece
    if flip is None:
        return column
    column += (place[2] ^ flip) * size
    if by_core is not None:
        column += (place[2] ^ by_core) * size * 2
    return pl.multiple_of(column, size)


def pack_kernel(place, code, *refs, pieces):
    *buffers, out = refs
    selects = [
        one_hot(code[:, pl.ds(piece_offset(place, column), size)], out.shape[0]) for _, _, size, column in pieces
    ]
    values = [buffers[source][start : start + size, :] for source, start, size, _ in pieces]
    select, values = jnp.concatenate(selects, axis=1), jnp.concatenate(values, axis=0)
    out[...] = lax.dot_general(select, values, NN, preferred_element_type=jnp.float32).astype(jnp.bfloat16)


def apply_kernel(target, refreshed, table, *refs):
    *arrived, out = refs
    values = jnp.concatenate([block[...] for block in arrived], axis=0)
    rows = lax.broadcasted_iota(jnp.int32, (out.shape[0], values.shape[0]), 0)
    chosen = jnp.where(rows == target[...], 1.0, 0.0).astype(jnp.bfloat16)
    fresh = lax.dot_general(chosen, values, NN, preferred_element_type=jnp.float32)
    for top in range(0, out.shape[0], LANES):
        part = slice(top, top + LANES)
        hit = to_lanes(refreshed[:, part].astype(jnp.float32)) > 0.5
        for left in range(0, out.shape[1], LANES):
            cols = slice(left, left + LANES)
            out[part, cols] = jnp.where(hit, fresh[part, cols], table[part, cols].astype(jnp.float32)).astype(jnp.bfloat16)


def to_lanes(row):
    return jnp.broadcast_to(row, (LANES, LANES)).T


def score_kernel(place, *refs, pieces, sources):
    positive, log_weight, row_ids, scale = refs[sources : sources + 4]
    out, total, pos_total, q_scale, pos_b, chosen = refs[-6:]
    queries = refs[0]
    count, width = queries.shape
    if sources == 2:
        at_end = (place[0] == 0) | (place[0] == 3)
        chosen[...] = jnp.where(at_end, refs[0][...], refs[1][...])
        queries = chosen
    for block in range(count // LANES):
        part = slice(block * LANES, (block + 1) * LANES)
        values = queries[part, :].astype(jnp.float32)
        squares = jnp.sum(values * values, axis=1, keepdims=True)
        q_scale[part, :] = jnp.broadcast_to(lax.rsqrt(squares / width + epsilon), (LANES, LANES))
        pos_b[part, :] = to_lanes(positive[block : block + 1, :])
    total[...] = jnp.zeros_like(total)
    pos_total[...] = jnp.zeros_like(pos_total)
    refs = refs[sources + 4 : -6]

    def product(group):
        rows = [refs[source][start : start + size, :] for source, start, size, _ in group]
        rows = rows[0] if len(rows) == 1 else jnp.concatenate(rows, axis=0)
        return lax.dot_general(queries[...], rows, NT, preferred_element_type=jnp.float32)

    narrow = [piece for piece in pieces if piece[2] < 256]
    groups = [[piece] for piece in pieces if piece[2] >= 256] + [narrow[i : i + 2] for i in range(0, len(narrow), 2)]
    following = product(groups[0])
    for i, group in enumerate(groups):
        raw = following
        if i + 1 < len(groups):
            following = product(groups[i + 1])
        columns = []
        for _, _, size, column in group:
            columns += [piece_offset(place, column) + chunk * LANES for chunk in range(size // LANES)]
        for top in range(0, count, 64):
            part = slice(top, top + 64)
            sums, positives = total[part, :], pos_total[part, :]
            query_scale, wanted = q_scale[part, :], pos_b[part, :]
            for chunk, first in enumerate(columns):
                cols = pl.ds(first, LANES)
                powers = raw[part, chunk * LANES : (chunk + 1) * LANES] * query_scale
                powers = powers * scale[:, cols] + log_weight[:, cols]
                sums = sums + jnp.exp2(powers)
                positives = positives + jnp.where(wanted == row_ids[:, cols], powers, 0.0)
            total[part, :] = sums
            pos_total[part, :] = positives
    for block in range(count // LANES):
        part = slice(block * LANES, (block + 1) * LANES)
        out[0, block : block + 1, :] = jnp.sum(total[part, :].T, axis=0, keepdims=True)
        out[1, block : block + 1, :] = jnp.sum(pos_total[part, :].T, axis=0, keepdims=True)


def whole(memory=pltpu.VMEM):
    return pl.BlockSpec(memory_space=memory)


def call(kernel, name, outs, place, *operands, scratch=(), **options):
    specs = [whole()] * len(operands)
    if place is not None:
        specs = [whole(pltpu.SMEM)] + specs
        operands = (place, *operands)
    return pl.pallas_call(
        functools.partial(kernel, **options),
        out_shape=tuple(outs),
        in_specs=specs,
        out_specs=tuple(whole() for _ in outs),
        scratch_shapes=list(scratch),
        compiler_params=pltpu.CompilerParams(vmem_limit_bytes=VMEM_LIMIT),
        cost_estimate=pl.CostEstimate(flops=1, bytes_accessed=1, transcendentals=0),
        name=name,
    )(*operands)


def swap(values, axis, flip):
    return lax.ppermute(values, axis, [(i, i ^ flip) for i in range(lax.axis_size(axis))])


def gather_line(values, small):
    planes = lax.axis_size("outer")
    if planes != 4:
        return [(swap(values, "outer", s),) for s in range(1, planes)], small
    middle, outward = [(1, 2), (2, 1)], [(1, 0), (2, 3)]
    beside = swap(values, "outer", 1)
    across = lax.ppermute(values, "outer", middle)
    beside, across, small = lax.optimization_barrier((beside, across, small))
    from_end = lax.ppermute(beside, "outer", middle)
    to_end = lax.ppermute(across, "outer", outward)
    last = lax.ppermute(from_end, "outer", outward)
    return [(beside,), (to_end, from_end), (last, across)], small


def on_device(table, ages, refresh_ids, fresh_rows, neg_ids, queries, pos_ids):
    rows_dev, width = table.shape
    refresh_dev = refresh_ids.shape[0]
    planes = lax.axis_size("outer")
    owners_plane = lax.axis_size("inner")
    replicas = lax.axis_size("query")
    owners = planes * owners_plane
    query_count = queries.shape[0]
    list_size = neg_ids.shape[1]
    place = jnp.stack([lax.axis_index(name) for name in ("outer", "inner", "query")]).astype(jnp.int32)
    plane_rows = owners_plane * rows_dev
    plane_refresh = owners_plane * refresh_dev
    all_rows = plane_rows + plane_refresh
    cap = max(2, (2 * refresh_dev + owners - 1) // owners)
    share = cap // replicas
    table_half, fresh_half = rows_dev // replicas, refresh_dev // replicas
    bf16, f32 = jnp.bfloat16, jnp.float32

    meta_lines = (2 * refresh_dev + 2 * rows_dev) // LANES
    rows_half, meta = call(
        prep_kernel,
        "prep",
        [jax.ShapeDtypeStruct((table_half + fresh_half, width), bf16), jax.ShapeDtypeStruct((meta_lines, LANES), f32)],
        place,
        table,
        fresh_rows,
        ages.reshape(-1, LANES),
        refresh_ids.reshape(-1, LANES),
        replicas=replicas,
    )
    metas = jnp.stack([meta] + [swap(meta, "inner", s) for s in range(1, owners_plane)])
    cuts = [refresh_dev, rows_dev, rows_dev, refresh_dev]
    ends = [sum(cuts[: i + 1]) // LANES for i in range(len(cuts))]

    def piece(i):
        return metas[:, ends[i] - cuts[i] // LANES : ends[i]].reshape(1, -1)

    ref_plane, log_weight_plane = piece(0), piece(1)
    scale_plane = jnp.concatenate([piece(2), piece(3)], axis=1)
    line = jnp.concatenate([ref_plane[0], neg_ids[0].astype(f32), pos_ids.astype(f32)])
    got_queries, line = gather_line(queries, line)
    got_queries = [(queries,)] + got_queries
    lines = jnp.stack([line] + [swap(line, "outer", s) for s in range(1, planes)])
    ref_all = lines[:, :plane_refresh].astype(jnp.int32)
    neg_line = lines[:, plane_refresh : plane_refresh + list_size].astype(jnp.int32)
    positive = lines[:, plane_refresh + list_size :].reshape(planes, -1, LANES)

    own_slots, part_slots = owners_plane * cap, owners_plane * share
    lw, row_ids, code, target, own, new_ages = call(
        meta_kernel,
        "meta",
        [
            jax.ShapeDtypeStruct((planes, all_rows), f32),
            jax.ShapeDtypeStruct((1, all_rows), f32),
            jax.ShapeDtypeStruct((1, plane_refresh), jnp.int32),
            jax.ShapeDtypeStruct((1, planes * own_slots), jnp.int32),
            jax.ShapeDtypeStruct((1, rows_dev), jnp.int32),
            jax.ShapeDtypeStruct((1, rows_dev), jnp.int32),
        ],
        place,
        ref_all,
        neg_line,
        log_weight_plane,
        ages.reshape(1, -1),
        rows_dev=rows_dev,
        refresh_dev=refresh_dev,
        cap=cap,
        replicas=replicas,
    )
    new_ages = new_ages.reshape(rows_dev)

    if replicas == 2 and owners_plane == 4:
        axes = ("inner", "query")
        first = [(2 * i + c, 2 * (i ^ (1 + c)) + c) for i in range(4) for c in range(2)]
        second = [(2 * i + c, 2 * (i ^ (2 - c)) + c) for i in range(4) for c in range(2)]
        near = lax.ppermute(rows_half, axes, first)
        near, rows_half, _ = lax.optimization_barrier((near, rows_half, metas))
        side = lax.ppermute(rows_half, axes, second)
        far = lax.ppermute(near, axes, second)
        buffers = [table, fresh_rows]
        table_pieces = [(0, 0, rows_dev, (0, rows_dev, None, None))]
        fresh_pieces = [(1, 0, refresh_dev, (0, refresh_dev, None, None))]
        for slot, by_core, mine in ((1, 0, near), (1, 1, side), (3, None, far)):
            for flip, rows in enumerate((mine, swap(mine, "query", 1))):
                by = None if by_core is None else by_core ^ flip
                table_pieces.append((len(buffers), 0, table_half, (slot * rows_dev, table_half, flip, by)))
                fresh_pieces.append((len(buffers), table_half, fresh_half, (slot * refresh_dev, fresh_half, flip, by)))
                buffers.append(rows)
    else:
        got_rows = [rows_half] + [swap(rows_half, "inner", s) for s in range(1, owners_plane)]
        gathered = lax.all_gather(jnp.stack(got_rows), "query", axis=0)
        gathered = jnp.swapaxes(gathered, 0, 1)
        buffers = [
            gathered[:, :, :table_half].reshape(plane_rows, width),
            gathered[:, :, table_half:].reshape(plane_refresh, width),
        ]
        table_pieces = [(0, i * 512, 512, (i * 512, 512, None, None)) for i in range(plane_rows // 512)]
        fresh_pieces = [(1, i * 512, 512, (i * 512, 512, None, None)) for i in range(plane_refresh // 512)]

    def shift(pieces, columns):
        return [(a, b, c, (d[0] + columns, *d[1:])) for a, b, c, d in pieces]

    (packed,) = call(
        pack_kernel,
        "pack",
        [jax.ShapeDtypeStruct((own_slots + (planes - 1) * part_slots, width), bf16)],
        place,
        code,
        *buffers,
        pieces=fresh_pieces,
    )
    parts = []
    for s in range(1, planes):
        first = own_slots + (s - 1) * part_slots
        parts.append(swap(packed[first : first + part_slots], "outer", s))
    parts, *given = lax.optimization_barrier((jnp.concatenate(parts), *got_queries[-1]))
    got_queries[-1] = tuple(given)
    arrived = [packed[:own_slots], parts] + [swap(parts, "query", flip) for flip in range(1, replicas)]

    pieces = table_pieces + shift(fresh_pieces, plane_rows)
    mine = None
    for s in [*range(1, planes), 0]:
        (partial,) = call(
            score_kernel,
            "score",
            [jax.ShapeDtypeStruct((2, query_count // LANES, LANES), f32)],
            place,
            *got_queries[s],
            positive[s],
            lw[s : s + 1],
            row_ids,
            scale_plane,
            *buffers,
            scratch=[pltpu.VMEM((query_count, LANES), f32)] * 4 + [pltpu.VMEM((query_count, width), bf16)],
            pieces=pieces,
            sources=len(got_queries[s]),
        )
        if s:
            partial = swap(partial, "outer", s)
        mine = partial if mine is None else mine + partial
    (new_table,) = call(
        apply_kernel, "apply", [jax.ShapeDtypeStruct(table.shape, bf16)], None, target, own, table, *arrived
    )
    loss = (jnp.log2(mine[0]) - mine[1]) * math.log(2.0)
    return new_table, new_ages, loss.reshape(query_count)


def solution(mesh):
    owners, replicas = mesh.shape["index"], mesh.shape["query"]
    inner = 1 << (int(math.log2(owners)) // 2)
    split = Mesh(mesh.devices.reshape(owners // inner, inner, replicas), ("outer", "inner", "query"))
    index = ("outer", "inner")
    placed = (
        P(index, None),
        P(index),
        P(index),
        P(index, None),
        P(index, None),
        P(("outer", "inner", "query"), None),
        P(("outer", "inner", "query")),
    )
    return jax.shard_map(
        on_device,
        mesh=split,
        in_specs=placed,
        out_specs=(P(index, None), P(index), P(("outer", "inner", "query"))),
        check_vma=False,
    )
```

```python
import functools
import math

import jax
import jax.numpy as jnp
from jax import lax
from jax.experimental import pallas as pl
from jax.experimental.pallas import tpu as pltpu
from jax.sharding import Mesh, PartitionSpec as P

score_scale = 20.0
age_scale = 16.0
epsilon = 1e-06
LOG2E = math.log2(math.e)
MASKED = -1e30
LANES = 128
VMEM_LIMIT = 48 * 1024 * 1024

NT = (((1,), (1,)), ((), ()))
NN = (((1,), (0,)), ((), ()))


def one_hot(ids, count):
    rows = lax.broadcasted_iota(jnp.int32, (count, ids.shape[1]), 0)
    if count <= 256:
        ids = jnp.where((ids < 0) | (ids >= count), -1, ids)
        rows, ids = rows.astype(jnp.float32).astype(jnp.bfloat16), ids.astype(jnp.float32).astype(jnp.bfloat16)
        return jnp.where(rows == ids, jnp.bfloat16(1), jnp.bfloat16(0))
    return jnp.where(rows == ids, 1.0, 0.0).astype(jnp.bfloat16)


def counted(hits):
    count = hits.shape[1]
    before = lax.broadcasted_iota(jnp.int32, (count, count), 0)
    after = lax.broadcasted_iota(jnp.int32, (count, count), 1)
    earlier = jnp.where(before < after, 1.0, 0.0).astype(jnp.bfloat16)
    return lax.dot_general(hits.astype(jnp.bfloat16), earlier, NN, preferred_element_type=jnp.float32)


def small(values):
    return values.astype(jnp.float32).astype(jnp.bfloat16)


def owner_ranks(rows, refresh_dev, cap):
    match = jnp.concatenate(rows, axis=0) == 0
    rank = counted(jnp.where(match, 1.0, 0.0)).astype(jnp.int32)
    return jnp.where(match, rank, -cap)


def one_hots(ids, high_count):
    return one_hot(ids >> 7, high_count), one_hot(ids & 127, LANES)


def bitmap(ids, high_count):
    high, low = one_hots(ids, high_count)
    return lax.dot_general(low, high, NT, preferred_element_type=jnp.float32).astype(jnp.bfloat16)


def lookup(one_map, pair):
    hit = lax.dot_general(one_map, pair[0], NN, preferred_element_type=jnp.float32)
    return jnp.sum(hit * pair[1].astype(jnp.float32), axis=0, keepdims=True)


def prep_kernel(place, table, fresh, ages, ref_ids, rows_out, meta_out, *, replicas):
    core = place[2]
    row = 0
    for source in (table, fresh):
        half = source.shape[0] // replicas
        rows_out[row : row + half, :] = source[pl.ds(pl.multiple_of(core * half, half), half), :]
        row += half
    width = table.shape[1]
    ref_rows, age_rows = ref_ids.shape[0], ages.shape[0]
    meta_out[:ref_rows, :] = ref_ids[...].astype(jnp.float32)
    weight = jnp.exp(-ages[...].astype(jnp.float32) / age_scale).astype(jnp.bfloat16).astype(jnp.float32)
    meta_out[ref_rows : ref_rows + age_rows, :] = jnp.log2(weight)
    line = ref_rows + age_rows
    for source in (table, fresh):
        for block in range(source.shape[0] // LANES):
            squares = jnp.zeros((LANES, LANES), jnp.float32)
            for chunk in range(width // LANES):
                values = source[block * LANES : (block + 1) * LANES, chunk * LANES : (chunk + 1) * LANES]
                values = values.astype(jnp.float32)
                squares += values * values
            mean = jnp.sum(squares.T, axis=0, keepdims=True) / width
            meta_out[line : line + 1, :] = lax.rsqrt(mean + epsilon) * (score_scale / width * LOG2E)
            line += 1


def meta_kernel(
    place, ref_ids, neg, log_weight, ages, lw_out, row_out, code_out, target_out, own_out, ages_out,
    *, rows_dev, refresh_dev, cap, replicas
):
    outer, inner, core = place[0], place[1], place[2]
    planes, plane_refresh = ref_ids.shape
    plane_rows = log_weight.shape[1]
    owners_plane = plane_rows // rows_dev
    high_count = planes * plane_rows // LANES
    own_owner = outer * owners_plane + inner
    share = cap // replicas
    plane_ids = ref_ids[0:1, :]
    column = lax.broadcasted_iota(jnp.int32, (1, plane_rows), 1)
    table_ids = (outer * owners_plane + (inner ^ (column // rows_dev))) * rows_dev + column % rows_dev

    pair = one_hots(jnp.concatenate([table_ids, plane_ids], axis=1), high_count)
    all_ids = jnp.concatenate([ref_ids[plane : plane + 1, :] for plane in range(planes)], axis=1)
    refreshed = lookup(bitmap(all_ids, high_count), (pair[0][:, :plane_rows], pair[1][:, :plane_rows])) > 0.5
    row_out[:, :plane_rows] = jnp.where(refreshed, -1, table_ids).astype(jnp.float32)
    row_out[:, plane_rows:] = plane_ids.astype(jnp.float32)
    own_out[...] = refreshed[:, :rows_dev].astype(jnp.int32)
    ages_out[...] = jnp.where(refreshed[:, :rows_dev], 0, ages[...])
    weights = jnp.where(refreshed, MASKED, log_weight[...])
    weights = jnp.concatenate([weights, jnp.zeros((1, plane_refresh), jnp.float32)], axis=1)
    for group in range(planes):
        hit = lookup(bitmap(neg[group : group + 1, :], high_count), pair)
        lw_out[group : group + 1, :] = jnp.where(hit > 0.5, weights, MASKED)

    pairs = [(plane, side) for plane in range(planes) for side in range(owners_plane)]

    def ids_of(plane, side):
        return ref_ids[plane : plane + 1, side * refresh_dev : (side + 1) * refresh_dev]

    sent = [ids_of(0, side) // rows_dev - ((outer ^ plane) * owners_plane + inner) for plane, side in pairs]
    taken = [ids_of(plane, side) // rows_dev - own_owner for plane, side in pairs]
    rank = owner_ranks(sent + taken, refresh_dev, cap)
    own_slots = owners_plane * cap
    codes = [jnp.full((1, refresh_dev), -1, jnp.int32)] * owners_plane
    for i, (plane, side) in enumerate(pairs):
        size = share if plane else cap
        base = own_slots + ((plane - 1) * owners_plane + side) * share if plane else side * cap
        sends = rank[i : i + 1, :] - (core * share if plane else 0)
        codes[side] = jnp.where((sends >= 0) & (sends < size), base + sends, codes[side])
        took = rank[len(pairs) + i : len(pairs) + i + 1, :]
        slot = jnp.where(took < 0, -1, ((took // share) ^ core) * share + took % share if plane else took)
        row = jnp.where(took < 0, 0, ids_of(plane, side) - own_owner * rows_dev)
        kinds = lax.broadcasted_iota(jnp.int32, (8, refresh_dev), 0)
        digits = jnp.where(kinds == 0, row // 16, jnp.where(kinds == 1, row % 16, 1))
        found = lax.dot_general(small(digits), one_hot(slot, cap), NT, preferred_element_type=jnp.float32)
        found = found.astype(jnp.int32)
        target = jnp.where(found[2:3, :] > 0, found[0:1, :] * 16 + found[1:2, :], -1)
        if plane == 0:
            target_out[:, base : base + cap] = target
            continue
        for part in range(replicas):
            first = base + part * (planes - 1) * owners_plane * share
            target_out[:, first : first + share] = target[:, part * share : (part + 1) * share]
    code_out[...] = jnp.concatenate(codes, axis=1)


def piece_offset(place, piece):
    column, size, flip, by_core = piece
    if flip is None:
        return column
    column += (place[2] ^ flip) * size
    if by_core is not None:
        column += (place[2] ^ by_core) * size * 2
    return pl.multiple_of(column, size)


def pack_kernel(place, code, *refs, pieces):
    *buffers, out = refs
    selects = [
        one_hot(code[:, pl.ds(piece_offset(place, column), size)], out.shape[0]) for _, _, size, column in pieces
    ]
    values = [buffers[source][start : start + size, :] for source, start, size, _ in pieces]
    select, values = jnp.concatenate(selects, axis=1), jnp.concatenate(values, axis=0)
    out[...] = lax.dot_general(select, values, NN, preferred_element_type=jnp.float32).astype(jnp.bfloat16)


def apply_kernel(target, refreshed, table, *refs):
    *arrived, out = refs
    values = jnp.concatenate([block[...] for block in arrived], axis=0)
    rows = lax.broadcasted_iota(jnp.int32, (out.shape[0], values.shape[0]), 0)
    chosen = jnp.where(rows == target[...], 1.0, 0.0).astype(jnp.bfloat16)
    fresh = lax.dot_general(chosen, values, NN, preferred_element_type=jnp.float32)
    for top in range(0, out.shape[0], LANES):
        part = slice(top, top + LANES)
        hit = to_lanes(refreshed[:, part].astype(jnp.float32)) > 0.5
        for left in range(0, out.shape[1], LANES):
            cols = slice(left, left + LANES)
            out[part, cols] = jnp.where(hit, fresh[part, cols], table[part, cols].astype(jnp.float32)).astype(jnp.bfloat16)


def to_lanes(row):
    return jnp.broadcast_to(row, (LANES, LANES)).T


def score_kernel(place, *refs, pieces, sources):
    positive, log_weight, row_ids, scale = refs[sources : sources + 4]
    out, total, pos_total, q_scale, pos_b, chosen = refs[-6:]
    queries = refs[0]
    count, width = queries.shape
    if sources == 2:
        at_end = (place[0] == 0) | (place[0] == 3)
        chosen[...] = jnp.where(at_end, refs[0][...], refs[1][...])
        queries = chosen
    for block in range(count // LANES):
        part = slice(block * LANES, (block + 1) * LANES)
        values = queries[part, :].astype(jnp.float32)
        squares = jnp.sum(values * values, axis=1, keepdims=True)
        q_scale[part, :] = jnp.broadcast_to(lax.rsqrt(squares / width + epsilon), (LANES, LANES))
        pos_b[part, :] = to_lanes(positive[block : block + 1, :])
    total[...] = jnp.zeros_like(total)
    pos_total[...] = jnp.zeros_like(pos_total)
    refs = refs[sources + 4 : -6]

    def product(group):
        rows = [refs[source][start : start + size, :] for source, start, size, _ in group]
        rows = rows[0] if len(rows) == 1 else jnp.concatenate(rows, axis=0)
        return lax.dot_general(queries[...], rows, NT, preferred_element_type=jnp.float32)

    narrow = [piece for piece in pieces if piece[2] < 256]
    groups = [[piece] for piece in pieces if piece[2] >= 256] + [narrow[i : i + 2] for i in range(0, len(narrow), 2)]
    following = product(groups[0])
    for i, group in enumerate(groups):
        raw = following
        if i + 1 < len(groups):
            following = product(groups[i + 1])
        columns = []
        for _, _, size, column in group:
            columns += [piece_offset(place, column) + chunk * LANES for chunk in range(size // LANES)]
        for top in range(0, count, 64):
            part = slice(top, top + 64)
            sums, positives = total[part, :], pos_total[part, :]
            query_scale, wanted = q_scale[part, :], pos_b[part, :]
            for chunk, first in enumerate(columns):
                cols = pl.ds(first, LANES)
                powers = raw[part, chunk * LANES : (chunk + 1) * LANES] * query_scale
                powers = powers * scale[:, cols] + log_weight[:, cols]
                sums = sums + jnp.exp2(powers)
                positives = positives + jnp.where(wanted == row_ids[:, cols], powers, 0.0)
            total[part, :] = sums
            pos_total[part, :] = positives
    for block in range(count // LANES):
        part = slice(block * LANES, (block + 1) * LANES)
        out[0, block : block + 1, :] = jnp.sum(total[part, :].T, axis=0, keepdims=True)
        out[1, block : block + 1, :] = jnp.sum(pos_total[part, :].T, axis=0, keepdims=True)


def whole(memory=pltpu.VMEM):
    return pl.BlockSpec(memory_space=memory)


def call(kernel, name, outs, place, *operands, scratch=(), **options):
    specs = [whole()] * len(operands)
    if place is not None:
        specs = [whole(pltpu.SMEM)] + specs
        operands = (place, *operands)
    return pl.pallas_call(
        functools.partial(kernel, **options),
        out_shape=tuple(outs),
        in_specs=specs,
        out_specs=tuple(whole() for _ in outs),
        scratch_shapes=list(scratch),
        compiler_params=pltpu.CompilerParams(vmem_limit_bytes=VMEM_LIMIT),
        cost_estimate=pl.CostEstimate(flops=1, bytes_accessed=1, transcendentals=0),
        name=name,
    )(*operands)


def swap(values, axis, flip):
    return lax.ppermute(values, axis, [(i, i ^ flip) for i in range(lax.axis_size(axis))])


def gather_line(values, small):
    planes = lax.axis_size("outer")
    if planes != 4:
        return [(swap(values, "outer", s),) for s in range(1, planes)], small
    middle, outward = [(1, 2), (2, 1)], [(1, 0), (2, 3)]
    beside = swap(values, "outer", 1)
    across = lax.ppermute(values, "outer", middle)
    beside, across, *small = lax.optimization_barrier((beside, across, *small))
    from_end = lax.ppermute(beside, "outer", middle)
    to_end = lax.ppermute(across, "outer", outward)
    last = lax.ppermute(from_end, "outer", outward)
    return [(beside,), (to_end, from_end), (last, across)], small


def on_device(table, ages, refresh_ids, fresh_rows, neg_ids, queries, pos_ids):
    rows_dev, width = table.shape
    refresh_dev = refresh_ids.shape[0]
    planes = lax.axis_size("outer")
    owners_plane = lax.axis_size("inner")
    replicas = lax.axis_size("query")
    owners = planes * owners_plane
    query_count = queries.shape[0]
    list_size = neg_ids.shape[1]
    place = jnp.stack([lax.axis_index(name) for name in ("outer", "inner", "query")]).astype(jnp.int32)
    plane_rows = owners_plane * rows_dev
    plane_refresh = owners_plane * refresh_dev
    all_rows = plane_rows + plane_refresh
    cap = max(2, (2 * refresh_dev + owners - 1) // owners)
    share = cap // replicas
    table_half, fresh_half = rows_dev // replicas, refresh_dev // replicas
    bf16, f32 = jnp.bfloat16, jnp.float32

    meta_lines = (2 * refresh_dev + 2 * rows_dev) // LANES
    rows_half, meta = call(
        prep_kernel,
        "prep",
        [jax.ShapeDtypeStruct((table_half + fresh_half, width), bf16), jax.ShapeDtypeStruct((meta_lines, LANES), f32)],
        place,
        table,
        fresh_rows,
        ages.reshape(-1, LANES),
        refresh_ids.reshape(-1, LANES),
        replicas=replicas,
    )
    metas = jnp.stack([meta] + [swap(meta, "inner", s) for s in range(1, owners_plane)])
    cuts = [refresh_dev, rows_dev, rows_dev, refresh_dev]
    ends = [sum(cuts[: i + 1]) // LANES for i in range(len(cuts))]

    def piece(i):
        return metas[:, ends[i] - cuts[i] // LANES : ends[i]].reshape(1, -1)

    ref_plane, log_weight_plane = piece(0), piece(1)
    scale_plane = jnp.concatenate([piece(2), piece(3)], axis=1)
    line = jnp.concatenate([ref_plane[0], neg_ids[0].astype(f32), pos_ids.astype(f32)])
    lines = [line] + [swap(line, "outer", s) for s in range(1, planes)]
    got_queries, lines = gather_line(queries, lines)
    got_queries = [(queries,)] + got_queries
    lines = jnp.stack(lines)
    ref_all = lines[:, :plane_refresh].astype(jnp.int32)
    neg_line = lines[:, plane_refresh : plane_refresh + list_size].astype(jnp.int32)
    positive = lines[:, plane_refresh + list_size :].reshape(planes, -1, LANES)

    own_slots, part_slots = owners_plane * cap, owners_plane * share
    lw, row_ids, code, target, own, new_ages = call(
        meta_kernel,
        "meta",
        [
            jax.ShapeDtypeStruct((planes, all_rows), f32),
            jax.ShapeDtypeStruct((1, all_rows), f32),
            jax.ShapeDtypeStruct((1, plane_refresh), jnp.int32),
            jax.ShapeDtypeStruct((1, planes * own_slots), jnp.int32),
            jax.ShapeDtypeStruct((1, rows_dev), jnp.int32),
            jax.ShapeDtypeStruct((1, rows_dev), jnp.int32),
        ],
        place,
        ref_all,
        neg_line,
        log_weight_plane,
        ages.reshape(1, -1),
        rows_dev=rows_dev,
        refresh_dev=refresh_dev,
        cap=cap,
        replicas=replicas,
    )
    new_ages = new_ages.reshape(rows_dev)

    if replicas == 2 and owners_plane == 4:
        axes = ("inner", "query")
        first = [(2 * i + c, 2 * (i ^ (1 + c)) + c) for i in range(4) for c in range(2)]
        second = [(2 * i + c, 2 * (i ^ (2 - c)) + c) for i in range(4) for c in range(2)]
        near = lax.ppermute(rows_half, axes, first)
        near, rows_half, _ = lax.optimization_barrier((near, rows_half, metas))
        side = lax.ppermute(rows_half, axes, second)
        far = lax.ppermute(near, axes, second)
        buffers = [table, fresh_rows]
        table_pieces = [(0, 0, rows_dev, (0, rows_dev, None, None))]
        fresh_pieces = [(1, 0, refresh_dev, (0, refresh_dev, None, None))]
        for slot, by_core, mine in ((1, 0, near), (1, 1, side), (3, None, far)):
            for flip, rows in enumerate((mine, swap(mine, "query", 1))):
                by = None if by_core is None else by_core ^ flip
                table_pieces.append((len(buffers), 0, table_half, (slot * rows_dev, table_half, flip, by)))
                fresh_pieces.append((len(buffers), table_half, fresh_half, (slot * refresh_dev, fresh_half, flip, by)))
                buffers.append(rows)
    else:
        got_rows = [rows_half] + [swap(rows_half, "inner", s) for s in range(1, owners_plane)]
        gathered = lax.all_gather(jnp.stack(got_rows), "query", axis=0)
        gathered = jnp.swapaxes(gathered, 0, 1)
        buffers = [
            gathered[:, :, :table_half].reshape(plane_rows, width),
            gathered[:, :, table_half:].reshape(plane_refresh, width),
        ]
        table_pieces = [(0, i * 512, 512, (i * 512, 512, None, None)) for i in range(plane_rows // 512)]
        fresh_pieces = [(1, i * 512, 512, (i * 512, 512, None, None)) for i in range(plane_refresh // 512)]

    def shift(pieces, columns):
        return [(a, b, c, (d[0] + columns, *d[1:])) for a, b, c, d in pieces]

    (packed,) = call(
        pack_kernel,
        "pack",
        [jax.ShapeDtypeStruct((own_slots + (planes - 1) * part_slots, width), bf16)],
        place,
        code,
        *buffers,
        pieces=fresh_pieces,
    )
    packed, row_ids = lax.optimization_barrier((packed, row_ids))
    parts = []
    for s in range(1, planes):
        first = own_slots + (s - 1) * part_slots
        parts.append(swap(packed[first : first + part_slots], "outer", s))
    parts = jnp.concatenate(parts)
    pieces = table_pieces + shift(fresh_pieces, plane_rows)

    def score(s):
        (partial,) = call(
            score_kernel,
            "score",
            [jax.ShapeDtypeStruct((2, query_count // LANES, LANES), f32)],
            place,
            *got_queries[s],
            positive[s],
            lw[s : s + 1],
            row_ids,
            scale_plane,
            *buffers,
            scratch=[pltpu.VMEM((query_count, LANES), f32)] * 4 + [pltpu.VMEM((query_count, width), bf16)],
            pieces=pieces,
            sources=len(got_queries[s]),
        )
        return partial

    mine = score(0)
    for s in range(1, planes - 1):
        mine = mine + swap(score(s), "outer", s)
    parts, own_part, *given = lax.optimization_barrier((parts, mine, *got_queries[-1]))
    mine, got_queries[-1] = own_part, tuple(given)
    arrived = [packed[:own_slots], parts] + [swap(parts, "query", flip) for flip in range(1, replicas)]
    mine = mine + swap(score(planes - 1), "outer", planes - 1)
    (new_table,) = call(
        apply_kernel, "apply", [jax.ShapeDtypeStruct(table.shape, bf16)], None, target, own, table, *arrived
    )
    loss = (jnp.log2(mine[0]) - mine[1]) * math.log(2.0)
    return new_table, new_ages, loss.reshape(query_count)


def solution(mesh):
    owners, replicas = mesh.shape["index"], mesh.shape["query"]
    inner = 1 << (int(math.log2(owners)) // 2)
    split = Mesh(mesh.devices.reshape(owners // inner, inner, replicas), ("outer", "inner", "query"))
    index = ("outer", "inner")
    placed = (
        P(index, None),
        P(index),
        P(index),
        P(index, None),
        P(index, None),
        P(("outer", "inner", "query"), None),
        P(("outer", "inner", "query")),
    )
    return jax.shard_map(
        on_device,
        mesh=split,
        in_specs=placed,
        out_specs=(P(index, None), P(index), P(("outer", "inner", "query"))),
        check_vma=False,
    )
```

```python
import functools
import math

import jax
import jax.numpy as jnp
from jax import lax
from jax.experimental import pallas as pl
from jax.experimental.pallas import tpu as pltpu
from jax.sharding import Mesh, PartitionSpec as P

score_scale = 20.0
age_scale = 16.0
epsilon = 1e-06
LOG2E = math.log2(math.e)
MASKED = -1e30
LANES = 128
VMEM_LIMIT = 48 * 1024 * 1024

NT = (((1,), (1,)), ((), ()))
NN = (((1,), (0,)), ((), ()))


def one_hot(ids, count):
    rows = lax.broadcasted_iota(jnp.int32, (count, ids.shape[1]), 0)
    if count <= 256:
        ids = jnp.where((ids < 0) | (ids >= count), -1, ids)
        rows, ids = rows.astype(jnp.float32).astype(jnp.bfloat16), ids.astype(jnp.float32).astype(jnp.bfloat16)
        return jnp.where(rows == ids, jnp.bfloat16(1), jnp.bfloat16(0))
    return jnp.where(rows == ids, 1.0, 0.0).astype(jnp.bfloat16)


def counted(hits):
    count = hits.shape[1]
    before = lax.broadcasted_iota(jnp.int32, (count, count), 0)
    after = lax.broadcasted_iota(jnp.int32, (count, count), 1)
    earlier = jnp.where(before < after, 1.0, 0.0).astype(jnp.bfloat16)
    return lax.dot_general(hits.astype(jnp.bfloat16), earlier, NN, preferred_element_type=jnp.float32)


def small(values):
    return values.astype(jnp.float32).astype(jnp.bfloat16)


def owner_ranks(rows, refresh_dev, cap):
    match = jnp.concatenate(rows, axis=0) == 0
    rank = counted(jnp.where(match, 1.0, 0.0)).astype(jnp.int32)
    return jnp.where(match, rank, -cap)


def one_hots(ids, high_count):
    return one_hot(ids >> 7, high_count), one_hot(ids & 127, LANES)


def bitmap(ids, high_count):
    high, low = one_hots(ids, high_count)
    return lax.dot_general(low, high, NT, preferred_element_type=jnp.float32).astype(jnp.bfloat16)


def lookup(one_map, pair):
    hit = lax.dot_general(one_map, pair[0], NN, preferred_element_type=jnp.float32)
    return jnp.sum(hit * pair[1].astype(jnp.float32), axis=0, keepdims=True)


def prep_kernel(place, table, fresh, ages, ref_ids, rows_out, meta_out, *, replicas):
    core = place[2]
    row = 0
    for source in (table, fresh):
        half = source.shape[0] // replicas
        rows_out[row : row + half, :] = source[pl.ds(pl.multiple_of(core * half, half), half), :]
        row += half
    width = table.shape[1]
    ref_rows, age_rows = ref_ids.shape[0], ages.shape[0]
    meta_out[:ref_rows, :] = ref_ids[...].astype(jnp.float32)
    weight = jnp.exp(-ages[...].astype(jnp.float32) / age_scale).astype(jnp.bfloat16).astype(jnp.float32)
    meta_out[ref_rows : ref_rows + age_rows, :] = jnp.log2(weight)
    line = ref_rows + age_rows
    for source in (table, fresh):
        for block in range(source.shape[0] // LANES):
            squares = jnp.zeros((LANES, LANES), jnp.float32)
            for chunk in range(width // LANES):
                values = source[block * LANES : (block + 1) * LANES, chunk * LANES : (chunk + 1) * LANES]
                values = values.astype(jnp.float32)
                squares += values * values
            mean = jnp.sum(squares.T, axis=0, keepdims=True) / width
            meta_out[line : line + 1, :] = lax.rsqrt(mean + epsilon) * (score_scale / width * LOG2E)
            line += 1


def meta_kernel(
    place, ref_ids, neg, log_weight, ages, lw_out, row_out, code_out, target_out, own_out, ages_out,
    *, rows_dev, refresh_dev, cap, replicas
):
    outer, inner, core = place[0], place[1], place[2]
    planes, plane_refresh = ref_ids.shape
    plane_rows = log_weight.shape[1]
    owners_plane = plane_rows // rows_dev
    high_count = planes * plane_rows // LANES
    own_owner = outer * owners_plane + inner
    share = cap // replicas
    plane_ids = ref_ids[0:1, :]
    column = lax.broadcasted_iota(jnp.int32, (1, plane_rows), 1)
    table_ids = (outer * owners_plane + (inner ^ (column // rows_dev))) * rows_dev + column % rows_dev

    pair = one_hots(jnp.concatenate([table_ids, plane_ids], axis=1), high_count)
    all_ids = jnp.concatenate([ref_ids[plane : plane + 1, :] for plane in range(planes)], axis=1)
    refreshed = lookup(bitmap(all_ids, high_count), (pair[0][:, :plane_rows], pair[1][:, :plane_rows])) > 0.5
    row_out[:, :plane_rows] = jnp.where(refreshed, -1, table_ids).astype(jnp.float32)
    row_out[:, plane_rows:] = plane_ids.astype(jnp.float32)
    own_out[...] = refreshed[:, :rows_dev].astype(jnp.int32)
    ages_out[...] = jnp.where(refreshed[:, :rows_dev], 0, ages[...])
    weights = jnp.where(refreshed, MASKED, log_weight[...])
    weights = jnp.concatenate([weights, jnp.zeros((1, plane_refresh), jnp.float32)], axis=1)
    for group in range(planes):
        hit = lookup(bitmap(neg[group : group + 1, :], high_count), pair)
        lw_out[group : group + 1, :] = jnp.where(hit > 0.5, weights, MASKED)

    pairs = [(plane, side) for plane in range(planes) for side in range(owners_plane)]

    def ids_of(plane, side):
        return ref_ids[plane : plane + 1, side * refresh_dev : (side + 1) * refresh_dev]

    sent = [ids_of(0, side) // rows_dev - ((outer ^ plane) * owners_plane + inner) for plane, side in pairs]
    taken = [ids_of(plane, side) // rows_dev - own_owner for plane, side in pairs]
    rank = owner_ranks(sent + taken, refresh_dev, cap)
    own_slots = owners_plane * cap
    codes = [jnp.full((1, refresh_dev), -1, jnp.int32)] * owners_plane
    for i, (plane, side) in enumerate(pairs):
        size = share if plane else cap
        base = own_slots + ((plane - 1) * owners_plane + side) * share if plane else side * cap
        sends = rank[i : i + 1, :] - (core * share if plane else 0)
        codes[side] = jnp.where((sends >= 0) & (sends < size), base + sends, codes[side])
        took = rank[len(pairs) + i : len(pairs) + i + 1, :]
        slot = jnp.where(took < 0, -1, ((took // share) ^ core) * share + took % share if plane else took)
        row = jnp.where(took < 0, 0, ids_of(plane, side) - own_owner * rows_dev)
        kinds = lax.broadcasted_iota(jnp.int32, (8, refresh_dev), 0)
        digits = jnp.where(kinds == 0, row // 16, jnp.where(kinds == 1, row % 16, 1))
        found = lax.dot_general(small(digits), one_hot(slot, cap), NT, preferred_element_type=jnp.float32)
        found = found.astype(jnp.int32)
        target = jnp.where(found[2:3, :] > 0, found[0:1, :] * 16 + found[1:2, :], -1)
        if plane == 0:
            target_out[:, base : base + cap] = target
            continue
        for part in range(replicas):
            first = base + part * (planes - 1) * owners_plane * share
            target_out[:, first : first + share] = target[:, part * share : (part + 1) * share]
    code_out[...] = jnp.concatenate(codes, axis=1)


def piece_offset(place, piece):
    column, size, flip, by_core = piece
    if flip is None:
        return column
    column += (place[2] ^ flip) * size
    if by_core is not None:
        column += (place[2] ^ by_core) * size * 2
    return pl.multiple_of(column, size)


def pack_kernel(place, code, *refs, pieces):
    *buffers, out = refs
    selects = [
        one_hot(code[:, pl.ds(piece_offset(place, column), size)], out.shape[0]) for _, _, size, column in pieces
    ]
    values = [buffers[source][start : start + size, :] for source, start, size, _ in pieces]
    select, values = jnp.concatenate(selects, axis=1), jnp.concatenate(values, axis=0)
    out[...] = lax.dot_general(select, values, NN, preferred_element_type=jnp.float32).astype(jnp.bfloat16)


def apply_kernel(target, refreshed, table, *refs):
    *arrived, out = refs
    values = jnp.concatenate([block[...] for block in arrived], axis=0)
    rows = lax.broadcasted_iota(jnp.int32, (out.shape[0], values.shape[0]), 0)
    chosen = jnp.where(rows == target[...], 1.0, 0.0).astype(jnp.bfloat16)
    fresh = lax.dot_general(chosen, values, NN, preferred_element_type=jnp.float32)
    for top in range(0, out.shape[0], LANES):
        part = slice(top, top + LANES)
        hit = to_lanes(refreshed[:, part].astype(jnp.float32)) > 0.5
        for left in range(0, out.shape[1], LANES):
            cols = slice(left, left + LANES)
            out[part, cols] = jnp.where(hit, fresh[part, cols], table[part, cols].astype(jnp.float32)).astype(jnp.bfloat16)


def to_lanes(row):
    return jnp.broadcast_to(row, (LANES, LANES)).T


def score_kernel(place, *refs, pieces, sources):
    positive, log_weight, row_ids, scale = refs[sources : sources + 4]
    out, total, pos_total, q_scale, pos_b, chosen = refs[-6:]
    queries = refs[0]
    count, width = queries.shape
    if sources == 2:
        at_end = (place[0] == 0) | (place[0] == 3)
        chosen[...] = jnp.where(at_end, refs[0][...], refs[1][...])
        queries = chosen
    for block in range(count // LANES):
        part = slice(block * LANES, (block + 1) * LANES)
        values = queries[part, :].astype(jnp.float32)
        squares = jnp.sum(values * values, axis=1, keepdims=True)
        q_scale[part, :] = jnp.broadcast_to(lax.rsqrt(squares / width + epsilon), (LANES, LANES))
        pos_b[part, :] = to_lanes(positive[block : block + 1, :])
    total[...] = jnp.zeros_like(total)
    pos_total[...] = jnp.zeros_like(pos_total)
    refs = refs[sources + 4 : -6]

    def product(group):
        rows = [refs[source][start : start + size, :] for source, start, size, _ in group]
        rows = rows[0] if len(rows) == 1 else jnp.concatenate(rows, axis=0)
        return lax.dot_general(queries[...], rows, NT, preferred_element_type=jnp.float32)

    narrow = [piece for piece in pieces if piece[2] < 256]
    groups = [[piece] for piece in pieces if piece[2] >= 256] + [narrow[i : i + 2] for i in range(0, len(narrow), 2)]
    following = product(groups[0])
    for i, group in enumerate(groups):
        raw = following
        if i + 1 < len(groups):
            following = product(groups[i + 1])
        columns = []
        for _, _, size, column in group:
            columns += [piece_offset(place, column) + chunk * LANES for chunk in range(size // LANES)]
        for top in range(0, count, 64):
            part = slice(top, top + 64)
            sums, positives = total[part, :], pos_total[part, :]
            query_scale, wanted = q_scale[part, :], pos_b[part, :]
            for chunk, first in enumerate(columns):
                cols = pl.ds(first, LANES)
                powers = raw[part, chunk * LANES : (chunk + 1) * LANES] * query_scale
                powers = powers * scale[:, cols] + log_weight[:, cols]
                sums = sums + jnp.exp2(powers)
                positives = positives + jnp.where(wanted == row_ids[:, cols], powers, 0.0)
            total[part, :] = sums
            pos_total[part, :] = positives
    for block in range(count // LANES):
        part = slice(block * LANES, (block + 1) * LANES)
        out[0, block : block + 1, :] = jnp.sum(total[part, :].T, axis=0, keepdims=True)
        out[1, block : block + 1, :] = jnp.sum(pos_total[part, :].T, axis=0, keepdims=True)


def whole(memory=pltpu.VMEM):
    return pl.BlockSpec(memory_space=memory)


def call(kernel, name, outs, place, *operands, scratch=(), **options):
    specs = [whole()] * len(operands)
    if place is not None:
        specs = [whole(pltpu.SMEM)] + specs
        operands = (place, *operands)
    return pl.pallas_call(
        functools.partial(kernel, **options),
        out_shape=tuple(outs),
        in_specs=specs,
        out_specs=tuple(whole() for _ in outs),
        scratch_shapes=list(scratch),
        compiler_params=pltpu.CompilerParams(vmem_limit_bytes=VMEM_LIMIT),
        cost_estimate=pl.CostEstimate(flops=1, bytes_accessed=1, transcendentals=0),
        name=name,
    )(*operands)


def swap(values, axis, flip):
    return lax.ppermute(values, axis, [(i, i ^ flip) for i in range(lax.axis_size(axis))])


def gather_line(values, small):
    planes = lax.axis_size("outer")
    if planes != 4:
        return [(swap(values, "outer", s),) for s in range(1, planes)], small
    middle, outward = [(1, 2), (2, 1)], [(1, 0), (2, 3)]
    beside = swap(values, "outer", 1)
    across = lax.ppermute(values, "outer", middle)
    beside, across, *small = lax.optimization_barrier((beside, across, *small))
    from_end = lax.ppermute(beside, "outer", middle)
    to_end = lax.ppermute(across, "outer", outward)
    last = lax.ppermute(from_end, "outer", outward)
    return [(beside,), (to_end, from_end), (last, across)], small


def on_device(table, ages, refresh_ids, fresh_rows, neg_ids, queries, pos_ids):
    rows_dev, width = table.shape
    refresh_dev = refresh_ids.shape[0]
    planes = lax.axis_size("outer")
    owners_plane = lax.axis_size("inner")
    replicas = lax.axis_size("query")
    owners = planes * owners_plane
    query_count = queries.shape[0]
    list_size = neg_ids.shape[1]
    place = jnp.stack([lax.axis_index(name) for name in ("outer", "inner", "query")]).astype(jnp.int32)
    plane_rows = owners_plane * rows_dev
    plane_refresh = owners_plane * refresh_dev
    all_rows = plane_rows + plane_refresh
    cap = max(2, (2 * refresh_dev + owners - 1) // owners)
    share = cap // replicas
    table_half, fresh_half = rows_dev // replicas, refresh_dev // replicas
    bf16, f32 = jnp.bfloat16, jnp.float32

    meta_lines = (2 * refresh_dev + 2 * rows_dev) // LANES
    rows_half, meta = call(
        prep_kernel,
        "prep",
        [jax.ShapeDtypeStruct((table_half + fresh_half, width), bf16), jax.ShapeDtypeStruct((meta_lines, LANES), f32)],
        place,
        table,
        fresh_rows,
        ages.reshape(-1, LANES),
        refresh_ids.reshape(-1, LANES),
        replicas=replicas,
    )
    metas = jnp.stack([meta] + [swap(meta, "inner", s) for s in range(1, owners_plane)])
    cuts = [refresh_dev, rows_dev, rows_dev, refresh_dev]
    ends = [sum(cuts[: i + 1]) // LANES for i in range(len(cuts))]

    def piece(i):
        return metas[:, ends[i] - cuts[i] // LANES : ends[i]].reshape(1, -1)

    ref_plane, log_weight_plane = piece(0), piece(1)
    scale_plane = jnp.concatenate([piece(2), piece(3)], axis=1)
    line = jnp.concatenate([ref_plane[0], neg_ids[0].astype(f32), pos_ids.astype(f32)])
    lines = [line] + [swap(line, "outer", s) for s in range(1, planes)]
    got_queries, lines = gather_line(queries, lines)
    got_queries = [(queries,)] + got_queries
    lines = jnp.stack(lines)
    ref_all = lines[:, :plane_refresh].astype(jnp.int32)
    neg_line = lines[:, plane_refresh : plane_refresh + list_size].astype(jnp.int32)
    positive = lines[:, plane_refresh + list_size :].reshape(planes, -1, LANES)

    own_slots, part_slots = owners_plane * cap, owners_plane * share
    lw, row_ids, code, target, own, new_ages = call(
        meta_kernel,
        "meta",
        [
            jax.ShapeDtypeStruct((planes, all_rows), f32),
            jax.ShapeDtypeStruct((1, all_rows), f32),
            jax.ShapeDtypeStruct((1, plane_refresh), jnp.int32),
            jax.ShapeDtypeStruct((1, planes * own_slots), jnp.int32),
            jax.ShapeDtypeStruct((1, rows_dev), jnp.int32),
            jax.ShapeDtypeStruct((1, rows_dev), jnp.int32),
        ],
        place,
        ref_all,
        neg_line,
        log_weight_plane,
        ages.reshape(1, -1),
        rows_dev=rows_dev,
        refresh_dev=refresh_dev,
        cap=cap,
        replicas=replicas,
    )
    new_ages = new_ages.reshape(rows_dev)

    if replicas == 2 and owners_plane == 4:
        axes = ("inner", "query")
        first = [(2 * i + c, 2 * (i ^ (1 + c)) + c) for i in range(4) for c in range(2)]
        second = [(2 * i + c, 2 * (i ^ (2 - c)) + c) for i in range(4) for c in range(2)]
        near = lax.ppermute(rows_half, axes, first)
        near, rows_half, _ = lax.optimization_barrier((near, rows_half, metas))
        side = lax.ppermute(rows_half, axes, second)
        far = lax.ppermute(near, axes, second)
        buffers = [table, fresh_rows]
        table_pieces = [(0, 0, rows_dev, (0, rows_dev, None, None))]
        fresh_pieces = [(1, 0, refresh_dev, (0, refresh_dev, None, None))]
        for slot, by_core, mine in ((1, 0, near), (1, 1, side), (3, None, far)):
            for flip, rows in enumerate((mine, swap(mine, "query", 1))):
                by = None if by_core is None else by_core ^ flip
                table_pieces.append((len(buffers), 0, table_half, (slot * rows_dev, table_half, flip, by)))
                fresh_pieces.append((len(buffers), table_half, fresh_half, (slot * refresh_dev, fresh_half, flip, by)))
                buffers.append(rows)
    else:
        got_rows = [rows_half] + [swap(rows_half, "inner", s) for s in range(1, owners_plane)]
        gathered = lax.all_gather(jnp.stack(got_rows), "query", axis=0)
        gathered = jnp.swapaxes(gathered, 0, 1)
        buffers = [
            gathered[:, :, :table_half].reshape(plane_rows, width),
            gathered[:, :, table_half:].reshape(plane_refresh, width),
        ]
        table_pieces = [(0, i * 512, 512, (i * 512, 512, None, None)) for i in range(plane_rows // 512)]
        fresh_pieces = [(1, i * 512, 512, (i * 512, 512, None, None)) for i in range(plane_refresh // 512)]

    def shift(pieces, columns):
        return [(a, b, c, (d[0] + columns, *d[1:])) for a, b, c, d in pieces]

    (packed,) = call(
        pack_kernel,
        "pack",
        [jax.ShapeDtypeStruct((own_slots + (planes - 1) * part_slots, width), bf16)],
        place,
        code,
        *buffers,
        pieces=fresh_pieces,
    )
    packed, row_ids = lax.optimization_barrier((packed, row_ids))
    parts = []
    for s in range(1, planes):
        first = own_slots + (s - 1) * part_slots
        parts.append(swap(packed[first : first + part_slots], "outer", s))
    parts = jnp.concatenate(parts)
    pieces = table_pieces + shift(fresh_pieces, plane_rows)

    def score(s):
        (partial,) = call(
            score_kernel,
            "score",
            [jax.ShapeDtypeStruct((2, query_count // LANES, LANES), f32)],
            place,
            *got_queries[s],
            positive[s],
            lw[s : s + 1],
            row_ids,
            scale_plane,
            *buffers,
            scratch=[pltpu.VMEM((query_count, LANES), f32)] * 4 + [pltpu.VMEM((query_count, width), bf16)],
            pieces=pieces,
            sources=len(got_queries[s]),
        )
        return partial

    partials = [score(s) for s in range(planes - 1)]
    parts, own_part, *given = lax.optimization_barrier((parts, partials[0], *got_queries[-1]))
    got_queries[-1] = tuple(given)
    arrived = [packed[:own_slots], parts] + [swap(parts, "query", flip) for flip in range(1, replicas)]
    mine = own_part
    for s in range(1, planes - 1):
        mine = mine + swap(partials[s], "outer", s)
    mine = mine + swap(score(planes - 1), "outer", planes - 1)
    (new_table,) = call(
        apply_kernel, "apply", [jax.ShapeDtypeStruct(table.shape, bf16)], None, target, own, table, *arrived
    )
    loss = (jnp.log2(mine[0]) - mine[1]) * math.log(2.0)
    return new_table, new_ages, loss.reshape(query_count)


def solution(mesh):
    owners, replicas = mesh.shape["index"], mesh.shape["query"]
    inner = 1 << (int(math.log2(owners)) // 2)
    split = Mesh(mesh.devices.reshape(owners // inner, inner, replicas), ("outer", "inner", "query"))
    index = ("outer", "inner")
    placed = (
        P(index, None),
        P(index),
        P(index),
        P(index, None),
        P(index, None),
        P(("outer", "inner", "query"), None),
        P(("outer", "inner", "query")),
    )
    return jax.shard_map(
        on_device,
        mesh=split,
        in_specs=placed,
        out_specs=(P(index, None), P(index), P(("outer", "inner", "query"))),
        check_vma=False,
    )
```

```python
import functools
import math

import jax
import jax.numpy as jnp
from jax import lax
from jax.experimental import pallas as pl
from jax.experimental.pallas import tpu as pltpu
from jax.sharding import Mesh, PartitionSpec as P

score_scale = 20.0
age_scale = 16.0
epsilon = 1e-06
LOG2E = math.log2(math.e)
MASKED = -1e30
LANES = 128
VMEM_LIMIT = 48 * 1024 * 1024

NT = (((1,), (1,)), ((), ()))
NN = (((1,), (0,)), ((), ()))


def one_hot(ids, count):
    rows = lax.broadcasted_iota(jnp.int32, (count, ids.shape[1]), 0)
    if count <= 256:
        ids = jnp.where((ids < 0) | (ids >= count), -1, ids)
        rows, ids = rows.astype(jnp.float32).astype(jnp.bfloat16), ids.astype(jnp.float32).astype(jnp.bfloat16)
        return jnp.where(rows == ids, jnp.bfloat16(1), jnp.bfloat16(0))
    return jnp.where(rows == ids, 1.0, 0.0).astype(jnp.bfloat16)


def counted(hits):
    count = hits.shape[1]
    before = lax.broadcasted_iota(jnp.int32, (count, count), 0)
    after = lax.broadcasted_iota(jnp.int32, (count, count), 1)
    earlier = jnp.where(before < after, 1.0, 0.0).astype(jnp.bfloat16)
    return lax.dot_general(hits.astype(jnp.bfloat16), earlier, NN, preferred_element_type=jnp.float32)


def small(values):
    return values.astype(jnp.float32).astype(jnp.bfloat16)


def owner_ranks(rows, refresh_dev, cap):
    match = jnp.concatenate(rows, axis=0) == 0
    rank = counted(jnp.where(match, 1.0, 0.0)).astype(jnp.int32)
    return jnp.where(match, rank, -cap)


def one_hots(ids, high_count):
    return one_hot(ids >> 7, high_count), one_hot(ids & 127, LANES)


def bitmap(ids, high_count):
    high, low = one_hots(ids, high_count)
    return lax.dot_general(low, high, NT, preferred_element_type=jnp.float32).astype(jnp.bfloat16)


def lookup(one_map, pair):
    hit = lax.dot_general(one_map, pair[0], NN, preferred_element_type=jnp.float32)
    return jnp.sum(hit * pair[1].astype(jnp.float32), axis=0, keepdims=True)


def prep_kernel(place, table, fresh, ages, ref_ids, rows_out, meta_out, *, replicas):
    core = place[2]
    row = 0
    for source in (table, fresh):
        half = source.shape[0] // replicas
        rows_out[row : row + half, :] = source[pl.ds(pl.multiple_of(core * half, half), half), :]
        row += half
    width = table.shape[1]
    ref_rows, age_rows = ref_ids.shape[0], ages.shape[0]
    meta_out[:ref_rows, :] = ref_ids[...].astype(jnp.float32)
    weight = jnp.exp(-ages[...].astype(jnp.float32) / age_scale).astype(jnp.bfloat16).astype(jnp.float32)
    meta_out[ref_rows : ref_rows + age_rows, :] = jnp.log2(weight)
    line = ref_rows + age_rows
    for source in (table, fresh):
        for block in range(source.shape[0] // LANES):
            squares = jnp.zeros((LANES, LANES), jnp.float32)
            for chunk in range(width // LANES):
                values = source[block * LANES : (block + 1) * LANES, chunk * LANES : (chunk + 1) * LANES]
                values = values.astype(jnp.float32)
                squares += values * values
            mean = jnp.sum(squares.T, axis=0, keepdims=True) / width
            meta_out[line : line + 1, :] = lax.rsqrt(mean + epsilon) * (score_scale / width * LOG2E)
            line += 1


def meta_kernel(
    place, ref_ids, neg, log_weight, ages, lw_out, row_out, code_out, target_out, own_out, ages_out,
    *, rows_dev, refresh_dev, cap, replicas
):
    outer, inner, core = place[0], place[1], place[2]
    planes, plane_refresh = ref_ids.shape
    plane_rows = log_weight.shape[1]
    owners_plane = plane_rows // rows_dev
    high_count = planes * plane_rows // LANES
    own_owner = outer * owners_plane + inner
    share = cap // replicas
    plane_ids = ref_ids[0:1, :]
    column = lax.broadcasted_iota(jnp.int32, (1, plane_rows), 1)
    table_ids = (outer * owners_plane + (inner ^ (column // rows_dev))) * rows_dev + column % rows_dev

    pair = one_hots(jnp.concatenate([table_ids, plane_ids], axis=1), high_count)
    all_ids = jnp.concatenate([ref_ids[plane : plane + 1, :] for plane in range(planes)], axis=1)
    refreshed = lookup(bitmap(all_ids, high_count), (pair[0][:, :plane_rows], pair[1][:, :plane_rows])) > 0.5
    row_out[:, :plane_rows] = jnp.where(refreshed, -1, table_ids).astype(jnp.float32)
    row_out[:, plane_rows:] = plane_ids.astype(jnp.float32)
    own_out[...] = refreshed[:, :rows_dev].astype(jnp.int32)
    ages_out[...] = jnp.where(refreshed[:, :rows_dev], 0, ages[...])
    weights = jnp.where(refreshed, MASKED, log_weight[...])
    weights = jnp.concatenate([weights, jnp.zeros((1, plane_refresh), jnp.float32)], axis=1)
    for group in range(planes):
        hit = lookup(bitmap(neg[group : group + 1, :], high_count), pair)
        lw_out[group : group + 1, :] = jnp.where(hit > 0.5, weights, MASKED)

    pairs = [(plane, side) for plane in range(planes) for side in range(owners_plane)]

    def ids_of(plane, side):
        return ref_ids[plane : plane + 1, side * refresh_dev : (side + 1) * refresh_dev]

    sent = [ids_of(0, side) // rows_dev - ((outer ^ plane) * owners_plane + inner) for plane, side in pairs]
    taken = [ids_of(plane, side) // rows_dev - own_owner for plane, side in pairs]
    rank = owner_ranks(sent + taken, refresh_dev, cap)
    own_slots = owners_plane * cap
    codes = [jnp.full((1, refresh_dev), -1, jnp.int32)] * owners_plane
    for i, (plane, side) in enumerate(pairs):
        size = share if plane else cap
        base = own_slots + ((plane - 1) * owners_plane + side) * share if plane else side * cap
        sends = rank[i : i + 1, :] - (core * share if plane else 0)
        codes[side] = jnp.where((sends >= 0) & (sends < size), base + sends, codes[side])
        took = rank[len(pairs) + i : len(pairs) + i + 1, :]
        slot = jnp.where(took < 0, -1, ((took // share) ^ core) * share + took % share if plane else took)
        row = jnp.where(took < 0, 0, ids_of(plane, side) - own_owner * rows_dev)
        kinds = lax.broadcasted_iota(jnp.int32, (8, refresh_dev), 0)
        digits = jnp.where(kinds == 0, row // 16, jnp.where(kinds == 1, row % 16, 1))
        found = lax.dot_general(small(digits), one_hot(slot, cap), NT, preferred_element_type=jnp.float32)
        found = found.astype(jnp.int32)
        target = jnp.where(found[2:3, :] > 0, found[0:1, :] * 16 + found[1:2, :], -1)
        if plane == 0:
            target_out[:, base : base + cap] = target
            continue
        for part in range(replicas):
            first = base + part * (planes - 1) * owners_plane * share
            target_out[:, first : first + share] = target[:, part * share : (part + 1) * share]
    code_out[...] = jnp.concatenate(codes, axis=1)


def piece_offset(place, piece):
    column, size, flip, by_core = piece
    if flip is None:
        return column
    column += (place[2] ^ flip) * size
    if by_core is not None:
        column += (place[2] ^ by_core) * size * 2
    return pl.multiple_of(column, size)


def pack_kernel(place, code, *refs, pieces):
    *buffers, out = refs
    selects = [
        one_hot(code[:, pl.ds(piece_offset(place, column), size)], out.shape[0]) for _, _, size, column in pieces
    ]
    values = [buffers[source][start : start + size, :] for source, start, size, _ in pieces]
    select, values = jnp.concatenate(selects, axis=1), jnp.concatenate(values, axis=0)
    out[...] = lax.dot_general(select, values, NN, preferred_element_type=jnp.float32).astype(jnp.bfloat16)


def apply_kernel(target, refreshed, table, *refs):
    *arrived, out = refs
    values = jnp.concatenate([block[...] for block in arrived], axis=0)
    rows = lax.broadcasted_iota(jnp.int32, (out.shape[0], values.shape[0]), 0)
    chosen = jnp.where(rows == target[...], 1.0, 0.0).astype(jnp.bfloat16)
    fresh = lax.dot_general(chosen, values, NN, preferred_element_type=jnp.float32)
    for top in range(0, out.shape[0], LANES):
        part = slice(top, top + LANES)
        hit = to_lanes(refreshed[:, part].astype(jnp.float32)) > 0.5
        for left in range(0, out.shape[1], LANES):
            cols = slice(left, left + LANES)
            out[part, cols] = jnp.where(hit, fresh[part, cols], table[part, cols].astype(jnp.float32)).astype(jnp.bfloat16)


def to_lanes(row):
    return jnp.broadcast_to(row, (LANES, LANES)).T


def score_kernel(place, *refs, pieces, sources):
    positive, log_weight, row_ids, scale = refs[sources : sources + 4]
    out, total, pos_total, q_scale, pos_b, chosen = refs[-6:]
    queries = refs[0]
    count, width = queries.shape
    if sources == 2:
        at_end = (place[0] == 0) | (place[0] == 3)
        chosen[...] = jnp.where(at_end, refs[0][...], refs[1][...])
        queries = chosen
    for block in range(count // LANES):
        part = slice(block * LANES, (block + 1) * LANES)
        values = queries[part, :].astype(jnp.float32)
        squares = jnp.sum(values * values, axis=1, keepdims=True)
        q_scale[part, :] = jnp.broadcast_to(lax.rsqrt(squares / width + epsilon), (LANES, LANES))
        pos_b[part, :] = to_lanes(positive[block : block + 1, :])
    total[...] = jnp.zeros_like(total)
    pos_total[...] = jnp.zeros_like(pos_total)
    refs = refs[sources + 4 : -6]

    def product(group):
        rows = [refs[source][start : start + size, :] for source, start, size, _ in group]
        rows = rows[0] if len(rows) == 1 else jnp.concatenate(rows, axis=0)
        return lax.dot_general(queries[...], rows, NT, preferred_element_type=jnp.float32)

    narrow = [piece for piece in pieces if piece[2] < 256]
    groups = [[piece] for piece in pieces if piece[2] >= 256] + [narrow[i : i + 2] for i in range(0, len(narrow), 2)]
    following = product(groups[0])
    for i, group in enumerate(groups):
        raw = following
        if i + 1 < len(groups):
            following = product(groups[i + 1])
        columns = []
        for _, _, size, column in group:
            columns += [piece_offset(place, column) + chunk * LANES for chunk in range(size // LANES)]
        for top in range(0, count, 64):
            part = slice(top, top + 64)
            sums, positives = total[part, :], pos_total[part, :]
            query_scale, wanted = q_scale[part, :], pos_b[part, :]
            for chunk, first in enumerate(columns):
                cols = pl.ds(first, LANES)
                powers = raw[part, chunk * LANES : (chunk + 1) * LANES] * query_scale
                powers = powers * scale[:, cols] + log_weight[:, cols]
                sums = sums + jnp.exp2(powers)
                positives = positives + jnp.where(wanted == row_ids[:, cols], powers, 0.0)
            total[part, :] = sums
            pos_total[part, :] = positives
    for block in range(count // LANES):
        part = slice(block * LANES, (block + 1) * LANES)
        out[0, block : block + 1, :] = jnp.sum(total[part, :].T, axis=0, keepdims=True)
        out[1, block : block + 1, :] = jnp.sum(pos_total[part, :].T, axis=0, keepdims=True)


def whole(memory=pltpu.VMEM):
    return pl.BlockSpec(memory_space=memory)


def call(kernel, name, outs, place, *operands, scratch=(), **options):
    specs = [whole()] * len(operands)
    if place is not None:
        specs = [whole(pltpu.SMEM)] + specs
        operands = (place, *operands)
    return pl.pallas_call(
        functools.partial(kernel, **options),
        out_shape=tuple(outs),
        in_specs=specs,
        out_specs=tuple(whole() for _ in outs),
        scratch_shapes=list(scratch),
        compiler_params=pltpu.CompilerParams(vmem_limit_bytes=VMEM_LIMIT),
        cost_estimate=pl.CostEstimate(flops=1, bytes_accessed=1, transcendentals=0),
        name=name,
    )(*operands)


def swap(values, axis, flip):
    return lax.ppermute(values, axis, [(i, i ^ flip) for i in range(lax.axis_size(axis))])


def gather_line(values, small):
    planes = lax.axis_size("outer")
    if planes != 4:
        return [(swap(values, "outer", s),) for s in range(1, planes)], small
    middle, outward = [(1, 2), (2, 1)], [(1, 0), (2, 3)]
    beside = swap(values, "outer", 1)
    across = lax.ppermute(values, "outer", middle)
    beside, across, *small = lax.optimization_barrier((beside, across, *small))
    from_end = lax.ppermute(beside, "outer", middle)
    to_end = lax.ppermute(across, "outer", outward)
    last = lax.ppermute(from_end, "outer", outward)
    return [(beside,), (to_end, from_end), (last, across)], small


def on_device(table, ages, refresh_ids, fresh_rows, neg_ids, queries, pos_ids):
    rows_dev, width = table.shape
    refresh_dev = refresh_ids.shape[0]
    planes = lax.axis_size("outer")
    owners_plane = lax.axis_size("inner")
    replicas = lax.axis_size("query")
    owners = planes * owners_plane
    query_count = queries.shape[0]
    list_size = neg_ids.shape[1]
    place = jnp.stack([lax.axis_index(name) for name in ("outer", "inner", "query")]).astype(jnp.int32)
    plane_rows = owners_plane * rows_dev
    plane_refresh = owners_plane * refresh_dev
    all_rows = plane_rows + plane_refresh
    cap = max(2, (2 * refresh_dev + owners - 1) // owners)
    share = cap // replicas
    table_half, fresh_half = rows_dev // replicas, refresh_dev // replicas
    bf16, f32 = jnp.bfloat16, jnp.float32

    meta_lines = (2 * refresh_dev + 2 * rows_dev) // LANES
    rows_half, meta = call(
        prep_kernel,
        "prep",
        [jax.ShapeDtypeStruct((table_half + fresh_half, width), bf16), jax.ShapeDtypeStruct((meta_lines, LANES), f32)],
        place,
        table,
        fresh_rows,
        ages.reshape(-1, LANES),
        refresh_ids.reshape(-1, LANES),
        replicas=replicas,
    )
    metas = jnp.stack([meta] + [swap(meta, "inner", s) for s in range(1, owners_plane)])
    cuts = [refresh_dev, rows_dev, rows_dev, refresh_dev]
    ends = [sum(cuts[: i + 1]) // LANES for i in range(len(cuts))]

    def piece(i):
        return metas[:, ends[i] - cuts[i] // LANES : ends[i]].reshape(1, -1)

    ref_plane, log_weight_plane = piece(0), piece(1)
    scale_plane = jnp.concatenate([piece(2), piece(3)], axis=1)
    line = jnp.concatenate([ref_plane[0], neg_ids[0].astype(f32), pos_ids.astype(f32)])
    lines = [line] + [swap(line, "outer", s) for s in range(1, planes)]
    fast = replicas == 2 and owners_plane == 4
    if fast:
        axes = ("inner", "query")
        first = [(2 * i + c, 2 * (i ^ (1 + c)) + c) for i in range(4) for c in range(2)]
        second = [(2 * i + c, 2 * (i ^ (2 - c)) + c) for i in range(4) for c in range(2)]
        near = lax.ppermute(rows_half, axes, first)
        lines += [near, rows_half]
    got_queries, lines = gather_line(queries, lines)
    if fast:
        *lines, near, rows_half = lines
    got_queries = [(queries,)] + got_queries
    lines = jnp.stack(lines)
    ref_all = lines[:, :plane_refresh].astype(jnp.int32)
    neg_line = lines[:, plane_refresh : plane_refresh + list_size].astype(jnp.int32)
    positive = lines[:, plane_refresh + list_size :].reshape(planes, -1, LANES)

    own_slots, part_slots = owners_plane * cap, owners_plane * share
    lw, row_ids, code, target, own, new_ages = call(
        meta_kernel,
        "meta",
        [
            jax.ShapeDtypeStruct((planes, all_rows), f32),
            jax.ShapeDtypeStruct((1, all_rows), f32),
            jax.ShapeDtypeStruct((1, plane_refresh), jnp.int32),
            jax.ShapeDtypeStruct((1, planes * own_slots), jnp.int32),
            jax.ShapeDtypeStruct((1, rows_dev), jnp.int32),
            jax.ShapeDtypeStruct((1, rows_dev), jnp.int32),
        ],
        place,
        ref_all,
        neg_line,
        log_weight_plane,
        ages.reshape(1, -1),
        rows_dev=rows_dev,
        refresh_dev=refresh_dev,
        cap=cap,
        replicas=replicas,
    )
    new_ages = new_ages.reshape(rows_dev)

    if fast:
        side = lax.ppermute(rows_half, axes, second)
        far = lax.ppermute(near, axes, second)
        side, far, lw, got_queries[2] = lax.optimization_barrier((side, far, lw, got_queries[2]))
        buffers = [table, fresh_rows]
        table_pieces = [(0, 0, rows_dev, (0, rows_dev, None, None))]
        fresh_pieces = [(1, 0, refresh_dev, (0, refresh_dev, None, None))]
        for slot, by_core, mine in ((1, 0, near), (1, 1, side), (3, None, far)):
            for flip, rows in enumerate((mine, swap(mine, "query", 1))):
                by = None if by_core is None else by_core ^ flip
                table_pieces.append((len(buffers), 0, table_half, (slot * rows_dev, table_half, flip, by)))
                fresh_pieces.append((len(buffers), table_half, fresh_half, (slot * refresh_dev, fresh_half, flip, by)))
                buffers.append(rows)
    else:
        got_rows = [rows_half] + [swap(rows_half, "inner", s) for s in range(1, owners_plane)]
        gathered = lax.all_gather(jnp.stack(got_rows), "query", axis=0)
        gathered = jnp.swapaxes(gathered, 0, 1)
        buffers = [
            gathered[:, :, :table_half].reshape(plane_rows, width),
            gathered[:, :, table_half:].reshape(plane_refresh, width),
        ]
        table_pieces = [(0, i * 512, 512, (i * 512, 512, None, None)) for i in range(plane_rows // 512)]
        fresh_pieces = [(1, i * 512, 512, (i * 512, 512, None, None)) for i in range(plane_refresh // 512)]

    def shift(pieces, columns):
        return [(a, b, c, (d[0] + columns, *d[1:])) for a, b, c, d in pieces]

    (packed,) = call(
        pack_kernel,
        "pack",
        [jax.ShapeDtypeStruct((own_slots + (planes - 1) * part_slots, width), bf16)],
        place,
        code,
        *buffers,
        pieces=fresh_pieces,
    )
    packed, row_ids = lax.optimization_barrier((packed, row_ids))
    parts = []
    for s in range(1, planes):
        first = own_slots + (s - 1) * part_slots
        parts.append(swap(packed[first : first + part_slots], "outer", s))
    parts = jnp.concatenate(parts)
    pieces = table_pieces + shift(fresh_pieces, plane_rows)

    def score(s):
        (partial,) = call(
            score_kernel,
            "score",
            [jax.ShapeDtypeStruct((2, query_count // LANES, LANES), f32)],
            place,
            *got_queries[s],
            positive[s],
            lw[s : s + 1],
            row_ids,
            scale_plane,
            *buffers,
            scratch=[pltpu.VMEM((query_count, LANES), f32)] * 4 + [pltpu.VMEM((query_count, width), bf16)],
            pieces=pieces,
            sources=len(got_queries[s]),
        )
        return partial

    partials = [score(s) for s in range(planes - 1)]
    parts, own_part, *given = lax.optimization_barrier((parts, partials[0], *got_queries[-1]))
    got_queries[-1] = tuple(given)
    arrived = [packed[:own_slots], parts] + [swap(parts, "query", flip) for flip in range(1, replicas)]
    mine = own_part
    for s in range(1, planes - 1):
        mine = mine + swap(partials[s], "outer", s)
    mine = mine + swap(score(planes - 1), "outer", planes - 1)
    (new_table,) = call(
        apply_kernel, "apply", [jax.ShapeDtypeStruct(table.shape, bf16)], None, target, own, table, *arrived
    )
    loss = (jnp.log2(mine[0]) - mine[1]) * math.log(2.0)
    return new_table, new_ages, loss.reshape(query_count)


def solution(mesh):
    owners, replicas = mesh.shape["index"], mesh.shape["query"]
    inner = 1 << (int(math.log2(owners)) // 2)
    split = Mesh(mesh.devices.reshape(owners // inner, inner, replicas), ("outer", "inner", "query"))
    index = ("outer", "inner")
    placed = (
        P(index, None),
        P(index),
        P(index),
        P(index, None),
        P(index, None),
        P(("outer", "inner", "query"), None),
        P(("outer", "inner", "query")),
    )
    return jax.shard_map(
        on_device,
        mesh=split,
        in_specs=placed,
        out_specs=(P(index, None), P(index), P(("outer", "inner", "query"))),
        check_vma=False,
    )
```

```python
import functools
import math

import jax
import jax.numpy as jnp
from jax import lax
from jax.experimental import pallas as pl
from jax.experimental.pallas import tpu as pltpu
from jax.sharding import Mesh, PartitionSpec as P

score_scale = 20.0
age_scale = 16.0
epsilon = 1e-06
LOG2E = math.log2(math.e)
MASKED = -1e30
LANES = 128
VMEM_LIMIT = 48 * 1024 * 1024

NT = (((1,), (1,)), ((), ()))
NN = (((1,), (0,)), ((), ()))


def one_hot(ids, count):
    rows = lax.broadcasted_iota(jnp.int32, (count, ids.shape[1]), 0)
    if count <= 256:
        ids = jnp.where((ids < 0) | (ids >= count), -1, ids)
        rows, ids = rows.astype(jnp.float32).astype(jnp.bfloat16), ids.astype(jnp.float32).astype(jnp.bfloat16)
        return jnp.where(rows == ids, jnp.bfloat16(1), jnp.bfloat16(0))
    return jnp.where(rows == ids, 1.0, 0.0).astype(jnp.bfloat16)


def counted(hits):
    count = hits.shape[1]
    before = lax.broadcasted_iota(jnp.int32, (count, count), 0)
    after = lax.broadcasted_iota(jnp.int32, (count, count), 1)
    earlier = jnp.where(before < after, 1.0, 0.0).astype(jnp.bfloat16)
    return lax.dot_general(hits.astype(jnp.bfloat16), earlier, NN, preferred_element_type=jnp.float32)


def small(values):
    return values.astype(jnp.float32).astype(jnp.bfloat16)


def owner_ranks(rows, refresh_dev, cap):
    match = jnp.concatenate(rows, axis=0) == 0
    rank = counted(jnp.where(match, 1.0, 0.0)).astype(jnp.int32)
    return jnp.where(match, rank, -cap)


def one_hots(ids, high_count):
    return one_hot(ids >> 7, high_count), one_hot(ids & 127, LANES)


def bitmap(ids, high_count):
    high, low = one_hots(ids, high_count)
    return lax.dot_general(low, high, NT, preferred_element_type=jnp.float32).astype(jnp.bfloat16)


def lookup(one_map, pair):
    hit = lax.dot_general(one_map, pair[0], NN, preferred_element_type=jnp.float32)
    return jnp.sum(hit * pair[1].astype(jnp.float32), axis=0, keepdims=True)


def prep_kernel(place, table, fresh, ages, ref_ids, rows_out, meta_out, *, replicas):
    core = place[2]
    row = 0
    for source in (table, fresh):
        half = source.shape[0] // replicas
        rows_out[row : row + half, :] = source[pl.ds(pl.multiple_of(core * half, half), half), :]
        row += half
    width = table.shape[1]
    ref_rows, age_rows = ref_ids.shape[0], ages.shape[0]
    meta_out[:ref_rows, :] = ref_ids[...].astype(jnp.float32)
    weight = jnp.exp(-ages[...].astype(jnp.float32) / age_scale).astype(jnp.bfloat16).astype(jnp.float32)
    meta_out[ref_rows : ref_rows + age_rows, :] = jnp.log2(weight)
    line = ref_rows + age_rows
    for source in (table, fresh):
        for block in range(source.shape[0] // LANES):
            squares = jnp.zeros((LANES, LANES), jnp.float32)
            for chunk in range(width // LANES):
                values = source[block * LANES : (block + 1) * LANES, chunk * LANES : (chunk + 1) * LANES]
                values = values.astype(jnp.float32)
                squares += values * values
            mean = jnp.sum(squares.T, axis=0, keepdims=True) / width
            meta_out[line : line + 1, :] = lax.rsqrt(mean + epsilon) * (score_scale / width * LOG2E)
            line += 1


def meta_kernel(
    place, ref_ids, neg, log_weight, lw_out, row_out, pack_out, apply_out, own_out, target_out,
    *, rows_dev, refresh_dev, cap, replicas
):
    outer, inner, core = place[0], place[1], place[2]
    planes, plane_refresh = ref_ids.shape
    plane_rows = log_weight.shape[1]
    owners_plane = plane_rows // rows_dev
    high_count = planes * plane_rows // LANES
    own_owner = outer * owners_plane + inner
    share = cap // replicas
    plane_ids = ref_ids[0:1, :]
    column = lax.broadcasted_iota(jnp.int32, (1, plane_rows), 1)
    table_ids = (outer * owners_plane + (inner ^ (column // rows_dev))) * rows_dev + column % rows_dev

    pair = one_hots(jnp.concatenate([table_ids, plane_ids], axis=1), high_count)
    all_ids = jnp.concatenate([ref_ids[plane : plane + 1, :] for plane in range(planes)], axis=1)
    refreshed = lookup(bitmap(all_ids, high_count), (pair[0][:, :plane_rows], pair[1][:, :plane_rows])) > 0.5
    row_out[:, :plane_rows] = jnp.where(refreshed, -1, table_ids).astype(jnp.float32)
    row_out[:, plane_rows:] = plane_ids.astype(jnp.float32)
    own_out[...] = refreshed[:, :rows_dev].astype(jnp.int32)
    weights = jnp.where(refreshed, MASKED, log_weight[...])
    weights = jnp.concatenate([weights, jnp.zeros((1, plane_refresh), jnp.float32)], axis=1)
    for group in range(planes):
        hit = lookup(bitmap(neg[group : group + 1, :], high_count), pair)
        lw_out[group : group + 1, :] = jnp.where(hit > 0.5, weights, MASKED)

    pairs = [(plane, side) for plane in range(planes) for side in range(owners_plane)]

    def ids_of(plane, side):
        return ref_ids[plane : plane + 1, side * refresh_dev : (side + 1) * refresh_dev]

    sent = [ids_of(0, side) // rows_dev - ((outer ^ plane) * owners_plane + inner) for plane, side in pairs]
    taken = [ids_of(plane, side) // rows_dev - own_owner for plane, side in pairs]
    rank = owner_ranks(sent + taken, refresh_dev, cap)
    own_slots = owners_plane * cap
    codes = [jnp.full((1, refresh_dev), -1, jnp.int32)] * owners_plane
    for i, (plane, side) in enumerate(pairs):
        size = share if plane else cap
        base = own_slots + ((plane - 1) * owners_plane + side) * share if plane else side * cap
        sends = rank[i : i + 1, :] - (core * share if plane else 0)
        codes[side] = jnp.where((sends >= 0) & (sends < size), base + sends, codes[side])
        took = rank[len(pairs) + i : len(pairs) + i + 1, :]
        slot = jnp.where(took < 0, -1, ((took // share) ^ core) * share + took % share if plane else took)
        row = jnp.where(took < 0, 0, ids_of(plane, side) - own_owner * rows_dev)
        kinds = lax.broadcasted_iota(jnp.int32, (8, refresh_dev), 0)
        digits = jnp.where(kinds == 0, row // 16, jnp.where(kinds == 1, row % 16, 1))
        found = lax.dot_general(small(digits), one_hot(slot, cap), NT, preferred_element_type=jnp.float32)
        found = found.astype(jnp.int32)
        target = jnp.where(found[2:3, :] > 0, found[0:1, :] * 16 + found[1:2, :], -1)
        if plane == 0:
            target_out[:, base : base + cap] = target
            continue
        for part in range(replicas):
            first = base + part * (planes - 1) * owners_plane * share
            target_out[:, first : first + share] = target[:, part * share : (part + 1) * share]
    pack_out[...] = one_hot(jnp.concatenate(codes, axis=1), pack_out.shape[0])
    rows = lax.broadcasted_iota(jnp.int32, apply_out.shape, 0)
    apply_out[...] = jnp.where(rows == target_out[...], 1.0, 0.0)


def piece_offset(place, piece):
    column, size, flip, by_core = piece
    if flip is None:
        return column
    column += (place[2] ^ flip) * size
    if by_core is not None:
        column += (place[2] ^ by_core) * size * 2
    return pl.multiple_of(column, size)


def pack_kernel(place, select, *refs, pieces):
    out = refs[-1]
    total = jnp.zeros(out.shape, jnp.float32)
    for source, start, size, column in pieces:
        columns = pl.ds(piece_offset(place, column), size)
        total += lax.dot_general(
            select[:, columns], refs[source][start : start + size, :], NN, preferred_element_type=jnp.float32
        )
    out[...] = total.astype(jnp.bfloat16)


def apply_kernel(select, table, *refs):
    out = refs[-1]
    fresh = jnp.zeros(out.shape, jnp.float32)
    first = 0
    for arrived in refs[:-1]:
        part = select[:, first : first + arrived.shape[0]].astype(jnp.bfloat16)
        fresh += lax.dot_general(part, arrived[...], NN, preferred_element_type=jnp.float32)
        first += arrived.shape[0]
    hit = jnp.sum(select[...], axis=1, keepdims=True) > 0.5
    out[...] = jnp.where(hit, fresh, table[...].astype(jnp.float32)).astype(jnp.bfloat16)


def to_lanes(row):
    return jnp.broadcast_to(row, (LANES, LANES)).T


def score_kernel(place, *refs, pieces, sources):
    positive, log_weight, row_ids, scale = refs[sources : sources + 4]
    out, total, pos_total, q_scale, pos_b, chosen = refs[-6:]
    queries = refs[0]
    count, width = queries.shape
    if sources == 2:
        at_end = (place[0] == 0) | (place[0] == 3)
        chosen[...] = jnp.where(at_end, refs[0][...], refs[1][...])
        queries = chosen
    for block in range(count // LANES):
        part = slice(block * LANES, (block + 1) * LANES)
        values = queries[part, :].astype(jnp.float32)
        squares = jnp.sum(values * values, axis=1, keepdims=True)
        q_scale[part, :] = jnp.broadcast_to(lax.rsqrt(squares / width + epsilon), (LANES, LANES))
        pos_b[part, :] = to_lanes(positive[block : block + 1, :])
    total[...] = jnp.zeros_like(total)
    pos_total[...] = jnp.zeros_like(pos_total)
    refs = refs[sources + 4 : -6]

    def product(group):
        rows = [refs[source][start : start + size, :] for source, start, size, _ in group]
        rows = rows[0] if len(rows) == 1 else jnp.concatenate(rows, axis=0)
        return lax.dot_general(queries[...], rows, NT, preferred_element_type=jnp.float32)

    narrow = [piece for piece in pieces if piece[2] < 256]
    groups = [[piece] for piece in pieces if piece[2] >= 256] + [narrow[i : i + 2] for i in range(0, len(narrow), 2)]
    following = product(groups[0])
    for i, group in enumerate(groups):
        raw = following
        if i + 1 < len(groups):
            following = product(groups[i + 1])
        columns = []
        for _, _, size, column in group:
            columns += [piece_offset(place, column) + chunk * LANES for chunk in range(size // LANES)]
        for top in range(0, count, 64):
            part = slice(top, top + 64)
            sums, positives = total[part, :], pos_total[part, :]
            query_scale, wanted = q_scale[part, :], pos_b[part, :]
            for chunk, first in enumerate(columns):
                cols = pl.ds(first, LANES)
                powers = raw[part, chunk * LANES : (chunk + 1) * LANES] * query_scale
                powers = powers * scale[:, cols] + log_weight[:, cols]
                sums = sums + jnp.exp2(powers)
                positives = positives + jnp.where(wanted == row_ids[:, cols], powers, 0.0)
            total[part, :] = sums
            pos_total[part, :] = positives
    for block in range(count // LANES):
        part = slice(block * LANES, (block + 1) * LANES)
        out[0, block : block + 1, :] = jnp.sum(total[part, :].T, axis=0, keepdims=True)
        out[1, block : block + 1, :] = jnp.sum(pos_total[part, :].T, axis=0, keepdims=True)


def whole(memory=pltpu.VMEM):
    return pl.BlockSpec(memory_space=memory)


def call(kernel, name, outs, place, *operands, scratch=(), **options):
    specs = [whole()] * len(operands)
    if place is not None:
        specs = [whole(pltpu.SMEM)] + specs
        operands = (place, *operands)
    return pl.pallas_call(
        functools.partial(kernel, **options),
        out_shape=tuple(outs),
        in_specs=specs,
        out_specs=tuple(whole() for _ in outs),
        scratch_shapes=list(scratch),
        compiler_params=pltpu.CompilerParams(vmem_limit_bytes=VMEM_LIMIT),
        cost_estimate=pl.CostEstimate(flops=1, bytes_accessed=1, transcendentals=0),
        name=name,
    )(*operands)


def swap(values, axis, flip):
    return lax.ppermute(values, axis, [(i, i ^ flip) for i in range(lax.axis_size(axis))])


def gather_line(values, small):
    planes = lax.axis_size("outer")
    if planes != 4:
        return [(swap(values, "outer", s),) for s in range(1, planes)], small
    middle, outward = [(1, 2), (2, 1)], [(1, 0), (2, 3)]
    beside = swap(values, "outer", 1)
    across = lax.ppermute(values, "outer", middle)
    beside, across, small = lax.optimization_barrier((beside, across, small))
    from_end = lax.ppermute(beside, "outer", middle)
    to_end = lax.ppermute(across, "outer", outward)
    last = lax.ppermute(from_end, "outer", outward)
    return [(beside,), (to_end, from_end), (last, across)], small


def on_device(table, ages, refresh_ids, fresh_rows, neg_ids, queries, pos_ids):
    rows_dev, width = table.shape
    refresh_dev = refresh_ids.shape[0]
    planes = lax.axis_size("outer")
    owners_plane = lax.axis_size("inner")
    replicas = lax.axis_size("query")
    owners = planes * owners_plane
    query_count = queries.shape[0]
    list_size = neg_ids.shape[1]
    place = jnp.stack([lax.axis_index(name) for name in ("outer", "inner", "query")]).astype(jnp.int32)
    plane_rows = owners_plane * rows_dev
    plane_refresh = owners_plane * refresh_dev
    all_rows = plane_rows + plane_refresh
    cap_each = max(2, (2 * refresh_dev + owners - 1) // owners)
    cap = owners_plane * cap_each
    share = cap // replicas
    table_half, fresh_half = rows_dev // replicas, refresh_dev // replicas
    bf16, f32 = jnp.bfloat16, jnp.float32

    meta_lines = (2 * refresh_dev + 2 * rows_dev) // LANES
    rows_half, meta = call(
        prep_kernel,
        "prep",
        [jax.ShapeDtypeStruct((table_half + fresh_half, width), bf16), jax.ShapeDtypeStruct((meta_lines, LANES), f32)],
        place,
        table,
        fresh_rows,
        ages.reshape(-1, LANES),
        refresh_ids.reshape(-1, LANES),
        replicas=replicas,
    )
    metas = jnp.stack([meta] + [swap(meta, "inner", s) for s in range(1, owners_plane)])
    cuts = [refresh_dev, rows_dev, rows_dev, refresh_dev]
    ends = [sum(cuts[: i + 1]) // LANES for i in range(len(cuts))]

    def piece(i):
        return metas[:, ends[i] - cuts[i] // LANES : ends[i]].reshape(1, -1)

    ref_plane, log_weight_plane = piece(0), piece(1)
    scale_plane = jnp.concatenate([piece(2), piece(3)], axis=1)
    line = jnp.concatenate([ref_plane[0], neg_ids[0].astype(f32), pos_ids.astype(f32)])
    got_queries, line = gather_line(queries, line)
    got_queries = [(queries,)] + got_queries
    lines = jnp.stack([line] + [swap(line, "outer", s) for s in range(1, planes)])
    ref_all = lines[:, :plane_refresh].astype(jnp.int32)
    neg_line = lines[:, plane_refresh : plane_refresh + list_size].astype(jnp.int32)
    positive = lines[:, plane_refresh + list_size :].reshape(planes, -1, LANES)

    lw, row_ids, pack, apply_to, own = call(
        meta_kernel,
        "meta",
        [
            jax.ShapeDtypeStruct((planes, all_rows), f32),
            jax.ShapeDtypeStruct((1, all_rows), f32),
            jax.ShapeDtypeStruct((cap + (planes - 1) * share, plane_refresh), bf16),
            jax.ShapeDtypeStruct((rows_dev, planes * cap), f32),
            jax.ShapeDtypeStruct((1, rows_dev), jnp.int32),
        ],
        place,
        ref_all,
        neg_line,
        log_weight_plane,
        rows_dev=rows_dev,
        scratch=[pltpu.VMEM((1, planes * cap), jnp.int32)],
        refresh_dev=refresh_dev,
        cap=cap_each,
        replicas=replicas,
    )
    new_ages = jnp.where(own.reshape(rows_dev) > 0, 0, ages)

    if replicas == 2 and owners_plane == 4:
        axes = ("inner", "query")
        first = [(2 * i + c, 2 * (i ^ (1 + c)) + c) for i in range(4) for c in range(2)]
        second = [(2 * i + c, 2 * (i ^ (2 - c)) + c) for i in range(4) for c in range(2)]
        near = lax.ppermute(rows_half, axes, first)
        side = lax.ppermute(rows_half, axes, second)
        far = lax.ppermute(near, axes, second)
        buffers = [table, fresh_rows]
        table_pieces = [(0, 0, rows_dev, (0, rows_dev, None, None))]
        fresh_pieces = [(1, 0, refresh_dev, (0, refresh_dev, None, None))]
        for slot, by_core, mine in ((1, 0, near), (1, 1, side), (3, None, far)):
            for flip, rows in enumerate((mine, swap(mine, "query", 1))):
                by = None if by_core is None else by_core ^ flip
                table_pieces.append((len(buffers), 0, table_half, (slot * rows_dev, table_half, flip, by)))
                fresh_pieces.append((len(buffers), table_half, fresh_half, (slot * refresh_dev, fresh_half, flip, by)))
                buffers.append(rows)
    else:
        got_rows = [rows_half] + [swap(rows_half, "inner", s) for s in range(1, owners_plane)]
        gathered = lax.all_gather(jnp.stack(got_rows), "query", axis=0)
        gathered = jnp.swapaxes(gathered, 0, 1)
        buffers = [
            gathered[:, :, :table_half].reshape(plane_rows, width),
            gathered[:, :, table_half:].reshape(plane_refresh, width),
        ]
        table_pieces = [(0, i * 512, 512, (i * 512, 512, None, None)) for i in range(plane_rows // 512)]
        fresh_pieces = [(1, i * 512, 512, (i * 512, 512, None, None)) for i in range(plane_refresh // 512)]

    def shift(pieces, columns):
        return [(a, b, c, (d[0] + columns, *d[1:])) for a, b, c, d in pieces]

    (packed,) = call(
        pack_kernel, "pack", [jax.ShapeDtypeStruct((pack.shape[0], width), bf16)], place, pack, *buffers, pieces=fresh_pieces
    )
    parts = []
    for s in range(1, planes):
        first = cap + (s - 1) * share
        parts.append(swap(packed[first : first + share], "outer", s))
    parts = jnp.concatenate(parts)
    arrived = [packed[:cap], parts] + [swap(parts, "query", flip) for flip in range(1, replicas)]

    pieces = table_pieces + shift(fresh_pieces, plane_rows)
    mine = None
    for s in [*range(1, planes), 0]:
        (partial,) = call(
            score_kernel,
            "score",
            [jax.ShapeDtypeStruct((2, query_count // LANES, LANES), f32)],
            place,
            *got_queries[s],
            positive[s],
            lw[s : s + 1],
            row_ids,
            scale_plane,
            *buffers,
            scratch=[pltpu.VMEM((query_count, LANES), f32)] * 4 + [pltpu.VMEM((query_count, width), bf16)],
            pieces=pieces,
            sources=len(got_queries[s]),
        )
        if s:
            partial = swap(partial, "outer", s)
        mine = partial if mine is None else mine + partial
    (new_table,) = call(
        apply_kernel, "apply", [jax.ShapeDtypeStruct(table.shape, bf16)], None, apply_to, table, *arrived
    )
    loss = (jnp.log2(mine[0]) - mine[1]) * math.log(2.0)
    return new_table, new_ages, loss.reshape(query_count)


def solution(mesh):
    owners, replicas = mesh.shape["index"], mesh.shape["query"]
    inner = 1 << (int(math.log2(owners)) // 2)
    split = Mesh(mesh.devices.reshape(owners // inner, inner, replicas), ("outer", "inner", "query"))
    index = ("outer", "inner")
    placed = (
        P(index, None),
        P(index),
        P(index),
        P(index, None),
        P(index, None),
        P(("outer", "inner", "query"), None),
        P(("outer", "inner", "query")),
    )
    return jax.shard_map(
        on_device,
        mesh=split,
        in_specs=placed,
        out_specs=(P(index, None), P(index), P(("outer", "inner", "query"))),
        check_vma=False,
    )
```

```python
import functools
import math

import jax
import jax.numpy as jnp
from jax import lax
from jax.experimental import pallas as pl
from jax.experimental.pallas import tpu as pltpu
from jax.sharding import Mesh, PartitionSpec as P

score_scale = 20.0
age_scale = 16.0
epsilon = 1e-06
LOG2E = math.log2(math.e)
MASKED = -1e30
LANES = 128
VMEM_LIMIT = 48 * 1024 * 1024

NT = (((1,), (1,)), ((), ()))
NN = (((1,), (0,)), ((), ()))


def one_hot(ids, count):
    rows = lax.broadcasted_iota(jnp.int32, (count, ids.shape[1]), 0)
    if count <= 256:
        ids = jnp.where((ids < 0) | (ids >= count), -1, ids)
        rows, ids = rows.astype(jnp.float32).astype(jnp.bfloat16), ids.astype(jnp.float32).astype(jnp.bfloat16)
        return jnp.where(rows == ids, jnp.bfloat16(1), jnp.bfloat16(0))
    return jnp.where(rows == ids, 1.0, 0.0).astype(jnp.bfloat16)


def counted(hits):
    count = hits.shape[1]
    before = lax.broadcasted_iota(jnp.int32, (count, count), 0)
    after = lax.broadcasted_iota(jnp.int32, (count, count), 1)
    earlier = jnp.where(before < after, 1.0, 0.0).astype(jnp.bfloat16)
    return lax.dot_general(hits.astype(jnp.bfloat16), earlier, NN, preferred_element_type=jnp.float32)


def small(values):
    return values.astype(jnp.float32).astype(jnp.bfloat16)


def owner_ranks(rows, refresh_dev, cap):
    match = jnp.concatenate(rows, axis=0) == 0
    rank = counted(jnp.where(match, 1.0, 0.0)).astype(jnp.int32)
    return jnp.where(match, rank, -cap)


def one_hots(ids, high_count):
    return one_hot(ids >> 7, high_count), one_hot(ids & 127, LANES)


def bitmap(ids, high_count):
    high, low = one_hots(ids, high_count)
    return lax.dot_general(low, high, NT, preferred_element_type=jnp.float32).astype(jnp.bfloat16)


def lookup(one_map, pair):
    hit = lax.dot_general(one_map, pair[0], NN, preferred_element_type=jnp.float32)
    return jnp.sum(hit * pair[1].astype(jnp.float32), axis=0, keepdims=True)


def prep_kernel(place, table, fresh, ages, ref_ids, rows_out, meta_out, *, replicas):
    core = place[2]
    row = 0
    for source in (table, fresh):
        half = source.shape[0] // replicas
        rows_out[row : row + half, :] = source[pl.ds(pl.multiple_of(core * half, half), half), :]
        row += half
    width = table.shape[1]
    ref_rows, age_rows = ref_ids.shape[0], ages.shape[0]
    meta_out[:ref_rows, :] = ref_ids[...].astype(jnp.float32)
    weight = jnp.exp(-ages[...].astype(jnp.float32) / age_scale).astype(jnp.bfloat16).astype(jnp.float32)
    meta_out[ref_rows : ref_rows + age_rows, :] = jnp.log2(weight)
    line = ref_rows + age_rows
    for source in (table, fresh):
        for block in range(source.shape[0] // LANES):
            squares = jnp.zeros((LANES, LANES), jnp.float32)
            for chunk in range(width // LANES):
                values = source[block * LANES : (block + 1) * LANES, chunk * LANES : (chunk + 1) * LANES]
                values = values.astype(jnp.float32)
                squares += values * values
            mean = jnp.sum(squares.T, axis=0, keepdims=True) / width
            meta_out[line : line + 1, :] = lax.rsqrt(mean + epsilon) * (score_scale / width * LOG2E)
            line += 1


def meta_kernel(
    place, ref_ids, neg, log_weight, lw_out, row_out, pack_out, apply_out, own_out, target_out,
    *, rows_dev, refresh_dev, cap, replicas
):
    outer, inner, core = place[0], place[1], place[2]
    planes, plane_refresh = ref_ids.shape
    plane_rows = log_weight.shape[1]
    owners_plane = plane_rows // rows_dev
    high_count = planes * plane_rows // LANES
    own_owner = outer * owners_plane + inner
    share = cap // replicas
    plane_ids = ref_ids[0:1, :]
    column = lax.broadcasted_iota(jnp.int32, (1, plane_rows), 1)
    table_ids = (outer * owners_plane + (inner ^ (column // rows_dev))) * rows_dev + column % rows_dev

    pair = one_hots(jnp.concatenate([table_ids, plane_ids], axis=1), high_count)
    all_ids = jnp.concatenate([ref_ids[plane : plane + 1, :] for plane in range(planes)], axis=1)
    refreshed = lookup(bitmap(all_ids, high_count), (pair[0][:, :plane_rows], pair[1][:, :plane_rows])) > 0.5
    row_out[:, :plane_rows] = jnp.where(refreshed, -1, table_ids).astype(jnp.float32)
    row_out[:, plane_rows:] = plane_ids.astype(jnp.float32)
    own_out[...] = refreshed[:, :rows_dev].astype(jnp.int32)
    weights = jnp.where(refreshed, MASKED, log_weight[...])
    weights = jnp.concatenate([weights, jnp.zeros((1, plane_refresh), jnp.float32)], axis=1)
    for group in range(planes):
        hit = lookup(bitmap(neg[group : group + 1, :], high_count), pair)
        lw_out[group : group + 1, :] = jnp.where(hit > 0.5, weights, MASKED)

    pairs = [(plane, side) for plane in range(planes) for side in range(owners_plane)]

    def ids_of(plane, side):
        return ref_ids[plane : plane + 1, side * refresh_dev : (side + 1) * refresh_dev]

    sent = [ids_of(0, side) // rows_dev - ((outer ^ plane) * owners_plane + inner) for plane, side in pairs]
    taken = [ids_of(plane, side) // rows_dev - own_owner for plane, side in pairs]
    rank = owner_ranks(sent + taken, refresh_dev, cap)
    own_slots = owners_plane * cap
    codes = [jnp.full((1, refresh_dev), -1, jnp.int32)] * owners_plane
    for i, (plane, side) in enumerate(pairs):
        size = share if plane else cap
        base = own_slots + ((plane - 1) * owners_plane + side) * share if plane else side * cap
        sends = rank[i : i + 1, :] - (core * share if plane else 0)
        codes[side] = jnp.where((sends >= 0) & (sends < size), base + sends, codes[side])
        took = rank[len(pairs) + i : len(pairs) + i + 1, :]
        slot = jnp.where(took < 0, -1, ((took // share) ^ core) * share + took % share if plane else took)
        row = jnp.where(took < 0, 0, ids_of(plane, side) - own_owner * rows_dev)
        kinds = lax.broadcasted_iota(jnp.int32, (8, refresh_dev), 0)
        digits = jnp.where(kinds == 0, row // 16, jnp.where(kinds == 1, row % 16, 1))
        found = lax.dot_general(small(digits), one_hot(slot, cap), NT, preferred_element_type=jnp.float32)
        found = found.astype(jnp.int32)
        target = jnp.where(found[2:3, :] > 0, found[0:1, :] * 16 + found[1:2, :], -1)
        if plane == 0:
            target_out[:, base : base + cap] = target
            continue
        for part in range(replicas):
            first = base + part * (planes - 1) * owners_plane * share
            target_out[:, first : first + share] = target[:, part * share : (part + 1) * share]
    pack_out[...] = one_hot(jnp.concatenate(codes, axis=1), pack_out.shape[0])
    rows = lax.broadcasted_iota(jnp.int32, apply_out.shape, 0)
    apply_out[...] = jnp.where(rows == target_out[...], 1.0, 0.0)


def piece_offset(place, piece):
    column, size, flip, by_core = piece
    if flip is None:
        return column
    column += (place[2] ^ flip) * size
    if by_core is not None:
        column += (place[2] ^ by_core) * size * 2
    return pl.multiple_of(column, size)


def pack_kernel(place, select, *refs, pieces):
    out = refs[-1]
    total = jnp.zeros(out.shape, jnp.float32)
    for source, start, size, column in pieces:
        columns = pl.ds(piece_offset(place, column), size)
        total += lax.dot_general(
            select[:, columns], refs[source][start : start + size, :], NN, preferred_element_type=jnp.float32
        )
    out[...] = total.astype(jnp.bfloat16)


def apply_kernel(select, table, *refs):
    out = refs[-1]
    fresh = jnp.zeros(out.shape, jnp.float32)
    first = 0
    for arrived in refs[:-1]:
        part = select[:, first : first + arrived.shape[0]].astype(jnp.bfloat16)
        fresh += lax.dot_general(part, arrived[...], NN, preferred_element_type=jnp.float32)
        first += arrived.shape[0]
    hit = jnp.sum(select[...], axis=1, keepdims=True) > 0.5
    out[...] = jnp.where(hit, fresh, table[...].astype(jnp.float32)).astype(jnp.bfloat16)


def to_lanes(row):
    return jnp.broadcast_to(row, (LANES, LANES)).T


def score_kernel(place, *refs, pieces, sources):
    positive, log_weight, row_ids, scale = refs[sources : sources + 4]
    out, total, pos_total, q_scale, pos_b, chosen = refs[-6:]
    queries = refs[0]
    count, width = queries.shape
    if sources == 2:
        at_end = (place[0] == 0) | (place[0] == 3)
        chosen[...] = jnp.where(at_end, refs[0][...], refs[1][...])
        queries = chosen
    for block in range(count // LANES):
        part = slice(block * LANES, (block + 1) * LANES)
        values = queries[part, :].astype(jnp.float32)
        squares = jnp.sum(values * values, axis=1, keepdims=True)
        q_scale[part, :] = jnp.broadcast_to(lax.rsqrt(squares / width + epsilon), (LANES, LANES))
        pos_b[part, :] = to_lanes(positive[block : block + 1, :])
    total[...] = jnp.zeros_like(total)
    pos_total[...] = jnp.zeros_like(pos_total)
    refs = refs[sources + 4 : -6]

    def product(group):
        rows = [refs[source][start : start + size, :] for source, start, size, _ in group]
        rows = rows[0] if len(rows) == 1 else jnp.concatenate(rows, axis=0)
        return lax.dot_general(queries[...], rows, NT, preferred_element_type=jnp.float32)

    narrow = [piece for piece in pieces if piece[2] < 256]
    groups = [[piece] for piece in pieces if piece[2] >= 256] + [narrow[i : i + 2] for i in range(0, len(narrow), 2)]
    following = product(groups[0])
    for i, group in enumerate(groups):
        raw = following
        if i + 1 < len(groups):
            following = product(groups[i + 1])
        columns = []
        for _, _, size, column in group:
            columns += [piece_offset(place, column) + chunk * LANES for chunk in range(size // LANES)]
        for top in range(0, count, 64):
            part = slice(top, top + 64)
            sums, positives = total[part, :], pos_total[part, :]
            query_scale, wanted = q_scale[part, :], pos_b[part, :]
            for chunk, first in enumerate(columns):
                cols = pl.ds(first, LANES)
                powers = raw[part, chunk * LANES : (chunk + 1) * LANES] * query_scale
                powers = powers * scale[:, cols] + log_weight[:, cols]
                sums = sums + jnp.exp2(powers)
                positives = positives + jnp.where(wanted == row_ids[:, cols], powers, 0.0)
            total[part, :] = sums
            pos_total[part, :] = positives
    for block in range(count // LANES):
        part = slice(block * LANES, (block + 1) * LANES)
        out[0, block : block + 1, :] = jnp.sum(total[part, :].T, axis=0, keepdims=True)
        out[1, block : block + 1, :] = jnp.sum(pos_total[part, :].T, axis=0, keepdims=True)


def whole(memory=pltpu.VMEM):
    return pl.BlockSpec(memory_space=memory)


def call(kernel, name, outs, place, *operands, scratch=(), **options):
    specs = [whole()] * len(operands)
    if place is not None:
        specs = [whole(pltpu.SMEM)] + specs
        operands = (place, *operands)
    return pl.pallas_call(
        functools.partial(kernel, **options),
        out_shape=tuple(outs),
        in_specs=specs,
        out_specs=tuple(whole() for _ in outs),
        scratch_shapes=list(scratch),
        compiler_params=pltpu.CompilerParams(vmem_limit_bytes=VMEM_LIMIT),
        cost_estimate=pl.CostEstimate(flops=1, bytes_accessed=1, transcendentals=0),
        name=name,
    )(*operands)


def swap(values, axis, flip):
    return lax.ppermute(values, axis, [(i, i ^ flip) for i in range(lax.axis_size(axis))])


def gather_line(values, small):
    planes = lax.axis_size("outer")
    if planes != 4:
        return [(swap(values, "outer", s),) for s in range(1, planes)], small
    middle, outward = [(1, 2), (2, 1)], [(1, 0), (2, 3)]
    beside = swap(values, "outer", 1)
    across = lax.ppermute(values, "outer", middle)
    beside, across, small = lax.optimization_barrier((beside, across, small))
    from_end = lax.ppermute(beside, "outer", middle)
    to_end = lax.ppermute(across, "outer", outward)
    last = lax.ppermute(from_end, "outer", outward)
    return [(beside,), (to_end, from_end), (last, across)], small


def on_device(table, ages, refresh_ids, fresh_rows, neg_ids, queries, pos_ids):
    rows_dev, width = table.shape
    refresh_dev = refresh_ids.shape[0]
    planes = lax.axis_size("outer")
    owners_plane = lax.axis_size("inner")
    replicas = lax.axis_size("query")
    owners = planes * owners_plane
    query_count = queries.shape[0]
    list_size = neg_ids.shape[1]
    place = jnp.stack([lax.axis_index(name) for name in ("outer", "inner", "query")]).astype(jnp.int32)
    plane_rows = owners_plane * rows_dev
    plane_refresh = owners_plane * refresh_dev
    all_rows = plane_rows + plane_refresh
    cap_each = max(2, (2 * refresh_dev + owners - 1) // owners)
    cap = owners_plane * cap_each
    share = cap // replicas
    table_half, fresh_half = rows_dev // replicas, refresh_dev // replicas
    bf16, f32 = jnp.bfloat16, jnp.float32

    meta_lines = (2 * refresh_dev + 2 * rows_dev) // LANES
    rows_half, meta = call(
        prep_kernel,
        "prep",
        [jax.ShapeDtypeStruct((table_half + fresh_half, width), bf16), jax.ShapeDtypeStruct((meta_lines, LANES), f32)],
        place,
        table,
        fresh_rows,
        ages.reshape(-1, LANES),
        refresh_ids.reshape(-1, LANES),
        replicas=replicas,
    )
    metas = jnp.stack([meta] + [swap(meta, "inner", s) for s in range(1, owners_plane)])
    cuts = [refresh_dev, rows_dev, rows_dev, refresh_dev]
    ends = [sum(cuts[: i + 1]) // LANES for i in range(len(cuts))]

    def piece(i):
        return metas[:, ends[i] - cuts[i] // LANES : ends[i]].reshape(1, -1)

    ref_plane, log_weight_plane = piece(0), piece(1)
    scale_plane = jnp.concatenate([piece(2), piece(3)], axis=1)
    line = jnp.concatenate([ref_plane[0], neg_ids[0].astype(f32), pos_ids.astype(f32)])
    got_queries, line = gather_line(queries, line)
    got_queries = [(queries,)] + got_queries
    lines = jnp.stack([line] + [swap(line, "outer", s) for s in range(1, planes)])
    ref_all = lines[:, :plane_refresh].astype(jnp.int32)
    neg_line = lines[:, plane_refresh : plane_refresh + list_size].astype(jnp.int32)
    positive = lines[:, plane_refresh + list_size :].reshape(planes, -1, LANES)

    lw, row_ids, pack, apply_to, own = call(
        meta_kernel,
        "meta",
        [
            jax.ShapeDtypeStruct((planes, all_rows), f32),
            jax.ShapeDtypeStruct((1, all_rows), f32),
            jax.ShapeDtypeStruct((cap + (planes - 1) * share, plane_refresh), bf16),
            jax.ShapeDtypeStruct((rows_dev, planes * cap), f32),
            jax.ShapeDtypeStruct((1, rows_dev), jnp.int32),
        ],
        place,
        ref_all,
        neg_line,
        log_weight_plane,
        rows_dev=rows_dev,
        scratch=[pltpu.VMEM((1, planes * cap), jnp.int32)],
        refresh_dev=refresh_dev,
        cap=cap_each,
        replicas=replicas,
    )
    new_ages = jnp.where(own.reshape(rows_dev) > 0, 0, ages)

    if replicas == 2 and owners_plane == 4:
        axes = ("inner", "query")
        first = [(2 * i + c, 2 * (i ^ (1 + c)) + c) for i in range(4) for c in range(2)]
        second = [(2 * i + c, 2 * (i ^ (2 - c)) + c) for i in range(4) for c in range(2)]
        near = lax.ppermute(rows_half, axes, first)
        side = lax.ppermute(rows_half, axes, second)
        far = lax.ppermute(near, axes, second)
        buffers = [table, fresh_rows]
        table_pieces = [(0, 0, rows_dev, (0, rows_dev, None, None))]
        fresh_pieces = [(1, 0, refresh_dev, (0, refresh_dev, None, None))]
        for slot, by_core, mine in ((1, 0, near), (1, 1, side), (3, None, far)):
            for flip, rows in enumerate((mine, swap(mine, "query", 1))):
                by = None if by_core is None else by_core ^ flip
                table_pieces.append((len(buffers), 0, table_half, (slot * rows_dev, table_half, flip, by)))
                fresh_pieces.append((len(buffers), table_half, fresh_half, (slot * refresh_dev, fresh_half, flip, by)))
                buffers.append(rows)
    else:
        got_rows = [rows_half] + [swap(rows_half, "inner", s) for s in range(1, owners_plane)]
        gathered = lax.all_gather(jnp.stack(got_rows), "query", axis=0)
        gathered = jnp.swapaxes(gathered, 0, 1)
        buffers = [
            gathered[:, :, :table_half].reshape(plane_rows, width),
            gathered[:, :, table_half:].reshape(plane_refresh, width),
        ]
        table_pieces = [(0, i * 512, 512, (i * 512, 512, None, None)) for i in range(plane_rows // 512)]
        fresh_pieces = [(1, i * 512, 512, (i * 512, 512, None, None)) for i in range(plane_refresh // 512)]

    def shift(pieces, columns):
        return [(a, b, c, (d[0] + columns, *d[1:])) for a, b, c, d in pieces]

    (packed,) = call(
        pack_kernel, "pack", [jax.ShapeDtypeStruct((pack.shape[0], width), bf16)], place, pack, *buffers, pieces=fresh_pieces
    )
    parts = []
    for s in range(1, planes):
        first = cap + (s - 1) * share
        parts.append(swap(packed[first : first + share], "outer", s))
    parts, own_queries = lax.optimization_barrier((jnp.concatenate(parts), queries))
    got_queries[0] = (own_queries,)
    arrived = [packed[:cap], parts] + [swap(parts, "query", flip) for flip in range(1, replicas)]

    pieces = table_pieces + shift(fresh_pieces, plane_rows)
    mine = None
    for s in [*range(1, planes), 0]:
        (partial,) = call(
            score_kernel,
            "score",
            [jax.ShapeDtypeStruct((2, query_count // LANES, LANES), f32)],
            place,
            *got_queries[s],
            positive[s],
            lw[s : s + 1],
            row_ids,
            scale_plane,
            *buffers,
            scratch=[pltpu.VMEM((query_count, LANES), f32)] * 4 + [pltpu.VMEM((query_count, width), bf16)],
            pieces=pieces,
            sources=len(got_queries[s]),
        )
        if s:
            partial = swap(partial, "outer", s)
        mine = partial if mine is None else mine + partial
    (new_table,) = call(
        apply_kernel, "apply", [jax.ShapeDtypeStruct(table.shape, bf16)], None, apply_to, table, *arrived
    )
    loss = (jnp.log2(mine[0]) - mine[1]) * math.log(2.0)
    return new_table, new_ages, loss.reshape(query_count)


def solution(mesh):
    owners, replicas = mesh.shape["index"], mesh.shape["query"]
    inner = 1 << (int(math.log2(owners)) // 2)
    split = Mesh(mesh.devices.reshape(owners // inner, inner, replicas), ("outer", "inner", "query"))
    index = ("outer", "inner")
    placed = (
        P(index, None),
        P(index),
        P(index),
        P(index, None),
        P(index, None),
        P(("outer", "inner", "query"), None),
        P(("outer", "inner", "query")),
    )
    return jax.shard_map(
        on_device,
        mesh=split,
        in_specs=placed,
        out_specs=(P(index, None), P(index), P(("outer", "inner", "query"))),
        check_vma=False,
    )
```

```python
import functools
import math

import jax
import jax.numpy as jnp
from jax import lax
from jax.experimental import pallas as pl
from jax.experimental.pallas import tpu as pltpu
from jax.sharding import Mesh, PartitionSpec as P

score_scale = 20.0
age_scale = 16.0
epsilon = 1e-06
LOG2E = math.log2(math.e)
MASKED = -1e30
LANES = 128
VMEM_LIMIT = 48 * 1024 * 1024

NT = (((1,), (1,)), ((), ()))
NN = (((1,), (0,)), ((), ()))


def one_hot(ids, count):
    rows = lax.broadcasted_iota(jnp.int32, (count, ids.shape[1]), 0)
    if count <= 256:
        ids = jnp.where((ids < 0) | (ids >= count), -1, ids)
        rows, ids = rows.astype(jnp.float32).astype(jnp.bfloat16), ids.astype(jnp.float32).astype(jnp.bfloat16)
        return jnp.where(rows == ids, jnp.bfloat16(1), jnp.bfloat16(0))
    return jnp.where(rows == ids, 1.0, 0.0).astype(jnp.bfloat16)


def counted(hits):
    count = hits.shape[1]
    before = lax.broadcasted_iota(jnp.int32, (count, count), 0)
    after = lax.broadcasted_iota(jnp.int32, (count, count), 1)
    earlier = jnp.where(before < after, 1.0, 0.0).astype(jnp.bfloat16)
    return lax.dot_general(hits.astype(jnp.bfloat16), earlier, NN, preferred_element_type=jnp.float32)


def small(values):
    return values.astype(jnp.float32).astype(jnp.bfloat16)


def owner_ranks(rows, refresh_dev, cap):
    match = jnp.concatenate(rows, axis=0) == 0
    rank = counted(jnp.where(match, 1.0, 0.0)).astype(jnp.int32)
    return jnp.where(match, rank, -cap)


def one_hots(ids, high_count):
    return one_hot(ids >> 7, high_count), one_hot(ids & 127, LANES)


def bitmap(ids, high_count):
    high, low = one_hots(ids, high_count)
    return lax.dot_general(low, high, NT, preferred_element_type=jnp.float32).astype(jnp.bfloat16)


def lookup(one_map, pair):
    hit = lax.dot_general(one_map, pair[0], NN, preferred_element_type=jnp.float32)
    return jnp.sum(hit * pair[1].astype(jnp.float32), axis=0, keepdims=True)


def prep_kernel(place, table, fresh, ages, ref_ids, rows_out, meta_out, *, replicas):
    core = place[2]
    row = 0
    for source in (table, fresh):
        half = source.shape[0] // replicas
        rows_out[row : row + half, :] = source[pl.ds(pl.multiple_of(core * half, half), half), :]
        row += half
    width = table.shape[1]
    ref_rows, age_rows = ref_ids.shape[0], ages.shape[0]
    meta_out[:ref_rows, :] = ref_ids[...].astype(jnp.float32)
    weight = jnp.exp(-ages[...].astype(jnp.float32) / age_scale).astype(jnp.bfloat16).astype(jnp.float32)
    meta_out[ref_rows : ref_rows + age_rows, :] = jnp.log2(weight)
    line = ref_rows + age_rows
    for source in (table, fresh):
        for block in range(source.shape[0] // LANES):
            squares = jnp.zeros((LANES, LANES), jnp.float32)
            for chunk in range(width // LANES):
                values = source[block * LANES : (block + 1) * LANES, chunk * LANES : (chunk + 1) * LANES]
                values = values.astype(jnp.float32)
                squares += values * values
            mean = jnp.sum(squares.T, axis=0, keepdims=True) / width
            meta_out[line : line + 1, :] = lax.rsqrt(mean + epsilon) * (score_scale / width * LOG2E)
            line += 1


def meta_kernel(
    place, ref_ids, neg, log_weight, lw_out, row_out, pack_out, apply_out, own_out, target_out,
    *, rows_dev, refresh_dev, cap, replicas
):
    outer, inner, core = place[0], place[1], place[2]
    planes, plane_refresh = ref_ids.shape
    plane_rows = log_weight.shape[1]
    owners_plane = plane_rows // rows_dev
    high_count = planes * plane_rows // LANES
    own_owner = outer * owners_plane + inner
    share = cap // replicas
    plane_ids = ref_ids[0:1, :]
    column = lax.broadcasted_iota(jnp.int32, (1, plane_rows), 1)
    table_ids = (outer * owners_plane + (inner ^ (column // rows_dev))) * rows_dev + column % rows_dev

    pair = one_hots(jnp.concatenate([table_ids, plane_ids], axis=1), high_count)
    all_ids = jnp.concatenate([ref_ids[plane : plane + 1, :] for plane in range(planes)], axis=1)
    refreshed = lookup(bitmap(all_ids, high_count), (pair[0][:, :plane_rows], pair[1][:, :plane_rows])) > 0.5
    row_out[:, :plane_rows] = jnp.where(refreshed, -1, table_ids).astype(jnp.float32)
    row_out[:, plane_rows:] = plane_ids.astype(jnp.float32)
    own_out[...] = refreshed[:, :rows_dev].astype(jnp.int32)
    weights = jnp.where(refreshed, MASKED, log_weight[...])
    weights = jnp.concatenate([weights, jnp.zeros((1, plane_refresh), jnp.float32)], axis=1)
    for group in range(planes):
        hit = lookup(bitmap(neg[group : group + 1, :], high_count), pair)
        lw_out[group : group + 1, :] = jnp.where(hit > 0.5, weights, MASKED)

    pairs = [(plane, side) for plane in range(planes) for side in range(owners_plane)]

    def ids_of(plane, side):
        return ref_ids[plane : plane + 1, side * refresh_dev : (side + 1) * refresh_dev]

    sent = [ids_of(0, side) // rows_dev - ((outer ^ plane) * owners_plane + inner) for plane, side in pairs]
    taken = [ids_of(plane, side) // rows_dev - own_owner for plane, side in pairs]
    rank = owner_ranks(sent + taken, refresh_dev, cap)
    own_slots = owners_plane * cap
    codes = [jnp.full((1, refresh_dev), -1, jnp.int32)] * owners_plane
    for i, (plane, side) in enumerate(pairs):
        size = share if plane else cap
        base = own_slots + ((plane - 1) * owners_plane + side) * share if plane else side * cap
        sends = rank[i : i + 1, :] - (core * share if plane else 0)
        codes[side] = jnp.where((sends >= 0) & (sends < size), base + sends, codes[side])
        took = rank[len(pairs) + i : len(pairs) + i + 1, :]
        slot = jnp.where(took < 0, -1, ((took // share) ^ core) * share + took % share if plane else took)
        row = jnp.where(took < 0, 0, ids_of(plane, side) - own_owner * rows_dev)
        kinds = lax.broadcasted_iota(jnp.int32, (8, refresh_dev), 0)
        digits = jnp.where(kinds == 0, row // 16, jnp.where(kinds == 1, row % 16, 1))
        found = lax.dot_general(small(digits), one_hot(slot, cap), NT, preferred_element_type=jnp.float32)
        found = found.astype(jnp.int32)
        target = jnp.where(found[2:3, :] > 0, found[0:1, :] * 16 + found[1:2, :], -1)
        if plane == 0:
            target_out[:, base : base + cap] = target
            continue
        for part in range(replicas):
            first = base + part * (planes - 1) * owners_plane * share
            target_out[:, first : first + share] = target[:, part * share : (part + 1) * share]
    pack_out[...] = one_hot(jnp.concatenate(codes, axis=1), pack_out.shape[0])
    rows = lax.broadcasted_iota(jnp.int32, apply_out.shape, 0)
    apply_out[...] = jnp.where(rows == target_out[...], 1.0, 0.0)


def piece_offset(place, piece):
    column, size, flip, by_core = piece
    if flip is None:
        return column
    column += (place[2] ^ flip) * size
    if by_core is not None:
        column += (place[2] ^ by_core) * size * 2
    return pl.multiple_of(column, size)


def pack_kernel(place, select, *refs, pieces):
    *buffers, out = refs
    selects = [select[:, pl.ds(piece_offset(place, column), size)] for _, _, size, column in pieces]
    values = [buffers[source][start : start + size, :] for source, start, size, _ in pieces]
    selects, values = jnp.concatenate(selects, axis=1), jnp.concatenate(values, axis=0)
    out[...] = lax.dot_general(selects, values, NN, preferred_element_type=jnp.float32).astype(jnp.bfloat16)


def apply_kernel(select, table, *refs):
    *arrived, out = refs
    values = jnp.concatenate([block[...] for block in arrived], axis=0)
    fresh = lax.dot_general(select[...].astype(jnp.bfloat16), values, NN, preferred_element_type=jnp.float32)
    hit = jnp.sum(select[...], axis=1, keepdims=True) > 0.5
    out[...] = jnp.where(hit, fresh, table[...].astype(jnp.float32)).astype(jnp.bfloat16)


def to_lanes(row):
    return jnp.broadcast_to(row, (LANES, LANES)).T


def score_kernel(place, *refs, pieces, sources):
    positive, log_weight, row_ids, scale = refs[sources : sources + 4]
    out, total, pos_total, q_scale, pos_b, chosen = refs[-6:]
    queries = refs[0]
    count, width = queries.shape
    if sources == 2:
        at_end = (place[0] == 0) | (place[0] == 3)
        chosen[...] = jnp.where(at_end, refs[0][...], refs[1][...])
        queries = chosen
    for block in range(count // LANES):
        part = slice(block * LANES, (block + 1) * LANES)
        values = queries[part, :].astype(jnp.float32)
        squares = jnp.sum(values * values, axis=1, keepdims=True)
        q_scale[part, :] = jnp.broadcast_to(lax.rsqrt(squares / width + epsilon), (LANES, LANES))
        pos_b[part, :] = to_lanes(positive[block : block + 1, :])
    total[...] = jnp.zeros_like(total)
    pos_total[...] = jnp.zeros_like(pos_total)
    refs = refs[sources + 4 : -6]

    def product(group):
        rows = [refs[source][start : start + size, :] for source, start, size, _ in group]
        rows = rows[0] if len(rows) == 1 else jnp.concatenate(rows, axis=0)
        return lax.dot_general(queries[...], rows, NT, preferred_element_type=jnp.float32)

    narrow = [piece for piece in pieces if piece[2] < 256]
    groups = [[piece] for piece in pieces if piece[2] >= 256] + [narrow[i : i + 2] for i in range(0, len(narrow), 2)]
    following = product(groups[0])
    for i, group in enumerate(groups):
        raw = following
        if i + 1 < len(groups):
            following = product(groups[i + 1])
        columns = []
        for _, _, size, column in group:
            columns += [piece_offset(place, column) + chunk * LANES for chunk in range(size // LANES)]
        for top in range(0, count, 64):
            part = slice(top, top + 64)
            sums, positives = total[part, :], pos_total[part, :]
            query_scale, wanted = q_scale[part, :], pos_b[part, :]
            for chunk, first in enumerate(columns):
                cols = pl.ds(first, LANES)
                powers = raw[part, chunk * LANES : (chunk + 1) * LANES] * query_scale
                powers = powers * scale[:, cols] + log_weight[:, cols]
                sums = sums + jnp.exp2(powers)
                positives = positives + jnp.where(wanted == row_ids[:, cols], powers, 0.0)
            total[part, :] = sums
            pos_total[part, :] = positives
    for block in range(count // LANES):
        part = slice(block * LANES, (block + 1) * LANES)
        out[0, block : block + 1, :] = jnp.sum(total[part, :].T, axis=0, keepdims=True)
        out[1, block : block + 1, :] = jnp.sum(pos_total[part, :].T, axis=0, keepdims=True)


def whole(memory=pltpu.VMEM):
    return pl.BlockSpec(memory_space=memory)


def call(kernel, name, outs, place, *operands, scratch=(), **options):
    specs = [whole()] * len(operands)
    if place is not None:
        specs = [whole(pltpu.SMEM)] + specs
        operands = (place, *operands)
    return pl.pallas_call(
        functools.partial(kernel, **options),
        out_shape=tuple(outs),
        in_specs=specs,
        out_specs=tuple(whole() for _ in outs),
        scratch_shapes=list(scratch),
        compiler_params=pltpu.CompilerParams(vmem_limit_bytes=VMEM_LIMIT),
        cost_estimate=pl.CostEstimate(flops=1, bytes_accessed=1, transcendentals=0),
        name=name,
    )(*operands)


def swap(values, axis, flip):
    return lax.ppermute(values, axis, [(i, i ^ flip) for i in range(lax.axis_size(axis))])


def gather_line(values, small):
    planes = lax.axis_size("outer")
    if planes != 4:
        return [(swap(values, "outer", s),) for s in range(1, planes)], small
    middle, outward = [(1, 2), (2, 1)], [(1, 0), (2, 3)]
    beside = swap(values, "outer", 1)
    across = lax.ppermute(values, "outer", middle)
    beside, across, small = lax.optimization_barrier((beside, across, small))
    from_end = lax.ppermute(beside, "outer", middle)
    to_end = lax.ppermute(across, "outer", outward)
    last = lax.ppermute(from_end, "outer", outward)
    return [(beside,), (to_end, from_end), (last, across)], small


def on_device(table, ages, refresh_ids, fresh_rows, neg_ids, queries, pos_ids):
    rows_dev, width = table.shape
    refresh_dev = refresh_ids.shape[0]
    planes = lax.axis_size("outer")
    owners_plane = lax.axis_size("inner")
    replicas = lax.axis_size("query")
    owners = planes * owners_plane
    query_count = queries.shape[0]
    list_size = neg_ids.shape[1]
    place = jnp.stack([lax.axis_index(name) for name in ("outer", "inner", "query")]).astype(jnp.int32)
    plane_rows = owners_plane * rows_dev
    plane_refresh = owners_plane * refresh_dev
    all_rows = plane_rows + plane_refresh
    cap_each = max(2, (2 * refresh_dev + owners - 1) // owners)
    cap = owners_plane * cap_each
    share = cap // replicas
    table_half, fresh_half = rows_dev // replicas, refresh_dev // replicas
    bf16, f32 = jnp.bfloat16, jnp.float32

    meta_lines = (2 * refresh_dev + 2 * rows_dev) // LANES
    rows_half, meta = call(
        prep_kernel,
        "prep",
        [jax.ShapeDtypeStruct((table_half + fresh_half, width), bf16), jax.ShapeDtypeStruct((meta_lines, LANES), f32)],
        place,
        table,
        fresh_rows,
        ages.reshape(-1, LANES),
        refresh_ids.reshape(-1, LANES),
        replicas=replicas,
    )
    metas = jnp.stack([meta] + [swap(meta, "inner", s) for s in range(1, owners_plane)])
    cuts = [refresh_dev, rows_dev, rows_dev, refresh_dev]
    ends = [sum(cuts[: i + 1]) // LANES for i in range(len(cuts))]

    def piece(i):
        return metas[:, ends[i] - cuts[i] // LANES : ends[i]].reshape(1, -1)

    ref_plane, log_weight_plane = piece(0), piece(1)
    scale_plane = jnp.concatenate([piece(2), piece(3)], axis=1)
    line = jnp.concatenate([ref_plane[0], neg_ids[0].astype(f32), pos_ids.astype(f32)])
    got_queries, line = gather_line(queries, line)
    got_queries = [(queries,)] + got_queries
    lines = jnp.stack([line] + [swap(line, "outer", s) for s in range(1, planes)])
    ref_all = lines[:, :plane_refresh].astype(jnp.int32)
    neg_line = lines[:, plane_refresh : plane_refresh + list_size].astype(jnp.int32)
    positive = lines[:, plane_refresh + list_size :].reshape(planes, -1, LANES)

    lw, row_ids, pack, apply_to, own = call(
        meta_kernel,
        "meta",
        [
            jax.ShapeDtypeStruct((planes, all_rows), f32),
            jax.ShapeDtypeStruct((1, all_rows), f32),
            jax.ShapeDtypeStruct((cap + (planes - 1) * share, plane_refresh), bf16),
            jax.ShapeDtypeStruct((rows_dev, planes * cap), f32),
            jax.ShapeDtypeStruct((1, rows_dev), jnp.int32),
        ],
        place,
        ref_all,
        neg_line,
        log_weight_plane,
        rows_dev=rows_dev,
        scratch=[pltpu.VMEM((1, planes * cap), jnp.int32)],
        refresh_dev=refresh_dev,
        cap=cap_each,
        replicas=replicas,
    )
    new_ages = jnp.where(own.reshape(rows_dev) > 0, 0, ages)

    if replicas == 2 and owners_plane == 4:
        axes = ("inner", "query")
        first = [(2 * i + c, 2 * (i ^ (1 + c)) + c) for i in range(4) for c in range(2)]
        second = [(2 * i + c, 2 * (i ^ (2 - c)) + c) for i in range(4) for c in range(2)]
        near = lax.ppermute(rows_half, axes, first)
        side = lax.ppermute(rows_half, axes, second)
        far = lax.ppermute(near, axes, second)
        buffers = [table, fresh_rows]
        table_pieces = [(0, 0, rows_dev, (0, rows_dev, None, None))]
        fresh_pieces = [(1, 0, refresh_dev, (0, refresh_dev, None, None))]
        for slot, by_core, mine in ((1, 0, near), (1, 1, side), (3, None, far)):
            for flip, rows in enumerate((mine, swap(mine, "query", 1))):
                by = None if by_core is None else by_core ^ flip
                table_pieces.append((len(buffers), 0, table_half, (slot * rows_dev, table_half, flip, by)))
                fresh_pieces.append((len(buffers), table_half, fresh_half, (slot * refresh_dev, fresh_half, flip, by)))
                buffers.append(rows)
    else:
        got_rows = [rows_half] + [swap(rows_half, "inner", s) for s in range(1, owners_plane)]
        gathered = lax.all_gather(jnp.stack(got_rows), "query", axis=0)
        gathered = jnp.swapaxes(gathered, 0, 1)
        buffers = [
            gathered[:, :, :table_half].reshape(plane_rows, width),
            gathered[:, :, table_half:].reshape(plane_refresh, width),
        ]
        table_pieces = [(0, i * 512, 512, (i * 512, 512, None, None)) for i in range(plane_rows // 512)]
        fresh_pieces = [(1, i * 512, 512, (i * 512, 512, None, None)) for i in range(plane_refresh // 512)]

    def shift(pieces, columns):
        return [(a, b, c, (d[0] + columns, *d[1:])) for a, b, c, d in pieces]

    (packed,) = call(
        pack_kernel, "pack", [jax.ShapeDtypeStruct((pack.shape[0], width), bf16)], place, pack, *buffers, pieces=fresh_pieces
    )
    parts = []
    for s in range(1, planes):
        first = cap + (s - 1) * share
        parts.append(swap(packed[first : first + share], "outer", s))
    parts, own_queries = lax.optimization_barrier((jnp.concatenate(parts), queries))
    got_queries[0] = (own_queries,)
    arrived = [packed[:cap], parts] + [swap(parts, "query", flip) for flip in range(1, replicas)]

    pieces = table_pieces + shift(fresh_pieces, plane_rows)
    mine = None
    for s in [*range(1, planes), 0]:
        (partial,) = call(
            score_kernel,
            "score",
            [jax.ShapeDtypeStruct((2, query_count // LANES, LANES), f32)],
            place,
            *got_queries[s],
            positive[s],
            lw[s : s + 1],
            row_ids,
            scale_plane,
            *buffers,
            scratch=[pltpu.VMEM((query_count, LANES), f32)] * 4 + [pltpu.VMEM((query_count, width), bf16)],
            pieces=pieces,
            sources=len(got_queries[s]),
        )
        if s:
            partial = swap(partial, "outer", s)
        mine = partial if mine is None else mine + partial
    (new_table,) = call(
        apply_kernel, "apply", [jax.ShapeDtypeStruct(table.shape, bf16)], None, apply_to, table, *arrived
    )
    loss = (jnp.log2(mine[0]) - mine[1]) * math.log(2.0)
    return new_table, new_ages, loss.reshape(query_count)


def solution(mesh):
    owners, replicas = mesh.shape["index"], mesh.shape["query"]
    inner = 1 << (int(math.log2(owners)) // 2)
    split = Mesh(mesh.devices.reshape(owners // inner, inner, replicas), ("outer", "inner", "query"))
    index = ("outer", "inner")
    placed = (
        P(index, None),
        P(index),
        P(index),
        P(index, None),
        P(index, None),
        P(("outer", "inner", "query"), None),
        P(("outer", "inner", "query")),
    )
    return jax.shard_map(
        on_device,
        mesh=split,
        in_specs=placed,
        out_specs=(P(index, None), P(index), P(("outer", "inner", "query"))),
        check_vma=False,
    )
```
